32 devices in a mesh: grp: 2 (over y), space: 4 (over z), tm: 4 (over x, core).
Axes of the slice: x: 2, y: 2, z: 4, core: 2. Of those that a mesh axis runs over, the one named last changes fastest.
Arguments:
- snapshots: bfloat16 [128, 512, 1024], P(('grp', 'tm'), None, 'space'), parts along dimension 0, may hold values from -100 to 100
- entry_weight: float32 [2048], P(('grp', 'space')), parts along dimension 0, may hold values from 0.3 to 9
- freq_index: int32 [256], replicated, may hold values from 0 to 256, as said below
Outputs:
- energy_map: float32 [512, 1024], P(('grp', 'tm'), 'space'), parts along dimension 0
- filters: float32 [512, 2, 64, 64], P(('grp', 'tm')), parts along dimension 0
The draws below stay inside these ranges and needn't reach their ends.
There are 2 independent parts, one for each index of `grp`. The reference program is written for one: setup_inputs(seed, part) draws one part's arguments, and reference() takes and returns one part's arrays. A program takes and returns all parts, laid end to end along the dimension named above; an argument that names none is the same for every part. Nothing has to cross between parts.
Inputs may be any that keep to these rules, and one draw needn't show every extreme that they name: `freq_index`: distinct and increasing; 0 and 256 are always retained.
All inputs are finite; a program needn't handle non-finite values.
Results may differ from the reference program's by a relative error of at most 0.0019.
Values may be sent and summed in bfloat16 or wider, within the bound.
No kernel may reach another device: no remote copies, remote signals or barrier semaphores. Data moves between devices by JAX's collectives and lax.ppermute only.
A program may use at most 128 MiB of HBM per device.

```python
import math
import jax
import jax.numpy as jnp
from jax import lax

NB = 64
NFFT = 512
NF = 256
STATE = 1024


def draw_snapshots(key, part):
    key = jax.random.fold_in(key, 23)
    keys = jax.random.split(key, 5)
    count = 8
    decay = jnp.exp(-math.log(10.0) / 7.0 * jnp.arange(count, dtype=jnp.float32))
    values = jax.random.truncated_normal(keys[0], -4.0, 4.0, (NB, NFFT, STATE), jnp.float32)
    fields = jax.random.truncated_normal(keys[1], -3.0, 3.0, (count, NFFT, STATE), jnp.float32)
    scale = jnp.exp(jax.random.uniform(keys[4], (NB, 1, 1), jnp.float32, 0.0, math.log(10.0)))
    mixing = decay[None, :] * jax.random.truncated_normal(keys[2], -2.5, 2.5, (NB, count), jnp.float32)
    offsets = jax.random.randint(keys[3], (NB, count), 0, NFFT // 8).astype(jnp.int32)
    times = jnp.arange(NFFT, dtype=jnp.int32)
    for field_number in range(count):
        index = (times[None, :] + offsets[:, field_number][:, None]) % NFFT
        values = values + mixing[:, field_number][:, None, None] * fields[field_number][index]
    return (scale / 3.0 * values).astype(jnp.bfloat16)


def draw_entry_weight(key, part):
    key = jax.random.fold_in(key, 11)
    position = jnp.arange(STATE, dtype=jnp.float32) / STATE
    rise = jnp.exp(math.log(3.0) * position)
    factor = jnp.exp(jax.random.uniform(key, (STATE,), jnp.float32, 0.0, math.log(10.0)))
    return (0.3 * rise * factor).astype(jnp.float32)


def draw_freq_index(key, part):
    key = jax.random.fold_in(key, 37)
    inner = jax.random.permutation(key, NFFT // 2 - 1).astype(jnp.int32) + 1
    ends = jnp.array([0, NFFT // 2], dtype=jnp.int32)
    chosen = jnp.concatenate([ends, inner[:NF - 2]])
    return jnp.sort(chosen).astype(jnp.int32)


def setup_inputs(seed: int = 0, part: int = 0) -> dict:
    key_list = jax.random.split(jax.random.key(seed), 4)
    own_keys = jax.random.split(jax.random.fold_in(key_list[3], part), 4)
    return {
        "snapshots": draw_snapshots(jax.random.fold_in(jax.random.fold_in(key_list[3], part), 71), part),
        "entry_weight": draw_entry_weight(jax.random.fold_in(jax.random.fold_in(key_list[3], part), 71), part),
        "freq_index": draw_freq_index(jax.random.fold_in(key_list[3], 71), part),
    }


def dft_table(freq_index, length):
    times = jnp.arange(length, dtype=jnp.int32)
    phase = freq_index[:, None] * times[None, :] % length
    angle = 2.0 * math.pi / length * phase.astype(jnp.float32)
    window = 0.5 - 0.5 * jnp.cos(2.0 * math.pi / length * times.astype(jnp.float32))
    norm = math.sqrt(0.375 * length)
    rows = jnp.stack([window * jnp.cos(angle), -window * jnp.sin(angle)], axis=1) / norm
    return rows.reshape(2 * freq_index.shape[0], length).astype(jnp.bfloat16)

def reference(snapshots, entry_weight, freq_index):
    table = dft_table(freq_index, NFFT)
    root = jnp.sqrt(entry_weight)

    def transform(block):
        return (jnp.dot(table.astype(jnp.float32), block.astype(jnp.float32), preferred_element_type=jnp.float32) * root[None, :]).astype(jnp.bfloat16)
    spectra = lax.map(transform, snapshots)
    spectra = jnp.moveaxis(spectra.reshape(NB, NF, 2, STATE), 1, 0)
    highest = lax.Precision.HIGHEST
    eye = jnp.eye(NB, dtype=jnp.float32)

    def per_freq(spectrum):
        real_z = spectrum[:, 0].astype(jnp.float32)
        imag_z = spectrum[:, 1].astype(jnp.float32)
        real_gram = (jnp.dot(real_z, real_z.T, precision=highest) + jnp.dot(imag_z, imag_z.T, precision=highest)) / NB
        imag_gram = (jnp.dot(real_z, imag_z.T, precision=highest) - jnp.dot(imag_z, real_z.T, precision=highest)) / NB
        shift = jnp.trace(real_gram) / NB
        shifted = real_gram + shift * eye
        system = jnp.concatenate([jnp.concatenate([shifted, -imag_gram], 1), jnp.concatenate([imag_gram, shifted], 1)], 0)
        solved = jnp.linalg.solve(system, jnp.concatenate([real_gram, imag_gram], 0))
        filt = jnp.stack([solved[:NB], solved[NB:]], 0)
        rounded = lax.optimization_barrier(filt.astype(jnp.bfloat16)).astype(jnp.float32)
        real_part = jnp.dot(real_z.T, rounded[0], precision=highest) - jnp.dot(imag_z.T, rounded[1], precision=highest)
        imag_part = jnp.dot(real_z.T, rounded[1], precision=highest) + jnp.dot(imag_z.T, rounded[0], precision=highest)
        energy = lax.optimization_barrier(jnp.sum(real_part * real_part + imag_part * imag_part, axis=1))
        return (filt, STATE * energy / jnp.sum(energy))
    filters, energy_map = lax.map(per_freq, spectra)
    return (energy_map, filters)
```

```python
import functools
import math

import jax
import jax.numpy as jnp
from jax import lax
from jax.experimental import pallas as pl
from jax.experimental.pallas import tpu as pltpu
from jax.sharding import PartitionSpec as P

F32 = jnp.float32
BF16 = jnp.bfloat16
VMEM_LIMIT = 30 * 1024 * 1024
DIRECT_LIMIT = 8
LANES = 128


def params(**kwargs):
    return pltpu.CompilerParams(vmem_limit_bytes=VMEM_LIMIT, **kwargs)


def whole_spec():
    return pl.BlockSpec(memory_space=pltpu.VMEM)


def dot(a, b):
    return lax.dot_general(a, b, (((1,), (0,)), ((), ())), preferred_element_type=F32)


def cos_sin(phase, length):
    quarter = length // 4
    eighth = length // 8
    shifted = phase + eighth
    low = (shifted & (quarter - 1)) - eighth
    quadrant = (shifted // quarter) & 3
    x = low.astype(F32) * F32(2.0 * math.pi / length)
    x2 = x * x
    cos = F32(1 / 40320)
    for c in (-1 / 720, 1 / 24, -0.5, 1.0):
        cos = cos * x2 + F32(c)
    sin = F32(1 / 362880)
    for c in (-1 / 5040, 1 / 120, -1 / 6, 1.0):
        sin = sin * x2 + F32(c)
    sin = sin * x
    odd = (quadrant & 1) == 1
    c0 = jnp.where(odd, sin, cos)
    s0 = jnp.where(odd, cos, sin)
    c1 = jnp.where((quadrant == 1) | (quadrant == 2), -c0, c0)
    s1 = jnp.where(quadrant >= 2, -s0, s0)
    return c1, s1


def transform_kernel(peers, count, first, step_blocks, freq_ref, root_ref, snap_ref, *refs):
    outs, (table, wide) = refs[:peers], refs[peers:]
    me = lax.axis_index("tm")
    length = snap_ref.shape[1]
    entries = snap_ref.shape[2]
    rows = peers * count
    per_peer = freq_ref.shape[0] // peers
    step = pl.program_id(0)

    @pl.when(step == 0)
    def _():
        times = lax.broadcasted_iota(jnp.int32, (8, length), 1)
        sub = lax.broadcasted_iota(jnp.int32, (8, length), 0)
        window = 0.5 - 0.5 * cos_sin(times, length)[0]
        scaled = window / F32(math.sqrt(0.375 * length))

        def eight(group):
            base = group * 8
            peer = base // count
            start = jnp.bitwise_xor(me, peer) * per_peer + first + (base - peer * count)
            k = jnp.zeros((8, length), jnp.int32)
            for i in range(8):
                k = jnp.where(sub == i, freq_ref[start + i], k)
            cos, sin = cos_sin((k * times) & (length - 1), length)
            return scaled * cos, -(scaled * sin)

        for pair in range(rows // 16):
            re0, im0 = eight(2 * pair)
            re1, im1 = eight(2 * pair + 1)
            table[16 * pair : 16 * pair + 16, :] = jnp.concatenate([re0, re1], 0).astype(BF16)
            table[rows + 16 * pair : rows + 16 * pair + 16, :] = jnp.concatenate(
                [im0, im1], 0
            ).astype(BF16)

    root = jnp.sqrt(root_ref[...])
    blocks = outs[0].shape[1]
    tiles = entries // LANES
    for i in range(step_blocks):
        spec = dot(table[...], snap_ref[i]) * root
        b = step * step_blocks + i
        for tile in range(tiles):
            lanes = slice(tile * LANES, (tile + 1) * LANES)
            wide[tile, pl.ds(b, rows, stride=blocks), :] = spec[:rows, lanes]
            wide[tiles + tile, pl.ds(b, rows, stride=blocks), :] = spec[rows:, lanes]

    @pl.when(step == pl.num_programs(0) - 1)
    def _():
        for peer in range(peers):
            for j in range(count):
                at = (peer * count + j) * blocks
                for tile in range(2 * tiles):
                    lanes = slice(tile * LANES, (tile + 1) * LANES)
                    outs[peer][j, :, lanes] = wide[tile, at : at + blocks, :].astype(BF16)


def transform(snapshots, weight, freq_index, peers, count, first):
    blocks, length, entries = snapshots.shape
    step_blocks = 4
    return pl.pallas_call(
        functools.partial(transform_kernel, peers, count, first, step_blocks),
        grid=(blocks // step_blocks,),
        in_specs=[
            pl.BlockSpec(memory_space=pltpu.SMEM),
            pl.BlockSpec((1, entries), lambda b: (0, 0)),
            pl.BlockSpec((step_blocks, length, entries), lambda b: (b, 0, 0)),
        ],
        out_specs=[pl.BlockSpec((count, blocks, 2 * entries), lambda b: (0, 0, 0))] * peers,
        out_shape=[jax.ShapeDtypeStruct((count, blocks, 2 * entries), BF16)] * peers,
        scratch_shapes=[
            pltpu.VMEM((2 * peers * count, length), BF16),
            pltpu.VMEM((2 * entries // LANES, peers * count * blocks, LANES), F32),
        ],
        compiler_params=params(),
        cost_estimate=pl.CostEstimate(
            flops=4 * peers * count * length * entries * blocks,
            bytes_accessed=2 * blocks * length * entries + 4 * peers * count * blocks * entries,
            transcendentals=0,
        ),
        name="transform",
    )(freq_index, weight, snapshots)


def lane_low(shape, half):
    return lax.broadcasted_iota(jnp.int32, shape, 1) < half


def swap(x):
    return pltpu.roll(x, x.shape[1] // 2, 1)


def pack(compact):
    half = compact.shape[0]
    both = compact + swap(compact)
    low = lane_low((half // 2, 2 * half), half)
    return jnp.where(low, both[: half // 2], both[half // 2 :])


def unpack(packed):
    rows, half = packed.shape[0], packed.shape[1] // 2
    low = lane_low(packed.shape, half)
    other = swap(packed)
    both = jnp.concatenate(
        [jnp.where(low, packed, other), jnp.where(low, other, packed)], 0
    )
    turned = jnp.transpose(jnp.concatenate([both, both], 0))[:half]
    low = lane_low(both.shape, half)
    return 0.5 * jnp.where(low, both + turned, both - turned)


def full(compact):
    half = compact.shape[0]
    turned = swap(compact)
    low = lane_low(compact.shape, half)
    return jnp.concatenate([compact, jnp.where(low, -turned, turned)], 0)


def slot_owner(direct, slot):
    return jnp.bitwise_xor(lax.axis_index("space"), slot) if direct else slot


def gram_kernel(peers, slots, direct, *refs):
    pieces, merged, grams = refs[:peers], refs[peers], refs[peers + 1 :]
    me = lax.axis_index("tm")
    here = pieces[0].shape[1]
    entries = pieces[0].shape[2] // 2
    blocks = here * peers
    per_slot = pieces[0].shape[0] // slots
    stage = None
    if here % 16:
        grams, stage = grams[:-1], grams[-1]
    low = lane_low((blocks, 2 * blocks), blocks)
    for slot in range(slots):
        owner = slot_owner(direct, slot)
        for i in range(per_slot):
            f = owner * per_slot + i
            if stage is None:
                for peer in range(peers):
                    start = pl.multiple_of(jnp.bitwise_xor(me, peer) * here, here)
                    merged[f, pl.ds(start, here), :] = pieces[peer][f]
                z = merged[f]
            else:
                for peer in range(peers):
                    start = pl.multiple_of(jnp.bitwise_xor(me, peer) * here, here)
                    stage[pl.ds(start, here), :] = pieces[peer][f].astype(F32)
                z = stage[...].astype(BF16)
                merged[f] = z
            w = jnp.concatenate([z[:, :entries], z[:, entries:]], 0)
            s = lax.dot_general(w, w, (((1,), (1,)), ((), ())), preferred_element_type=F32)
            s = s * F32(1.0 / blocks)
            top, bottom = s[:blocks], swap(s[blocks:])
            compact = jnp.where(low, top + bottom, top - bottom)
            if direct:
                grams[slot][i] = pack(compact)
            else:
                grams[0][f] = pack(compact)


def gram(pieces, slots, direct):
    peers = len(pieces)
    count, here, width = pieces[0].shape
    blocks = here * peers
    if direct:
        shapes = [(count // slots, blocks // 2, 2 * blocks)] * slots
    else:
        shapes = [(count, blocks // 2, 2 * blocks)]
    out = pl.pallas_call(
        functools.partial(gram_kernel, peers, slots, direct),
        in_specs=[whole_spec()] * peers,
        out_specs=[whole_spec()] * (1 + len(shapes)),
        out_shape=[jax.ShapeDtypeStruct((count, blocks, width), BF16)]
        + [jax.ShapeDtypeStruct(s, F32) for s in shapes],
        scratch_shapes=[pltpu.VMEM((blocks, width), F32)] if here % 16 else [],
        compiler_params=params(),
        cost_estimate=pl.CostEstimate(
            flops=4 * count * blocks * blocks * width,
            bytes_accessed=4 * count * blocks * width + 4 * count * blocks * blocks,
            transcendentals=0,
        ),
        name="gram",
    )(*pieces)
    return out[0], out[1:]


def split(x):
    high = x.astype(BF16)
    return high, (x - high.astype(F32)).astype(BF16)


def each(fn, *lists):
    return [fn(*items) for items in zip(*lists)]


def solve_kernel(parts, *refs):
    ins, out = refs[:parts], refs[parts]
    number, half_rows, width = ins[0].shape
    half = width // 2
    shape = (half, width)
    row = lax.broadcasted_iota(jnp.int32, shape, 0)
    lane = lax.broadcasted_iota(jnp.int32, shape, 1)
    eye = jnp.where(row == lane, F32(1), F32(0))

    def load(i):
        total = ins[0][i]
        for r in ins[1:]:
            total = total + r[i]
        return unpack(total)

    grams = [load(i) for i in range(number)]
    shift = each(lambda g: jnp.sum(g * eye, keepdims=True) * F32(1.0 / half), grams)
    system = each(lambda g, m: g / m + eye, grams, shift)
    parts_a = each(lambda a: split(full(a)), system)
    high = [p[0] for p in parts_a]
    both = parts_a

    low_end, high_end = 1.0, float(half + 1)
    mid, radius = (high_end + low_end) / 2, (high_end - low_end) / 2
    ratio = mid / radius
    t = 2 * ratio * ratio - 1
    scale = 2.0 / (radius * radius * t)
    x = each(lambda a: F32(scale) * (F32(2 * mid) * eye - a), system)
    for kind in ("one", "one", "one", "two", "last"):
        xb = each(lambda v: v.astype(BF16), x)
        if kind == "one":
            residual = each(lambda v, a: eye - dot(v, a), xb, high)
        else:
            residual = each(lambda v, a: eye - (dot(v, a[0]) + dot(v, a[1])), xb, both)
        xw = each(lambda v: v.astype(F32), xb)
        xf = each(lambda v: full(v).astype(BF16), xw)
        step = each(lambda r, v: dot(r.astype(BF16), v), residual, xf)
        if kind == "last":
            factor = 1.0
        else:
            t_next = 2 * t * t - 1
            factor = 2 * t * t / t_next
            t = t_next
        x = each(lambda v, s: F32(factor) * (v + s), xw, step)
    packed = each(lambda v: pack(eye - v), x)
    for i in range(number):
        out[i * half_rows : (i + 1) * half_rows, :] = packed[i]
    filters = each(unpack, packed)
    rounded = each(lambda c: c.astype(BF16), filters)
    turned = each(lambda c: full(c.astype(F32)).astype(BF16), rounded)
    split_g = each(split, grams)
    moved = each(lambda g, c: dot(g[0], c) + dot(g[1], c), split_g, turned)
    energy = each(
        lambda c, h: jnp.sum(c.astype(F32) * h, keepdims=True) * F32(half), rounded, moved
    )
    tail = out.shape[0] - number * half_rows
    line = lax.broadcasted_iota(jnp.int32, (tail, width), 0)
    totals = jnp.ones((tail, width), F32)
    for i in range(number):
        totals = jnp.where(line == i, energy[i], totals)
    out[number * half_rows :, :] = totals


def tail_rows(number):
    return -(-number // 8) * 8


def solve(parts):
    number, half_rows, width = parts[0].shape
    rows = number * half_rows + tail_rows(number)
    return pl.pallas_call(
        functools.partial(solve_kernel, len(parts)),
        in_specs=[whole_spec()] * len(parts),
        out_specs=whole_spec(),
        out_shape=jax.ShapeDtypeStruct((rows, width), F32),
        compiler_params=params(),
        cost_estimate=pl.CostEstimate(
            flops=40 * number * width * width * width,
            bytes_accessed=4 * number * half_rows * width * (len(parts) + 1),
            transcendentals=0,
        ),
        name="filters",
    )(*parts)


def energy_kernel(slots, direct, carried, merged, *refs):
    pieces, refs = refs[: len(refs) - 2 - carried], refs[len(refs) - 2 - carried :]
    energies, filters = refs[-2:]
    count, blocks, width = merged.shape
    entries = width // 2
    per_slot = count // slots
    half_rows = blocks // 2
    states = entries * lax.axis_size("space")
    for slot in range(slots):
        owner = slot_owner(direct, slot)
        piece = pieces[slot] if direct else pieces[0].at[slot]
        for i in range(per_slot):
            f = owner * per_slot + i
            compact = unpack(piece[i * half_rows : (i + 1) * half_rows, :])
            filters[f, 0] = compact[:, :blocks]
            filters[f, 1] = compact[:, blocks:]
            wide = compact.astype(BF16).astype(F32)
            both = full(wide).astype(BF16)
            z = merged[f]
            w = jnp.concatenate([z[:, :entries], z[:, entries:]], 0)
            r = dot(both, w)
            energy = jnp.sum(r * r, axis=0, keepdims=True)
            at = per_slot * half_rows + i
            total = piece[at : at + 1, 0:1]
            energies[pl.ds(f, 1), :] = energy * (F32(states) / total)


def filtered(merged, pieces, slots, direct, carry, owned, first):
    count, blocks, width = merged.shape
    entries = width // 2
    carried = 0 if carry is None else 2
    args = [merged, *pieces] + ([] if carry is None else list(carry))
    fixed = 1 + len(pieces)
    index = first // count
    out = pl.pallas_call(
        functools.partial(energy_kernel, slots, direct, carried),
        grid=(1,),
        in_specs=[whole_spec()] * fixed + [pl.BlockSpec(memory_space=pl.ANY)] * carried,
        out_specs=[
            pl.BlockSpec((count, entries), lambda g: (index, 0)),
            pl.BlockSpec((count, 2, blocks, blocks), lambda g: (index, 0, 0, 0)),
        ],
        out_shape=[
            jax.ShapeDtypeStruct((owned, entries), F32),
            jax.ShapeDtypeStruct((owned, 2, blocks, blocks), F32),
        ],
        input_output_aliases={fixed: 0, fixed + 1: 1} if carried else {},
        compiler_params=params(),
        cost_estimate=pl.CostEstimate(
            flops=4 * count * blocks * blocks * width,
            bytes_accessed=2 * count * blocks * width + 24 * count * blocks * blocks,
            transcendentals=0,
        ),
        name="energy",
    )(*args)
    return out


def exchange(arrays, axis):
    size = lax.axis_size(axis)
    got = [arrays[0]]
    for offset in range(1, size):
        pairs = [(i, i ^ offset) for i in range(size)]
        got.append(lax.ppermute(arrays[offset], axis, pairs))
    return got


def on_device(snapshots, entry_weight, freq_index):
    peers = lax.axis_size("tm")
    slots = lax.axis_size("space")
    retained = freq_index.shape[0]
    owned = retained // peers
    direct = slots <= DIRECT_LIMIT
    chunks = 4
    while chunks > 1 and (owned // chunks) % max(slots, 8):
        chunks //= 2
    count = owned // chunks
    weight = entry_weight.reshape(1, -1)
    carry = None
    for c in range(chunks):
        first = c * count
        sent = transform(snapshots, weight, freq_index, peers, count, first)
        merged, grams = gram(exchange(sent, "tm"), slots, direct)
        if direct:
            parts = exchange(grams, "space")
        else:
            parts = [lax.psum_scatter(grams[0], "space", scatter_dimension=0, tiled=True)]
        own = solve(parts)
        if direct:
            pieces = exchange([own] * slots, "space")
        else:
            pieces = [lax.all_gather(own, "space", axis=0, tiled=False)]
        carry = filtered(merged, pieces, slots, direct, carry, owned, first)
    return (carry[0], carry[1])


def solution(mesh):
    in_specs = (P(("grp", "tm"), None, "space"), P(("grp", "space")), P())
    out_specs = (P(("grp", "tm"), "space"), P(("grp", "tm"), None, None, None))
    return jax.shard_map(
        on_device, mesh=mesh, in_specs=in_specs, out_specs=out_specs, check_vma=False
    )
```

```python
import functools
import math

import jax
import jax.numpy as jnp
from jax import lax
from jax.experimental import pallas as pl
from jax.experimental.pallas import tpu as pltpu
from jax.sharding import PartitionSpec as P

F32 = jnp.float32
BF16 = jnp.bfloat16
VMEM_LIMIT = 30 * 1024 * 1024
DIRECT_LIMIT = 8
LANES = 128


def params(**kwargs):
    return pltpu.CompilerParams(vmem_limit_bytes=VMEM_LIMIT, **kwargs)


def whole_spec():
    return pl.BlockSpec(memory_space=pltpu.VMEM)


TOKEN = jax.ShapeDtypeStruct((8, LANES), F32)


def light():
    return pl.CostEstimate(flops=1024, bytes_accessed=1024, transcendentals=0)


def in_hbm(x):
    return pltpu.with_memory_space_constraint(x, pltpu.HBM)


def any_spec():
    return pl.BlockSpec(memory_space=pl.ANY)


def dot(a, b):
    return lax.dot_general(a, b, (((1,), (0,)), ((), ())), preferred_element_type=F32)


def cos_sin(phase, length):
    quarter = length // 4
    eighth = length // 8
    shifted = phase + eighth
    low = (shifted & (quarter - 1)) - eighth
    quadrant = (shifted // quarter) & 3
    x = low.astype(F32) * F32(2.0 * math.pi / length)
    x2 = x * x
    cos = F32(1 / 40320)
    for c in (-1 / 720, 1 / 24, -0.5, 1.0):
        cos = cos * x2 + F32(c)
    sin = F32(1 / 362880)
    for c in (-1 / 5040, 1 / 120, -1 / 6, 1.0):
        sin = sin * x2 + F32(c)
    sin = sin * x
    odd = (quadrant & 1) == 1
    c0 = jnp.where(odd, sin, cos)
    s0 = jnp.where(odd, cos, sin)
    c1 = jnp.where((quadrant == 1) | (quadrant == 2), -c0, c0)
    s1 = jnp.where(quadrant >= 2, -s0, s0)
    return c1, s1


def transform_kernel(peers, count, first, group, *refs):
    freq_hbm, weight_hbm, snap_hbm = refs[:3]
    outs, token = refs[-peers - 8 : -8], refs[-8]
    freq, weight, snap, table, wide, small_sem, snap_sem = refs[-7:]
    blocks, length, entries = snap.shape
    steps = blocks // group
    get_freq = pltpu.make_async_copy(freq_hbm, freq, small_sem.at[0])
    get_weight = pltpu.make_async_copy(weight_hbm, weight, small_sem.at[1])
    get_snap = [
        pltpu.make_async_copy(
            snap_hbm.at[pl.ds(i * group, group)], snap.at[pl.ds(i * group, group)], snap_sem.at[i]
        )
        for i in range(steps)
    ]
    token[...] = jnp.zeros_like(token)
    get_freq.start()
    for get in get_snap:
        get.start()
    get_weight.start()

    me = lax.axis_index("tm")
    rows = peers * count
    per_peer = freq.shape[0] // peers
    times = lax.broadcasted_iota(jnp.int32, (8, length), 1)
    sub = lax.broadcasted_iota(jnp.int32, (8, length), 0)
    window = 0.5 - 0.5 * cos_sin(times, length)[0]
    scaled = window / F32(math.sqrt(0.375 * length))
    get_freq.wait()

    def eight(index):
        base = index * 8
        peer = base // count
        start = jnp.bitwise_xor(me, peer) * per_peer + first + (base - peer * count)
        k = jnp.zeros((8, length), jnp.int32)
        for i in range(8):
            k = jnp.where(sub == i, freq[start + i], k)
        cos, sin = cos_sin((k * times) & (length - 1), length)
        return scaled * cos, -(scaled * sin)

    for pair in range(rows // 16):
        re0, im0 = eight(2 * pair)
        re1, im1 = eight(2 * pair + 1)
        table[16 * pair : 16 * pair + 16, :] = jnp.concatenate([re0, re1], 0).astype(BF16)
        table[rows + 16 * pair : rows + 16 * pair + 16, :] = jnp.concatenate(
            [im0, im1], 0
        ).astype(BF16)

    get_weight.wait()
    root = jnp.sqrt(weight[...])
    tiles = entries // LANES
    for step in range(steps):
        get_snap[step].wait()
        for b in range(step * group, (step + 1) * group):
            spec = dot(table[...], snap[b]) * root
            for tile in range(tiles):
                lanes = slice(tile * LANES, (tile + 1) * LANES)
                wide[tile, pl.ds(b, rows, stride=blocks), :] = spec[:rows, lanes]
                wide[tiles + tile, pl.ds(b, rows, stride=blocks), :] = spec[rows:, lanes]
    for peer in range(peers):
        for j in range(count):
            at = (peer * count + j) * blocks
            for tile in range(2 * tiles):
                lanes = slice(tile * LANES, (tile + 1) * LANES)
                outs[peer][j, :, lanes] = wide[tile, at : at + blocks, :].astype(BF16)


def transform(snapshots, weight, freq_index, peers, count, first, after):
    blocks, length, entries = snapshots.shape
    group = min(blocks, 4)
    hbm = pl.BlockSpec(memory_space=pltpu.HBM)
    return pl.pallas_call(
        functools.partial(transform_kernel, peers, count, first, group),
        in_specs=[hbm] * 3 + [any_spec()] * len(after),
        out_specs=[whole_spec()] * (peers + 1),
        out_shape=[jax.ShapeDtypeStruct((count, blocks, 2 * entries), BF16)] * peers + [TOKEN],
        scratch_shapes=[
            pltpu.SMEM(freq_index.shape, jnp.int32),
            pltpu.VMEM(weight.shape, F32),
            pltpu.VMEM(snapshots.shape, BF16),
            pltpu.VMEM((2 * peers * count, length), BF16),
            pltpu.VMEM((2 * entries // LANES, peers * count * blocks, LANES), F32),
            pltpu.SemaphoreType.DMA((2,)),
            pltpu.SemaphoreType.DMA((blocks // group,)),
        ],
        compiler_params=params(),
        cost_estimate=light(),
        name="transform",
    )(in_hbm(freq_index), in_hbm(weight), in_hbm(snapshots), *after)


def lane_low(shape, half):
    return lax.broadcasted_iota(jnp.int32, shape, 1) < half


def swap(x):
    return pltpu.roll(x, x.shape[1] // 2, 1)


def pack(compact):
    half = compact.shape[0]
    both = compact + swap(compact)
    low = lane_low((half // 2, 2 * half), half)
    return jnp.where(low, both[: half // 2], both[half // 2 :])


def unpack(packed):
    rows, half = packed.shape[0], packed.shape[1] // 2
    low = lane_low(packed.shape, half)
    other = swap(packed)
    both = jnp.concatenate(
        [jnp.where(low, packed, other), jnp.where(low, other, packed)], 0
    )
    turned = jnp.transpose(jnp.concatenate([both, both], 0))[:half]
    low = lane_low(both.shape, half)
    return 0.5 * jnp.where(low, both + turned, both - turned)


def full(compact):
    half = compact.shape[0]
    turned = swap(compact)
    low = lane_low(compact.shape, half)
    return jnp.concatenate([compact, jnp.where(low, -turned, turned)], 0)


def slot_owner(direct, slot):
    return jnp.bitwise_xor(lax.axis_index("space"), slot) if direct else slot


def gram_kernel(peers, slots, direct, after, *refs):
    pieces, refs = refs[:peers], refs[peers + after :]
    merged, token, grams = refs[0], refs[1], refs[2:]
    token[...] = jnp.zeros_like(token)
    me = lax.axis_index("tm")
    here = pieces[0].shape[1]
    entries = pieces[0].shape[2] // 2
    blocks = here * peers
    per_slot = pieces[0].shape[0] // slots
    stage = None
    if here % 16:
        grams, stage = grams[:-1], grams[-1]
    low = lane_low((blocks, 2 * blocks), blocks)
    for slot in range(slots):
        owner = slot_owner(direct, slot)
        for i in range(per_slot):
            f = owner * per_slot + i
            if stage is None:
                for peer in range(peers):
                    start = pl.multiple_of(jnp.bitwise_xor(me, peer) * here, here)
                    merged[f, pl.ds(start, here), :] = pieces[peer][f]
                z = merged[f]
            else:
                for peer in range(peers):
                    start = pl.multiple_of(jnp.bitwise_xor(me, peer) * here, here)
                    stage[pl.ds(start, here), :] = pieces[peer][f].astype(F32)
                z = stage[...].astype(BF16)
                merged[f] = z
            w = jnp.concatenate([z[:, :entries], z[:, entries:]], 0)
            s = lax.dot_general(w, w, (((1,), (1,)), ((), ())), preferred_element_type=F32)
            s = s * F32(1.0 / blocks)
            top, bottom = s[:blocks], swap(s[blocks:])
            compact = jnp.where(low, top + bottom, top - bottom)
            if direct:
                grams[slot][i] = pack(compact)
            else:
                grams[0][f] = pack(compact)


def gram(pieces, slots, direct, after):
    peers = len(pieces)
    count, here, width = pieces[0].shape
    blocks = here * peers
    if direct:
        shapes = [(count // slots, blocks // 2, 2 * blocks)] * slots
    else:
        shapes = [(count, blocks // 2, 2 * blocks)]
    out = pl.pallas_call(
        functools.partial(gram_kernel, peers, slots, direct, len(after)),
        in_specs=[whole_spec()] * peers + [any_spec()] * len(after),
        out_specs=[whole_spec()] * (2 + len(shapes)),
        out_shape=[jax.ShapeDtypeStruct((count, blocks, width), BF16), TOKEN]
        + [jax.ShapeDtypeStruct(s, F32) for s in shapes],
        scratch_shapes=[pltpu.VMEM((blocks, width), F32)] if here % 16 else [],
        compiler_params=params(),
        cost_estimate=light(),
        name="gram",
    )(*pieces, *after)
    return out[0], out[2:], out[1]


def split(x):
    high = x.astype(BF16)
    return high, (x - high.astype(F32)).astype(BF16)


def each(fn, *lists):
    return [fn(*items) for items in zip(*lists)]


def solve_kernel(parts, *refs):
    ins, out, token = refs[:parts], refs[-2], refs[-1]
    token[...] = jnp.zeros_like(token)
    number, half_rows, width = ins[0].shape
    half = width // 2
    shape = (half, width)
    row = lax.broadcasted_iota(jnp.int32, shape, 0)
    lane = lax.broadcasted_iota(jnp.int32, shape, 1)
    eye = jnp.where(row == lane, F32(1), F32(0))

    def load(i):
        total = ins[0][i]
        for r in ins[1:]:
            total = total + r[i]
        return unpack(total)

    grams = [load(i) for i in range(number)]
    shift = each(lambda g: jnp.sum(g * eye, keepdims=True) * F32(1.0 / half), grams)
    system = each(lambda g, m: g / m + eye, grams, shift)
    parts_a = each(lambda a: split(full(a)), system)
    high = [p[0] for p in parts_a]
    both = parts_a

    low_end, high_end = 1.0, float(half + 1)
    mid, radius = (high_end + low_end) / 2, (high_end - low_end) / 2
    ratio = mid / radius
    t = 2 * ratio * ratio - 1
    scale = 2.0 / (radius * radius * t)
    x = each(lambda a: F32(scale) * (F32(2 * mid) * eye - a), system)
    for kind in ("one", "one", "one", "two", "last"):
        xb = each(lambda v: v.astype(BF16), x)
        if kind == "one":
            residual = each(lambda v, a: eye - dot(v, a), xb, high)
        else:
            residual = each(lambda v, a: eye - (dot(v, a[0]) + dot(v, a[1])), xb, both)
        xw = each(lambda v: v.astype(F32), xb)
        xf = each(lambda v: full(v).astype(BF16), xw)
        step = each(lambda r, v: dot(r.astype(BF16), v), residual, xf)
        if kind == "last":
            factor = 1.0
        else:
            t_next = 2 * t * t - 1
            factor = 2 * t * t / t_next
            t = t_next
        x = each(lambda v, s: F32(factor) * (v + s), xw, step)
    packed = each(lambda v: pack(eye - v), x)
    for i in range(number):
        out[i * half_rows : (i + 1) * half_rows, :] = packed[i]
    filters = each(unpack, packed)
    rounded = each(lambda c: c.astype(BF16), filters)
    turned = each(lambda c: full(c.astype(F32)).astype(BF16), rounded)
    split_g = each(split, grams)
    moved = each(lambda g, c: dot(g[0], c) + dot(g[1], c), split_g, turned)
    energy = each(
        lambda c, h: jnp.sum(c.astype(F32) * h, keepdims=True) * F32(half), rounded, moved
    )
    tail = out.shape[0] - number * half_rows
    line = lax.broadcasted_iota(jnp.int32, (tail, width), 0)
    totals = jnp.ones((tail, width), F32)
    for i in range(number):
        totals = jnp.where(line == i, energy[i], totals)
    out[number * half_rows :, :] = totals


def tail_rows(number):
    return -(-number // 8) * 8


def solve(parts, after):
    number, half_rows, width = parts[0].shape
    rows = number * half_rows + tail_rows(number)
    return pl.pallas_call(
        functools.partial(solve_kernel, len(parts)),
        in_specs=[whole_spec()] * len(parts) + [any_spec()] * len(after),
        out_specs=[whole_spec()] * 2,
        out_shape=[jax.ShapeDtypeStruct((rows, width), F32), TOKEN],
        compiler_params=params(),
        cost_estimate=light(),
        name="filters",
    )(*parts, *after)


def energy_kernel(slots, direct, number, first, merged, *refs):
    pieces = refs[:number]
    energies_out, filters_out, token, energies, filters, energies_sem, filters_sem = refs[-7:]
    token[...] = jnp.zeros_like(token)
    count, blocks, width = merged.shape
    entries = width // 2
    per_slot = count // slots
    half_rows = blocks // 2
    states = entries * lax.axis_size("space")
    puts = []
    for slot in range(slots):
        owner = slot_owner(direct, slot)
        piece = pieces[slot] if direct else pieces[0].at[slot]
        for i in range(per_slot):
            f = owner * per_slot + i
            compact = unpack(piece[i * half_rows : (i + 1) * half_rows, :])
            filters[f, 0] = compact[:, :blocks]
            filters[f, 1] = compact[:, blocks:]
            wide = compact.astype(BF16).astype(F32)
            both = full(wide).astype(BF16)
            z = merged[f]
            w = jnp.concatenate([z[:, :entries], z[:, entries:]], 0)
            r = dot(both, w)
            energy = jnp.sum(r * r, axis=0, keepdims=True)
            at = per_slot * half_rows + i
            total = piece[at : at + 1, 0:1]
            energies[pl.ds(f, 1), :] = energy * (F32(states) / total)
        put = pltpu.make_async_copy(
            filters.at[pl.ds(owner * per_slot, per_slot)],
            filters_out.at[pl.ds(first + owner * per_slot, per_slot)],
            filters_sem.at[slot],
        )
        put.start()
        puts.append(put)
    put = pltpu.make_async_copy(
        energies, energies_out.at[pl.ds(first, count)], energies_sem.at[0]
    )
    put.start()
    for p in [*puts, put]:
        p.wait()


def filtered(merged, pieces, slots, direct, carry, owned, first, after):
    count, blocks, width = merged.shape
    entries = width // 2
    fixed = 1 + len(pieces)
    args = [merged, *pieces] + ([] if carry is None else list(carry)) + list(after)
    hbm = pl.BlockSpec(memory_space=pltpu.HBM)
    return pl.pallas_call(
        functools.partial(energy_kernel, slots, direct, len(pieces), first),
        in_specs=[whole_spec()] * fixed
        + ([] if carry is None else [hbm] * 2)
        + [any_spec()] * len(after),
        out_specs=[hbm] * 2 + [whole_spec()],
        out_shape=[
            jax.ShapeDtypeStruct((owned, entries), F32),
            jax.ShapeDtypeStruct((owned, 2, blocks, blocks), F32),
            TOKEN,
        ],
        input_output_aliases={} if carry is None else {fixed: 0, fixed + 1: 1},
        scratch_shapes=[
            pltpu.VMEM((count, entries), F32),
            pltpu.VMEM((count, 2, blocks, blocks), F32),
            pltpu.SemaphoreType.DMA((1,)),
            pltpu.SemaphoreType.DMA((slots,)),
        ],
        compiler_params=params(),
        cost_estimate=light(),
        name="energy",
    )(*args)


def exchange(arrays, axis):
    size = lax.axis_size(axis)
    got = [arrays[0]]
    for offset in range(1, size):
        pairs = [(i, i ^ offset) for i in range(size)]
        got.append(lax.ppermute(arrays[offset], axis, pairs))
    return got


def plan(owned, slots):
    unit = max(slots, 8)
    if owned % unit or owned // unit < 8:
        return [owned]
    return [owned // 4] * 4


def order(chunks):
    if chunks != 4:
        return [(stage, c) for c in range(chunks) for stage in "TGFE"]
    steps = "T0 T1 G0 T2 G1 F0 T3 G2 F1 E0 F2 E1 G3 E2 F3 E3"
    return [(step[0], int(step[1:])) for step in steps.split()]


def on_device(snapshots, entry_weight, freq_index):
    peers = lax.axis_size("tm")
    slots = lax.axis_size("space")
    owned = freq_index.shape[0] // peers
    sizes = plan(owned, slots)
    starts = [sum(sizes[:c]) for c in range(len(sizes))]
    chunks = len(sizes)
    direct = [False] * chunks
    weight = entry_weight.reshape(1, -1)
    sent, merged, parts, pieces = {}, {}, {}, {}
    carry = None
    token = []

    def do_transform(c):
        nonlocal token
        out = transform(snapshots, weight, freq_index, peers, sizes[c], starts[c], token)
        token = [out[peers]]
        sent[c] = exchange(out[:peers], "tm")
        if c + 1 < chunks:
            token.append(sent[c][1])

    def do_gram(c):
        nonlocal token
        merged[c], grams, done = gram(sent[c], slots, direct[c], token)
        token = [done]
        if direct[c]:
            parts[c] = exchange(grams, "space")
        else:
            parts[c] = [lax.psum_scatter(grams[0], "space", scatter_dimension=0, tiled=True)]

    def do_solve(c):
        nonlocal token
        own, done = solve(parts[c], token)
        token = [done]
        if direct[c]:
            pieces[c] = exchange([own] * slots, "space")
        else:
            pieces[c] = [lax.all_gather(own, "space", axis=0, tiled=False)]

    def do_energy(c):
        nonlocal token, carry
        *carry, done = filtered(
            merged[c], pieces[c], slots, direct[c], carry, owned, starts[c], token
        )
        token = [done]

    stages = {"T": do_transform, "G": do_gram, "F": do_solve, "E": do_energy}
    for stage, c in order(chunks):
        stages[stage](c)
    return (carry[0], carry[1])


def solution(mesh):
    in_specs = (P(("grp", "tm"), None, "space"), P(("grp", "space")), P())
    out_specs = (P(("grp", "tm"), "space"), P(("grp", "tm"), None, None, None))
    return jax.shard_map(
        on_device, mesh=mesh, in_specs=in_specs, out_specs=out_specs, check_vma=False
    )
```

```python
import functools
import math

import jax
import jax.numpy as jnp
from jax import lax
from jax.experimental import pallas as pl
from jax.experimental.pallas import tpu as pltpu
from jax.sharding import PartitionSpec as P

F32 = jnp.float32
BF16 = jnp.bfloat16
VMEM_LIMIT = 30 * 1024 * 1024
LANES = 128


def params(**kwargs):
    return pltpu.CompilerParams(vmem_limit_bytes=VMEM_LIMIT, **kwargs)


def whole_spec():
    return pl.BlockSpec(memory_space=pltpu.VMEM)


TOKEN = jax.ShapeDtypeStruct((8, LANES), F32)


def light():
    return pl.CostEstimate(flops=1024, bytes_accessed=1024, transcendentals=0)


def in_hbm(x):
    return pltpu.with_memory_space_constraint(x, pltpu.HBM)


def any_spec():
    return pl.BlockSpec(memory_space=pl.ANY)


def dot(a, b):
    return lax.dot_general(a, b, (((1,), (0,)), ((), ())), preferred_element_type=F32)


def cos_sin(phase, length):
    quarter = length // 4
    eighth = length // 8
    shifted = phase + eighth
    low = (shifted & (quarter - 1)) - eighth
    quadrant = (shifted // quarter) & 3
    x = low.astype(F32) * F32(2.0 * math.pi / length)
    x2 = x * x
    cos = F32(1 / 40320)
    for c in (-1 / 720, 1 / 24, -0.5, 1.0):
        cos = cos * x2 + F32(c)
    sin = F32(1 / 362880)
    for c in (-1 / 5040, 1 / 120, -1 / 6, 1.0):
        sin = sin * x2 + F32(c)
    sin = sin * x
    odd = (quadrant & 1) == 1
    c0 = jnp.where(odd, sin, cos)
    s0 = jnp.where(odd, cos, sin)
    c1 = jnp.where((quadrant == 1) | (quadrant == 2), -c0, c0)
    s1 = jnp.where(quadrant >= 2, -s0, s0)
    return c1, s1


def transform_kernel(peers, parts, group, *refs):
    freq_hbm, weight_hbm, snap_hbm = refs[:3]
    outs, token = refs[-peers * len(parts) - 8 : -8], refs[-8]
    freq, weight, snap, table, wide, small_sem, snap_sem = refs[-7:]
    blocks, length, entries = snap.shape
    steps = blocks // group
    get_freq = pltpu.make_async_copy(freq_hbm, freq, small_sem.at[0])
    get_weight = pltpu.make_async_copy(weight_hbm, weight, small_sem.at[1])
    get_snap = [
        pltpu.make_async_copy(
            snap_hbm.at[pl.ds(i * group, group)], snap.at[pl.ds(i * group, group)], snap_sem.at[i]
        )
        for i in range(steps)
    ]
    token[...] = jnp.zeros_like(token)
    get_freq.start()
    for get in get_snap:
        get.start()
    get_weight.start()

    me = lax.axis_index("tm")
    groups = [
        (peer, first + j)
        for first, count in parts
        for peer in range(peers)
        for j in range(0, count, 8)
    ]
    rows = 8 * len(groups)
    per_peer = freq.shape[0] // peers
    times = lax.broadcasted_iota(jnp.int32, (8, length), 1)
    sub = lax.broadcasted_iota(jnp.int32, (8, length), 0)
    window = 0.5 - 0.5 * cos_sin(times, length)[0]
    scaled = window / F32(math.sqrt(0.375 * length))
    get_freq.wait()

    def eight(index):
        peer, offset = groups[index]
        start = jnp.bitwise_xor(me, peer) * per_peer + offset
        k = jnp.zeros((8, length), jnp.int32)
        for i in range(8):
            k = jnp.where(sub == i, freq[start + i], k)
        cos, sin = cos_sin((k * times) & (length - 1), length)
        return scaled * cos, -(scaled * sin)

    for pair in range(rows // 16):
        re0, im0 = eight(2 * pair)
        re1, im1 = eight(2 * pair + 1)
        table[16 * pair : 16 * pair + 16, :] = jnp.concatenate([re0, re1], 0).astype(BF16)
        table[rows + 16 * pair : rows + 16 * pair + 16, :] = jnp.concatenate(
            [im0, im1], 0
        ).astype(BF16)

    get_weight.wait()
    root = jnp.sqrt(weight[...])
    tiles = entries // LANES
    for step in range(steps):
        get_snap[step].wait()
        for b in range(step * group, (step + 1) * group):
            spec = dot(table[...], snap[b]) * root
            for tile in range(tiles):
                lanes = slice(tile * LANES, (tile + 1) * LANES)
                wide[tile, pl.ds(b, rows, stride=blocks), :] = spec[:rows, lanes]
                wide[tiles + tile, pl.ds(b, rows, stride=blocks), :] = spec[rows:, lanes]
    at = 0
    for out in outs:
        for j in range(out.shape[0]):
            for tile in range(2 * tiles):
                lanes = slice(tile * LANES, (tile + 1) * LANES)
                out[j, :, lanes] = wide[tile, at : at + blocks, :].astype(BF16)
            at += blocks


def transform(snapshots, weight, freq_index, peers, parts, after):
    blocks, length, entries = snapshots.shape
    group = min(blocks, 4)
    total = peers * sum(count for _, count in parts)
    shapes = [
        jax.ShapeDtypeStruct((count, blocks, 2 * entries), BF16)
        for _, count in parts
        for _ in range(peers)
    ]
    hbm = pl.BlockSpec(memory_space=pltpu.HBM)
    out = pl.pallas_call(
        functools.partial(transform_kernel, peers, parts, group),
        in_specs=[hbm] * 3 + [any_spec()] * len(after),
        out_specs=[whole_spec()] * (len(shapes) + 1),
        out_shape=shapes + [TOKEN],
        scratch_shapes=[
            pltpu.SMEM(freq_index.shape, jnp.int32),
            pltpu.VMEM(weight.shape, F32),
            pltpu.VMEM(snapshots.shape, BF16),
            pltpu.VMEM((2 * total, length), BF16),
            pltpu.VMEM((2 * entries // LANES, total * blocks, LANES), F32),
            pltpu.SemaphoreType.DMA((2,)),
            pltpu.SemaphoreType.DMA((blocks // group,)),
        ],
        compiler_params=params(),
        cost_estimate=light(),
        name="transform",
    )(in_hbm(freq_index), in_hbm(weight), in_hbm(snapshots), *after)
    return [out[i * peers : (i + 1) * peers] for i in range(len(parts))], out[-1]


def lane_low(shape, half):
    return lax.broadcasted_iota(jnp.int32, shape, 1) < half


def swap(x):
    return pltpu.roll(x, x.shape[1] // 2, 1)


def pack(compact):
    half = compact.shape[0]
    both = compact + swap(compact)
    low = lane_low((half // 2, 2 * half), half)
    return jnp.where(low, both[: half // 2], both[half // 2 :])


def unpack(packed):
    rows, half = packed.shape[0], packed.shape[1] // 2
    low = lane_low(packed.shape, half)
    other = swap(packed)
    both = jnp.concatenate(
        [jnp.where(low, packed, other), jnp.where(low, other, packed)], 0
    )
    turned = jnp.transpose(jnp.concatenate([packed, packed], 0))
    turned = jnp.where(lane_low((half, half), rows), turned[:half], turned[half:])
    turned = jnp.concatenate([turned, turned], 1)
    low = lane_low(both.shape, half)
    return 0.5 * jnp.where(low, both + turned, both - turned)


def full(compact):
    half = compact.shape[0]
    turned = swap(compact)
    low = lane_low(compact.shape, half)
    return jnp.concatenate([compact, jnp.where(low, -turned, turned)], 0)


def slot_owner(direct, slot):
    return jnp.bitwise_xor(lax.axis_index("space") & 1, slot) if direct else slot


def gram_kernel(peers, slots, direct, after, *refs):
    pieces, refs = refs[:peers], refs[peers + after :]
    merged, token, grams = refs[0], refs[1], refs[2:]
    token[...] = jnp.zeros_like(token)
    me = lax.axis_index("tm")
    here = pieces[0].shape[1]
    entries = pieces[0].shape[2] // 2
    blocks = here * peers
    per_slot = pieces[0].shape[0] // slots
    stage = None
    if here % 16:
        grams, stage = grams[:-1], grams[-1]
    low = lane_low((blocks, 2 * blocks), blocks)
    for slot in range(slots):
        owner = slot_owner(direct, slot)
        for i in range(per_slot):
            f = owner * per_slot + i
            if stage is None:
                for peer in range(peers):
                    start = pl.multiple_of(jnp.bitwise_xor(me, peer) * here, here)
                    merged[f, pl.ds(start, here), :] = pieces[peer][f]
                z = merged[f]
            else:
                for peer in range(peers):
                    start = pl.multiple_of(jnp.bitwise_xor(me, peer) * here, here)
                    stage[pl.ds(start, here), :] = pieces[peer][f].astype(F32)
                z = stage[...].astype(BF16)
                merged[f] = z
            w = jnp.concatenate([z[:, :entries], z[:, entries:]], 0)
            s = lax.dot_general(w, w, (((1,), (1,)), ((), ())), preferred_element_type=F32)
            s = s * F32(1.0 / blocks)
            top, bottom = s[:blocks], swap(s[blocks:])
            compact = jnp.where(low, top + bottom, top - bottom)
            if direct:
                grams[slot][i] = pack(compact)
            else:
                grams[0][f] = pack(compact)


def gram(pieces, slots, direct, after):
    peers = len(pieces)
    count, here, width = pieces[0].shape
    blocks = here * peers
    if direct:
        shapes = [(count // slots, blocks // 2, 2 * blocks)] * slots
    else:
        shapes = [(count, blocks // 2, 2 * blocks)]
    out = pl.pallas_call(
        functools.partial(gram_kernel, peers, slots, direct, len(after)),
        in_specs=[whole_spec()] * peers + [any_spec()] * len(after),
        out_specs=[whole_spec()] * (2 + len(shapes)),
        out_shape=[jax.ShapeDtypeStruct((count, blocks, width), BF16), TOKEN]
        + [jax.ShapeDtypeStruct(s, F32) for s in shapes],
        scratch_shapes=[pltpu.VMEM((blocks, width), F32)] if here % 16 else [],
        compiler_params=params(),
        cost_estimate=light(),
        name="gram",
    )(*pieces, *after)
    return out[0], out[2:], out[1]


def add_kernel(one, two, *refs):
    out, token = refs[-2:]
    token[...] = jnp.zeros_like(token)
    out[...] = one[...] + two[...]


def add(one, two, after):
    return pl.pallas_call(
        add_kernel,
        in_specs=[whole_spec()] * 2 + [any_spec()] * len(after),
        out_specs=[whole_spec()] * 2,
        out_shape=[jax.ShapeDtypeStruct(one.shape, F32), TOKEN],
        compiler_params=params(),
        cost_estimate=light(),
        name="add",
    )(one, two, *after)


def split(x):
    high = x.astype(BF16)
    return high, (x - high.astype(F32)).astype(BF16)


def each(fn, *lists):
    return [fn(*items) for items in zip(*lists)]


def solve_kernel(parts, *refs):
    ins, out, token = refs[:parts], refs[-2], refs[-1]
    token[...] = jnp.zeros_like(token)
    number, half_rows, width = ins[0].shape
    half = width // 2
    shape = (half, width)
    row = lax.broadcasted_iota(jnp.int32, shape, 0)
    lane = lax.broadcasted_iota(jnp.int32, shape, 1)
    eye = jnp.where(row == lane, F32(1), F32(0))

    def load(i):
        total = ins[0][i]
        for r in ins[1:]:
            total = total + r[i]
        return unpack(total)

    grams = [load(i) for i in range(number)]
    shift = each(lambda g: jnp.sum(g * eye, keepdims=True) * F32(1.0 / half), grams)
    system = each(lambda g, m: g / m + eye, grams, shift)
    parts_a = each(lambda a: split(full(a)), system)
    high = [p[0] for p in parts_a]
    both = parts_a

    low_end, high_end = 1.0, float(half + 1)
    mid, radius = (high_end + low_end) / 2, (high_end - low_end) / 2
    ratio = mid / radius
    t = 2 * ratio * ratio - 1
    scale = 2.0 / (radius * radius * t)
    x = each(lambda a: F32(scale) * (F32(2 * mid) * eye - a), system)
    for kind in ("one", "one", "one", "two", "last"):
        xb = each(lambda v: v.astype(BF16), x)
        if kind == "one":
            residual = each(lambda v, a: eye - dot(v, a), xb, high)
        else:
            residual = each(lambda v, a: eye - (dot(v, a[0]) + dot(v, a[1])), xb, both)
        xw = each(lambda v: v.astype(F32), xb)
        xf = each(lambda v: full(v).astype(BF16), xw)
        step = each(lambda r, v: dot(r.astype(BF16), v), residual, xf)
        if kind == "last":
            factor = 1.0
        else:
            t_next = 2 * t * t - 1
            factor = 2 * t * t / t_next
            t = t_next
        x = each(lambda v, s: F32(factor) * (v + s), xw, step)
    packed = each(lambda v: pack(eye - v), x)
    for i in range(number):
        out[i * half_rows : (i + 1) * half_rows, :] = packed[i]
    filters = each(unpack, packed)
    rounded = each(lambda c: c.astype(BF16), filters)
    turned = each(lambda c: full(c.astype(F32)).astype(BF16), rounded)
    split_g = each(split, grams)
    moved = each(lambda g, c: dot(g[0], c) + dot(g[1], c), split_g, turned)
    energy = each(
        lambda c, h: jnp.sum(c.astype(F32) * h, keepdims=True) * F32(half), rounded, moved
    )
    tail = out.shape[0] - number * half_rows
    line = lax.broadcasted_iota(jnp.int32, (tail, width), 0)
    totals = jnp.ones((tail, width), F32)
    for i in range(number):
        totals = jnp.where(line == i, energy[i], totals)
    out[number * half_rows :, :] = totals


def tail_rows(number):
    return -(-number // 8) * 8


def solve(parts, after):
    number, half_rows, width = parts[0].shape
    rows = number * half_rows + tail_rows(number)
    return pl.pallas_call(
        functools.partial(solve_kernel, len(parts)),
        in_specs=[whole_spec()] * len(parts) + [any_spec()] * len(after),
        out_specs=[whole_spec()] * 2,
        out_shape=[jax.ShapeDtypeStruct((rows, width), F32), TOKEN],
        compiler_params=params(),
        cost_estimate=light(),
        name="filters",
    )(*parts, *after)


def energy_kernel(slots, direct, number, first, merged, *refs):
    pieces = refs[:number]
    energies_out, filters_out, token, energies, filters, energies_sem, filters_sem = refs[-7:]
    token[...] = jnp.zeros_like(token)
    count, blocks, width = merged.shape
    entries = width // 2
    per_slot = count // slots
    half_rows = blocks // 2
    states = entries * lax.axis_size("space")
    puts = []
    for slot in range(slots):
        owner = slot_owner(direct, slot)
        piece = pieces[slot] if direct else pieces[0].at[slot]
        for begin in range(0, per_slot, 4):
            some = range(begin, min(begin + 4, per_slot))
            at = [owner * per_slot + i for i in some]
            packed = [piece[i * half_rows : (i + 1) * half_rows, :] for i in some]
            tail = per_slot * half_rows
            total = [piece[tail + i : tail + i + 1, 0:1] for i in some]
            z = [merged[f] for f in at]
            compact = each(unpack, packed)
            both = each(lambda c: full(c.astype(BF16).astype(F32)).astype(BF16), compact)
            w = each(lambda v: jnp.concatenate([v[:, :entries], v[:, entries:]], 0), z)
            r = each(dot, both, w)
            energy = each(
                lambda v, t: jnp.sum(v * v, axis=0, keepdims=True) * (F32(states) / t), r, total
            )
            for f, c, e in zip(at, compact, energy):
                filters[f, 0] = c[:, :blocks]
                filters[f, 1] = c[:, blocks:]
                energies[pl.ds(f, 1), :] = e
        put = pltpu.make_async_copy(
            filters.at[pl.ds(owner * per_slot, per_slot)],
            filters_out.at[pl.ds(first + owner * per_slot, per_slot)],
            filters_sem.at[slot],
        )
        put.start()
        puts.append(put)
    put = pltpu.make_async_copy(
        energies, energies_out.at[pl.ds(first, count)], energies_sem.at[0]
    )
    put.start()
    for p in [*puts, put]:
        p.wait()


def filtered(merged, pieces, slots, direct, carry, owned, first, after):
    count, blocks, width = merged.shape
    entries = width // 2
    fixed = 1 + len(pieces)
    args = [merged, *pieces] + ([] if carry is None else list(carry)) + list(after)
    hbm = pl.BlockSpec(memory_space=pltpu.HBM)
    return pl.pallas_call(
        functools.partial(energy_kernel, slots, direct, len(pieces), first),
        in_specs=[whole_spec()] * fixed
        + ([] if carry is None else [hbm] * 2)
        + [any_spec()] * len(after),
        out_specs=[hbm] * 2 + [whole_spec()],
        out_shape=[
            jax.ShapeDtypeStruct((owned, entries), F32),
            jax.ShapeDtypeStruct((owned, 2, blocks, blocks), F32),
            TOKEN,
        ],
        input_output_aliases={} if carry is None else {fixed: 0, fixed + 1: 1},
        scratch_shapes=[
            pltpu.VMEM((count, entries), F32),
            pltpu.VMEM((count, 2, blocks, blocks), F32),
            pltpu.SemaphoreType.DMA((1,)),
            pltpu.SemaphoreType.DMA((slots,)),
        ],
        compiler_params=params(),
        cost_estimate=light(),
        name="energy",
    )(*args)


def exchange(arrays, axis):
    size = lax.axis_size(axis)
    got = [arrays[0]]
    for offset in range(1, size):
        pairs = [(i, i ^ offset) for i in range(size)]
        got.append(lax.ppermute(arrays[offset], axis, pairs))
    return got


def plan(owned, slots):
    if slots != 4 or owned != 64:
        return [owned], (("T", 0), ("G", 0), ("F", 0), ("E", 0))
    return SIZES, ORDER


SIZES = [24, 24, 16]
ORDER = (
    ("T", 0), ("T", 1), ("G", 0), ("A", 0), ("G", 1), ("F", 0), ("A", 1), ("E", 0),
    ("G", 2), ("A", 2), ("F", 1), ("E", 1), ("F", 2), ("E", 2),
)


def permute(x, axis, offset):
    pairs = [(i, i ^ offset) for i in range(lax.axis_size(axis))]
    return lax.ppermute(x, axis, pairs)


def on_device(snapshots, entry_weight, freq_index):
    peers = lax.axis_size("tm")
    slots = lax.axis_size("space")
    owned = freq_index.shape[0] // peers
    sizes, order = plan(owned, slots)
    starts = [sum(sizes[:c]) for c in range(len(sizes))]
    paired = slots == 4
    halves = 2 if paired else slots
    weight = entry_weight.reshape(1, -1)
    sent, merged, grams, parts, pieces = {}, {}, {}, {}, {}
    carry = None
    token = []

    def do_transform(c):
        nonlocal token
        chunks = [0] if c == 0 else range(1, len(sizes))
        out, done = transform(
            snapshots, weight, freq_index, peers, [(starts[k], sizes[k]) for k in chunks], token
        )
        token = [done]
        for k, pieces_out in zip(chunks, out):
            sent[k] = [pieces_out[0]] + [
                permute(pieces_out[offset], "tm", offset) for offset in range(1, peers)
            ]

    def do_gram(c):
        nonlocal token
        merged[c], grams[c], done = gram(sent[c], halves, paired, token)
        token = [done]
        if paired:
            grams[c] = [grams[c][0], permute(grams[c][1], "space", 1)]
        else:
            parts[c] = [lax.psum_scatter(grams[c][0], "space", scatter_dimension=0, tiled=True)]

    def do_add(c):
        nonlocal token
        half, done = add(*grams[c], token)
        token = [done]
        parts[c] = [half, permute(half, "space", 2)]

    def do_solve(c):
        nonlocal token
        own, done = solve(parts[c], token)
        token = [done]
        if paired:
            pieces[c] = [own, permute(own, "space", 1)]
        else:
            pieces[c] = [lax.all_gather(own, "space", axis=0, tiled=False)]

    def do_energy(c):
        nonlocal token, carry
        *carry, done = filtered(
            merged[c], pieces[c], halves, paired, carry, owned, starts[c], token
        )
        token = [done]

    stages = {"T": do_transform, "G": do_gram, "A": do_add, "F": do_solve, "E": do_energy}
    for stage, c in order:
        stages[stage](c)
    return (carry[0], carry[1])


def solution(mesh):
    in_specs = (P(("grp", "tm"), None, "space"), P(("grp", "space")), P())
    out_specs = (P(("grp", "tm"), "space"), P(("grp", "tm"), None, None, None))
    return jax.shard_map(
        on_device, mesh=mesh, in_specs=in_specs, out_specs=out_specs, check_vma=False
    )
```

```python
import functools
import math

import jax
import jax.numpy as jnp
from jax import lax
from jax.experimental import pallas as pl
from jax.experimental.pallas import tpu as pltpu
from jax.sharding import PartitionSpec as P

F32 = jnp.float32
BF16 = jnp.bfloat16
VMEM_LIMIT = 30 * 1024 * 1024
LANES = 128


def params(**kwargs):
    return pltpu.CompilerParams(vmem_limit_bytes=VMEM_LIMIT, **kwargs)


def whole_spec():
    return pl.BlockSpec(memory_space=pltpu.VMEM)


TOKEN = jax.ShapeDtypeStruct((8, LANES), F32)


def light():
    return pl.CostEstimate(flops=1024, bytes_accessed=1024, transcendentals=0)


def in_hbm(x):
    return pltpu.with_memory_space_constraint(x, pltpu.HBM)


def any_spec():
    return pl.BlockSpec(memory_space=pl.ANY)


def dot(a, b):
    return lax.dot_general(a, b, (((1,), (0,)), ((), ())), preferred_element_type=F32)


def cos_sin(phase, length):
    quarter = length // 4
    eighth = length // 8
    shifted = phase + eighth
    low = (shifted & (quarter - 1)) - eighth
    quadrant = (shifted // quarter) & 3
    x = low.astype(F32) * F32(2.0 * math.pi / length)
    x2 = x * x
    cos = F32(1 / 40320)
    for c in (-1 / 720, 1 / 24, -0.5, 1.0):
        cos = cos * x2 + F32(c)
    sin = F32(1 / 362880)
    for c in (-1 / 5040, 1 / 120, -1 / 6, 1.0):
        sin = sin * x2 + F32(c)
    sin = sin * x
    odd = (quadrant & 1) == 1
    c0 = jnp.where(odd, sin, cos)
    s0 = jnp.where(odd, cos, sin)
    c1 = jnp.where((quadrant == 1) | (quadrant == 2), -c0, c0)
    s1 = jnp.where(quadrant >= 2, -s0, s0)
    return c1, s1


def transform_kernel(peers, parts, group, *refs):
    freq_hbm, weight_hbm, snap_hbm = refs[:3]
    outs, token = refs[-peers * len(parts) - 8 : -8], refs[-8]
    freq, weight, snap, table, wide, small_sem, snap_sem = refs[-7:]
    blocks, length, entries = snap.shape
    steps = blocks // group
    get_freq = pltpu.make_async_copy(freq_hbm, freq, small_sem.at[0])
    get_weight = pltpu.make_async_copy(weight_hbm, weight, small_sem.at[1])
    get_snap = [
        pltpu.make_async_copy(
            snap_hbm.at[pl.ds(i * group, group)], snap.at[pl.ds(i * group, group)], snap_sem.at[i]
        )
        for i in range(steps)
    ]
    token[...] = jnp.zeros_like(token)
    get_freq.start()
    for get in get_snap:
        get.start()
    get_weight.start()

    me = lax.axis_index("tm")
    groups = [
        (peer, first + j)
        for first, count in parts
        for peer in range(peers)
        for j in range(0, count, 8)
    ]
    rows = 8 * len(groups)
    per_peer = freq.shape[0] // peers
    times = lax.broadcasted_iota(jnp.int32, (8, length), 1)
    sub = lax.broadcasted_iota(jnp.int32, (8, length), 0)
    window = 0.5 - 0.5 * cos_sin(times, length)[0]
    scaled = window / F32(math.sqrt(0.375 * length))
    get_freq.wait()

    def eight(index):
        peer, offset = groups[index]
        start = jnp.bitwise_xor(me, peer) * per_peer + offset
        k = jnp.zeros((8, length), jnp.int32)
        for i in range(8):
            k = jnp.where(sub == i, freq[start + i], k)
        cos, sin = cos_sin((k * times) & (length - 1), length)
        return scaled * cos, -(scaled * sin)

    for pair in range(rows // 16):
        re0, im0 = eight(2 * pair)
        re1, im1 = eight(2 * pair + 1)
        table[16 * pair : 16 * pair + 16, :] = jnp.concatenate([re0, re1], 0).astype(BF16)
        table[rows + 16 * pair : rows + 16 * pair + 16, :] = jnp.concatenate(
            [im0, im1], 0
        ).astype(BF16)

    get_weight.wait()
    root = jnp.sqrt(weight[...])
    tiles = entries // LANES
    for step in range(steps):
        get_snap[step].wait()
        for b in range(step * group, (step + 1) * group):
            spec = dot(table[...], snap[b]) * root
            for tile in range(tiles):
                lanes = slice(tile * LANES, (tile + 1) * LANES)
                wide[tile, pl.ds(b, rows, stride=blocks), :] = spec[:rows, lanes]
                wide[tiles + tile, pl.ds(b, rows, stride=blocks), :] = spec[rows:, lanes]
    at = 0
    for out in outs:
        for j in range(out.shape[0]):
            for tile in range(2 * tiles):
                lanes = slice(tile * LANES, (tile + 1) * LANES)
                out[j, :, lanes] = wide[tile, at : at + blocks, :].astype(BF16)
            at += blocks


def transform(snapshots, weight, freq_index, peers, parts, after):
    blocks, length, entries = snapshots.shape
    group = min(blocks, 4)
    total = peers * sum(count for _, count in parts)
    shapes = [
        jax.ShapeDtypeStruct((count, blocks, 2 * entries), BF16)
        for _, count in parts
        for _ in range(peers)
    ]
    hbm = pl.BlockSpec(memory_space=pltpu.HBM)
    out = pl.pallas_call(
        functools.partial(transform_kernel, peers, parts, group),
        in_specs=[hbm] * 3 + [any_spec()] * len(after),
        out_specs=[whole_spec()] * (len(shapes) + 1),
        out_shape=shapes + [TOKEN],
        scratch_shapes=[
            pltpu.SMEM(freq_index.shape, jnp.int32),
            pltpu.VMEM(weight.shape, F32),
            pltpu.VMEM(snapshots.shape, BF16),
            pltpu.VMEM((2 * total, length), BF16),
            pltpu.VMEM((2 * entries // LANES, total * blocks, LANES), F32),
            pltpu.SemaphoreType.DMA((2,)),
            pltpu.SemaphoreType.DMA((blocks // group,)),
        ],
        compiler_params=params(),
        cost_estimate=light(),
        name="transform",
    )(in_hbm(freq_index), in_hbm(weight), in_hbm(snapshots), *after)
    return [out[i * peers : (i + 1) * peers] for i in range(len(parts))], out[-1]


def lane_low(shape, half):
    return lax.broadcasted_iota(jnp.int32, shape, 1) < half


def swap(x):
    return pltpu.roll(x, x.shape[1] // 2, 1)


def pack(compact):
    half = compact.shape[0]
    both = compact + swap(compact)
    low = lane_low((half // 2, 2 * half), half)
    return jnp.where(low, both[: half // 2], both[half // 2 :])


def unpack(packed):
    rows, half = packed.shape[0], packed.shape[1] // 2
    low = lane_low(packed.shape, half)
    other = swap(packed)
    both = jnp.concatenate(
        [jnp.where(low, packed, other), jnp.where(low, other, packed)], 0
    )
    turned = jnp.transpose(jnp.concatenate([packed, packed], 0))
    turned = jnp.where(lane_low((half, half), rows), turned[:half], turned[half:])
    turned = jnp.concatenate([turned, turned], 1)
    low = lane_low(both.shape, half)
    return 0.5 * jnp.where(low, both + turned, both - turned)


def full(compact):
    half = compact.shape[0]
    turned = swap(compact)
    low = lane_low(compact.shape, half)
    return jnp.concatenate([compact, jnp.where(low, -turned, turned)], 0)


def slot_owner(direct, slot):
    return jnp.bitwise_xor(lax.axis_index("space") & 1, slot) if direct else slot


def gram_kernel(peers, slots, direct, after, *refs):
    pieces, refs = refs[:peers], refs[peers + after :]
    merged, token, grams = refs[0], refs[1], refs[2:]
    token[...] = jnp.zeros_like(token)
    me = lax.axis_index("tm")
    here = pieces[0].shape[1]
    entries = pieces[0].shape[2] // 2
    blocks = here * peers
    per_slot = pieces[0].shape[0] // slots
    stage = None
    if here % 16:
        grams, stage = grams[:-1], grams[-1]
    low = lane_low((blocks, 2 * blocks), blocks)
    for slot in range(slots):
        owner = slot_owner(direct, slot)
        for i in range(per_slot):
            f = owner * per_slot + i
            if stage is None:
                for peer in range(peers):
                    start = pl.multiple_of(jnp.bitwise_xor(me, peer) * here, here)
                    merged[f, pl.ds(start, here), :] = pieces[peer][f]
                z = merged[f]
            else:
                for peer in range(peers):
                    start = pl.multiple_of(jnp.bitwise_xor(me, peer) * here, here)
                    stage[pl.ds(start, here), :] = pieces[peer][f].astype(F32)
                z = stage[...].astype(BF16)
                merged[f] = z
            w = jnp.concatenate([z[:, :entries], z[:, entries:]], 0)
            s = lax.dot_general(w, w, (((1,), (1,)), ((), ())), preferred_element_type=F32)
            s = s * F32(1.0 / blocks)
            top, bottom = s[:blocks], swap(s[blocks:])
            compact = jnp.where(low, top + bottom, top - bottom)
            if direct:
                grams[slot][i] = pack(compact)
            else:
                grams[0][f] = pack(compact)


def gram(pieces, slots, direct, after):
    peers = len(pieces)
    count, here, width = pieces[0].shape
    blocks = here * peers
    if direct:
        shapes = [(count // slots, blocks // 2, 2 * blocks)] * slots
    else:
        shapes = [(count, blocks // 2, 2 * blocks)]
    out = pl.pallas_call(
        functools.partial(gram_kernel, peers, slots, direct, len(after)),
        in_specs=[whole_spec()] * peers + [any_spec()] * len(after),
        out_specs=[whole_spec()] * (2 + len(shapes)),
        out_shape=[jax.ShapeDtypeStruct((count, blocks, width), BF16), TOKEN]
        + [jax.ShapeDtypeStruct(s, F32) for s in shapes],
        scratch_shapes=[pltpu.VMEM((blocks, width), F32)] if here % 16 else [],
        compiler_params=params(),
        cost_estimate=light(),
        name="gram",
    )(*pieces, *after)
    return out[0], out[2:], out[1]


def add_kernel(one, two, *refs):
    out, token = refs[-2:]
    token[...] = jnp.zeros_like(token)
    out[...] = one[...] + two[...]


def add(one, two, after):
    return pl.pallas_call(
        add_kernel,
        in_specs=[whole_spec()] * 2 + [any_spec()] * len(after),
        out_specs=[whole_spec()] * 2,
        out_shape=[jax.ShapeDtypeStruct(one.shape, F32), TOKEN],
        compiler_params=params(),
        cost_estimate=light(),
        name="add",
    )(one, two, *after)


def split(x):
    high = x.astype(BF16)
    return high, (x - high.astype(F32)).astype(BF16)


def each(fn, *lists):
    return [fn(*items) for items in zip(*lists)]


def solve_kernel(parts, *refs):
    ins, out, token = refs[:parts], refs[-2], refs[-1]
    token[...] = jnp.zeros_like(token)
    number, half_rows, width = ins[0].shape
    half = width // 2
    shape = (half, width)
    row = lax.broadcasted_iota(jnp.int32, shape, 0)
    lane = lax.broadcasted_iota(jnp.int32, shape, 1)
    eye = jnp.where(row == lane, F32(1), F32(0))

    def load(i):
        total = ins[0][i]
        for r in ins[1:]:
            total = total + r[i]
        return unpack(total)

    grams = [load(i) for i in range(number)]
    shift = each(lambda g: jnp.sum(g * eye, keepdims=True) * F32(1.0 / half), grams)
    system = each(lambda g, m: g / m + eye, grams, shift)
    both = each(lambda a: split(full(a)), system)

    low_end, high_end = 1.0, float(half + 1)
    mid, radius = (high_end + low_end) / 2, (high_end - low_end) / 2
    ratio = mid / radius
    t = 2 * ratio * ratio - 1
    scale = 2.0 / (radius * radius * t)
    x = each(lambda a: (F32(scale) * (F32(2 * mid) * eye - a)).astype(BF16), system)
    p = each(lambda v, a: eye - (dot(v, a[0]) + dot(v, a[1])), x, both)
    x = each(lambda v: v.astype(F32), x)
    for _ in range(3):
        t_next = 2 * t * t - 1
        c = F32(2 * t * t / t_next)
        pf = each(lambda q: full(q).astype(BF16), p)
        xp = each(lambda v, q: jnp.concatenate([v, q], 0).astype(BF16), x, p)
        moved = each(dot, xp, pf)
        x = each(lambda v, m: c * (v + m[:half]), x, moved)
        p = each(lambda m: c * m[half:] - F32(1 / t_next) * eye, moved)
        t = t_next
    for kind in ("scaled", "last"):
        xb = each(lambda v: v.astype(BF16), x)
        xw = each(lambda v: v.astype(F32), xb)
        xf = each(lambda v: full(v).astype(BF16), xw)
        residual = each(lambda v, a: eye - (dot(v, a[0]) + dot(v, a[1])), xb, both)
        step = each(lambda r, v: dot(r.astype(BF16), v), residual, xf)
        factor = 1.0 if kind == "last" else 2 * t * t / (2 * t * t - 1)
        x = each(lambda v, m: F32(factor) * (v + m), xw, step)
    packed = each(lambda v: pack(eye - v), x)
    for i in range(number):
        out[i * half_rows : (i + 1) * half_rows, :] = packed[i]
    filters = each(unpack, packed)
    rounded = each(lambda c: c.astype(BF16), filters)
    turned = each(lambda c: full(c.astype(F32)).astype(BF16), rounded)
    split_g = each(split, grams)
    moved = each(lambda g, c: dot(g[0], c) + dot(g[1], c), split_g, turned)
    energy = each(
        lambda c, h: jnp.sum(c.astype(F32) * h, keepdims=True) * F32(half), rounded, moved
    )
    tail = out.shape[0] - number * half_rows
    line = lax.broadcasted_iota(jnp.int32, (tail, width), 0)
    totals = jnp.ones((tail, width), F32)
    for i in range(number):
        totals = jnp.where(line == i, energy[i], totals)
    out[number * half_rows :, :] = totals


def tail_rows(number):
    return -(-number // 8) * 8


def solve(parts, after):
    number, half_rows, width = parts[0].shape
    rows = number * half_rows + tail_rows(number)
    return pl.pallas_call(
        functools.partial(solve_kernel, len(parts)),
        in_specs=[whole_spec()] * len(parts) + [any_spec()] * len(after),
        out_specs=[whole_spec()] * 2,
        out_shape=[jax.ShapeDtypeStruct((rows, width), F32), TOKEN],
        compiler_params=params(),
        cost_estimate=light(),
        name="filters",
    )(*parts, *after)


def energy_kernel(slots, direct, number, first, merged, *refs):
    pieces = refs[:number]
    energies_out, filters_out, token, energies, filters, energies_sem, filters_sem = refs[-7:]
    token[...] = jnp.zeros_like(token)
    count, blocks, width = merged.shape
    entries = width // 2
    per_slot = count // slots
    half_rows = blocks // 2
    states = entries * lax.axis_size("space")
    puts = []
    for slot in range(slots):
        owner = slot_owner(direct, slot)
        piece = pieces[slot] if direct else pieces[0].at[slot]
        for begin in range(0, per_slot, 4):
            some = range(begin, min(begin + 4, per_slot))
            at = [owner * per_slot + i for i in some]
            packed = [piece[i * half_rows : (i + 1) * half_rows, :] for i in some]
            tail = per_slot * half_rows
            total = [piece[tail + i : tail + i + 1, 0:1] for i in some]
            z = [merged[f] for f in at]
            compact = each(unpack, packed)
            both = each(lambda c: full(c.astype(BF16).astype(F32)).astype(BF16), compact)
            w = each(lambda v: jnp.concatenate([v[:, :entries], v[:, entries:]], 0), z)
            r = each(dot, both, w)
            energy = each(
                lambda v, t: jnp.sum(v * v, axis=0, keepdims=True) * (F32(states) / t), r, total
            )
            for f, c, e in zip(at, compact, energy):
                filters[f, 0] = c[:, :blocks]
                filters[f, 1] = c[:, blocks:]
                energies[pl.ds(f, 1), :] = e
            put = pltpu.make_async_copy(
                filters.at[pl.ds(at[0], len(at))],
                filters_out.at[pl.ds(first + at[0], len(at))],
                filters_sem.at[len(puts)],
            )
            put.start()
            puts.append(put)
    put = pltpu.make_async_copy(
        energies, energies_out.at[pl.ds(first, count)], energies_sem.at[0]
    )
    put.start()
    for p in [*puts, put]:
        p.wait()


def filtered(merged, pieces, slots, direct, carry, owned, first, after):
    count, blocks, width = merged.shape
    entries = width // 2
    fixed = 1 + len(pieces)
    args = [merged, *pieces] + ([] if carry is None else list(carry)) + list(after)
    hbm = pl.BlockSpec(memory_space=pltpu.HBM)
    return pl.pallas_call(
        functools.partial(energy_kernel, slots, direct, len(pieces), first),
        in_specs=[whole_spec()] * fixed
        + ([] if carry is None else [hbm] * 2)
        + [any_spec()] * len(after),
        out_specs=[hbm] * 2 + [whole_spec()],
        out_shape=[
            jax.ShapeDtypeStruct((owned, entries), F32),
            jax.ShapeDtypeStruct((owned, 2, blocks, blocks), F32),
            TOKEN,
        ],
        input_output_aliases={} if carry is None else {fixed: 0, fixed + 1: 1},
        scratch_shapes=[
            pltpu.VMEM((count, entries), F32),
            pltpu.VMEM((count, 2, blocks, blocks), F32),
            pltpu.SemaphoreType.DMA((1,)),
            pltpu.SemaphoreType.DMA((slots * -(-(count // slots) // 4),)),
        ],
        compiler_params=params(),
        cost_estimate=light(),
        name="energy",
    )(*args)


def exchange(arrays, axis):
    size = lax.axis_size(axis)
    got = [arrays[0]]
    for offset in range(1, size):
        pairs = [(i, i ^ offset) for i in range(size)]
        got.append(lax.ppermute(arrays[offset], axis, pairs))
    return got


def plan(owned, slots):
    if slots != 4 or owned != 64:
        return [owned], (("T", 0), ("G", 0), ("F", 0), ("E", 0))
    return SIZES, ORDER


SIZES = [24, 24, 16]
ORDER = (
    ("T", 0), ("T", 1), ("G", 0), ("A", 0), ("G", 1), ("F", 0), ("A", 1), ("G", 2),
    ("E", 0), ("A", 2), ("F", 1), ("F", 2), ("E", 1), ("E", 2),
)


def permute(x, axis, offset):
    pairs = [(i, i ^ offset) for i in range(lax.axis_size(axis))]
    return lax.ppermute(x, axis, pairs)


def on_device(snapshots, entry_weight, freq_index):
    peers = lax.axis_size("tm")
    slots = lax.axis_size("space")
    owned = freq_index.shape[0] // peers
    sizes, order = plan(owned, slots)
    starts = [sum(sizes[:c]) for c in range(len(sizes))]
    paired = slots == 4
    halves = 2 if paired else slots
    weight = entry_weight.reshape(1, -1)
    sent, merged, grams, parts, pieces = {}, {}, {}, {}, {}
    carry = None
    token = []

    def do_transform(c):
        nonlocal token
        chunks = [0] if c == 0 else range(1, len(sizes))
        out, done = transform(
            snapshots, weight, freq_index, peers, [(starts[k], sizes[k]) for k in chunks], token
        )
        token = [done]
        for k, pieces_out in zip(chunks, out):
            sent[k] = [pieces_out[0]] + [
                permute(pieces_out[offset], "tm", offset) for offset in range(1, peers)
            ]

    def do_gram(c):
        nonlocal token
        merged[c], grams[c], done = gram(sent[c], halves, paired, token)
        token = [done]
        if paired:
            grams[c] = [grams[c][0], permute(grams[c][1], "space", 1)]
        else:
            parts[c] = [lax.psum_scatter(grams[c][0], "space", scatter_dimension=0, tiled=True)]

    def do_add(c):
        nonlocal token
        half, done = add(*grams[c], token)
        token = [done]
        parts[c] = [half, permute(half, "space", 2)]

    def do_solve(c):
        nonlocal token
        own, done = solve(parts[c], token)
        token = [done]
        if paired:
            pieces[c] = [own, permute(own, "space", 1)]
        else:
            pieces[c] = [lax.all_gather(own, "space", axis=0, tiled=False)]

    def do_energy(c):
        nonlocal token, carry
        *carry, done = filtered(
            merged[c], pieces[c], halves, paired, carry, owned, starts[c], token
        )
        token = [done]

    stages = {"T": do_transform, "G": do_gram, "A": do_add, "F": do_solve, "E": do_energy}
    for stage, c in order:
        stages[stage](c)
    return (carry[0], carry[1])


def solution(mesh):
    in_specs = (P(("grp", "tm"), None, "space"), P(("grp", "space")), P())
    out_specs = (P(("grp", "tm"), "space"), P(("grp", "tm"), None, None, None))
    return jax.shard_map(
        on_device, mesh=mesh, in_specs=in_specs, out_specs=out_specs, check_vma=False
    )
```

```python
import functools
import math

import jax
import jax.numpy as jnp
from jax import lax
from jax.experimental import pallas as pl
from jax.experimental.pallas import tpu as pltpu
from jax.sharding import PartitionSpec as P

F32 = jnp.float32
BF16 = jnp.bfloat16
VMEM_LIMIT = 30 * 1024 * 1024
LANES = 128


def params(**kwargs):
    return pltpu.CompilerParams(vmem_limit_bytes=VMEM_LIMIT, **kwargs)


def whole_spec():
    return pl.BlockSpec(memory_space=pltpu.VMEM)


TOKEN = jax.ShapeDtypeStruct((8, LANES), F32)


def light():
    return pl.CostEstimate(flops=1024, bytes_accessed=1024, transcendentals=0)


def in_hbm(x):
    return pltpu.with_memory_space_constraint(x, pltpu.HBM)


def any_spec():
    return pl.BlockSpec(memory_space=pl.ANY)


def dot(a, b):
    return lax.dot_general(a, b, (((1,), (0,)), ((), ())), preferred_element_type=F32)


def cos_sin(phase, length):
    quarter = length // 4
    eighth = length // 8
    shifted = phase + eighth
    low = (shifted & (quarter - 1)) - eighth
    quadrant = (shifted // quarter) & 3
    x = low.astype(F32) * F32(2.0 * math.pi / length)
    x2 = x * x
    cos = F32(1 / 40320)
    for c in (-1 / 720, 1 / 24, -0.5, 1.0):
        cos = cos * x2 + F32(c)
    sin = F32(1 / 362880)
    for c in (-1 / 5040, 1 / 120, -1 / 6, 1.0):
        sin = sin * x2 + F32(c)
    sin = sin * x
    odd = (quadrant & 1) == 1
    c0 = jnp.where(odd, sin, cos)
    s0 = jnp.where(odd, cos, sin)
    c1 = jnp.where((quadrant == 1) | (quadrant == 2), -c0, c0)
    s1 = jnp.where(quadrant >= 2, -s0, s0)
    return c1, s1


def transform_kernel(peers, parts, group, *refs):
    freq_hbm, weight_hbm, snap_hbm = refs[:3]
    outs, token = refs[-peers * len(parts) - 8 : -8], refs[-8]
    freq, weight, snap, table, wide, small_sem, snap_sem = refs[-7:]
    blocks, length, entries = snap.shape
    steps = blocks // group
    get_freq = pltpu.make_async_copy(freq_hbm, freq, small_sem.at[0])
    get_weight = pltpu.make_async_copy(weight_hbm, weight, small_sem.at[1])
    get_snap = [
        pltpu.make_async_copy(
            snap_hbm.at[pl.ds(i * group, group)], snap.at[pl.ds(i * group, group)], snap_sem.at[i]
        )
        for i in range(steps)
    ]
    token[...] = jnp.zeros_like(token)
    get_freq.start()
    for get in get_snap:
        get.start()
    get_weight.start()

    me = lax.axis_index("tm")
    groups = [
        (peer, first + j)
        for first, count in parts
        for peer in range(peers)
        for j in range(0, count, 8)
    ]
    rows = 8 * len(groups)
    per_peer = freq.shape[0] // peers
    times = lax.broadcasted_iota(jnp.int32, (8, length), 1)
    sub = lax.broadcasted_iota(jnp.int32, (8, length), 0)
    window = 0.5 - 0.5 * cos_sin(times, length)[0]
    scaled = window / F32(math.sqrt(0.375 * length))
    get_freq.wait()

    def eight(index):
        peer, offset = groups[index]
        start = jnp.bitwise_xor(me, peer) * per_peer + offset
        k = jnp.zeros((8, length), jnp.int32)
        for i in range(8):
            k = jnp.where(sub == i, freq[start + i], k)
        cos, sin = cos_sin((k * times) & (length - 1), length)
        return scaled * cos, -(scaled * sin)

    for pair in range(rows // 16):
        re0, im0 = eight(2 * pair)
        re1, im1 = eight(2 * pair + 1)
        table[16 * pair : 16 * pair + 16, :] = jnp.concatenate([re0, re1], 0).astype(BF16)
        table[rows + 16 * pair : rows + 16 * pair + 16, :] = jnp.concatenate(
            [im0, im1], 0
        ).astype(BF16)

    get_weight.wait()
    root = jnp.sqrt(weight[...])
    tiles = entries // LANES

    for step in range(steps):
        get_snap[step].wait()

        def block(i, _):
            b = step * group + i
            spec = dot(table[...], snap[b]) * root
            for tile in range(tiles):
                lanes = slice(tile * LANES, (tile + 1) * LANES)
                wide[tile, pl.ds(b, rows, stride=blocks), :] = spec[:rows, lanes]
                wide[tiles + tile, pl.ds(b, rows, stride=blocks), :] = spec[rows:, lanes]
            return 0

        lax.fori_loop(0, group, block, 0)
    base = 0
    for out in outs:

        def row(j, _):
            at = pl.multiple_of(base + j * blocks, blocks)
            for tile in range(2 * tiles):
                lanes = slice(tile * LANES, (tile + 1) * LANES)
                out[j, :, lanes] = wide[tile, pl.ds(at, blocks), :].astype(BF16)
            return 0

        lax.fori_loop(0, out.shape[0], row, 0, unroll=4)
        base += out.shape[0] * blocks


def transform(snapshots, weight, freq_index, peers, parts, after):
    blocks, length, entries = snapshots.shape
    group = min(blocks, 4)
    total = peers * sum(count for _, count in parts)
    shapes = [
        jax.ShapeDtypeStruct((count, blocks, 2 * entries), BF16)
        for _, count in parts
        for _ in range(peers)
    ]
    hbm = pl.BlockSpec(memory_space=pltpu.HBM)
    out = pl.pallas_call(
        functools.partial(transform_kernel, peers, parts, group),
        in_specs=[hbm] * 3 + [any_spec()] * len(after),
        out_specs=[whole_spec()] * (len(shapes) + 1),
        out_shape=shapes + [TOKEN],
        scratch_shapes=[
            pltpu.SMEM(freq_index.shape, jnp.int32),
            pltpu.VMEM(weight.shape, F32),
            pltpu.VMEM(snapshots.shape, BF16),
            pltpu.VMEM((2 * total, length), BF16),
            pltpu.VMEM((2 * entries // LANES, total * blocks, LANES), F32),
            pltpu.SemaphoreType.DMA((2,)),
            pltpu.SemaphoreType.DMA((blocks // group,)),
        ],
        compiler_params=params(),
        cost_estimate=light(),
        name="transform",
    )(in_hbm(freq_index), in_hbm(weight), in_hbm(snapshots), *after)
    return [out[i * peers : (i + 1) * peers] for i in range(len(parts))], out[-1]


def lane_low(shape, half):
    return lax.broadcasted_iota(jnp.int32, shape, 1) < half


def swap(x):
    return pltpu.roll(x, x.shape[1] // 2, 1)


def pack(compact):
    half = compact.shape[0]
    both = compact + swap(compact)
    low = lane_low((half // 2, 2 * half), half)
    return jnp.where(low, both[: half // 2], both[half // 2 :])


def unpack(packed):
    rows, half = packed.shape[0], packed.shape[1] // 2
    low = lane_low(packed.shape, half)
    other = swap(packed)
    both = jnp.concatenate(
        [jnp.where(low, packed, other), jnp.where(low, other, packed)], 0
    )
    turned = jnp.transpose(jnp.concatenate([packed, packed], 0))
    turned = jnp.where(lane_low((half, half), rows), turned[:half], turned[half:])
    turned = jnp.concatenate([turned, turned], 1)
    low = lane_low(both.shape, half)
    return 0.5 * jnp.where(low, both + turned, both - turned)


def full(compact):
    half = compact.shape[0]
    turned = swap(compact)
    low = lane_low(compact.shape, half)
    return jnp.concatenate([compact, jnp.where(low, -turned, turned)], 0)


def slot_owner(direct, slot):
    return jnp.bitwise_xor(lax.axis_index("space") & 1, slot) if direct else slot


def gram_kernel(peers, slots, direct, after, *refs):
    pieces, refs = refs[:peers], refs[peers + after :]
    merged, token, grams = refs[0], refs[1], refs[2:]
    token[...] = jnp.zeros_like(token)
    me = lax.axis_index("tm")
    here = pieces[0].shape[1]
    entries = pieces[0].shape[2] // 2
    blocks = here * peers
    per_slot = pieces[0].shape[0] // slots
    stage = None
    if here % 16:
        grams, stage = grams[:-1], grams[-1]
    low = lane_low((blocks, 2 * blocks), blocks)
    for slot in range(slots):
        owner = slot_owner(direct, slot)
        for i in range(per_slot):
            f = owner * per_slot + i
            if stage is None:
                for peer in range(peers):
                    start = pl.multiple_of(jnp.bitwise_xor(me, peer) * here, here)
                    merged[f, pl.ds(start, here), :] = pieces[peer][f]
                z = merged[f]
            else:
                for peer in range(peers):
                    start = pl.multiple_of(jnp.bitwise_xor(me, peer) * here, here)
                    stage[pl.ds(start, here), :] = pieces[peer][f].astype(F32)
                z = stage[...].astype(BF16)
                merged[f] = z
            w = jnp.concatenate([z[:, :entries], z[:, entries:]], 0)
            s = lax.dot_general(w, w, (((1,), (1,)), ((), ())), preferred_element_type=F32)
            s = s * F32(1.0 / blocks)
            top, bottom = s[:blocks], swap(s[blocks:])
            compact = jnp.where(low, top + bottom, top - bottom)
            if direct:
                grams[slot][i] = pack(compact)
            else:
                grams[0][f] = pack(compact)


def gram(pieces, slots, direct, after):
    peers = len(pieces)
    count, here, width = pieces[0].shape
    blocks = here * peers
    if direct:
        shapes = [(count // slots, blocks // 2, 2 * blocks)] * slots
    else:
        shapes = [(count, blocks // 2, 2 * blocks)]
    out = pl.pallas_call(
        functools.partial(gram_kernel, peers, slots, direct, len(after)),
        in_specs=[whole_spec()] * peers + [any_spec()] * len(after),
        out_specs=[whole_spec()] * (2 + len(shapes)),
        out_shape=[jax.ShapeDtypeStruct((count, blocks, width), BF16), TOKEN]
        + [jax.ShapeDtypeStruct(s, F32) for s in shapes],
        scratch_shapes=[pltpu.VMEM((blocks, width), F32)] if here % 16 else [],
        compiler_params=params(),
        cost_estimate=light(),
        name="gram",
    )(*pieces, *after)
    return out[0], out[2:], out[1]


def add_kernel(one, two, *refs):
    out, token = refs[-2:]
    token[...] = jnp.zeros_like(token)
    out[...] = one[...] + two[...]


def add(one, two, after):
    return pl.pallas_call(
        add_kernel,
        in_specs=[whole_spec()] * 2 + [any_spec()] * len(after),
        out_specs=[whole_spec()] * 2,
        out_shape=[jax.ShapeDtypeStruct(one.shape, F32), TOKEN],
        compiler_params=params(),
        cost_estimate=light(),
        name="add",
    )(one, two, *after)


def split(x):
    high = x.astype(BF16)
    return high, (x - high.astype(F32)).astype(BF16)


def each(fn, *lists):
    return [fn(*items) for items in zip(*lists)]


def solve_kernel(parts, *refs):
    ins, out, token = refs[:parts], refs[-2], refs[-1]
    token[...] = jnp.zeros_like(token)
    number, half_rows, width = ins[0].shape
    half = width // 2
    shape = (half, width)
    row = lax.broadcasted_iota(jnp.int32, shape, 0)
    lane = lax.broadcasted_iota(jnp.int32, shape, 1)
    eye = jnp.where(row == lane, F32(1), F32(0))

    def load(i):
        total = ins[0][i]
        for r in ins[1:]:
            total = total + r[i]
        return unpack(total)

    grams = [load(i) for i in range(number)]
    shift = each(lambda g: jnp.sum(g * eye, keepdims=True) * F32(1.0 / half), grams)
    system = each(lambda g, m: g / m + eye, grams, shift)
    both = each(lambda a: split(full(a)), system)

    low_end, high_end = 1.0, float(half + 1)
    mid, radius = (high_end + low_end) / 2, (high_end - low_end) / 2
    ratio = mid / radius
    t = 2 * ratio * ratio - 1
    scale = 2.0 / (radius * radius * t)
    x = each(lambda a: (F32(scale) * (F32(2 * mid) * eye - a)).astype(BF16), system)
    p = each(lambda v, a: eye - (dot(v, a[0]) + dot(v, a[1])), x, both)
    x = each(lambda v: v.astype(F32), x)
    for _ in range(3):
        t_next = 2 * t * t - 1
        c = F32(2 * t * t / t_next)
        pf = each(lambda q: full(q).astype(BF16), p)
        xp = each(lambda v, q: jnp.concatenate([v, q], 0).astype(BF16), x, p)
        moved = each(dot, xp, pf)
        x = each(lambda v, m: c * (v + m[:half]), x, moved)
        p = each(lambda m: c * m[half:] - F32(1 / t_next) * eye, moved)
        t = t_next
    for kind in ("scaled", "last"):
        xb = each(lambda v: v.astype(BF16), x)
        xw = each(lambda v: v.astype(F32), xb)
        xf = each(lambda v: full(v).astype(BF16), xw)
        residual = each(lambda v, a: eye - (dot(v, a[0]) + dot(v, a[1])), xb, both)
        step = each(lambda r, v: dot(r.astype(BF16), v), residual, xf)
        factor = 1.0 if kind == "last" else 2 * t * t / (2 * t * t - 1)
        x = each(lambda v, m: F32(factor) * (v + m), xw, step)
    packed = each(lambda v: pack(eye - v), x)
    for i in range(number):
        out[i * half_rows : (i + 1) * half_rows, :] = packed[i]
    filters = each(unpack, packed)
    rounded = each(lambda c: c.astype(BF16), filters)
    turned = each(lambda c: full(c.astype(F32)).astype(BF16), rounded)
    split_g = each(split, grams)
    moved = each(lambda g, c: dot(g[0], c) + dot(g[1], c), split_g, turned)
    energy = each(
        lambda c, h: jnp.sum(c.astype(F32) * h, keepdims=True) * F32(half), rounded, moved
    )
    tail = out.shape[0] - number * half_rows
    line = lax.broadcasted_iota(jnp.int32, (tail, width), 0)
    totals = jnp.ones((tail, width), F32)
    for i in range(number):
        totals = jnp.where(line == i, energy[i], totals)
    out[number * half_rows :, :] = totals


def tail_rows(number):
    return -(-number // 8) * 8


def solve(parts, after):
    number, half_rows, width = parts[0].shape
    rows = number * half_rows + tail_rows(number)
    return pl.pallas_call(
        functools.partial(solve_kernel, len(parts)),
        in_specs=[whole_spec()] * len(parts) + [any_spec()] * len(after),
        out_specs=[whole_spec()] * 2,
        out_shape=[jax.ShapeDtypeStruct((rows, width), F32), TOKEN],
        compiler_params=params(),
        cost_estimate=light(),
        name="filters",
    )(*parts, *after)


def energy_kernel(slots, direct, number, first, merged, *refs):
    pieces = refs[:number]
    energies_out, filters_out, token, energies, filters, energies_sem, filters_sem = refs[-7:]
    token[...] = jnp.zeros_like(token)
    count, blocks, width = merged.shape
    entries = width // 2
    per_slot = count // slots
    half_rows = blocks // 2
    states = entries * lax.axis_size("space")
    group = 4 if per_slot % 4 == 0 else 1
    tail = per_slot * half_rows
    for slot in range(slots):
        owner = slot_owner(direct, slot)
        piece = pieces[slot] if direct else pieces[0].at[slot]

        def some(step, _):
            begin = step * group
            base = owner * per_slot + begin
            at = [base + i for i in range(group)]
            packed = [
                piece[pl.ds(pl.multiple_of((begin + i) * half_rows, half_rows), half_rows), :]
                for i in range(group)
            ]
            total = [piece[pl.ds(tail + begin + i, 1), :][:, 0:1] for i in range(group)]
            z = [merged[f] for f in at]
            compact = each(unpack, packed)
            both = each(lambda c: full(c.astype(BF16).astype(F32)).astype(BF16), compact)
            w = each(lambda v: jnp.concatenate([v[:, :entries], v[:, entries:]], 0), z)
            r = each(dot, both, w)
            energy = each(
                lambda v, t: jnp.sum(v * v, axis=0, keepdims=True) * (F32(states) / t), r, total
            )
            for f, c, e in zip(at, compact, energy):
                filters[f, 0] = c[:, :blocks]
                filters[f, 1] = c[:, blocks:]
                energies[pl.ds(f, 1), :] = e
            pltpu.make_async_copy(
                filters.at[pl.ds(base, group)],
                filters_out.at[pl.ds(first + base, group)],
                filters_sem.at[0],
            ).start()
            return 0

        lax.fori_loop(0, per_slot // group, some, 0)
    put = pltpu.make_async_copy(
        energies, energies_out.at[pl.ds(first, count)], energies_sem.at[0]
    )
    put.start()
    pltpu.make_async_copy(
        filters, filters_out.at[pl.ds(first, count)], filters_sem.at[0]
    ).wait()
    put.wait()


def filtered(merged, pieces, slots, direct, carry, owned, first, after):
    count, blocks, width = merged.shape
    entries = width // 2
    fixed = 1 + len(pieces)
    args = [merged, *pieces] + ([] if carry is None else list(carry)) + list(after)
    hbm = pl.BlockSpec(memory_space=pltpu.HBM)
    return pl.pallas_call(
        functools.partial(energy_kernel, slots, direct, len(pieces), first),
        in_specs=[whole_spec()] * fixed
        + ([] if carry is None else [hbm] * 2)
        + [any_spec()] * len(after),
        out_specs=[hbm] * 2 + [whole_spec()],
        out_shape=[
            jax.ShapeDtypeStruct((owned, entries), F32),
            jax.ShapeDtypeStruct((owned, 2, blocks, blocks), F32),
            TOKEN,
        ],
        input_output_aliases={} if carry is None else {fixed: 0, fixed + 1: 1},
        scratch_shapes=[
            pltpu.VMEM((count, entries), F32),
            pltpu.VMEM((count, 2, blocks, blocks), F32),
            pltpu.SemaphoreType.DMA((1,)),
            pltpu.SemaphoreType.DMA((1,)),
        ],
        compiler_params=params(),
        cost_estimate=light(),
        name="energy",
    )(*args)


def exchange(arrays, axis):
    size = lax.axis_size(axis)
    got = [arrays[0]]
    for offset in range(1, size):
        pairs = [(i, i ^ offset) for i in range(size)]
        got.append(lax.ppermute(arrays[offset], axis, pairs))
    return got


def plan(owned, slots):
    if slots != 4 or owned != 64:
        return [owned], (("T", 0), ("G", 0), ("F", 0), ("E", 0))
    return SIZES, ORDER


SIZES = [24, 24, 16]
ORDER = (
    ("T", 0), ("T", 1), ("G", 0), ("A", 0), ("G", 1), ("F", 0), ("A", 1), ("G", 2),
    ("E", 0), ("A", 2), ("F", 1), ("F", 2), ("E", 1), ("E", 2),
)


def permute(x, axis, offset):
    pairs = [(i, i ^ offset) for i in range(lax.axis_size(axis))]
    return lax.ppermute(x, axis, pairs)


def on_device(snapshots, entry_weight, freq_index):
    peers = lax.axis_size("tm")
    slots = lax.axis_size("space")
    owned = freq_index.shape[0] // peers
    sizes, order = plan(owned, slots)
    starts = [sum(sizes[:c]) for c in range(len(sizes))]
    paired = slots == 4
    halves = 2 if paired else slots
    weight = entry_weight.reshape(1, -1)
    sent, merged, grams, parts, pieces = {}, {}, {}, {}, {}
    carry = None
    token = []

    def do_transform(c):
        nonlocal token
        chunks = [0] if c == 0 else range(1, len(sizes))
        out, done = transform(
            snapshots, weight, freq_index, peers, [(starts[k], sizes[k]) for k in chunks], token
        )
        token = [done]
        for k, pieces_out in zip(chunks, out):
            sent[k] = [pieces_out[0]] + [
                permute(pieces_out[offset], "tm", offset) for offset in range(1, peers)
            ]

    def do_gram(c):
        nonlocal token
        merged[c], grams[c], done = gram(sent[c], halves, paired, token)
        token = [done]
        if paired:
            grams[c] = [grams[c][0], permute(grams[c][1], "space", 1)]
        else:
            parts[c] = [lax.psum_scatter(grams[c][0], "space", scatter_dimension=0, tiled=True)]

    def do_add(c):
        nonlocal token
        half, done = add(*grams[c], token)
        token = [done]
        parts[c] = [half, permute(half, "space", 2)]

    def do_solve(c):
        nonlocal token
        own, done = solve(parts[c], token)
        token = [done]
        if paired:
            pieces[c] = [own, permute(own, "space", 1)]
        else:
            pieces[c] = [lax.all_gather(own, "space", axis=0, tiled=False)]

    def do_energy(c):
        nonlocal token, carry
        *carry, done = filtered(
            merged[c], pieces[c], halves, paired, carry, owned, starts[c], token
        )
        token = [done]

    stages = {"T": do_transform, "G": do_gram, "A": do_add, "F": do_solve, "E": do_energy}
    for stage, c in order:
        stages[stage](c)
    return (carry[0], carry[1])


def solution(mesh):
    in_specs = (P(("grp", "tm"), None, "space"), P(("grp", "space")), P())
    out_specs = (P(("grp", "tm"), "space"), P(("grp", "tm"), None, None, None))
    return jax.shard_map(
        on_device, mesh=mesh, in_specs=in_specs, out_specs=out_specs, check_vma=False
    )
```

```python
import functools
import math

import jax
import jax.numpy as jnp
from jax import lax
from jax.experimental import pallas as pl
from jax.experimental.pallas import tpu as pltpu
from jax.sharding import PartitionSpec as P

F32 = jnp.float32
BF16 = jnp.bfloat16
VMEM_LIMIT = 30 * 1024 * 1024
LANES = 128


def params(**kwargs):
    return pltpu.CompilerParams(vmem_limit_bytes=VMEM_LIMIT, **kwargs)


def whole_spec():
    return pl.BlockSpec(memory_space=pltpu.VMEM)


TOKEN = jax.ShapeDtypeStruct((8, LANES), F32)


def light():
    return pl.CostEstimate(flops=1024, bytes_accessed=1024, transcendentals=0)


def in_hbm(x):
    return pltpu.with_memory_space_constraint(x, pltpu.HBM)


def any_spec():
    return pl.BlockSpec(memory_space=pl.ANY)


def dot(a, b):
    return lax.dot_general(a, b, (((1,), (0,)), ((), ())), preferred_element_type=F32)


def cos_sin(phase, length):
    quarter = length // 4
    eighth = length // 8
    shifted = phase + eighth
    low = (shifted & (quarter - 1)) - eighth
    quadrant = (shifted // quarter) & 3
    x = low.astype(F32) * F32(2.0 * math.pi / length)
    x2 = x * x
    cos = F32(1 / 40320)
    for c in (-1 / 720, 1 / 24, -0.5, 1.0):
        cos = cos * x2 + F32(c)
    sin = F32(1 / 362880)
    for c in (-1 / 5040, 1 / 120, -1 / 6, 1.0):
        sin = sin * x2 + F32(c)
    sin = sin * x
    odd = (quadrant & 1) == 1
    c0 = jnp.where(odd, sin, cos)
    s0 = jnp.where(odd, cos, sin)
    c1 = jnp.where((quadrant == 1) | (quadrant == 2), -c0, c0)
    s1 = jnp.where(quadrant >= 2, -s0, s0)
    return c1, s1


def transform_kernel(peers, parts, group, *refs):
    freq_hbm, weight_hbm, snap_hbm = refs[:3]
    outs, token = refs[-peers * len(parts) - 8 : -8], refs[-8]
    freq, weight, snap, table, wide, small_sem, snap_sem = refs[-7:]
    blocks, length, entries = snap.shape
    steps = blocks // group
    get_freq = pltpu.make_async_copy(freq_hbm, freq, small_sem.at[0])
    get_weight = pltpu.make_async_copy(weight_hbm, weight, small_sem.at[1])
    get_snap = [
        pltpu.make_async_copy(
            snap_hbm.at[pl.ds(i * group, group)], snap.at[pl.ds(i * group, group)], snap_sem.at[i]
        )
        for i in range(steps)
    ]
    token[...] = jnp.zeros_like(token)
    get_freq.start()
    for get in get_snap:
        get.start()
    get_weight.start()

    me = lax.axis_index("tm")
    groups = [
        (peer, first + j)
        for first, count in parts
        for peer in range(peers)
        for j in range(0, count, 8)
    ]
    rows = 8 * len(groups)
    per_peer = freq.shape[0] // peers
    times = lax.broadcasted_iota(jnp.int32, (8, length), 1)
    sub = lax.broadcasted_iota(jnp.int32, (8, length), 0)
    window = 0.5 - 0.5 * cos_sin(times, length)[0]
    scaled = window / F32(math.sqrt(0.375 * length))
    get_freq.wait()

    def eight(index):
        peer, offset = groups[index]
        start = jnp.bitwise_xor(me, peer) * per_peer + offset
        k = jnp.zeros((8, length), jnp.int32)
        for i in range(8):
            k = jnp.where(sub == i, freq[start + i], k)
        cos, sin = cos_sin((k * times) & (length - 1), length)
        return scaled * cos, -(scaled * sin)

    for pair in range(rows // 16):
        re0, im0 = eight(2 * pair)
        re1, im1 = eight(2 * pair + 1)
        table[16 * pair : 16 * pair + 16, :] = jnp.concatenate([re0, re1], 0).astype(BF16)
        table[rows + 16 * pair : rows + 16 * pair + 16, :] = jnp.concatenate(
            [im0, im1], 0
        ).astype(BF16)

    get_weight.wait()
    root = jnp.sqrt(weight[...])
    tiles = entries // LANES
    for step in range(steps):
        get_snap[step].wait()
        for b in range(step * group, (step + 1) * group):
            spec = dot(table[...], snap[b]) * root
            for tile in range(tiles):
                lanes = slice(tile * LANES, (tile + 1) * LANES)
                wide[tile, pl.ds(b, rows, stride=blocks), :] = spec[:rows, lanes]
                wide[tiles + tile, pl.ds(b, rows, stride=blocks), :] = spec[rows:, lanes]
    at = 0
    for out in outs:
        for j in range(out.shape[0]):
            for tile in range(2 * tiles):
                lanes = slice(tile * LANES, (tile + 1) * LANES)
                out[j, :, lanes] = wide[tile, at : at + blocks, :].astype(BF16)
            at += blocks


def transform(snapshots, weight, freq_index, peers, parts, after):
    blocks, length, entries = snapshots.shape
    group = min(blocks, 4)
    total = peers * sum(count for _, count in parts)
    shapes = [
        jax.ShapeDtypeStruct((count, blocks, 2 * entries), BF16)
        for _, count in parts
        for _ in range(peers)
    ]
    hbm = pl.BlockSpec(memory_space=pltpu.HBM)
    out = pl.pallas_call(
        functools.partial(transform_kernel, peers, parts, group),
        in_specs=[hbm] * 3 + [any_spec()] * len(after),
        out_specs=[whole_spec()] * (len(shapes) + 1),
        out_shape=shapes + [TOKEN],
        scratch_shapes=[
            pltpu.SMEM(freq_index.shape, jnp.int32),
            pltpu.VMEM(weight.shape, F32),
            pltpu.VMEM(snapshots.shape, BF16),
            pltpu.VMEM((2 * total, length), BF16),
            pltpu.VMEM((2 * entries // LANES, total * blocks, LANES), F32),
            pltpu.SemaphoreType.DMA((2,)),
            pltpu.SemaphoreType.DMA((blocks // group,)),
        ],
        compiler_params=params(),
        cost_estimate=light(),
        name="transform",
    )(in_hbm(freq_index), in_hbm(weight), in_hbm(snapshots), *after)
    return [out[i * peers : (i + 1) * peers] for i in range(len(parts))], out[-1]


def lane_low(shape, half):
    return lax.broadcasted_iota(jnp.int32, shape, 1) < half


def swap(x):
    return pltpu.roll(x, x.shape[1] // 2, 1)


def pack(compact):
    half = compact.shape[0]
    both = compact + swap(compact)
    low = lane_low((half // 2, 2 * half), half)
    return jnp.where(low, both[: half // 2], both[half // 2 :])


LOG_STEPS = 64.0
TOP = 23169.0
FINE = float(2**21)


def outer(code):
    scale = jnp.exp2(code * F32(1 / LOG_STEPS))
    width = code.shape[1]
    rows = width // 4
    shape = (rows, width)
    row = lax.broadcasted_iota(jnp.int32, shape, 0)
    lane = lax.broadcasted_iota(jnp.int32, shape, 1)
    first = jnp.sum(jnp.where(lane == row, scale, F32(0)), axis=1, keepdims=True)
    second = jnp.sum(jnp.where(lane == row + rows, scale, F32(0)), axis=1, keepdims=True)
    return scale * jnp.where(lane < width // 2, first, second)


def encode(packed):
    rows, width = packed.shape
    row = lax.broadcasted_iota(jnp.int32, packed.shape, 0)
    lane = lax.broadcasted_iota(jnp.int32, packed.shape, 1)
    on = (lane == row) | (lane == row + 3 * rows)
    diagonal = jnp.sum(jnp.where(on, packed, F32(0)), axis=0, keepdims=True)
    diagonal = diagonal + pltpu.roll(diagonal, width // 2, 1)
    logs = jnp.log(jnp.maximum(diagonal, F32(1e-30))) * F32(0.5 * LOG_STEPS / math.log(2.0))
    code = jnp.ceil(logs)
    value = jnp.round(packed * (F32(TOP) / outer(code)))
    return jnp.clip(value, F32(-32767), F32(32767)), code


def decode(value, code):
    return value * (outer(code) * F32(1 / TOP))


def to_short(x):
    return x.astype(jnp.int32).astype(jnp.int16)


def from_short(x):
    return x.astype(jnp.int32).astype(F32)


def coded_rows(number, half_rows):
    return number * half_rows + -(-number // 16) * 16


def write_coded(out, coded):
    half_rows = coded[0][0].shape[0]
    number = len(coded)
    shape = (out.shape[0] - number * half_rows, out.shape[1])
    line = lax.broadcasted_iota(jnp.int32, shape, 0)
    codes = jnp.zeros(shape, F32)
    for i, (value, code) in enumerate(coded):
        out[i * half_rows : (i + 1) * half_rows, :] = to_short(value)
        codes = jnp.where(line == i, code, codes)
    out[number * half_rows :, :] = to_short(codes)


def read_coded(ref, number, half_rows):
    codes = from_short(ref[number * half_rows :, :])
    values = [from_short(ref[i * half_rows : (i + 1) * half_rows, :]) for i in range(number)]
    return values, [codes[i : i + 1] for i in range(number)]


def unpack(packed):
    rows, half = packed.shape[0], packed.shape[1] // 2
    low = lane_low(packed.shape, half)
    other = swap(packed)
    both = jnp.concatenate(
        [jnp.where(low, packed, other), jnp.where(low, other, packed)], 0
    )
    turned = jnp.transpose(jnp.concatenate([packed, packed], 0))
    turned = jnp.where(lane_low((half, half), rows), turned[:half], turned[half:])
    turned = jnp.concatenate([turned, turned], 1)
    low = lane_low(both.shape, half)
    return 0.5 * jnp.where(low, both + turned, both - turned)


def full(compact):
    half = compact.shape[0]
    turned = swap(compact)
    low = lane_low(compact.shape, half)
    return jnp.concatenate([compact, jnp.where(low, -turned, turned)], 0)


def slot_owner(direct, slot):
    return jnp.bitwise_xor(lax.axis_index("space") & 1, slot) if direct else slot


def gram_kernel(peers, slots, direct, after, *refs):
    pieces, refs = refs[:peers], refs[peers + after :]
    merged, token, grams = refs[0], refs[1], refs[2:]
    token[...] = jnp.zeros_like(token)
    me = lax.axis_index("tm")
    here = pieces[0].shape[1]
    entries = pieces[0].shape[2] // 2
    blocks = here * peers
    per_slot = pieces[0].shape[0] // slots
    stage = None
    if here % 16:
        grams, stage = grams[:-1], grams[-1]
    low = lane_low((blocks, 2 * blocks), blocks)
    for slot in range(slots):
        owner = slot_owner(direct, slot)
        coded = []
        for i in range(per_slot):
            f = owner * per_slot + i
            if stage is None:
                for peer in range(peers):
                    start = pl.multiple_of(jnp.bitwise_xor(me, peer) * here, here)
                    merged[f, pl.ds(start, here), :] = pieces[peer][f]
                z = merged[f]
            else:
                for peer in range(peers):
                    start = pl.multiple_of(jnp.bitwise_xor(me, peer) * here, here)
                    stage[pl.ds(start, here), :] = pieces[peer][f].astype(F32)
                z = stage[...].astype(BF16)
                merged[f] = z
            w = jnp.concatenate([z[:, :entries], z[:, entries:]], 0)
            s = lax.dot_general(w, w, (((1,), (1,)), ((), ())), preferred_element_type=F32)
            s = s * F32(1.0 / blocks)
            top, bottom = s[:blocks], swap(s[blocks:])
            compact = jnp.where(low, top + bottom, top - bottom)
            if direct and slot:
                coded.append(encode(pack(compact)))
            elif direct:
                grams[0][i] = pack(compact)
            else:
                grams[0][f] = pack(compact)
        if coded:
            write_coded(grams[slot], coded)


def gram(pieces, slots, direct, after):
    peers = len(pieces)
    count, here, width = pieces[0].shape
    blocks = here * peers
    if direct:
        rows = coded_rows(count // slots, blocks // 2)
        shapes = [((count // slots, blocks // 2, 2 * blocks), F32)]
        shapes += [((rows, 2 * blocks), jnp.int16)] * (slots - 1)
    else:
        shapes = [((count, blocks // 2, 2 * blocks), F32)]
    out = pl.pallas_call(
        functools.partial(gram_kernel, peers, slots, direct, len(after)),
        in_specs=[whole_spec()] * peers + [any_spec()] * len(after),
        out_specs=[whole_spec()] * (2 + len(shapes)),
        out_shape=[jax.ShapeDtypeStruct((count, blocks, width), BF16), TOKEN]
        + [jax.ShapeDtypeStruct(*s) for s in shapes],
        scratch_shapes=[pltpu.VMEM((blocks, width), F32)] if here % 16 else [],
        compiler_params=params(),
        cost_estimate=light(),
        name="gram",
    )(*pieces, *after)
    return out[0], out[2:], out[1]


def add_kernel(own, other, *refs):
    out, token = refs[-2:]
    token[...] = jnp.zeros_like(token)
    number, half_rows, _ = own.shape
    values, codes = read_coded(other, number, half_rows)
    sums = [own[i] + decode(values[i], codes[i]) for i in range(number)]
    write_coded(out, each(encode, sums))


def add(own, other, after):
    return pl.pallas_call(
        add_kernel,
        in_specs=[whole_spec()] * 2 + [any_spec()] * len(after),
        out_specs=[whole_spec()] * 2,
        out_shape=[jax.ShapeDtypeStruct(other.shape, jnp.int16), TOKEN],
        compiler_params=params(),
        cost_estimate=light(),
        name="add",
    )(own, other, *after)


def split(x):
    high = x.astype(BF16)
    return high, (x - high.astype(F32)).astype(BF16)


def each(fn, *lists):
    return [fn(*items) for items in zip(*lists)]


def solve_kernel(parts, number, half_rows, *refs):
    ins, out, token = refs[:parts], refs[-2], refs[-1]
    token[...] = jnp.zeros_like(token)
    width = out.shape[1]
    half = width // 2
    shape = (half, width)
    row = lax.broadcasted_iota(jnp.int32, shape, 0)
    lane = lax.broadcasted_iota(jnp.int32, shape, 1)
    eye = jnp.where(row == lane, F32(1), F32(0))

    if parts == 1:
        sums = [ins[0][i] for i in range(number)]
    else:
        one = each(decode, *read_coded(ins[0], number, half_rows))
        two = each(decode, *read_coded(ins[1], number, half_rows))
        sums = [p + q for p, q in zip(one, two)]
    grams = each(unpack, sums)
    shift = each(lambda g: jnp.sum(g * eye, keepdims=True) * F32(1.0 / half), grams)
    system = each(lambda g, m: g / m + eye, grams, shift)
    both = each(lambda a: split(full(a)), system)

    low_end, high_end = 1.0, float(half + 1)
    mid, radius = (high_end + low_end) / 2, (high_end - low_end) / 2
    ratio = mid / radius
    t = 2 * ratio * ratio - 1
    scale = 2.0 / (radius * radius * t)
    x = each(lambda a: (F32(scale) * (F32(2 * mid) * eye - a)).astype(BF16), system)
    p = each(lambda v, a: eye - (dot(v, a[0]) + dot(v, a[1])), x, both)
    x = each(lambda v: v.astype(F32), x)
    for _ in range(3):
        t_next = 2 * t * t - 1
        c = F32(2 * t * t / t_next)
        pf = each(lambda q: full(q).astype(BF16), p)
        xp = each(lambda v, q: jnp.concatenate([v, q], 0).astype(BF16), x, p)
        moved = each(dot, xp, pf)
        x = each(lambda v, m: c * (v + m[:half]), x, moved)
        p = each(lambda m: c * m[half:] - F32(1 / t_next) * eye, moved)
        t = t_next
    for kind in ("scaled", "last"):
        xb = each(lambda v: v.astype(BF16), x)
        xw = each(lambda v: v.astype(F32), xb)
        xf = each(lambda v: full(v).astype(BF16), xw)
        residual = each(lambda v, a: eye - (dot(v, a[0]) + dot(v, a[1])), xb, both)
        step = each(lambda r, v: dot(r.astype(BF16), v), residual, xf)
        factor = 1.0 if kind == "last" else 2 * t * t / (2 * t * t - 1)
        x = each(lambda v, m: F32(factor) * (v + m), xw, step)
    coded = each(lambda v: encode(pack(eye - v)), x)
    filters = each(lambda c: unpack(decode(*c)), coded)
    rounded = each(lambda c: c.astype(BF16), filters)
    turned = each(lambda c: full(c.astype(F32)).astype(BF16), rounded)
    split_g = each(split, grams)
    moved = each(lambda g, c: dot(g[0], c) + dot(g[1], c), split_g, turned)
    energy = each(
        lambda c, h: jnp.sum(c.astype(F32) * h, keepdims=True) * F32(half), rounded, moved
    )
    spot = lax.broadcasted_iota(jnp.int32, (1, width), 1)

    def with_total(c, e):
        whole = jnp.floor(jnp.log(e) * F32(LOG_STEPS / math.log(2.0)))
        rest = jnp.round((e * jnp.exp2(whole * F32(-1 / LOG_STEPS)) - 1.0) * F32(FINE))
        return c[0], jnp.where(spot == half, whole, jnp.where(spot == half + 1, rest, c[1]))

    write_coded(out, each(with_total, coded, energy))


def solve(parts, number, half_rows, after):
    width = parts[0].shape[-1]
    return pl.pallas_call(
        functools.partial(solve_kernel, len(parts), number, half_rows),
        in_specs=[whole_spec()] * len(parts) + [any_spec()] * len(after),
        out_specs=[whole_spec()] * 2,
        out_shape=[
            jax.ShapeDtypeStruct((coded_rows(number, half_rows), width), jnp.int16),
            TOKEN,
        ],
        compiler_params=params(),
        cost_estimate=light(),
        name="filters",
    )(*parts, *after)


def energy_kernel(slots, direct, number, first, merged, *refs):
    pieces = refs[:number]
    energies_out, filters_out, token, energies, filters, energies_sem, filters_sem = refs[-7:]
    token[...] = jnp.zeros_like(token)
    count, blocks, width = merged.shape
    entries = width // 2
    per_slot = count // slots
    half_rows = blocks // 2
    states = entries * lax.axis_size("space")
    puts = []
    for slot in range(slots):
        owner = slot_owner(direct, slot)
        piece = pieces[slot] if direct else pieces[0].at[slot]
        values, codes = read_coded(piece, per_slot, half_rows)
        for begin in range(0, per_slot, 4):
            some = range(begin, min(begin + 4, per_slot))
            at = [owner * per_slot + i for i in some]
            code = [codes[i] for i in some]
            total = each(
                lambda c: jnp.exp2(c[:, blocks : blocks + 1] * F32(1 / LOG_STEPS))
                * (1.0 + c[:, blocks + 1 : blocks + 2] * F32(1 / FINE)),
                code,
            )
            low = lane_low((1, 2 * blocks), blocks)
            code = each(lambda c: jnp.where(low, c, swap(c)), code)
            packed = each(decode, [values[i] for i in some], code)
            z = [merged[f] for f in at]
            compact = each(unpack, packed)
            both = each(lambda c: full(c.astype(BF16).astype(F32)).astype(BF16), compact)
            w = each(lambda v: jnp.concatenate([v[:, :entries], v[:, entries:]], 0), z)
            r = each(dot, both, w)
            energy = each(
                lambda v, t: jnp.sum(v * v, axis=0, keepdims=True) * (F32(states) / t), r, total
            )
            for f, c, e in zip(at, compact, energy):
                filters[f, 0] = c[:, :blocks]
                filters[f, 1] = c[:, blocks:]
                energies[pl.ds(f, 1), :] = e
            put = pltpu.make_async_copy(
                filters.at[pl.ds(at[0], len(at))],
                filters_out.at[pl.ds(first + at[0], len(at))],
                filters_sem.at[len(puts)],
            )
            put.start()
            puts.append(put)
    put = pltpu.make_async_copy(
        energies, energies_out.at[pl.ds(first, count)], energies_sem.at[0]
    )
    put.start()
    for p in [*puts, put]:
        p.wait()


def filtered(merged, pieces, slots, direct, carry, owned, first, after):
    count, blocks, width = merged.shape
    entries = width // 2
    fixed = 1 + len(pieces)
    args = [merged, *pieces] + ([] if carry is None else list(carry)) + list(after)
    hbm = pl.BlockSpec(memory_space=pltpu.HBM)
    return pl.pallas_call(
        functools.partial(energy_kernel, slots, direct, len(pieces), first),
        in_specs=[whole_spec()] * fixed
        + ([] if carry is None else [hbm] * 2)
        + [any_spec()] * len(after),
        out_specs=[hbm] * 2 + [whole_spec()],
        out_shape=[
            jax.ShapeDtypeStruct((owned, entries), F32),
            jax.ShapeDtypeStruct((owned, 2, blocks, blocks), F32),
            TOKEN,
        ],
        input_output_aliases={} if carry is None else {fixed: 0, fixed + 1: 1},
        scratch_shapes=[
            pltpu.VMEM((count, entries), F32),
            pltpu.VMEM((count, 2, blocks, blocks), F32),
            pltpu.SemaphoreType.DMA((1,)),
            pltpu.SemaphoreType.DMA((slots * -(-(count // slots) // 4),)),
        ],
        compiler_params=params(),
        cost_estimate=light(),
        name="energy",
    )(*args)


def exchange(arrays, axis):
    size = lax.axis_size(axis)
    got = [arrays[0]]
    for offset in range(1, size):
        pairs = [(i, i ^ offset) for i in range(size)]
        got.append(lax.ppermute(arrays[offset], axis, pairs))
    return got


def plan(owned, slots):
    if slots != 4 or owned != 64:
        return [owned], (("T", 0), ("G", 0), ("F", 0), ("E", 0))
    return SIZES, ORDER


SIZES = [24, 24, 16]
ORDER = (
    ("T", 0), ("T", 1), ("G", 0), ("A", 0), ("G", 1), ("F", 0), ("A", 1), ("G", 2),
    ("E", 0), ("A", 2), ("F", 1), ("F", 2), ("E", 1), ("E", 2),
)


def permute(x, axis, offset):
    pairs = [(i, i ^ offset) for i in range(lax.axis_size(axis))]
    return lax.ppermute(x, axis, pairs)


def on_device(snapshots, entry_weight, freq_index):
    peers = lax.axis_size("tm")
    slots = lax.axis_size("space")
    owned = freq_index.shape[0] // peers
    sizes, order = plan(owned, slots)
    starts = [sum(sizes[:c]) for c in range(len(sizes))]
    paired = slots == 4
    halves = 2 if paired else slots
    weight = entry_weight.reshape(1, -1)
    sent, merged, grams, parts, pieces = {}, {}, {}, {}, {}
    carry = None
    token = []

    def do_transform(c):
        nonlocal token
        chunks = [0] if c == 0 else range(1, len(sizes))
        out, done = transform(
            snapshots, weight, freq_index, peers, [(starts[k], sizes[k]) for k in chunks], token
        )
        token = [done]
        for k, pieces_out in zip(chunks, out):
            sent[k] = [pieces_out[0]] + [
                permute(pieces_out[offset], "tm", offset) for offset in range(1, peers)
            ]

    def do_gram(c):
        nonlocal token
        merged[c], grams[c], done = gram(sent[c], halves, paired, token)
        token = [done]
        if paired:
            grams[c] = [grams[c][0], permute(grams[c][1], "space", 1)]
        else:
            parts[c] = [lax.psum_scatter(grams[c][0], "space", scatter_dimension=0, tiled=True)]

    def do_add(c):
        nonlocal token
        half, done = add(*grams[c], token)
        token = [done]
        parts[c] = [half, permute(half, "space", 2)]

    def do_solve(c):
        nonlocal token
        count = sizes[c] // halves
        own, done = solve(parts[c], count, merged[c].shape[1] // 2, token)
        token = [done]
        if paired:
            pieces[c] = [own, permute(own, "space", 1)]
        else:
            pieces[c] = [lax.all_gather(own, "space", axis=0, tiled=False)]

    def do_energy(c):
        nonlocal token, carry
        *carry, done = filtered(
            merged[c], pieces[c], halves, paired, carry, owned, starts[c], token
        )
        token = [done]

    stages = {"T": do_transform, "G": do_gram, "A": do_add, "F": do_solve, "E": do_energy}
    for stage, c in order:
        stages[stage](c)
    return (carry[0], carry[1])


def solution(mesh):
    in_specs = (P(("grp", "tm"), None, "space"), P(("grp", "space")), P())
    out_specs = (P(("grp", "tm"), "space"), P(("grp", "tm"), None, None, None))
    return jax.shard_map(
        on_device, mesh=mesh, in_specs=in_specs, out_specs=out_specs, check_vma=False
    )
```

```python
import functools
import math

import jax
import jax.numpy as jnp
from jax import lax
from jax.experimental import pallas as pl
from jax.experimental.pallas import tpu as pltpu
from jax.sharding import PartitionSpec as P

F32 = jnp.float32
BF16 = jnp.bfloat16
VMEM_LIMIT = 30 * 1024 * 1024
LANES = 128


def params(**kwargs):
    return pltpu.CompilerParams(vmem_limit_bytes=VMEM_LIMIT, **kwargs)


def whole_spec():
    return pl.BlockSpec(memory_space=pltpu.VMEM)


TOKEN = jax.ShapeDtypeStruct((8, LANES), F32)


def light():
    return pl.CostEstimate(flops=1024, bytes_accessed=1024, transcendentals=0)


def in_hbm(x):
    return pltpu.with_memory_space_constraint(x, pltpu.HBM)


def any_spec():
    return pl.BlockSpec(memory_space=pl.ANY)


def dot(a, b):
    return lax.dot_general(a, b, (((1,), (0,)), ((), ())), preferred_element_type=F32)


def cos_sin(phase, length):
    quarter = length // 4
    eighth = length // 8
    shifted = phase + eighth
    low = (shifted & (quarter - 1)) - eighth
    quadrant = (shifted // quarter) & 3
    x = low.astype(F32) * F32(2.0 * math.pi / length)
    x2 = x * x
    cos = F32(1 / 40320)
    for c in (-1 / 720, 1 / 24, -0.5, 1.0):
        cos = cos * x2 + F32(c)
    sin = F32(1 / 362880)
    for c in (-1 / 5040, 1 / 120, -1 / 6, 1.0):
        sin = sin * x2 + F32(c)
    sin = sin * x
    odd = (quadrant & 1) == 1
    c0 = jnp.where(odd, sin, cos)
    s0 = jnp.where(odd, cos, sin)
    c1 = jnp.where((quadrant == 1) | (quadrant == 2), -c0, c0)
    s1 = jnp.where(quadrant >= 2, -s0, s0)
    return c1, s1


def transform_kernel(peers, parts, group, *refs):
    freq_hbm, weight_hbm, snap_hbm = refs[:3]
    outs, token = refs[-peers * len(parts) - 8 : -8], refs[-8]
    freq, weight, snap, table, wide, small_sem, snap_sem = refs[-7:]
    blocks, length, entries = snap.shape
    steps = blocks // group
    get_freq = pltpu.make_async_copy(freq_hbm, freq, small_sem.at[0])
    get_weight = pltpu.make_async_copy(weight_hbm, weight, small_sem.at[1])
    get_snap = [
        pltpu.make_async_copy(
            snap_hbm.at[pl.ds(i * group, group)], snap.at[pl.ds(i * group, group)], snap_sem.at[i]
        )
        for i in range(steps)
    ]
    token[...] = jnp.zeros_like(token)
    get_freq.start()
    for get in get_snap:
        get.start()
    get_weight.start()

    me = lax.axis_index("tm")
    groups = [
        (peer, first + j)
        for first, count in parts
        for peer in range(peers)
        for j in range(0, count, 8)
    ]
    rows = 8 * len(groups)
    per_peer = freq.shape[0] // peers
    times = lax.broadcasted_iota(jnp.int32, (8, length), 1)
    sub = lax.broadcasted_iota(jnp.int32, (8, length), 0)
    window = 0.5 - 0.5 * cos_sin(times, length)[0]
    scaled = window / F32(math.sqrt(0.375 * length))
    get_freq.wait()

    def eight(index):
        peer, offset = groups[index]
        start = jnp.bitwise_xor(me, peer) * per_peer + offset
        k = jnp.zeros((8, length), jnp.int32)
        for i in range(8):
            k = jnp.where(sub == i, freq[start + i], k)
        cos, sin = cos_sin((k * times) & (length - 1), length)
        return scaled * cos, -(scaled * sin)

    for pair in range(rows // 16):
        re0, im0 = eight(2 * pair)
        re1, im1 = eight(2 * pair + 1)
        table[16 * pair : 16 * pair + 16, :] = jnp.concatenate([re0, re1], 0).astype(BF16)
        table[rows + 16 * pair : rows + 16 * pair + 16, :] = jnp.concatenate(
            [im0, im1], 0
        ).astype(BF16)

    get_weight.wait()
    root = jnp.sqrt(weight[...])
    tiles = entries // LANES
    for step in range(steps):
        get_snap[step].wait()
        for b in range(step * group, (step + 1) * group):
            spec = dot(table[...], snap[b]) * root
            for tile in range(tiles):
                lanes = slice(tile * LANES, (tile + 1) * LANES)
                wide[tile, pl.ds(b, rows, stride=blocks), :] = spec[:rows, lanes]
                wide[tiles + tile, pl.ds(b, rows, stride=blocks), :] = spec[rows:, lanes]
    at = 0
    for out in outs:
        for j in range(out.shape[0]):
            for tile in range(2 * tiles):
                lanes = slice(tile * LANES, (tile + 1) * LANES)
                out[j, :, lanes] = wide[tile, at : at + blocks, :].astype(BF16)
            at += blocks


def transform(snapshots, weight, freq_index, peers, parts, after):
    blocks, length, entries = snapshots.shape
    group = min(blocks, 4)
    total = peers * sum(count for _, count in parts)
    shapes = [
        jax.ShapeDtypeStruct((count, blocks, 2 * entries), BF16)
        for _, count in parts
        for _ in range(peers)
    ]
    hbm = pl.BlockSpec(memory_space=pltpu.HBM)
    out = pl.pallas_call(
        functools.partial(transform_kernel, peers, parts, group),
        in_specs=[hbm] * 3 + [any_spec()] * len(after),
        out_specs=[whole_spec()] * (len(shapes) + 1),
        out_shape=shapes + [TOKEN],
        scratch_shapes=[
            pltpu.SMEM(freq_index.shape, jnp.int32),
            pltpu.VMEM(weight.shape, F32),
            pltpu.VMEM(snapshots.shape, BF16),
            pltpu.VMEM((2 * total, length), BF16),
            pltpu.VMEM((2 * entries // LANES, total * blocks, LANES), F32),
            pltpu.SemaphoreType.DMA((2,)),
            pltpu.SemaphoreType.DMA((blocks // group,)),
        ],
        compiler_params=params(),
        cost_estimate=light(),
        name="transform",
    )(in_hbm(freq_index), in_hbm(weight), in_hbm(snapshots), *after)
    return [out[i * peers : (i + 1) * peers] for i in range(len(parts))], out[-1]


def lane_low(shape, half):
    return lax.broadcasted_iota(jnp.int32, shape, 1) < half


def swap(x):
    return pltpu.roll(x, x.shape[1] // 2, 1)


def each(fn, *lists):
    return [fn(*items) for items in zip(*lists)]


def double(compact):
    return compact + swap(compact)


def pack(both):
    half = both.shape[0]
    low = lane_low((half // 2, 2 * half), half)
    return jnp.where(low, both[: half // 2], both[half // 2 :])


def unpack(packed, scale=None):
    rows, half = packed.shape[0], packed.shape[1] // 2
    low = lane_low(packed.shape, half)
    other = swap(packed)
    both = jnp.concatenate(
        [jnp.where(low, packed, other), jnp.where(low, other, packed)], 0
    )
    turned = jnp.transpose(jnp.concatenate([packed, packed], 0))
    turned = jnp.where(lane_low((half, half), rows), turned[:half], turned[half:])
    turned = jnp.concatenate([turned, turned], 1)
    low = lane_low(both.shape, half)
    total = both + turned
    apart = both - turned
    top = jnp.where(low, total, apart)
    bottom = jnp.where(low, -apart, total)
    scale = F32(0.5) if scale is None else scale
    return scale * top, scale * bottom


def full(compact):
    half = compact.shape[0]
    turned = swap(compact)
    low = lane_low(compact.shape, half)
    return jnp.concatenate([compact, jnp.where(low, -turned, turned)], 0)


TOP = 23169.0
LOG_STEPS = 64.0
FINE = float(2**21)


def place(lines, rows):
    shape = (rows, lines[0].shape[1])
    row = lax.broadcasted_iota(jnp.int32, shape, 0)
    out = jnp.zeros(shape, F32)
    for i, line in enumerate(lines):
        out = jnp.where(row == i, line, out)
    return out


def pad_rows(number):
    return -(-number // 16) * 16


def scale_of(code):
    exponent = jnp.floor(code * F32(1 / 256))
    part = code - exponent * 256
    return (jnp.exp2(exponent) * (1 + part * F32(1 / 128))).astype(BF16)


def outer(scales, number):
    half = scales.shape[1] // 2
    wide = scales.astype(F32)
    row = lax.broadcasted_iota(jnp.int32, scales.shape, 0)
    turned = jnp.transpose(wide)[:half].astype(BF16)
    return [
        dot(turned, jnp.where(row == i, wide, F32(0)).astype(BF16)) for i in range(number)
    ]


def encode(both):
    half, width = both[0].shape
    row = lax.broadcasted_iota(jnp.int32, (half, width), 0)
    lane = lax.broadcasted_iota(jnp.int32, (half, width), 1)
    on = (lane == row) | (lane == row + half)
    diagonal = each(lambda b: jnp.sum(jnp.where(on, b, F32(0)), axis=0, keepdims=True), both)
    root = jnp.sqrt(jnp.maximum(place(diagonal, pad_rows(len(both))), F32(1e-30)))
    exponent = jnp.floor(jnp.log(root) * F32(1 / math.log(2.0)))
    part = jnp.maximum(jnp.ceil((root * jnp.exp2(-exponent) - 1) * 128), F32(0))
    codes = exponent * 256 + part
    products = outer(scale_of(codes), len(both))
    value = each(lambda b, p: jnp.round(b * (F32(TOP) / p)), both, products)
    return each(lambda v: pack(jnp.clip(v, F32(-32767), F32(32767))), value), codes


def decode(values, codes):
    products = outer(scale_of(codes), len(values))
    return each(lambda v, p: unpack(v, p * F32(0.5 / TOP)), values, products)


def to_short(x):
    return x.astype(jnp.int32).astype(jnp.int16)


def from_short(x):
    return x.astype(jnp.int32).astype(F32)


def coded_rows(number, half_rows):
    return number * half_rows + pad_rows(number)


def write_coded(out, values, codes):
    half_rows = values[0].shape[0]
    for i, value in enumerate(values):
        out[i * half_rows : (i + 1) * half_rows, :] = to_short(value)
    out[len(values) * half_rows :, :] = to_short(codes)


def read_coded(ref, number, half_rows):
    codes = from_short(ref[number * half_rows :, :])
    values = [from_short(ref[i * half_rows : (i + 1) * half_rows, :]) for i in range(number)]
    return values, codes


def slot_owner(direct, slot):
    return jnp.bitwise_xor(lax.axis_index("space") & 1, slot) if direct else slot


def gram_kernel(peers, slots, direct, after, *refs):
    pieces, refs = refs[:peers], refs[peers + after :]
    merged, token, grams = refs[0], refs[1], refs[2:]
    token[...] = jnp.zeros_like(token)
    me = lax.axis_index("tm")
    here = pieces[0].shape[1]
    entries = pieces[0].shape[2] // 2
    blocks = here * peers
    per_slot = pieces[0].shape[0] // slots
    stage = None
    if here % 16:
        grams, stage = grams[:-1], grams[-1]
    low = lane_low((blocks, 2 * blocks), blocks)
    for slot in range(slots):
        owner = slot_owner(direct, slot)
        coded = []
        for i in range(per_slot):
            f = owner * per_slot + i
            if stage is None:
                for peer in range(peers):
                    start = pl.multiple_of(jnp.bitwise_xor(me, peer) * here, here)
                    merged[f, pl.ds(start, here), :] = pieces[peer][f]
                z = merged[f]
            else:
                for peer in range(peers):
                    start = pl.multiple_of(jnp.bitwise_xor(me, peer) * here, here)
                    stage[pl.ds(start, here), :] = pieces[peer][f].astype(F32)
                z = stage[...].astype(BF16)
                merged[f] = z
            w = jnp.concatenate([z[:, :entries], z[:, entries:]], 0)
            s = lax.dot_general(w, w, (((1,), (1,)), ((), ())), preferred_element_type=F32)
            s = s * F32(1.0 / blocks)
            top, bottom = s[:blocks], swap(s[blocks:])
            compact = jnp.where(low, top + bottom, top - bottom)
            if direct and slot:
                coded.append(double(compact))
            elif direct:
                grams[0][i] = compact
            else:
                grams[0][f] = pack(double(compact))
        if coded:
            write_coded(grams[slot], *encode(coded))


def gram(pieces, slots, direct, after):
    peers = len(pieces)
    count, here, width = pieces[0].shape
    blocks = here * peers
    if direct:
        rows = coded_rows(count // slots, blocks // 2)
        shapes = [((count // slots, blocks, 2 * blocks), F32)]
        shapes += [((rows, 2 * blocks), jnp.int16)] * (slots - 1)
    else:
        shapes = [((count, blocks // 2, 2 * blocks), F32)]
    out = pl.pallas_call(
        functools.partial(gram_kernel, peers, slots, direct, len(after)),
        in_specs=[whole_spec()] * peers + [any_spec()] * len(after),
        out_specs=[whole_spec()] * (2 + len(shapes)),
        out_shape=[jax.ShapeDtypeStruct((count, blocks, width), BF16), TOKEN]
        + [jax.ShapeDtypeStruct(*s) for s in shapes],
        scratch_shapes=[pltpu.VMEM((blocks, width), F32)] if here % 16 else [],
        compiler_params=params(),
        cost_estimate=light(),
        name="gram",
    )(*pieces, *after)
    return out[0], out[2:], out[1]


def add_kernel(own, other, *refs):
    out, token = refs[-2:]
    token[...] = jnp.zeros_like(token)
    number, blocks, _ = own.shape
    received = decode(*read_coded(other, number, blocks // 2))
    sums = [double(own[i] + received[i][0]) for i in range(number)]
    write_coded(out, *encode(sums))


def add(own, other, after):
    return pl.pallas_call(
        add_kernel,
        in_specs=[whole_spec()] * 2 + [any_spec()] * len(after),
        out_specs=[whole_spec()] * 2,
        out_shape=[jax.ShapeDtypeStruct(other.shape, jnp.int16), TOKEN],
        compiler_params=params(),
        cost_estimate=light(),
        name="add",
    )(own, other, *after)


def split(x):
    high = x.astype(BF16)
    return high, (x - high.astype(F32)).astype(BF16)


def solve_kernel(parts, number, half_rows, *refs):
    ins, out, token = refs[:parts], refs[-2], refs[-1]
    token[...] = jnp.zeros_like(token)
    width = out.shape[1]
    half = width // 2
    shape = (half, width)
    row = lax.broadcasted_iota(jnp.int32, shape, 0)
    lane = lax.broadcasted_iota(jnp.int32, shape, 1)
    eye = jnp.where(row == lane, F32(1), F32(0))

    if parts == 1:
        both_halves = [unpack(ins[0][i]) for i in range(number)]
    else:
        one = decode(*read_coded(ins[0], number, half_rows))
        two = decode(*read_coded(ins[1], number, half_rows))
        both_halves = [(p[0] + q[0], p[1] + q[1]) for p, q in zip(one, two)]
    grams = [h[0] for h in both_halves]
    shift = each(lambda g: jnp.sum(g * eye, keepdims=True) * F32(1.0 / half), grams)
    eye_low = jnp.where(row + half == lane, F32(1), F32(0))
    system = each(lambda g, m: g / m + eye, grams, shift)
    under = each(lambda h, m: h[1] / m + eye_low, both_halves, shift)
    both = each(lambda a, u: split(jnp.concatenate([a, u], 0)), system, under)

    low_end, high_end = 1.0, float(half + 1)
    mid, radius = (high_end + low_end) / 2, (high_end - low_end) / 2
    ratio = mid / radius
    t = 2 * ratio * ratio - 1
    scale = 2.0 / (radius * radius * t)
    x = each(lambda a: (F32(scale) * (F32(2 * mid) * eye - a)).astype(BF16), system)
    p = each(lambda v, a: eye - (dot(v, a[0]) + dot(v, a[1])), x, both)
    x = each(lambda v: v.astype(F32), x)
    for _ in range(3):
        t_next = 2 * t * t - 1
        c = F32(2 * t * t / t_next)
        pf = each(lambda q: full(q).astype(BF16), p)
        xp = each(lambda v, q: jnp.concatenate([v, q], 0).astype(BF16), x, p)
        moved = each(dot, xp, pf)
        x = each(lambda v, m: c * (v + m[:half]), x, moved)
        p = each(lambda m: c * m[half:] - F32(1 / t_next) * eye, moved)
        t = t_next
    for kind in ("scaled", "last"):
        xb = each(lambda v: v.astype(BF16), x)
        xw = each(lambda v: v.astype(F32), xb)
        xf = each(lambda v: full(v).astype(BF16), xw)
        residual = each(lambda v, a: eye - (dot(v, a[0]) + dot(v, a[1])), xb, both)
        step = each(lambda r, v: dot(r.astype(BF16), v), residual, xf)
        factor = 1.0 if kind == "last" else 2 * t * t / (2 * t * t - 1)
        x = each(lambda v, m: F32(factor) * (v + m), xw, step)
    values, codes = encode(each(lambda v: double(eye - v), x))
    filters = decode(values, codes)
    rounded = each(lambda c: c[0].astype(BF16), filters)
    turned = each(
        lambda c: jnp.concatenate([c[0].astype(BF16), c[1].astype(BF16)], 0), filters
    )
    split_g = each(split, grams)
    moved = each(lambda g, c: dot(g[0], c) + dot(g[1], c), split_g, turned)
    energy = each(
        lambda c, h: jnp.sum(c.astype(F32) * h, keepdims=True) * F32(half), rounded, moved
    )
    energy = place([jnp.broadcast_to(e, (1, width)) for e in energy], codes.shape[0])
    energy = jnp.maximum(energy, F32(1e-30))
    whole = jnp.floor(jnp.log(energy) * F32(LOG_STEPS / math.log(2.0)))
    rest = jnp.round((energy * jnp.exp2(whole * F32(-1 / LOG_STEPS)) - 1.0) * F32(FINE))
    spot = lax.broadcasted_iota(jnp.int32, codes.shape, 1)
    codes = jnp.where(spot == half, whole, jnp.where(spot == half + 1, rest, codes))
    write_coded(out, values, codes)


def solve(parts, number, half_rows, after):
    width = parts[0].shape[-1]
    return pl.pallas_call(
        functools.partial(solve_kernel, len(parts), number, half_rows),
        in_specs=[whole_spec()] * len(parts) + [any_spec()] * len(after),
        out_specs=[whole_spec()] * 2,
        out_shape=[
            jax.ShapeDtypeStruct((coded_rows(number, half_rows), width), jnp.int16),
            TOKEN,
        ],
        compiler_params=params(),
        cost_estimate=light(),
        name="filters",
    )(*parts, *after)


def energy_kernel(slots, direct, number, first, merged, *refs):
    pieces = refs[:number]
    energies_out, filters_out, token, energies, filters, energies_sem, filters_sem = refs[-7:]
    token[...] = jnp.zeros_like(token)
    count, blocks, width = merged.shape
    entries = width // 2
    per_slot = count // slots
    half_rows = blocks // 2
    states = entries * lax.axis_size("space")
    puts = []
    for slot in range(slots):
        owner = slot_owner(direct, slot)
        piece = pieces[slot] if direct else pieces[0].at[slot]
        values, codes = read_coded(piece, per_slot, half_rows)
        whole = codes[:, blocks : blocks + 1]
        rest = codes[:, blocks + 1 : blocks + 2]
        total = jnp.exp2(whole * F32(1 / LOG_STEPS)) * (1.0 + rest * F32(1 / FINE))
        gains = F32(states) / total
        codes = jnp.where(lane_low(codes.shape, blocks), codes, swap(codes))
        products = outer(scale_of(codes), per_slot)
        for begin in range(0, per_slot, 4):
            some = range(begin, min(begin + 4, per_slot))
            at = [owner * per_slot + i for i in some]
            z = [merged[f] for f in at]
            scale = [products[i] * F32(0.5 / TOP) for i in some]
            halves = each(unpack, [values[i] for i in some], scale)
            compact = [h[0] for h in halves]
            both = each(
                lambda h: jnp.concatenate([h[0].astype(BF16), h[1].astype(BF16)], 0), halves
            )
            gain = [gains[i : i + 1] for i in some]
            w = each(lambda v: jnp.concatenate([v[:, :entries], v[:, entries:]], 0), z)
            r = each(dot, both, w)
            energy = each(
                lambda v, t: jnp.sum(v * v, axis=0, keepdims=True) * t, r, gain
            )
            for f, c, e in zip(at, compact, energy):
                filters[f, 0] = c[:, :blocks]
                filters[f, 1] = c[:, blocks:]
                energies[pl.ds(f, 1), :] = e
            put = pltpu.make_async_copy(
                filters.at[pl.ds(at[0], len(at))],
                filters_out.at[pl.ds(first + at[0], len(at))],
                filters_sem.at[len(puts)],
            )
            put.start()
            puts.append(put)
    put = pltpu.make_async_copy(
        energies, energies_out.at[pl.ds(first, count)], energies_sem.at[0]
    )
    put.start()
    for p in [*puts, put]:
        p.wait()


def filtered(merged, pieces, slots, direct, carry, owned, first, after):
    count, blocks, width = merged.shape
    entries = width // 2
    fixed = 1 + len(pieces)
    args = [merged, *pieces] + ([] if carry is None else list(carry)) + list(after)
    hbm = pl.BlockSpec(memory_space=pltpu.HBM)
    return pl.pallas_call(
        functools.partial(energy_kernel, slots, direct, len(pieces), first),
        in_specs=[whole_spec()] * fixed
        + ([] if carry is None else [hbm] * 2)
        + [any_spec()] * len(after),
        out_specs=[hbm] * 2 + [whole_spec()],
        out_shape=[
            jax.ShapeDtypeStruct((owned, entries), F32),
            jax.ShapeDtypeStruct((owned, 2, blocks, blocks), F32),
            TOKEN,
        ],
        input_output_aliases={} if carry is None else {fixed: 0, fixed + 1: 1},
        scratch_shapes=[
            pltpu.VMEM((count, entries), F32),
            pltpu.VMEM((count, 2, blocks, blocks), F32),
            pltpu.SemaphoreType.DMA((1,)),
            pltpu.SemaphoreType.DMA((slots * -(-(count // slots) // 4),)),
        ],
        compiler_params=params(),
        cost_estimate=light(),
        name="energy",
    )(*args)


def exchange(arrays, axis):
    size = lax.axis_size(axis)
    got = [arrays[0]]
    for offset in range(1, size):
        pairs = [(i, i ^ offset) for i in range(size)]
        got.append(lax.ppermute(arrays[offset], axis, pairs))
    return got


def plan(owned, slots):
    if slots != 4 or owned != 64:
        return [owned], (("T", 0), ("G", 0), ("F", 0), ("E", 0))
    return SIZES, ORDER


SIZES = [24, 24, 16]
ORDER = (
    ("T", 0), ("T", 1), ("G", 0), ("A", 0), ("F", 0), ("G", 1), ("A", 1), ("E", 0),
    ("G", 2), ("A", 2), ("F", 1), ("F", 2), ("E", 1), ("E", 2),
)


def permute(x, axis, offset):
    pairs = [(i, i ^ offset) for i in range(lax.axis_size(axis))]
    return lax.ppermute(x, axis, pairs)


def on_device(snapshots, entry_weight, freq_index):
    peers = lax.axis_size("tm")
    slots = lax.axis_size("space")
    owned = freq_index.shape[0] // peers
    sizes, order = plan(owned, slots)
    starts = [sum(sizes[:c]) for c in range(len(sizes))]
    paired = slots == 4
    halves = 2 if paired else slots
    weight = entry_weight.reshape(1, -1)
    sent, merged, grams, parts, pieces = {}, {}, {}, {}, {}
    carry = None
    token = []

    def do_transform(c):
        nonlocal token
        chunks = [0] if c == 0 else range(1, len(sizes))
        out, done = transform(
            snapshots, weight, freq_index, peers, [(starts[k], sizes[k]) for k in chunks], token
        )
        token = [done]
        for k, pieces_out in zip(chunks, out):
            sent[k] = [pieces_out[0]] + [
                permute(pieces_out[offset], "tm", offset) for offset in range(1, peers)
            ]
        if c == 0 and len(sizes) > 1:
            token.append(sent[0][1])

    def do_gram(c):
        nonlocal token
        if c == 0:
            token += [sent[k][1] for k in range(1, len(sizes))]
        merged[c], grams[c], done = gram(sent[c], halves, paired, token)
        token = [done]
        if paired:
            grams[c] = [grams[c][0], permute(grams[c][1], "space", 1)]
        else:
            parts[c] = [lax.psum_scatter(grams[c][0], "space", scatter_dimension=0, tiled=True)]

    def do_add(c):
        nonlocal token
        half, done = add(*grams[c], token)
        token = [done]
        parts[c] = [half, permute(half, "space", 2)]

    def do_solve(c):
        nonlocal token
        count = sizes[c] // halves
        own, done = solve(parts[c], count, merged[c].shape[1] // 2, token)
        token = [done]
        if paired:
            pieces[c] = [own, permute(own, "space", 1)]
        else:
            pieces[c] = [lax.all_gather(own, "space", axis=0, tiled=False)]

    def do_energy(c):
        nonlocal token, carry
        *carry, done = filtered(
            merged[c], pieces[c], halves, paired, carry, owned, starts[c], token
        )
        token = [done]

    stages = {"T": do_transform, "G": do_gram, "A": do_add, "F": do_solve, "E": do_energy}
    for stage, c in order:
        stages[stage](c)
    return (carry[0], carry[1])


def solution(mesh):
    in_specs = (P(("grp", "tm"), None, "space"), P(("grp", "space")), P())
    out_specs = (P(("grp", "tm"), "space"), P(("grp", "tm"), None, None, None))
    return jax.shard_map(
        on_device, mesh=mesh, in_specs=in_specs, out_specs=out_specs, check_vma=False
    )
```

```python
import functools
import math

import jax
import jax.numpy as jnp
from jax import lax
from jax.experimental import pallas as pl
from jax.experimental.pallas import tpu as pltpu
from jax.sharding import PartitionSpec as P

F32 = jnp.float32
BF16 = jnp.bfloat16
VMEM_LIMIT = 30 * 1024 * 1024
LANES = 128


def params(**kwargs):
    return pltpu.CompilerParams(vmem_limit_bytes=VMEM_LIMIT, **kwargs)


def whole_spec():
    return pl.BlockSpec(memory_space=pltpu.VMEM)


TOKEN = jax.ShapeDtypeStruct((8, LANES), F32)


def light():
    return pl.CostEstimate(flops=1024, bytes_accessed=1024, transcendentals=0)


def in_hbm(x):
    return pltpu.with_memory_space_constraint(x, pltpu.HBM)


def any_spec():
    return pl.BlockSpec(memory_space=pl.ANY)


def dot(a, b):
    return lax.dot_general(a, b, (((1,), (0,)), ((), ())), preferred_element_type=F32)


def cos_sin(phase, length):
    quarter = length // 4
    eighth = length // 8
    shifted = phase + eighth
    low = (shifted & (quarter - 1)) - eighth
    quadrant = (shifted // quarter) & 3
    x = low.astype(F32) * F32(2.0 * math.pi / length)
    x2 = x * x
    cos = F32(1 / 40320)
    for c in (-1 / 720, 1 / 24, -0.5, 1.0):
        cos = cos * x2 + F32(c)
    sin = F32(1 / 362880)
    for c in (-1 / 5040, 1 / 120, -1 / 6, 1.0):
        sin = sin * x2 + F32(c)
    sin = sin * x
    odd = (quadrant & 1) == 1
    c0 = jnp.where(odd, sin, cos)
    s0 = jnp.where(odd, cos, sin)
    c1 = jnp.where((quadrant == 1) | (quadrant == 2), -c0, c0)
    s1 = jnp.where(quadrant >= 2, -s0, s0)
    return c1, s1


def transform_kernel(peers, parts, group, *refs):
    freq_hbm, weight_hbm, snap_hbm = refs[:3]
    outs, token = refs[-peers * len(parts) - 8 : -8], refs[-8]
    freq, weight, snap, table, wide, small_sem, snap_sem = refs[-7:]
    blocks, length, entries = snap.shape
    steps = blocks // group
    get_freq = pltpu.make_async_copy(freq_hbm, freq, small_sem.at[0])
    get_weight = pltpu.make_async_copy(weight_hbm, weight, small_sem.at[1])
    get_snap = [
        pltpu.make_async_copy(
            snap_hbm.at[pl.ds(i * group, group)], snap.at[pl.ds(i * group, group)], snap_sem.at[i]
        )
        for i in range(steps)
    ]
    token[...] = jnp.zeros_like(token)
    get_freq.start()
    for get in get_snap:
        get.start()
    get_weight.start()

    me = lax.axis_index("tm")
    groups = [
        (peer, first + j)
        for first, count in parts
        for peer in range(peers)
        for j in range(0, count, 8)
    ]
    rows = 8 * len(groups)
    per_peer = freq.shape[0] // peers
    times = lax.broadcasted_iota(jnp.int32, (8, length), 1)
    sub = lax.broadcasted_iota(jnp.int32, (8, length), 0)
    window = 0.5 - 0.5 * cos_sin(times, length)[0]
    scaled = window / F32(math.sqrt(0.375 * length))
    get_freq.wait()

    def eight(index):
        peer, offset = groups[index]
        start = jnp.bitwise_xor(me, peer) * per_peer + offset
        k = jnp.zeros((8, length), jnp.int32)
        for i in range(8):
            k = jnp.where(sub == i, freq[start + i], k)
        cos, sin = cos_sin((k * times) & (length - 1), length)
        return scaled * cos, -(scaled * sin)

    for pair in range(rows // 16):
        re0, im0 = eight(2 * pair)
        re1, im1 = eight(2 * pair + 1)
        table[16 * pair : 16 * pair + 16, :] = jnp.concatenate([re0, re1], 0).astype(BF16)
        table[rows + 16 * pair : rows + 16 * pair + 16, :] = jnp.concatenate(
            [im0, im1], 0
        ).astype(BF16)

    get_weight.wait()
    root = jnp.sqrt(weight[...])
    tiles = entries // LANES
    for step in range(steps):
        get_snap[step].wait()
        for b in range(step * group, (step + 1) * group):
            spec = dot(table[...], snap[b]) * root
            for tile in range(tiles):
                lanes = slice(tile * LANES, (tile + 1) * LANES)
                wide[tile, pl.ds(b, rows, stride=blocks), :] = spec[:rows, lanes]
                wide[tiles + tile, pl.ds(b, rows, stride=blocks), :] = spec[rows:, lanes]
    at = 0
    for out in outs:
        for j in range(out.shape[0]):
            for tile in range(2 * tiles):
                lanes = slice(tile * LANES, (tile + 1) * LANES)
                out[j, :, lanes] = wide[tile, at : at + blocks, :].astype(BF16)
            at += blocks


def transform(snapshots, weight, freq_index, peers, parts, after):
    blocks, length, entries = snapshots.shape
    group = min(blocks, 4)
    total = peers * sum(count for _, count in parts)
    shapes = [
        jax.ShapeDtypeStruct((count, blocks, 2 * entries), BF16)
        for _, count in parts
        for _ in range(peers)
    ]
    hbm = pl.BlockSpec(memory_space=pltpu.HBM)
    out = pl.pallas_call(
        functools.partial(transform_kernel, peers, parts, group),
        in_specs=[hbm] * 3 + [any_spec()] * len(after),
        out_specs=[whole_spec()] * (len(shapes) + 1),
        out_shape=shapes + [TOKEN],
        scratch_shapes=[
            pltpu.SMEM(freq_index.shape, jnp.int32),
            pltpu.VMEM(weight.shape, F32),
            pltpu.VMEM(snapshots.shape, BF16),
            pltpu.VMEM((2 * total, length), BF16),
            pltpu.VMEM((2 * entries // LANES, total * blocks, LANES), F32),
            pltpu.SemaphoreType.DMA((2,)),
            pltpu.SemaphoreType.DMA((blocks // group,)),
        ],
        compiler_params=params(),
        cost_estimate=light(),
        name="transform",
    )(in_hbm(freq_index), in_hbm(weight), in_hbm(snapshots), *after)
    return [out[i * peers : (i + 1) * peers] for i in range(len(parts))], out[-1]


def lane_low(shape, half):
    return lax.broadcasted_iota(jnp.int32, shape, 1) < half


def swap(x):
    return pltpu.roll(x, x.shape[1] // 2, 1)


def each(fn, *lists):
    return [fn(*items) for items in zip(*lists)]


def double(compact):
    return compact + swap(compact)


def pack(both):
    half = both.shape[0]
    low = lane_low((half // 2, 2 * half), half)
    return jnp.where(low, both[: half // 2], both[half // 2 :])


def unpack(packed, scale=None):
    rows, half = packed.shape[0], packed.shape[1] // 2
    low = lane_low(packed.shape, half)
    other = swap(packed)
    both = jnp.concatenate(
        [jnp.where(low, packed, other), jnp.where(low, other, packed)], 0
    )
    turned = jnp.transpose(jnp.concatenate([packed, packed], 0))
    turned = jnp.where(lane_low((half, half), rows), turned[:half], turned[half:])
    turned = jnp.concatenate([turned, turned], 1)
    low = lane_low(both.shape, half)
    total = both + turned
    apart = both - turned
    top = jnp.where(low, total, apart)
    bottom = jnp.where(low, -apart, total)
    scale = F32(0.5) if scale is None else scale
    return scale * top, scale * bottom


def full(compact):
    half = compact.shape[0]
    turned = swap(compact)
    low = lane_low(compact.shape, half)
    return jnp.concatenate([compact, jnp.where(low, -turned, turned)], 0)


TOP = 23169.0
LOG_STEPS = 64.0
FINE = float(2**21)


def place(lines, rows):
    shape = (rows, lines[0].shape[1])
    row = lax.broadcasted_iota(jnp.int32, shape, 0)
    out = jnp.zeros(shape, F32)
    for i, line in enumerate(lines):
        out = jnp.where(row == i, line, out)
    return out


def pad_rows(number):
    return -(-number // 16) * 16


def scale_of(code):
    exponent = jnp.floor(code * F32(1 / 256))
    part = code - exponent * 256
    return (jnp.exp2(exponent) * (1 + part * F32(1 / 128))).astype(BF16)


def outer(scales, number):
    half = scales.shape[1] // 2
    wide = scales.astype(F32)
    row = lax.broadcasted_iota(jnp.int32, scales.shape, 0)
    turned = jnp.transpose(wide)[:half].astype(BF16)
    return [
        dot(turned, jnp.where(row == i, wide, F32(0)).astype(BF16)) for i in range(number)
    ]


def encode(both):
    half, width = both[0].shape
    row = lax.broadcasted_iota(jnp.int32, (half, width), 0)
    lane = lax.broadcasted_iota(jnp.int32, (half, width), 1)
    on = (lane == row) | (lane == row + half)
    diagonal = each(lambda b: jnp.sum(jnp.where(on, b, F32(0)), axis=0, keepdims=True), both)
    root = jnp.sqrt(jnp.maximum(place(diagonal, pad_rows(len(both))), F32(1e-30)))
    exponent = jnp.floor(jnp.log(root) * F32(1 / math.log(2.0)))
    part = jnp.maximum(jnp.ceil((root * jnp.exp2(-exponent) - 1) * 128), F32(0))
    codes = exponent * 256 + part
    products = outer(scale_of(codes), len(both))
    value = each(lambda b, p: jnp.round(b * (F32(TOP) / p)), both, products)
    return each(lambda v: pack(jnp.clip(v, F32(-32767), F32(32767))), value), codes


def decode(values, codes):
    products = outer(scale_of(codes), len(values))
    return each(lambda v, p: unpack(v, p * F32(0.5 / TOP)), values, products)


def spread(values, codes):
    products = outer(scale_of(codes), len(values))
    return each(lambda v, p: v * pack(p * F32(1 / TOP)), values, products)


def to_short(x):
    return x.astype(jnp.int32).astype(jnp.int16)


def from_short(x):
    return x.astype(jnp.int32).astype(F32)


def coded_rows(number, half_rows):
    return number * half_rows + pad_rows(number)


def write_coded(out, values, codes):
    half_rows = values[0].shape[0]
    for i, value in enumerate(values):
        out[i * half_rows : (i + 1) * half_rows, :] = to_short(value)
    out[len(values) * half_rows :, :] = to_short(codes)


def read_coded(ref, number, half_rows):
    codes = from_short(ref[number * half_rows :, :])
    values = [from_short(ref[i * half_rows : (i + 1) * half_rows, :]) for i in range(number)]
    return values, codes


def slot_owner(direct, slot):
    return jnp.bitwise_xor(lax.axis_index("space") & 1, slot) if direct else slot


def gram_kernel(peers, slots, direct, after, *refs):
    pieces, refs = refs[:peers], refs[peers + after :]
    merged, token, grams = refs[0], refs[1], refs[2:]
    token[...] = jnp.zeros_like(token)
    me = lax.axis_index("tm")
    here = pieces[0].shape[1]
    entries = pieces[0].shape[2] // 2
    blocks = here * peers
    per_slot = pieces[0].shape[0] // slots
    stage = None
    if here % 16:
        grams, stage = grams[:-1], grams[-1]
    low = lane_low((blocks, 2 * blocks), blocks)
    for slot in range(slots):
        owner = slot_owner(direct, slot)
        coded = []
        for i in range(per_slot):
            f = owner * per_slot + i
            if stage is None:
                for peer in range(peers):
                    start = pl.multiple_of(jnp.bitwise_xor(me, peer) * here, here)
                    merged[f, pl.ds(start, here), :] = pieces[peer][f]
                z = merged[f]
            else:
                for peer in range(peers):
                    start = pl.multiple_of(jnp.bitwise_xor(me, peer) * here, here)
                    stage[pl.ds(start, here), :] = pieces[peer][f].astype(F32)
                z = stage[...].astype(BF16)
                merged[f] = z
            w = jnp.concatenate([z[:, :entries], z[:, entries:]], 0)
            s = lax.dot_general(w, w, (((1,), (1,)), ((), ())), preferred_element_type=F32)
            s = s * F32(1.0 / blocks)
            top, bottom = s[:blocks], swap(s[blocks:])
            compact = jnp.where(low, top + bottom, top - bottom)
            if direct:
                coded.append(double(compact))
            else:
                grams[0][f] = pack(double(compact))
        if coded:
            write_coded(grams[slot], *encode(coded))


def gram(pieces, slots, direct, after):
    peers = len(pieces)
    count, here, width = pieces[0].shape
    blocks = here * peers
    if direct:
        rows = coded_rows(count // slots, blocks // 2)
        shapes = [((rows, 2 * blocks), jnp.int16)] * slots
    else:
        shapes = [((count, blocks // 2, 2 * blocks), F32)]
    out = pl.pallas_call(
        functools.partial(gram_kernel, peers, slots, direct, len(after)),
        in_specs=[whole_spec()] * peers + [any_spec()] * len(after),
        out_specs=[whole_spec()] * (2 + len(shapes)),
        out_shape=[jax.ShapeDtypeStruct((count, blocks, width), BF16), TOKEN]
        + [jax.ShapeDtypeStruct(*s) for s in shapes],
        scratch_shapes=[pltpu.VMEM((blocks, width), F32)] if here % 16 else [],
        compiler_params=params(),
        cost_estimate=light(),
        name="gram",
    )(*pieces, *after)
    return out[0], out[2:], out[1]


def split(x):
    high = x.astype(BF16)
    return high, (x - high.astype(F32)).astype(BF16)


def solve_kernel(parts, number, half_rows, *refs):
    ins, out, token = refs[:parts], refs[-2], refs[-1]
    token[...] = jnp.zeros_like(token)
    width = out.shape[1]
    half = width // 2
    shape = (half, width)
    row = lax.broadcasted_iota(jnp.int32, shape, 0)
    lane = lax.broadcasted_iota(jnp.int32, shape, 1)
    eye = jnp.where(row == lane, F32(1), F32(0))

    if parts == 1:
        sums = [ins[0][i] for i in range(number)]
    else:
        found = [spread(*read_coded(r, number, half_rows)) for r in ins]
        sums = [(o + a) + (b + c) for o, a, b, c in zip(*found)]
    both_halves = each(unpack, sums)
    grams = [h[0] for h in both_halves]
    shift = each(lambda g: jnp.sum(g * eye, keepdims=True) * F32(1.0 / half), grams)
    eye_low = jnp.where(row + half == lane, F32(1), F32(0))
    system = each(lambda g, m: g / m + eye, grams, shift)
    under = each(lambda h, m: h[1] / m + eye_low, both_halves, shift)
    both = each(lambda a, u: split(jnp.concatenate([a, u], 0)), system, under)

    low_end, high_end = 1.0, float(half + 1)
    mid, radius = (high_end + low_end) / 2, (high_end - low_end) / 2
    ratio = mid / radius
    t = 2 * ratio * ratio - 1
    scale = 2.0 / (radius * radius * t)
    x = each(lambda a: (F32(scale) * (F32(2 * mid) * eye - a)).astype(BF16), system)
    p = each(lambda v, a: eye - (dot(v, a[0]) + dot(v, a[1])), x, both)
    x = each(lambda v: v.astype(F32), x)
    for _ in range(3):
        t_next = 2 * t * t - 1
        c = F32(2 * t * t / t_next)
        pf = each(lambda q: full(q).astype(BF16), p)
        xp = each(lambda v, q: jnp.concatenate([v, q], 0).astype(BF16), x, p)
        moved = each(dot, xp, pf)
        x = each(lambda v, m: c * (v + m[:half]), x, moved)
        p = each(lambda m: c * m[half:] - F32(1 / t_next) * eye, moved)
        t = t_next
    for kind in ("scaled", "last"):
        xb = each(lambda v: v.astype(BF16), x)
        xw = each(lambda v: v.astype(F32), xb)
        xf = each(lambda v: full(v).astype(BF16), xw)
        residual = each(lambda v, a: eye - (dot(v, a[0]) + dot(v, a[1])), xb, both)
        step = each(lambda r, v: dot(r.astype(BF16), v), residual, xf)
        factor = 1.0 if kind == "last" else 2 * t * t / (2 * t * t - 1)
        x = each(lambda v, m: F32(factor) * (v + m), xw, step)
    values, codes = encode(each(lambda v: double(eye - v), x))
    filters = decode(values, codes)
    rounded = each(lambda c: c[0].astype(BF16), filters)
    turned = each(
        lambda c: jnp.concatenate([c[0].astype(BF16), c[1].astype(BF16)], 0), filters
    )
    split_g = each(split, grams)
    moved = each(lambda g, c: dot(g[0], c) + dot(g[1], c), split_g, turned)
    energy = each(
        lambda c, h: jnp.sum(c.astype(F32) * h, keepdims=True) * F32(half), rounded, moved
    )
    energy = place([jnp.broadcast_to(e, (1, width)) for e in energy], codes.shape[0])
    energy = jnp.maximum(energy, F32(1e-30))
    whole = jnp.floor(jnp.log(energy) * F32(LOG_STEPS / math.log(2.0)))
    rest = jnp.round((energy * jnp.exp2(whole * F32(-1 / LOG_STEPS)) - 1.0) * F32(FINE))
    spot = lax.broadcasted_iota(jnp.int32, codes.shape, 1)
    codes = jnp.where(spot == half, whole, jnp.where(spot == half + 1, rest, codes))
    write_coded(out, values, codes)


def solve(parts, number, half_rows, after):
    width = parts[0].shape[-1]
    return pl.pallas_call(
        functools.partial(solve_kernel, len(parts), number, half_rows),
        in_specs=[whole_spec()] * len(parts) + [any_spec()] * len(after),
        out_specs=[whole_spec()] * 2,
        out_shape=[
            jax.ShapeDtypeStruct((coded_rows(number, half_rows), width), jnp.int16),
            TOKEN,
        ],
        compiler_params=params(),
        cost_estimate=light(),
        name="filters",
    )(*parts, *after)


def energy_kernel(slots, direct, number, first, merged, *refs):
    pieces = refs[:number]
    energies_out, filters_out, token, energies, filters, energies_sem, filters_sem = refs[-7:]
    token[...] = jnp.zeros_like(token)
    count, blocks, width = merged.shape
    entries = width // 2
    per_slot = count // slots
    half_rows = blocks // 2
    states = entries * lax.axis_size("space")
    puts = []
    for slot in range(slots):
        owner = slot_owner(direct, slot)
        piece = pieces[slot] if direct else pieces[0].at[slot]
        values, codes = read_coded(piece, per_slot, half_rows)
        whole = codes[:, blocks : blocks + 1]
        rest = codes[:, blocks + 1 : blocks + 2]
        total = jnp.exp2(whole * F32(1 / LOG_STEPS)) * (1.0 + rest * F32(1 / FINE))
        gains = F32(states) / total
        codes = jnp.where(lane_low(codes.shape, blocks), codes, swap(codes))
        products = outer(scale_of(codes), per_slot)
        for begin in range(0, per_slot, 4):
            some = range(begin, min(begin + 4, per_slot))
            at = [owner * per_slot + i for i in some]
            z = [merged[f] for f in at]
            scale = [products[i] * F32(0.5 / TOP) for i in some]
            halves = each(unpack, [values[i] for i in some], scale)
            compact = [h[0] for h in halves]
            both = each(
                lambda h: jnp.concatenate([h[0].astype(BF16), h[1].astype(BF16)], 0), halves
            )
            gain = [gains[i : i + 1] for i in some]
            w = each(lambda v: jnp.concatenate([v[:, :entries], v[:, entries:]], 0), z)
            r = each(dot, both, w)
            energy = each(
                lambda v, t: jnp.sum(v * v, axis=0, keepdims=True) * t, r, gain
            )
            for f, c, e in zip(at, compact, energy):
                filters[f, 0] = c[:, :blocks]
                filters[f, 1] = c[:, blocks:]
                energies[pl.ds(f, 1), :] = e
            put = pltpu.make_async_copy(
                filters.at[pl.ds(at[0], len(at))],
                filters_out.at[pl.ds(first + at[0], len(at))],
                filters_sem.at[len(puts)],
            )
            put.start()
            puts.append(put)
    put = pltpu.make_async_copy(
        energies, energies_out.at[pl.ds(first, count)], energies_sem.at[0]
    )
    put.start()
    for p in [*puts, put]:
        p.wait()


def filtered(merged, pieces, slots, direct, carry, owned, first, after):
    count, blocks, width = merged.shape
    entries = width // 2
    fixed = 1 + len(pieces)
    args = [merged, *pieces] + ([] if carry is None else list(carry)) + list(after)
    hbm = pl.BlockSpec(memory_space=pltpu.HBM)
    return pl.pallas_call(
        functools.partial(energy_kernel, slots, direct, len(pieces), first),
        in_specs=[whole_spec()] * fixed
        + ([] if carry is None else [hbm] * 2)
        + [any_spec()] * len(after),
        out_specs=[hbm] * 2 + [whole_spec()],
        out_shape=[
            jax.ShapeDtypeStruct((owned, entries), F32),
            jax.ShapeDtypeStruct((owned, 2, blocks, blocks), F32),
            TOKEN,
        ],
        input_output_aliases={} if carry is None else {fixed: 0, fixed + 1: 1},
        scratch_shapes=[
            pltpu.VMEM((count, entries), F32),
            pltpu.VMEM((count, 2, blocks, blocks), F32),
            pltpu.SemaphoreType.DMA((1,)),
            pltpu.SemaphoreType.DMA((slots * -(-(count // slots) // 4),)),
        ],
        compiler_params=params(),
        cost_estimate=light(),
        name="energy",
    )(*args)


def exchange(arrays, axis):
    size = lax.axis_size(axis)
    got = [arrays[0]]
    for offset in range(1, size):
        pairs = [(i, i ^ offset) for i in range(size)]
        got.append(lax.ppermute(arrays[offset], axis, pairs))
    return got


def plan(owned, slots):
    if slots != 4 or owned != 64:
        return [owned], (("T", 0), ("G", 0), ("F", 0), ("E", 0))
    return SIZES, ORDER


SIZES = [16, 24, 24]
ORDER = (
    ("T", 0), ("T", 1), ("G", 0), ("T", 2), ("F", 0), ("G", 1), ("E", 0), ("F", 1),
    ("G", 2), ("E", 1), ("F", 2), ("E", 2),
)


def permute(x, axis, offset):
    pairs = [(i, i ^ offset) for i in range(lax.axis_size(axis))]
    return lax.ppermute(x, axis, pairs)


def on_device(snapshots, entry_weight, freq_index):
    peers = lax.axis_size("tm")
    slots = lax.axis_size("space")
    owned = freq_index.shape[0] // peers
    sizes, order = plan(owned, slots)
    starts = [sum(sizes[:c]) for c in range(len(sizes))]
    paired = slots == 4
    halves = 2 if paired else slots
    weight = entry_weight.reshape(1, -1)
    sent, merged, grams, parts, pieces = {}, {}, {}, {}, {}
    carry = None
    token = []

    def do_transform(c):
        nonlocal token
        (out,), done = transform(
            snapshots, weight, freq_index, peers, [(starts[c], sizes[c])], token
        )
        sent[c] = [out[0]] + [permute(out[offset], "tm", offset) for offset in range(1, peers)]
        token = [done, sent[c][1]] if c == 0 and len(sizes) > 1 else [done]

    def do_gram(c):
        nonlocal token
        merged[c], grams[c], done = gram(sent[c], halves, paired, token)
        token = [done]
        if paired:
            own, other = grams[c]
            parts[c] = [
                own,
                permute(own, "space", 2),
                permute(other, "space", 1),
                permute(other, "space", 3),
            ]
        else:
            parts[c] = [lax.psum_scatter(grams[c][0], "space", scatter_dimension=0, tiled=True)]

    def do_solve(c):
        nonlocal token
        count = sizes[c] // halves
        own, done = solve(parts[c], count, merged[c].shape[1] // 2, token)
        token = [done]
        if paired:
            pieces[c] = [own, permute(own, "space", 1)]
        else:
            pieces[c] = [lax.all_gather(own, "space", axis=0, tiled=False)]

    def do_energy(c):
        nonlocal token, carry
        *carry, done = filtered(
            merged[c], pieces[c], halves, paired, carry, owned, starts[c], token
        )
        token = [done]

    stages = {"T": do_transform, "G": do_gram, "F": do_solve, "E": do_energy}
    for stage, c in order:
        stages[stage](c)
    return (carry[0], carry[1])


def solution(mesh):
    in_specs = (P(("grp", "tm"), None, "space"), P(("grp", "space")), P())
    out_specs = (P(("grp", "tm"), "space"), P(("grp", "tm"), None, None, None))
    return jax.shard_map(
        on_device, mesh=mesh, in_specs=in_specs, out_specs=out_specs, check_vma=False
    )
```

```python
import functools
import math

import jax
import jax.numpy as jnp
from jax import lax
from jax.experimental import pallas as pl
from jax.experimental.pallas import tpu as pltpu
from jax.sharding import PartitionSpec as P

F32 = jnp.float32
BF16 = jnp.bfloat16
VMEM_LIMIT = 30 * 1024 * 1024
LANES = 128


def params(**kwargs):
    return pltpu.CompilerParams(vmem_limit_bytes=VMEM_LIMIT, **kwargs)


def whole_spec():
    return pl.BlockSpec(memory_space=pltpu.VMEM)


TOKEN = jax.ShapeDtypeStruct((8, LANES), F32)


def light():
    return pl.CostEstimate(flops=1024, bytes_accessed=1024, transcendentals=0)


def in_hbm(x):
    return pltpu.with_memory_space_constraint(x, pltpu.HBM)


def any_spec():
    return pl.BlockSpec(memory_space=pl.ANY)


def dot(a, b):
    return lax.dot_general(a, b, (((1,), (0,)), ((), ())), preferred_element_type=F32)


def cos_sin(phase, length):
    quarter = length // 4
    eighth = length // 8
    shifted = phase + eighth
    low = (shifted & (quarter - 1)) - eighth
    quadrant = (shifted // quarter) & 3
    x = low.astype(F32) * F32(2.0 * math.pi / length)
    x2 = x * x
    cos = F32(1 / 40320)
    for c in (-1 / 720, 1 / 24, -0.5, 1.0):
        cos = cos * x2 + F32(c)
    sin = F32(1 / 362880)
    for c in (-1 / 5040, 1 / 120, -1 / 6, 1.0):
        sin = sin * x2 + F32(c)
    sin = sin * x
    odd = (quadrant & 1) == 1
    c0 = jnp.where(odd, sin, cos)
    s0 = jnp.where(odd, cos, sin)
    c1 = jnp.where((quadrant == 1) | (quadrant == 2), -c0, c0)
    s1 = jnp.where(quadrant >= 2, -s0, s0)
    return c1, s1


def transform_kernel(peers, parts, group, *refs):
    freq_hbm, weight_hbm, snap_hbm = refs[:3]
    outs, token = refs[-peers * len(parts) - 8 : -8], refs[-8]
    freq, weight, snap, table, wide, small_sem, snap_sem = refs[-7:]
    blocks, length, entries = snap.shape
    steps = blocks // group
    get_freq = pltpu.make_async_copy(freq_hbm, freq, small_sem.at[0])
    get_weight = pltpu.make_async_copy(weight_hbm, weight, small_sem.at[1])
    get_snap = [
        pltpu.make_async_copy(
            snap_hbm.at[pl.ds(i * group, group)], snap.at[pl.ds(i * group, group)], snap_sem.at[i]
        )
        for i in range(steps)
    ]
    token[...] = jnp.zeros_like(token)
    get_freq.start()
    for get in get_snap:
        get.start()
    get_weight.start()

    me = lax.axis_index("tm")
    groups = [
        (peer, first + j)
        for first, count in parts
        for peer in range(peers)
        for j in range(0, count, 8)
    ]
    rows = 8 * len(groups)
    per_peer = freq.shape[0] // peers
    times = lax.broadcasted_iota(jnp.int32, (8, length), 1)
    sub = lax.broadcasted_iota(jnp.int32, (8, length), 0)
    window = 0.5 - 0.5 * cos_sin(times, length)[0]
    scaled = window / F32(math.sqrt(0.375 * length))
    get_freq.wait()

    def eight(index):
        peer, offset = groups[index]
        start = jnp.bitwise_xor(me, peer) * per_peer + offset
        k = jnp.zeros((8, length), jnp.int32)
        for i in range(8):
            k = jnp.where(sub == i, freq[start + i], k)
        cos, sin = cos_sin((k * times) & (length - 1), length)
        return scaled * cos, -(scaled * sin)

    for pair in range(rows // 16):
        re0, im0 = eight(2 * pair)
        re1, im1 = eight(2 * pair + 1)
        table[16 * pair : 16 * pair + 16, :] = jnp.concatenate([re0, re1], 0).astype(BF16)
        table[rows + 16 * pair : rows + 16 * pair + 16, :] = jnp.concatenate(
            [im0, im1], 0
        ).astype(BF16)

    get_weight.wait()
    root = jnp.sqrt(weight[...])
    tiles = entries // LANES
    for step in range(steps):
        get_snap[step].wait()
        for b in range(step * group, (step + 1) * group):
            spec = dot(table[...], snap[b]) * root
            for tile in range(tiles):
                lanes = slice(tile * LANES, (tile + 1) * LANES)
                wide[tile, pl.ds(b, rows, stride=blocks), :] = spec[:rows, lanes]
                wide[tiles + tile, pl.ds(b, rows, stride=blocks), :] = spec[rows:, lanes]
    at = 0
    for out in outs:
        for j in range(out.shape[0]):
            for tile in range(2 * tiles):
                lanes = slice(tile * LANES, (tile + 1) * LANES)
                out[j, :, lanes] = wide[tile, at : at + blocks, :].astype(BF16)
            at += blocks


def transform(snapshots, weight, freq_index, peers, parts, after):
    blocks, length, entries = snapshots.shape
    group = min(blocks, 4)
    total = peers * sum(count for _, count in parts)
    shapes = [
        jax.ShapeDtypeStruct((count, blocks, 2 * entries), BF16)
        for _, count in parts
        for _ in range(peers)
    ]
    hbm = pl.BlockSpec(memory_space=pltpu.HBM)
    out = pl.pallas_call(
        functools.partial(transform_kernel, peers, parts, group),
        in_specs=[hbm] * 3 + [any_spec()] * len(after),
        out_specs=[whole_spec()] * (len(shapes) + 1),
        out_shape=shapes + [TOKEN],
        scratch_shapes=[
            pltpu.SMEM(freq_index.shape, jnp.int32),
            pltpu.VMEM(weight.shape, F32),
            pltpu.VMEM(snapshots.shape, BF16),
            pltpu.VMEM((2 * total, length), BF16),
            pltpu.VMEM((2 * entries // LANES, total * blocks, LANES), F32),
            pltpu.SemaphoreType.DMA((2,)),
            pltpu.SemaphoreType.DMA((blocks // group,)),
        ],
        compiler_params=params(),
        cost_estimate=light(),
        name="transform",
    )(in_hbm(freq_index), in_hbm(weight), in_hbm(snapshots), *after)
    return [out[i * peers : (i + 1) * peers] for i in range(len(parts))], out[-1]


def lane_low(shape, half):
    return lax.broadcasted_iota(jnp.int32, shape, 1) < half


def swap(x):
    return pltpu.roll(x, x.shape[1] // 2, 1)


def each(fn, *lists):
    return [fn(*items) for items in zip(*lists)]


def double(compact):
    return compact + swap(compact)


def pack(both):
    half = both.shape[0]
    low = lane_low((half // 2, 2 * half), half)
    return jnp.where(low, both[: half // 2], both[half // 2 :])


def unpack(packed, scale=None):
    rows, half = packed.shape[0], packed.shape[1] // 2
    low = lane_low(packed.shape, half)
    other = swap(packed)
    both = jnp.concatenate(
        [jnp.where(low, packed, other), jnp.where(low, other, packed)], 0
    )
    turned = jnp.transpose(jnp.concatenate([packed, packed], 0))
    turned = jnp.where(lane_low((half, half), rows), turned[:half], turned[half:])
    turned = jnp.concatenate([turned, turned], 1)
    low = lane_low(both.shape, half)
    total = both + turned
    apart = both - turned
    top = jnp.where(low, total, apart)
    bottom = jnp.where(low, -apart, total)
    scale = F32(0.5) if scale is None else scale
    return scale * top, scale * bottom


def full(compact):
    half = compact.shape[0]
    turned = swap(compact)
    low = lane_low(compact.shape, half)
    return jnp.concatenate([compact, jnp.where(low, -turned, turned)], 0)


TOP = 23169.0
LOG_STEPS = 64.0
FINE = float(2**21)


def place(lines, rows):
    shape = (rows, lines[0].shape[1])
    row = lax.broadcasted_iota(jnp.int32, shape, 0)
    out = jnp.zeros(shape, F32)
    for i, line in enumerate(lines):
        out = jnp.where(row == i, line, out)
    return out


def pad_rows(number):
    return -(-number // 16) * 16


def scale_of(code):
    exponent = jnp.floor(code * F32(1 / 256))
    part = code - exponent * 256
    return (jnp.exp2(exponent) * (1 + part * F32(1 / 128))).astype(BF16)


def outer(scales, number):
    half = scales.shape[1] // 2
    wide = scales.astype(F32)
    row = lax.broadcasted_iota(jnp.int32, scales.shape, 0)
    turned = jnp.transpose(wide)[:half].astype(BF16)
    return [
        dot(turned, jnp.where(row == i, wide, F32(0)).astype(BF16)) for i in range(number)
    ]


def encode(both):
    half, width = both[0].shape
    row = lax.broadcasted_iota(jnp.int32, (half, width), 0)
    lane = lax.broadcasted_iota(jnp.int32, (half, width), 1)
    on = (lane == row) | (lane == row + half)
    diagonal = each(lambda b: jnp.sum(jnp.where(on, b, F32(0)), axis=0, keepdims=True), both)
    root = jnp.sqrt(jnp.maximum(place(diagonal, pad_rows(len(both))), F32(1e-30)))
    exponent = jnp.floor(jnp.log(root) * F32(1 / math.log(2.0)))
    part = jnp.maximum(jnp.ceil((root * jnp.exp2(-exponent) - 1) * 128), F32(0))
    codes = exponent * 256 + part
    products = outer(scale_of(codes), len(both))
    value = each(lambda b, p: jnp.round(b * (F32(TOP) / p)), both, products)
    return each(lambda v: pack(jnp.clip(v, F32(-32767), F32(32767))), value), codes


def decode(values, codes):
    products = outer(scale_of(codes), len(values))
    return each(lambda v, p: unpack(v, p * F32(0.5 / TOP)), values, products)


def spread(values, codes):
    products = outer(scale_of(codes), len(values))
    return each(lambda v, p: v * pack(p * F32(1 / TOP)), values, products)


def to_short(x):
    return x.astype(jnp.int32).astype(jnp.int16)


def from_short(x):
    return x.astype(jnp.int32).astype(F32)


def coded_rows(number, half_rows):
    return number * half_rows + pad_rows(number)


def write_coded(out, values, codes):
    half_rows = values[0].shape[0]
    for i, value in enumerate(values):
        out[i * half_rows : (i + 1) * half_rows, :] = to_short(value)
    out[len(values) * half_rows :, :] = to_short(codes)


def read_coded(ref, number, half_rows):
    codes = from_short(ref[number * half_rows :, :])
    values = [from_short(ref[i * half_rows : (i + 1) * half_rows, :]) for i in range(number)]
    return values, codes


def slot_owner(direct, slot):
    return jnp.bitwise_xor(lax.axis_index("space") & 1, slot) if direct else slot


def gram_kernel(peers, slots, direct, after, *refs):
    pieces, refs = refs[:peers], refs[peers + after :]
    merged, token, grams = refs[0], refs[1], refs[2:]
    token[...] = jnp.zeros_like(token)
    me = lax.axis_index("tm")
    here = pieces[0].shape[1]
    entries = pieces[0].shape[2] // 2
    blocks = here * peers
    per_slot = pieces[0].shape[0] // slots
    stage = None
    if here % 16:
        grams, stage = grams[:-1], grams[-1]
    low = lane_low((blocks, 2 * blocks), blocks)
    for slot in range(slots):
        owner = slot_owner(direct, slot)
        coded = []
        for i in range(per_slot):
            f = owner * per_slot + i
            if stage is None:
                for peer in range(peers):
                    start = pl.multiple_of(jnp.bitwise_xor(me, peer) * here, here)
                    merged[f, pl.ds(start, here), :] = pieces[peer][f]
                z = merged[f]
            else:
                for peer in range(peers):
                    start = pl.multiple_of(jnp.bitwise_xor(me, peer) * here, here)
                    stage[pl.ds(start, here), :] = pieces[peer][f].astype(F32)
                z = stage[...].astype(BF16)
                merged[f] = z
            w = jnp.concatenate([z[:, :entries], z[:, entries:]], 0)
            s = lax.dot_general(w, w, (((1,), (1,)), ((), ())), preferred_element_type=F32)
            s = s * F32(1.0 / blocks)
            top, bottom = s[:blocks], swap(s[blocks:])
            compact = jnp.where(low, top + bottom, top - bottom)
            if direct:
                coded.append(double(compact))
            else:
                grams[0][f] = pack(double(compact))
        if coded:
            write_coded(grams[slot], *encode(coded))


def gram(pieces, slots, direct, after):
    peers = len(pieces)
    count, here, width = pieces[0].shape
    blocks = here * peers
    if direct:
        rows = coded_rows(count // slots, blocks // 2)
        shapes = [((rows, 2 * blocks), jnp.int16)] * slots
    else:
        shapes = [((count, blocks // 2, 2 * blocks), F32)]
    out = pl.pallas_call(
        functools.partial(gram_kernel, peers, slots, direct, len(after)),
        in_specs=[whole_spec()] * peers + [any_spec()] * len(after),
        out_specs=[whole_spec()] * (2 + len(shapes)),
        out_shape=[jax.ShapeDtypeStruct((count, blocks, width), BF16), TOKEN]
        + [jax.ShapeDtypeStruct(*s) for s in shapes],
        scratch_shapes=[pltpu.VMEM((blocks, width), F32)] if here % 16 else [],
        compiler_params=params(),
        cost_estimate=light(),
        name="gram",
    )(*pieces, *after)
    return out[0], out[2:], out[1]


def split(x):
    high = x.astype(BF16)
    return high, (x - high.astype(F32)).astype(BF16)


def solve_kernel(parts, number, half_rows, *refs):
    ins, out, token = refs[:parts], refs[-2], refs[-1]
    token[...] = jnp.zeros_like(token)
    width = out.shape[1]
    half = width // 2
    shape = (half, width)
    row = lax.broadcasted_iota(jnp.int32, shape, 0)
    lane = lax.broadcasted_iota(jnp.int32, shape, 1)
    eye = jnp.where(row == lane, F32(1), F32(0))

    if parts == 1:
        sums = [ins[0][i] for i in range(number)]
    else:
        found = [spread(*read_coded(r, number, half_rows)) for r in ins]
        sums = [(o + a) + (b + c) for o, a, b, c in zip(*found)]
    both_halves = each(unpack, sums)
    grams = [h[0] for h in both_halves]
    shift = each(lambda g: jnp.sum(g * eye, keepdims=True) * F32(1.0 / half), grams)
    eye_low = jnp.where(row + half == lane, F32(1), F32(0))
    system = each(lambda g, m: g / m + eye, grams, shift)
    under = each(lambda h, m: h[1] / m + eye_low, both_halves, shift)
    both = each(
        lambda a, u: jnp.concatenate(split(jnp.concatenate([a, u], 0)), 1), system, under
    )

    def times(v, a):
        wide = dot(v, a)
        return wide[:, :width] + wide[:, width:]


    low_end, high_end = 1.0, float(half + 1)
    mid, radius = (high_end + low_end) / 2, (high_end - low_end) / 2
    ratio = mid / radius
    t = 2 * ratio * ratio - 1
    scale = 2.0 / (radius * radius * t)
    x = each(lambda a: (F32(scale) * (F32(2 * mid) * eye - a)).astype(BF16), system)
    p = each(lambda v, a: eye - times(v, a), x, both)
    x = each(lambda v: v.astype(F32), x)
    for _ in range(3):
        t_next = 2 * t * t - 1
        c = F32(2 * t * t / t_next)
        pf = each(lambda q: full(q).astype(BF16), p)
        xp = each(lambda v, q: jnp.concatenate([v, q], 0).astype(BF16), x, p)
        moved = each(dot, xp, pf)
        x = each(lambda v, m: c * (v + m[:half]), x, moved)
        p = each(lambda m: c * m[half:] - F32(1 / t_next) * eye, moved)
        t = t_next
    for kind in ("scaled", "last"):
        xb = each(lambda v: v.astype(BF16), x)
        xw = each(lambda v: v.astype(F32), xb)
        xf = each(lambda v: full(v).astype(BF16), xw)
        residual = each(lambda v, a: eye - times(v, a), xb, both)
        step = each(lambda r, v: dot(r.astype(BF16), v), residual, xf)
        factor = 1.0 if kind == "last" else 2 * t * t / (2 * t * t - 1)
        x = each(lambda v, m: F32(factor) * (v + m), xw, step)
    values, codes = encode(each(lambda v: double(eye - v), x))
    filters = decode(values, codes)
    rounded = each(lambda c: c[0].astype(BF16), filters)
    turned = each(
        lambda c: jnp.concatenate([c[0].astype(BF16), c[1].astype(BF16)], 0), filters
    )
    split_g = each(lambda g: jnp.concatenate(split(g), 0), grams)
    moved = each(dot, split_g, turned)
    moved = each(lambda m: m[:half] + m[half:], moved)
    energy = each(
        lambda c, h: jnp.sum(c.astype(F32) * h, keepdims=True) * F32(half), rounded, moved
    )
    energy = place([jnp.broadcast_to(e, (1, width)) for e in energy], codes.shape[0])
    energy = jnp.maximum(energy, F32(1e-30))
    whole = jnp.floor(jnp.log(energy) * F32(LOG_STEPS / math.log(2.0)))
    rest = jnp.round((energy * jnp.exp2(whole * F32(-1 / LOG_STEPS)) - 1.0) * F32(FINE))
    spot = lax.broadcasted_iota(jnp.int32, codes.shape, 1)
    codes = jnp.where(spot == half, whole, jnp.where(spot == half + 1, rest, codes))
    write_coded(out, values, codes)


def solve(parts, number, half_rows, after):
    width = parts[0].shape[-1]
    return pl.pallas_call(
        functools.partial(solve_kernel, len(parts), number, half_rows),
        in_specs=[whole_spec()] * len(parts) + [any_spec()] * len(after),
        out_specs=[whole_spec()] * 2,
        out_shape=[
            jax.ShapeDtypeStruct((coded_rows(number, half_rows), width), jnp.int16),
            TOKEN,
        ],
        compiler_params=params(),
        cost_estimate=light(),
        name="filters",
    )(*parts, *after)


def energy_kernel(slots, direct, number, first, merged, *refs):
    pieces = refs[:number]
    energies_out, filters_out, token, energies, filters, energies_sem, filters_sem = refs[-7:]
    token[...] = jnp.zeros_like(token)
    count, blocks, width = merged.shape
    entries = width // 2
    per_slot = count // slots
    half_rows = blocks // 2
    states = entries * lax.axis_size("space")
    puts = []
    for slot in range(slots):
        owner = slot_owner(direct, slot)
        piece = pieces[slot] if direct else pieces[0].at[slot]
        values, codes = read_coded(piece, per_slot, half_rows)
        whole = codes[:, blocks : blocks + 1]
        rest = codes[:, blocks + 1 : blocks + 2]
        total = jnp.exp2(whole * F32(1 / LOG_STEPS)) * (1.0 + rest * F32(1 / FINE))
        gains = F32(states) / total
        codes = jnp.where(lane_low(codes.shape, blocks), codes, swap(codes))
        products = outer(scale_of(codes), per_slot)
        for begin in range(0, per_slot, 4):
            some = range(begin, min(begin + 4, per_slot))
            at = [owner * per_slot + i for i in some]
            z = [merged[f] for f in at]
            scale = [products[i] * F32(0.5 / TOP) for i in some]
            halves = each(unpack, [values[i] for i in some], scale)
            compact = [h[0] for h in halves]
            both = each(
                lambda h: jnp.concatenate([h[0].astype(BF16), h[1].astype(BF16)], 0), halves
            )
            gain = [gains[i : i + 1] for i in some]
            w = each(lambda v: jnp.concatenate([v[:, :entries], v[:, entries:]], 0), z)
            r = each(dot, both, w)
            energy = each(
                lambda v, t: jnp.sum(v * v, axis=0, keepdims=True) * t, r, gain
            )
            for f, c, e in zip(at, compact, energy):
                filters[f, 0] = c[:, :blocks]
                filters[f, 1] = c[:, blocks:]
                energies[pl.ds(f, 1), :] = e
            put = pltpu.make_async_copy(
                filters.at[pl.ds(at[0], len(at))],
                filters_out.at[pl.ds(first + at[0], len(at))],
                filters_sem.at[len(puts)],
            )
            put.start()
            puts.append(put)
    put = pltpu.make_async_copy(
        energies, energies_out.at[pl.ds(first, count)], energies_sem.at[0]
    )
    put.start()
    for p in [*puts, put]:
        p.wait()


def filtered(merged, pieces, slots, direct, carry, owned, first, after):
    count, blocks, width = merged.shape
    entries = width // 2
    fixed = 1 + len(pieces)
    args = [merged, *pieces] + ([] if carry is None else list(carry)) + list(after)
    hbm = pl.BlockSpec(memory_space=pltpu.HBM)
    return pl.pallas_call(
        functools.partial(energy_kernel, slots, direct, len(pieces), first),
        in_specs=[whole_spec()] * fixed
        + ([] if carry is None else [hbm] * 2)
        + [any_spec()] * len(after),
        out_specs=[hbm] * 2 + [whole_spec()],
        out_shape=[
            jax.ShapeDtypeStruct((owned, entries), F32),
            jax.ShapeDtypeStruct((owned, 2, blocks, blocks), F32),
            TOKEN,
        ],
        input_output_aliases={} if carry is None else {fixed: 0, fixed + 1: 1},
        scratch_shapes=[
            pltpu.VMEM((count, entries), F32),
            pltpu.VMEM((count, 2, blocks, blocks), F32),
            pltpu.SemaphoreType.DMA((1,)),
            pltpu.SemaphoreType.DMA((slots * -(-(count // slots) // 4),)),
        ],
        compiler_params=params(),
        cost_estimate=light(),
        name="energy",
    )(*args)


def exchange(arrays, axis):
    size = lax.axis_size(axis)
    got = [arrays[0]]
    for offset in range(1, size):
        pairs = [(i, i ^ offset) for i in range(size)]
        got.append(lax.ppermute(arrays[offset], axis, pairs))
    return got


def plan(owned, slots):
    if slots != 4 or owned != 64:
        return [owned], (("T", 0), ("G", 0), ("F", 0), ("E", 0))
    return SIZES, ORDER


SIZES = [16, 24, 24]
ORDER = (
    ("T", 0), ("T", 1), ("T", 2), ("G", 0), ("F", 0), ("G", 1), ("E", 0), ("F", 1),
    ("G", 2), ("E", 1), ("F", 2), ("E", 2),
)


def permute(x, axis, offset):
    pairs = [(i, i ^ offset) for i in range(lax.axis_size(axis))]
    return lax.ppermute(x, axis, pairs)


def on_device(snapshots, entry_weight, freq_index):
    peers = lax.axis_size("tm")
    slots = lax.axis_size("space")
    owned = freq_index.shape[0] // peers
    sizes, order = plan(owned, slots)
    starts = [sum(sizes[:c]) for c in range(len(sizes))]
    paired = slots == 4
    halves = 2 if paired else slots
    weight = entry_weight.reshape(1, -1)
    sent, merged, grams, parts, pieces = {}, {}, {}, {}, {}
    carry = None
    token = []

    def do_transform(c):
        nonlocal token
        (out,), done = transform(
            snapshots, weight, freq_index, peers, [(starts[c], sizes[c])], token
        )
        sent[c] = [out[0]] + [permute(out[offset], "tm", offset) for offset in range(1, peers)]
        token = [done, sent[c][1]] if c == 0 and len(sizes) > 1 else [done]

    def do_gram(c):
        nonlocal token
        merged[c], grams[c], done = gram(sent[c], halves, paired, token)
        token = [done]
        if paired:
            own, other = grams[c]
            parts[c] = [
                own,
                permute(own, "space", 2),
                permute(other, "space", 1),
                permute(other, "space", 3),
            ]
        else:
            parts[c] = [lax.psum_scatter(grams[c][0], "space", scatter_dimension=0, tiled=True)]

    def do_solve(c):
        nonlocal token
        count = sizes[c] // halves
        own, done = solve(parts[c], count, merged[c].shape[1] // 2, token)
        token = [done]
        if paired:
            pieces[c] = [own, permute(own, "space", 1)]
        else:
            pieces[c] = [lax.all_gather(own, "space", axis=0, tiled=False)]

    def do_energy(c):
        nonlocal token, carry
        *carry, done = filtered(
            merged[c], pieces[c], halves, paired, carry, owned, starts[c], token
        )
        token = [done]

    stages = {"T": do_transform, "G": do_gram, "F": do_solve, "E": do_energy}
    for stage, c in order:
        stages[stage](c)
    return (carry[0], carry[1])


def solution(mesh):
    in_specs = (P(("grp", "tm"), None, "space"), P(("grp", "space")), P())
    out_specs = (P(("grp", "tm"), "space"), P(("grp", "tm"), None, None, None))
    return jax.shard_map(
        on_device, mesh=mesh, in_specs=in_specs, out_specs=out_specs, check_vma=False
    )
```

```python
import functools
import math

import jax
import jax.numpy as jnp
from jax import lax
from jax.experimental import pallas as pl
from jax.experimental.pallas import tpu as pltpu
from jax.sharding import PartitionSpec as P

F32 = jnp.float32
BF16 = jnp.bfloat16
VMEM_LIMIT = 30 * 1024 * 1024
LANES = 128


def params(**kwargs):
    return pltpu.CompilerParams(vmem_limit_bytes=VMEM_LIMIT, **kwargs)


def whole_spec():
    return pl.BlockSpec(memory_space=pltpu.VMEM)


TOKEN = jax.ShapeDtypeStruct((8, LANES), F32)


def light():
    return pl.CostEstimate(flops=1024, bytes_accessed=1024, transcendentals=0)


def in_hbm(x):
    return pltpu.with_memory_space_constraint(x, pltpu.HBM)


def any_spec():
    return pl.BlockSpec(memory_space=pl.ANY)


def dot(a, b):
    return lax.dot_general(a, b, (((1,), (0,)), ((), ())), preferred_element_type=F32)


def cos_sin(phase, length):
    quarter = length // 4
    eighth = length // 8
    shifted = phase + eighth
    low = (shifted & (quarter - 1)) - eighth
    quadrant = (shifted // quarter) & 3
    x = low.astype(F32) * F32(2.0 * math.pi / length)
    x2 = x * x
    cos = F32(1 / 40320)
    for c in (-1 / 720, 1 / 24, -0.5, 1.0):
        cos = cos * x2 + F32(c)
    sin = F32(1 / 362880)
    for c in (-1 / 5040, 1 / 120, -1 / 6, 1.0):
        sin = sin * x2 + F32(c)
    sin = sin * x
    odd = (quadrant & 1) == 1
    c0 = jnp.where(odd, sin, cos)
    s0 = jnp.where(odd, cos, sin)
    c1 = jnp.where((quadrant == 1) | (quadrant == 2), -c0, c0)
    s1 = jnp.where(quadrant >= 2, -s0, s0)
    return c1, s1


def transform_kernel(peers, parts, group, *refs):
    freq_hbm, weight_hbm, snap_hbm = refs[:3]
    outs, token = refs[-peers * len(parts) - 8 : -8], refs[-8]
    freq, weight, snap, table, wide, small_sem, snap_sem = refs[-7:]
    blocks, length, entries = snap.shape
    steps = blocks // group
    get_freq = pltpu.make_async_copy(freq_hbm, freq, small_sem.at[0])
    get_weight = pltpu.make_async_copy(weight_hbm, weight, small_sem.at[1])
    get_snap = [
        pltpu.make_async_copy(
            snap_hbm.at[pl.ds(i * group, group)], snap.at[pl.ds(i * group, group)], snap_sem.at[i]
        )
        for i in range(steps)
    ]
    token[...] = jnp.zeros_like(token)
    get_freq.start()
    for get in get_snap:
        get.start()
    get_weight.start()

    me = lax.axis_index("tm")
    groups = [
        (peer, first + j)
        for first, count in parts
        for peer in range(peers)
        for j in range(0, count, 8)
    ]
    rows = 8 * len(groups)
    per_peer = freq.shape[0] // peers
    times = lax.broadcasted_iota(jnp.int32, (8, length), 1)
    sub = lax.broadcasted_iota(jnp.int32, (8, length), 0)
    window = 0.5 - 0.5 * cos_sin(times, length)[0]
    scaled = window / F32(math.sqrt(0.375 * length))
    get_freq.wait()

    def eight(index):
        peer, offset = groups[index]
        start = jnp.bitwise_xor(me, peer) * per_peer + offset
        k = jnp.zeros((8, length), jnp.int32)
        for i in range(8):
            k = jnp.where(sub == i, freq[start + i], k)
        cos, sin = cos_sin((k * times) & (length - 1), length)
        return scaled * cos, -(scaled * sin)

    for pair in range(rows // 16):
        re0, im0 = eight(2 * pair)
        re1, im1 = eight(2 * pair + 1)
        table[16 * pair : 16 * pair + 16, :] = jnp.concatenate([re0, re1], 0).astype(BF16)
        table[rows + 16 * pair : rows + 16 * pair + 16, :] = jnp.concatenate(
            [im0, im1], 0
        ).astype(BF16)

    get_weight.wait()
    root = jnp.sqrt(weight[...])
    tiles = entries // LANES
    for step in range(steps):
        get_snap[step].wait()
        for b in range(step * group, (step + 1) * group):
            spec = dot(table[...], snap[b]) * root
            for tile in range(tiles):
                lanes = slice(tile * LANES, (tile + 1) * LANES)
                wide[tile, pl.ds(b, rows, stride=blocks), :] = spec[:rows, lanes]
                wide[tiles + tile, pl.ds(b, rows, stride=blocks), :] = spec[rows:, lanes]
    at = 0
    for out in outs:
        for j in range(out.shape[0]):
            for tile in range(2 * tiles):
                lanes = slice(tile * LANES, (tile + 1) * LANES)
                out[j, :, lanes] = wide[tile, at : at + blocks, :].astype(BF16)
            at += blocks


def transform(snapshots, weight, freq_index, peers, parts, after):
    blocks, length, entries = snapshots.shape
    group = min(blocks, 4)
    total = peers * sum(count for _, count in parts)
    shapes = [
        jax.ShapeDtypeStruct((count, blocks, 2 * entries), BF16)
        for _, count in parts
        for _ in range(peers)
    ]
    hbm = pl.BlockSpec(memory_space=pltpu.HBM)
    out = pl.pallas_call(
        functools.partial(transform_kernel, peers, parts, group),
        in_specs=[hbm] * 3 + [any_spec()] * len(after),
        out_specs=[whole_spec()] * (len(shapes) + 1),
        out_shape=shapes + [TOKEN],
        scratch_shapes=[
            pltpu.SMEM(freq_index.shape, jnp.int32),
            pltpu.VMEM(weight.shape, F32),
            pltpu.VMEM(snapshots.shape, BF16),
            pltpu.VMEM((2 * total, length), BF16),
            pltpu.VMEM((2 * entries // LANES, total * blocks, LANES), F32),
            pltpu.SemaphoreType.DMA((2,)),
            pltpu.SemaphoreType.DMA((blocks // group,)),
        ],
        compiler_params=params(),
        cost_estimate=light(),
        name="transform",
    )(in_hbm(freq_index), in_hbm(weight), in_hbm(snapshots), *after)
    return [out[i * peers : (i + 1) * peers] for i in range(len(parts))], out[-1]


def lane_low(shape, half):
    return lax.broadcasted_iota(jnp.int32, shape, 1) < half


def swap(x):
    return pltpu.roll(x, x.shape[1] // 2, 1)


def each(fn, *lists):
    return [fn(*items) for items in zip(*lists)]


def double(compact):
    return compact + swap(compact)


def pack(both):
    half = both.shape[0]
    low = lane_low((half // 2, 2 * half), half)
    return jnp.where(low, both[: half // 2], both[half // 2 :])


def unpack(packed, scale=None):
    rows, half = packed.shape[0], packed.shape[1] // 2
    low = lane_low(packed.shape, half)
    other = swap(packed)
    both = jnp.concatenate(
        [jnp.where(low, packed, other), jnp.where(low, other, packed)], 0
    )
    turned = jnp.transpose(jnp.concatenate([packed, packed], 0))
    turned = jnp.where(lane_low((half, half), rows), turned[:half], turned[half:])
    turned = jnp.concatenate([turned, turned], 1)
    low = lane_low(both.shape, half)
    total = both + turned
    apart = both - turned
    top = jnp.where(low, total, apart)
    bottom = jnp.where(low, -apart, total)
    scale = F32(0.5) if scale is None else scale
    return scale * top, scale * bottom


def full(compact):
    half = compact.shape[0]
    turned = swap(compact)
    low = lane_low(compact.shape, half)
    return jnp.concatenate([compact, jnp.where(low, -turned, turned)], 0)


TOP = 23169.0
LOG_STEPS = 64.0
FINE = float(2**21)


def place(lines, rows):
    shape = (rows, lines[0].shape[1])
    row = lax.broadcasted_iota(jnp.int32, shape, 0)
    out = jnp.zeros(shape, F32)
    for i, line in enumerate(lines):
        out = jnp.where(row == i, line, out)
    return out


def pad_rows(number):
    return -(-number // 16) * 16


def scale_of(code):
    exponent = jnp.floor(code * F32(1 / 256))
    part = code - exponent * 256
    return (jnp.exp2(exponent) * (1 + part * F32(1 / 128))).astype(BF16)


def outer(scales, number):
    half = scales.shape[1] // 2
    wide = scales.astype(F32)
    row = lax.broadcasted_iota(jnp.int32, scales.shape, 0)
    turned = jnp.transpose(wide)[:half].astype(BF16)
    return [
        dot(turned, jnp.where(row == i, wide, F32(0)).astype(BF16)) for i in range(number)
    ]


def inverse_outer(scales, number):
    half = scales.shape[1] // 2
    rows = scales.shape[0]
    inverse = 1.0 / scales.astype(F32)
    high = inverse.astype(BF16).astype(F32)
    low = inverse - high
    left = jnp.transpose(jnp.concatenate([high, high, low], 0))[:half].astype(BF16)
    right = jnp.concatenate([high, low, high], 0)
    row = lax.broadcasted_iota(jnp.int32, right.shape, 0) & (rows - 1)
    return [
        dot(left, jnp.where(row == i, right, F32(0)).astype(BF16)) for i in range(number)
    ]


def encode(both):
    half, width = both[0].shape
    row = lax.broadcasted_iota(jnp.int32, (half, width), 0)
    lane = lax.broadcasted_iota(jnp.int32, (half, width), 1)
    on = (lane == row) | (lane == row + half)
    diagonal = each(lambda b: jnp.sum(jnp.where(on, b, F32(0)), axis=0, keepdims=True), both)
    root = jnp.sqrt(jnp.maximum(place(diagonal, pad_rows(len(both))), F32(1e-30)))
    exponent = jnp.floor(jnp.log(root) * F32(1 / math.log(2.0)))
    part = jnp.maximum(jnp.ceil((root * jnp.exp2(-exponent) - 1) * 128), F32(0))
    codes = exponent * 256 + part
    scales = scale_of(codes)
    inverse = inverse_outer(scales, len(both))
    value = each(lambda b, p: jnp.round((b * F32(TOP)) * p), both, inverse)
    return each(lambda v: pack(jnp.clip(v, F32(-32767), F32(32767))), value), codes, scales


def spread(values, codes):
    products = outer(scale_of(codes), len(values))
    return each(lambda v, p: v * pack(p * F32(1 / TOP)), values, products)


def to_short(x):
    return x.astype(jnp.int32).astype(jnp.int16)


def from_short(x):
    return x.astype(jnp.int32).astype(F32)


def coded_rows(number, half_rows):
    return number * half_rows + pad_rows(number)


def write_coded(out, values, codes):
    half_rows = values[0].shape[0]
    for i, value in enumerate(values):
        out[i * half_rows : (i + 1) * half_rows, :] = to_short(value)
    out[len(values) * half_rows :, :] = to_short(codes)


def read_coded(ref, number, half_rows):
    codes = from_short(ref[number * half_rows :, :])
    values = [from_short(ref[i * half_rows : (i + 1) * half_rows, :]) for i in range(number)]
    return values, codes


def slot_owner(direct, slot):
    return jnp.bitwise_xor(lax.axis_index("space") & 1, slot) if direct else slot


def gram_kernel(peers, slots, direct, after, *refs):
    pieces, refs = refs[:peers], refs[peers + after :]
    merged, token, grams = refs[0], refs[1], refs[2:]
    token[...] = jnp.zeros_like(token)
    me = lax.axis_index("tm")
    here = pieces[0].shape[1]
    entries = pieces[0].shape[2] // 2
    blocks = here * peers
    per_slot = pieces[0].shape[0] // slots
    stage = None
    if here % 16:
        grams, stage = grams[:-1], grams[-1]
    low = lane_low((blocks, 2 * blocks), blocks)
    for slot in range(slots):
        owner = slot_owner(direct, slot)
        coded = []
        for i in range(per_slot):
            f = owner * per_slot + i
            if stage is None:
                for peer in range(peers):
                    start = pl.multiple_of(jnp.bitwise_xor(me, peer) * here, here)
                    merged[f, pl.ds(start, here), :] = pieces[peer][f]
                z = merged[f]
            else:
                for peer in range(peers):
                    start = pl.multiple_of(jnp.bitwise_xor(me, peer) * here, here)
                    stage[pl.ds(start, here), :] = pieces[peer][f].astype(F32)
                z = stage[...].astype(BF16)
                merged[f] = z
            w = jnp.concatenate([z[:, :entries], z[:, entries:]], 0)
            s = lax.dot_general(w, w, (((1,), (1,)), ((), ())), preferred_element_type=F32)
            s = s * F32(1.0 / blocks)
            top, bottom = s[:blocks], swap(s[blocks:])
            compact = jnp.where(low, top + bottom, top - bottom)
            if direct and slot == 0 and grams[0].dtype == F32:
                grams[0][i] = compact
            elif direct:
                coded.append(double(compact))
            else:
                grams[0][f] = pack(double(compact))
        if coded:
            write_coded(grams[slot], *encode(coded)[:2])


def gram(pieces, slots, direct, in_steps, after):
    peers = len(pieces)
    count, here, width = pieces[0].shape
    blocks = here * peers
    if direct:
        rows = coded_rows(count // slots, blocks // 2)
        shapes = [((rows, 2 * blocks), jnp.int16)] * slots
        if in_steps:
            shapes[0] = ((count // slots, blocks, 2 * blocks), F32)
    else:
        shapes = [((count, blocks // 2, 2 * blocks), F32)]
    out = pl.pallas_call(
        functools.partial(gram_kernel, peers, slots, direct, len(after)),
        in_specs=[whole_spec()] * peers + [any_spec()] * len(after),
        out_specs=[whole_spec()] * (2 + len(shapes)),
        out_shape=[jax.ShapeDtypeStruct((count, blocks, width), BF16), TOKEN]
        + [jax.ShapeDtypeStruct(*s) for s in shapes],
        scratch_shapes=[pltpu.VMEM((blocks, width), F32)] if here % 16 else [],
        compiler_params=params(),
        cost_estimate=light(),
        name="gram",
    )(*pieces, *after)
    return out[0], out[2:], out[1]


def add_kernel(own, other, *refs):
    out, token = refs[-2:]
    token[...] = jnp.zeros_like(token)
    number, blocks, _ = own.shape
    received = spread(*read_coded(other, number, blocks // 2))
    sums = [double(own[i] + unpack(received[i])[0]) for i in range(number)]
    write_coded(out, *encode(sums)[:2])


def add(own, other, after):
    return pl.pallas_call(
        add_kernel,
        in_specs=[whole_spec()] * 2 + [any_spec()] * len(after),
        out_specs=[whole_spec()] * 2,
        out_shape=[jax.ShapeDtypeStruct(other.shape, jnp.int16), TOKEN],
        compiler_params=params(),
        cost_estimate=light(),
        name="add",
    )(own, other, *after)


def split(x):
    high = x.astype(BF16)
    return high, (x - high.astype(F32)).astype(BF16)


def solve_kernel(parts, number, half_rows, *refs):
    ins, out, token = refs[:parts], refs[-2], refs[-1]
    token[...] = jnp.zeros_like(token)
    width = out.shape[1]
    half = width // 2
    shape = (half, width)
    row = lax.broadcasted_iota(jnp.int32, shape, 0)
    lane = lax.broadcasted_iota(jnp.int32, shape, 1)
    eye = jnp.where(row == lane, F32(1), F32(0))

    if parts == 1:
        sums = [ins[0][i] for i in range(number)]
    else:
        found = [spread(*read_coded(r, number, half_rows)) for r in ins]
        sums = [p + q for p, q in zip(found[0], found[1])]
        if parts == 4:
            sums = [p + (q + r) for p, q, r in zip(sums, found[2], found[3])]
    both_halves = each(unpack, sums)
    grams = [h[0] for h in both_halves]
    shift = each(lambda g: jnp.sum(g * eye, keepdims=True) * F32(1.0 / half), grams)
    eye_low = jnp.where(row + half == lane, F32(1), F32(0))
    inverse = each(lambda m: 1.0 / m, shift)
    system = each(lambda g, m: g * m + eye, grams, inverse)
    under = each(lambda h, m: h[1] * m + eye_low, both_halves, inverse)
    both = each(
        lambda a, u: jnp.concatenate(split(jnp.concatenate([a, u], 0)), 1), system, under
    )

    def times(v, a):
        wide = dot(v, a)
        return wide[:, :width] + wide[:, width:]


    low_end, high_end = 1.0, float(half + 1)
    mid, radius = (high_end + low_end) / 2, (high_end - low_end) / 2
    ratio = mid / radius
    t = 2 * ratio * ratio - 1
    scale = 2.0 / (radius * radius * t)
    x = each(lambda a: (F32(scale) * (F32(2 * mid) * eye - a)).astype(BF16), system)
    p = each(lambda v, a: eye - times(v, a), x, both)
    x = each(lambda v: v.astype(F32), x)
    for _ in range(3):
        t_next = 2 * t * t - 1
        c = F32(2 * t * t / t_next)
        pf = each(lambda q: full(q).astype(BF16), p)
        xp = each(lambda v, q: jnp.concatenate([v, q], 0).astype(BF16), x, p)
        moved = each(dot, xp, pf)
        x = each(lambda v, m: c * (v + m[:half]), x, moved)
        p = each(lambda m: c * m[half:] - F32(1 / t_next) * eye, moved)
        t = t_next
    for kind in ("scaled", "last"):
        xb = each(lambda v: v.astype(BF16), x)
        xw = each(lambda v: v.astype(F32), xb)
        xf = each(lambda v: full(v).astype(BF16), xw)
        residual = each(lambda v, a: eye - times(v, a), xb, both)
        step = each(lambda r, v: dot(r.astype(BF16), v), residual, xf)
        factor = 1.0 if kind == "last" else 2 * t * t / (2 * t * t - 1)
        x = each(lambda v, m: F32(factor) * (v + m), xw, step)
    values, codes, scales = encode(each(lambda v: double(eye - v), x))
    products = outer(scales, number)
    filters = each(lambda v, p: unpack(v, p * F32(0.5 / TOP)), values, products)
    rounded = each(lambda c: c[0].astype(BF16), filters)
    turned = each(
        lambda c: jnp.concatenate([c[0].astype(BF16), c[1].astype(BF16)], 0), filters
    )
    split_g = each(lambda g: jnp.concatenate(split(g), 0), grams)
    moved = each(dot, split_g, turned)
    moved = each(lambda m: m[:half] + m[half:], moved)
    energy = each(
        lambda c, h: jnp.sum(c.astype(F32) * h, keepdims=True) * F32(half), rounded, moved
    )
    energy = place([jnp.broadcast_to(e, (1, width)) for e in energy], codes.shape[0])
    energy = jnp.maximum(energy, F32(1e-30))
    whole = jnp.floor(jnp.log(energy) * F32(LOG_STEPS / math.log(2.0)))
    rest = jnp.round((energy * jnp.exp2(whole * F32(-1 / LOG_STEPS)) - 1.0) * F32(FINE))
    spot = lax.broadcasted_iota(jnp.int32, codes.shape, 1)
    codes = jnp.where(spot == half, whole, jnp.where(spot == half + 1, rest, codes))
    write_coded(out, values, codes)


def solve(parts, number, half_rows, after):
    width = parts[0].shape[-1]
    return pl.pallas_call(
        functools.partial(solve_kernel, len(parts), number, half_rows),
        in_specs=[whole_spec()] * len(parts) + [any_spec()] * len(after),
        out_specs=[whole_spec()] * 2,
        out_shape=[
            jax.ShapeDtypeStruct((coded_rows(number, half_rows), width), jnp.int16),
            TOKEN,
        ],
        compiler_params=params(),
        cost_estimate=light(),
        name="filters",
    )(*parts, *after)


def energy_kernel(slots, direct, number, first, merged, *refs):
    pieces = refs[:number]
    energies_out, filters_out, token, energies, filters, energies_sem, filters_sem = refs[-7:]
    token[...] = jnp.zeros_like(token)
    count, blocks, width = merged.shape
    entries = width // 2
    per_slot = count // slots
    half_rows = blocks // 2
    states = entries * lax.axis_size("space")
    puts = []
    for slot in range(slots):
        owner = slot_owner(direct, slot)
        piece = pieces[slot] if direct else pieces[0].at[slot]
        values, codes = read_coded(piece, per_slot, half_rows)
        whole = codes[:, blocks : blocks + 1]
        rest = codes[:, blocks + 1 : blocks + 2]
        total = jnp.exp2(whole * F32(1 / LOG_STEPS)) * (1.0 + rest * F32(1 / FINE))
        gains = F32(states) / total
        codes = jnp.where(lane_low(codes.shape, blocks), codes, swap(codes))
        products = outer(scale_of(codes), per_slot)
        for begin in range(0, per_slot, 4):
            some = range(begin, min(begin + 4, per_slot))
            at = [owner * per_slot + i for i in some]
            z = [merged[f] for f in at]
            scale = [products[i] * F32(0.5 / TOP) for i in some]
            halves = each(unpack, [values[i] for i in some], scale)
            compact = [h[0] for h in halves]
            both = each(
                lambda h: jnp.concatenate([h[0].astype(BF16), h[1].astype(BF16)], 0), halves
            )
            gain = [gains[i : i + 1] for i in some]
            w = each(lambda v: jnp.concatenate([v[:, :entries], v[:, entries:]], 0), z)
            r = each(dot, both, w)
            energy = each(
                lambda v, t: jnp.sum(v * v, axis=0, keepdims=True) * t, r, gain
            )
            for f, c, e in zip(at, compact, energy):
                filters[f, 0] = c[:, :blocks]
                filters[f, 1] = c[:, blocks:]
                energies[pl.ds(f, 1), :] = e
            put = pltpu.make_async_copy(
                filters.at[pl.ds(at[0], len(at))],
                filters_out.at[pl.ds(first + at[0], len(at))],
                filters_sem.at[len(puts)],
            )
            put.start()
            puts.append(put)
    put = pltpu.make_async_copy(
        energies, energies_out.at[pl.ds(first, count)], energies_sem.at[0]
    )
    put.start()
    for p in [*puts, put]:
        p.wait()


def filtered(merged, pieces, slots, direct, carry, owned, first, after):
    count, blocks, width = merged.shape
    entries = width // 2
    fixed = 1 + len(pieces)
    args = [merged, *pieces] + ([] if carry is None else list(carry)) + list(after)
    hbm = pl.BlockSpec(memory_space=pltpu.HBM)
    return pl.pallas_call(
        functools.partial(energy_kernel, slots, direct, len(pieces), first),
        in_specs=[whole_spec()] * fixed
        + ([] if carry is None else [hbm] * 2)
        + [any_spec()] * len(after),
        out_specs=[hbm] * 2 + [whole_spec()],
        out_shape=[
            jax.ShapeDtypeStruct((owned, entries), F32),
            jax.ShapeDtypeStruct((owned, 2, blocks, blocks), F32),
            TOKEN,
        ],
        input_output_aliases={} if carry is None else {fixed: 0, fixed + 1: 1},
        scratch_shapes=[
            pltpu.VMEM((count, entries), F32),
            pltpu.VMEM((count, 2, blocks, blocks), F32),
            pltpu.SemaphoreType.DMA((1,)),
            pltpu.SemaphoreType.DMA((slots * -(-(count // slots) // 4),)),
        ],
        compiler_params=params(),
        cost_estimate=light(),
        name="energy",
    )(*args)


def exchange(arrays, axis):
    size = lax.axis_size(axis)
    got = [arrays[0]]
    for offset in range(1, size):
        pairs = [(i, i ^ offset) for i in range(size)]
        got.append(lax.ppermute(arrays[offset], axis, pairs))
    return got


def plan(owned, slots):
    if slots != 4 or owned != 64:
        return [owned], (("T", 0), ("G", 0), ("F", 0), ("E", 0))
    return SIZES, ORDER


SIZES = [24, 24, 16]
ORDER = (
    ("T", 0), ("T", 1), ("G", 0), ("A", 0), ("F", 0), ("G", 1), ("E", 0), ("A", 1),
    ("G", 2), ("F", 1), ("F", 2), ("E", 1), ("E", 2),
)


TIES = {("T", 1): (0,)}


def permute(x, axis, offset):
    pairs = [(i, i ^ offset) for i in range(lax.axis_size(axis))]
    return lax.ppermute(x, axis, pairs)


def on_device(snapshots, entry_weight, freq_index):
    peers = lax.axis_size("tm")
    slots = lax.axis_size("space")
    owned = freq_index.shape[0] // peers
    sizes, order = plan(owned, slots)
    starts = [sum(sizes[:c]) for c in range(len(sizes))]
    paired = slots == 4
    halves = 2 if paired else slots
    weight = entry_weight.reshape(1, -1)
    sent, merged, grams, parts, pieces = {}, {}, {}, {}, {}
    carry = None
    token = []

    def do_transform(c):
        nonlocal token
        joint = [k for k in range(c, len(sizes)) if k == c or ("T", k) not in order]
        out, done = transform(
            snapshots, weight, freq_index, peers, [(starts[k], sizes[k]) for k in joint], token
        )
        token = [done]
        for k, own in zip(joint, out):
            sent[k] = [own[0]] + [permute(own[i], "tm", i) for i in range(1, peers)]

    def do_gram(c):
        nonlocal token
        in_steps = paired and ("A", c) in order
        merged[c], grams[c], done = gram(sent[c], halves, paired, in_steps, token)
        token = [done]
        if in_steps:
            grams[c] = [grams[c][0], permute(grams[c][1], "space", 1)]
        elif paired:
            own, other = grams[c]
            parts[c] = [
                own,
                permute(own, "space", 2),
                permute(other, "space", 1),
                permute(other, "space", 3),
            ]
        else:
            parts[c] = [lax.psum_scatter(grams[c][0], "space", scatter_dimension=0, tiled=True)]

    def do_add(c):
        nonlocal token
        half, done = add(*grams[c], token)
        token = [done]
        parts[c] = [half, permute(half, "space", 2)]

    def do_solve(c):
        nonlocal token
        count = sizes[c] // halves
        own, done = solve(parts[c], count, merged[c].shape[1] // 2, token)
        token = [done]
        if paired:
            pieces[c] = [own, permute(own, "space", 1)]
        else:
            pieces[c] = [lax.all_gather(own, "space", axis=0, tiled=False)]

    def do_energy(c):
        nonlocal token, carry
        *carry, done = filtered(
            merged[c], pieces[c], halves, paired, carry, owned, starts[c], token
        )
        token = [done]

    stages = {"T": do_transform, "G": do_gram, "A": do_add, "F": do_solve, "E": do_energy}
    for stage, c in order:
        token = token + [sent[k][1] for k in TIES.get((stage, c), ()) if k in sent]
        stages[stage](c)
    return (carry[0], carry[1])


def solution(mesh):
    in_specs = (P(("grp", "tm"), None, "space"), P(("grp", "space")), P())
    out_specs = (P(("grp", "tm"), "space"), P(("grp", "tm"), None, None, None))
    return jax.shard_map(
        on_device, mesh=mesh, in_specs=in_specs, out_specs=out_specs, check_vma=False
    )
```

```python
import functools
import math

import jax
import jax.numpy as jnp
from jax import lax
from jax.experimental import pallas as pl
from jax.experimental.pallas import tpu as pltpu
from jax.sharding import PartitionSpec as P

F32 = jnp.float32
BF16 = jnp.bfloat16
VMEM_LIMIT = 30 * 1024 * 1024
LANES = 128


def params(**kwargs):
    return pltpu.CompilerParams(vmem_limit_bytes=VMEM_LIMIT, **kwargs)


def whole_spec():
    return pl.BlockSpec(memory_space=pltpu.VMEM)


TOKEN = jax.ShapeDtypeStruct((8, LANES), F32)


def light():
    return pl.CostEstimate(flops=1024, bytes_accessed=1024, transcendentals=0)


def in_hbm(x):
    return pltpu.with_memory_space_constraint(x, pltpu.HBM)


def any_spec():
    return pl.BlockSpec(memory_space=pl.ANY)


def dot(a, b):
    return lax.dot_general(a, b, (((1,), (0,)), ((), ())), preferred_element_type=F32)


def cos_sin(phase, length):
    quarter = length // 4
    eighth = length // 8
    shifted = phase + eighth
    low = (shifted & (quarter - 1)) - eighth
    quadrant = (shifted // quarter) & 3
    x = low.astype(F32) * F32(2.0 * math.pi / length)
    x2 = x * x
    cos = F32(1 / 40320)
    for c in (-1 / 720, 1 / 24, -0.5, 1.0):
        cos = cos * x2 + F32(c)
    sin = F32(1 / 362880)
    for c in (-1 / 5040, 1 / 120, -1 / 6, 1.0):
        sin = sin * x2 + F32(c)
    sin = sin * x
    odd = (quadrant & 1) == 1
    c0 = jnp.where(odd, sin, cos)
    s0 = jnp.where(odd, cos, sin)
    c1 = jnp.where((quadrant == 1) | (quadrant == 2), -c0, c0)
    s1 = jnp.where(quadrant >= 2, -s0, s0)
    return c1, s1


def transform_kernel(peers, parts, group, *refs):
    freq_hbm, weight_hbm, snap_hbm = refs[:3]
    outs, token = refs[-peers * len(parts) - 8 : -8], refs[-8]
    freq, weight, snap, table, wide, small_sem, snap_sem = refs[-7:]
    blocks, length, entries = snap.shape
    steps = blocks // group
    get_freq = pltpu.make_async_copy(freq_hbm, freq, small_sem.at[0])
    get_weight = pltpu.make_async_copy(weight_hbm, weight, small_sem.at[1])
    get_snap = [
        pltpu.make_async_copy(
            snap_hbm.at[pl.ds(i * group, group)], snap.at[pl.ds(i * group, group)], snap_sem.at[i]
        )
        for i in range(steps)
    ]
    token[...] = jnp.zeros_like(token)
    get_freq.start()
    for get in get_snap:
        get.start()
    get_weight.start()

    me = lax.axis_index("tm")
    groups = [
        (peer, first + j)
        for first, count in parts
        for peer in range(peers)
        for j in range(0, count, 8)
    ]
    rows = 8 * len(groups)
    per_peer = freq.shape[0] // peers
    times = lax.broadcasted_iota(jnp.int32, (8, length), 1)
    sub = lax.broadcasted_iota(jnp.int32, (8, length), 0)
    window = 0.5 - 0.5 * cos_sin(times, length)[0]
    scaled = window / F32(math.sqrt(0.375 * length))
    get_freq.wait()

    def eight(index):
        peer, offset = groups[index]
        start = jnp.bitwise_xor(me, peer) * per_peer + offset
        k = jnp.zeros((8, length), jnp.int32)
        for i in range(8):
            k = jnp.where(sub == i, freq[start + i], k)
        cos, sin = cos_sin((k * times) & (length - 1), length)
        return scaled * cos, -(scaled * sin)

    for pair in range(rows // 16):
        re0, im0 = eight(2 * pair)
        re1, im1 = eight(2 * pair + 1)
        table[16 * pair : 16 * pair + 16, :] = jnp.concatenate([re0, re1], 0).astype(BF16)
        table[rows + 16 * pair : rows + 16 * pair + 16, :] = jnp.concatenate(
            [im0, im1], 0
        ).astype(BF16)

    get_weight.wait()
    root = jnp.sqrt(weight[...])
    tiles = entries // LANES
    for step in range(steps):
        get_snap[step].wait()
        for b in range(step * group, (step + 1) * group):
            spec = dot(table[...], snap[b]) * root
            for tile in range(tiles):
                lanes = slice(tile * LANES, (tile + 1) * LANES)
                wide[tile, pl.ds(b, rows, stride=blocks), :] = spec[:rows, lanes]
                wide[tiles + tile, pl.ds(b, rows, stride=blocks), :] = spec[rows:, lanes]
    at = 0
    for out in outs:
        for j in range(out.shape[0]):
            for tile in range(2 * tiles):
                lanes = slice(tile * LANES, (tile + 1) * LANES)
                out[j, :, lanes] = wide[tile, at : at + blocks, :].astype(BF16)
            at += blocks


def transform(snapshots, weight, freq_index, peers, parts, after):
    blocks, length, entries = snapshots.shape
    group = min(blocks, 4)
    total = peers * sum(count for _, count in parts)
    shapes = [
        jax.ShapeDtypeStruct((count, blocks, 2 * entries), BF16)
        for _, count in parts
        for _ in range(peers)
    ]
    hbm = pl.BlockSpec(memory_space=pltpu.HBM)
    out = pl.pallas_call(
        functools.partial(transform_kernel, peers, parts, group),
        in_specs=[hbm] * 3 + [any_spec()] * len(after),
        out_specs=[whole_spec()] * (len(shapes) + 1),
        out_shape=shapes + [TOKEN],
        scratch_shapes=[
            pltpu.SMEM(freq_index.shape, jnp.int32),
            pltpu.VMEM(weight.shape, F32),
            pltpu.VMEM(snapshots.shape, BF16),
            pltpu.VMEM((2 * total, length), BF16),
            pltpu.VMEM((2 * entries // LANES, total * blocks, LANES), F32),
            pltpu.SemaphoreType.DMA((2,)),
            pltpu.SemaphoreType.DMA((blocks // group,)),
        ],
        compiler_params=params(),
        cost_estimate=light(),
        name="transform",
    )(in_hbm(freq_index), in_hbm(weight), in_hbm(snapshots), *after)
    return [out[i * peers : (i + 1) * peers] for i in range(len(parts))], out[-1]


def lane_low(shape, half):
    return lax.broadcasted_iota(jnp.int32, shape, 1) < half


def swap(x):
    return pltpu.roll(x, x.shape[1] // 2, 1)


def each(fn, *lists):
    return [fn(*items) for items in zip(*lists)]


def double(compact):
    return compact + swap(compact)


def pack(both):
    half = both.shape[0]
    low = lane_low((half // 2, 2 * half), half)
    return jnp.where(low, both[: half // 2], both[half // 2 :])


def unpack(packed, scale=None):
    rows, half = packed.shape[0], packed.shape[1] // 2
    low = lane_low(packed.shape, half)
    other = swap(packed)
    both = jnp.concatenate(
        [jnp.where(low, packed, other), jnp.where(low, other, packed)], 0
    )
    turned = jnp.transpose(jnp.concatenate([packed, packed], 0))
    turned = jnp.where(lane_low((half, half), rows), turned[:half], turned[half:])
    turned = jnp.concatenate([turned, turned], 1)
    low = lane_low(both.shape, half)
    total = both + turned
    apart = both - turned
    top = jnp.where(low, total, apart)
    bottom = jnp.where(low, -apart, total)
    scale = F32(0.5) if scale is None else scale
    return scale * top, scale * bottom


def full(compact):
    half = compact.shape[0]
    turned = swap(compact)
    low = lane_low(compact.shape, half)
    return jnp.concatenate([compact, jnp.where(low, -turned, turned)], 0)


TOP = 23169.0
LOG_STEPS = 64.0
FINE = float(2**21)


def place(lines, rows):
    shape = (rows, lines[0].shape[1])
    row = lax.broadcasted_iota(jnp.int32, shape, 0)
    out = jnp.zeros(shape, F32)
    for i, line in enumerate(lines):
        out = jnp.where(row == i, line, out)
    return out


def pad_rows(number):
    return -(-number // 16) * 16


def scale_of(code):
    exponent = jnp.floor(code * F32(1 / 256))
    part = code - exponent * 256
    return (jnp.exp2(exponent) * (1 + part * F32(1 / 128))).astype(BF16)


def outer(scales, number):
    half = scales.shape[1] // 2
    wide = scales.astype(F32)
    row = lax.broadcasted_iota(jnp.int32, scales.shape, 0)
    turned = jnp.transpose(wide)[:half].astype(BF16)
    return [
        dot(turned, jnp.where(row == i, wide, F32(0)).astype(BF16)) for i in range(number)
    ]


def inverse_outer(scales, number):
    half = scales.shape[1] // 2
    rows = scales.shape[0]
    inverse = 1.0 / scales.astype(F32)
    high = inverse.astype(BF16).astype(F32)
    low = inverse - high
    left = jnp.transpose(jnp.concatenate([high, high, low], 0))[:half].astype(BF16)
    right = jnp.concatenate([high, low, high], 0)
    row = lax.broadcasted_iota(jnp.int32, right.shape, 0) & (rows - 1)
    return [
        dot(left, jnp.where(row == i, right, F32(0)).astype(BF16)) for i in range(number)
    ]


def encode(both):
    half, width = both[0].shape
    row = lax.broadcasted_iota(jnp.int32, (half, width), 0)
    lane = lax.broadcasted_iota(jnp.int32, (half, width), 1)
    on = (lane == row) | (lane == row + half)
    diagonal = each(lambda b: jnp.sum(jnp.where(on, b, F32(0)), axis=0, keepdims=True), both)
    root = jnp.sqrt(jnp.maximum(place(diagonal, pad_rows(len(both))), F32(1e-30)))
    exponent = jnp.floor(jnp.log(root) * F32(1 / math.log(2.0)))
    part = jnp.maximum(jnp.ceil((root * jnp.exp2(-exponent) - 1) * 128), F32(0))
    codes = exponent * 256 + part
    scales = scale_of(codes)
    inverse = inverse_outer(scales, len(both))
    value = each(lambda b, p: jnp.round((b * F32(TOP)) * p), both, inverse)
    return each(lambda v: pack(jnp.clip(v, F32(-32767), F32(32767))), value), codes, scales


def spread(values, codes):
    products = outer(scale_of(codes), len(values))
    return each(lambda v, p: v * pack(p * F32(1 / TOP)), values, products)


def to_short(x):
    return x.astype(jnp.int32).astype(jnp.int16)


def from_short(x):
    return x.astype(jnp.int32).astype(F32)


def coded_rows(number, half_rows):
    return number * half_rows + pad_rows(number)


def write_coded(out, values, codes):
    half_rows = values[0].shape[0]
    for i, value in enumerate(values):
        out[i * half_rows : (i + 1) * half_rows, :] = to_short(value)
    out[len(values) * half_rows :, :] = to_short(codes)


def read_coded(ref, number, half_rows):
    codes = from_short(ref[number * half_rows :, :])
    values = [from_short(ref[i * half_rows : (i + 1) * half_rows, :]) for i in range(number)]
    return values, codes


def slot_owner(direct, slot):
    return jnp.bitwise_xor(lax.axis_index("space") & 1, slot) if direct else slot


def gram_kernel(peers, slots, direct, after, *refs):
    pieces, refs = refs[:peers], refs[peers + after :]
    merged, token, grams = refs[0], refs[1], refs[2:]
    token[...] = jnp.zeros_like(token)
    me = lax.axis_index("tm")
    here = pieces[0].shape[1]
    entries = pieces[0].shape[2] // 2
    blocks = here * peers
    per_slot = pieces[0].shape[0] // slots
    stage = None
    if here % 16:
        grams, stage = grams[:-1], grams[-1]
    low = lane_low((blocks, 2 * blocks), blocks)
    for slot in range(slots):
        owner = slot_owner(direct, slot)
        coded = []
        for i in range(per_slot):
            f = owner * per_slot + i
            if stage is None:
                for peer in range(peers):
                    start = pl.multiple_of(jnp.bitwise_xor(me, peer) * here, here)
                    merged[f, pl.ds(start, here), :] = pieces[peer][f]
                z = merged[f]
            else:
                for peer in range(peers):
                    start = pl.multiple_of(jnp.bitwise_xor(me, peer) * here, here)
                    stage[pl.ds(start, here), :] = pieces[peer][f].astype(F32)
                z = stage[...].astype(BF16)
                merged[f] = z
            w = jnp.concatenate([z[:, :entries], z[:, entries:]], 0)
            s = lax.dot_general(w, w, (((1,), (1,)), ((), ())), preferred_element_type=F32)
            s = s * F32(1.0 / blocks)
            top, bottom = s[:blocks], swap(s[blocks:])
            compact = jnp.where(low, top + bottom, top - bottom)
            if direct and slot == 0 and grams[0].dtype == F32:
                grams[0][i] = compact
            elif direct:
                coded.append(double(compact))
            else:
                grams[0][f] = pack(double(compact))
        if coded:
            write_coded(grams[slot], *encode(coded)[:2])


def gram(pieces, slots, direct, in_steps, after):
    peers = len(pieces)
    count, here, width = pieces[0].shape
    blocks = here * peers
    if direct:
        rows = coded_rows(count // slots, blocks // 2)
        shapes = [((rows, 2 * blocks), jnp.int16)] * slots
        if in_steps:
            shapes[0] = ((count // slots, blocks, 2 * blocks), F32)
    else:
        shapes = [((count, blocks // 2, 2 * blocks), F32)]
    out = pl.pallas_call(
        functools.partial(gram_kernel, peers, slots, direct, len(after)),
        in_specs=[whole_spec()] * peers + [any_spec()] * len(after),
        out_specs=[whole_spec()] * (2 + len(shapes)),
        out_shape=[jax.ShapeDtypeStruct((count, blocks, width), BF16), TOKEN]
        + [jax.ShapeDtypeStruct(*s) for s in shapes],
        scratch_shapes=[pltpu.VMEM((blocks, width), F32)] if here % 16 else [],
        compiler_params=params(),
        cost_estimate=light(),
        name="gram",
    )(*pieces, *after)
    return out[0], out[2:], out[1]


def add_kernel(own, other, *refs):
    out, token = refs[-2:]
    token[...] = jnp.zeros_like(token)
    number, blocks, _ = own.shape
    received = spread(*read_coded(other, number, blocks // 2))
    sums = [double(own[i] + unpack(received[i])[0]) for i in range(number)]
    write_coded(out, *encode(sums)[:2])


def add(own, other, after):
    return pl.pallas_call(
        add_kernel,
        in_specs=[whole_spec()] * 2 + [any_spec()] * len(after),
        out_specs=[whole_spec()] * 2,
        out_shape=[jax.ShapeDtypeStruct(other.shape, jnp.int16), TOKEN],
        compiler_params=params(),
        cost_estimate=light(),
        name="add",
    )(own, other, *after)


def split(x):
    high = x.astype(BF16)
    return high, (x - high.astype(F32)).astype(BF16)


def solve_kernel(parts, number, half_rows, *refs):
    ins, out, token = refs[:parts], refs[-2], refs[-1]
    token[...] = jnp.zeros_like(token)
    width = out.shape[1]
    half = width // 2
    shape = (half, width)
    row = lax.broadcasted_iota(jnp.int32, shape, 0)
    lane = lax.broadcasted_iota(jnp.int32, shape, 1)
    eye = jnp.where(row == lane, F32(1), F32(0))

    if parts == 1:
        sums = [ins[0][i] for i in range(number)]
    else:
        found = [spread(*read_coded(r, number, half_rows)) for r in ins]
        sums = [p + q for p, q in zip(found[0], found[1])]
        if parts == 4:
            sums = [p + (q + r) for p, q, r in zip(sums, found[2], found[3])]
    both_halves = each(unpack, sums)
    grams = [h[0] for h in both_halves]
    shift = each(lambda g: jnp.sum(g * eye, keepdims=True) * F32(1.0 / half), grams)
    eye_low = jnp.where(row + half == lane, F32(1), F32(0))
    inverse = each(lambda m: 1.0 / m, shift)
    system = each(lambda g, m: g * m + eye, grams, inverse)
    under = each(lambda h, m: h[1] * m + eye_low, both_halves, inverse)
    both = each(
        lambda a, u: jnp.concatenate(split(jnp.concatenate([a, u], 0)), 1), system, under
    )

    def times(v, a):
        wide = dot(v, a)
        return wide[:, :width] + wide[:, width:]


    low_end, high_end = 1.0, float(half + 1)
    mid, radius = (high_end + low_end) / 2, (high_end - low_end) / 2
    ratio = mid / radius
    t = 2 * ratio * ratio - 1
    scale = 2.0 / (radius * radius * t)
    x = each(lambda a: (F32(scale) * (F32(2 * mid) * eye - a)).astype(BF16), system)
    p = each(lambda v, a: eye - times(v, a), x, both)
    x = each(lambda v: v.astype(F32), x)
    for _ in range(3):
        t_next = 2 * t * t - 1
        c = F32(2 * t * t / t_next)
        pf = each(lambda q: full(q).astype(BF16), p)
        xp = each(lambda v, q: jnp.concatenate([v, q], 0).astype(BF16), x, p)
        moved = each(dot, xp, pf)
        x = each(lambda v, m: c * (v + m[:half]), x, moved)
        p = each(lambda m: c * m[half:] - F32(1 / t_next) * eye, moved)
        t = t_next
    for kind in ("scaled", "last"):
        xb = each(lambda v: v.astype(BF16), x)
        xw = each(lambda v: v.astype(F32), xb)
        xf = each(lambda v: full(v).astype(BF16), xw)
        residual = each(lambda v, a: eye - times(v, a), xb, both)
        step = each(lambda r, v: dot(r.astype(BF16), v), residual, xf)
        factor = 1.0 if kind == "last" else 2 * t * t / (2 * t * t - 1)
        x = each(lambda v, m: F32(factor) * (v + m), xw, step)
    values, codes, scales = encode(each(lambda v: double(eye - v), x))
    products = outer(scales, number)
    filters = each(lambda v, p: unpack(v, p * F32(0.5 / TOP)), values, products)
    rounded = each(lambda c: c[0].astype(BF16), filters)
    turned = each(
        lambda c: jnp.concatenate([c[0].astype(BF16), c[1].astype(BF16)], 0), filters
    )
    split_g = each(lambda g: jnp.concatenate(split(g), 0), grams)
    moved = each(dot, split_g, turned)
    moved = each(lambda m: m[:half] + m[half:], moved)
    energy = each(
        lambda c, h: jnp.sum(c.astype(F32) * h, keepdims=True) * F32(half), rounded, moved
    )
    energy = place([jnp.broadcast_to(e, (1, width)) for e in energy], codes.shape[0])
    energy = jnp.maximum(energy, F32(1e-30))
    whole = jnp.floor(jnp.log(energy) * F32(LOG_STEPS / math.log(2.0)))
    rest = jnp.round((energy * jnp.exp2(whole * F32(-1 / LOG_STEPS)) - 1.0) * F32(FINE))
    spot = lax.broadcasted_iota(jnp.int32, codes.shape, 1)
    codes = jnp.where(spot == half, whole, jnp.where(spot == half + 1, rest, codes))
    write_coded(out, values, codes)


def solve(parts, number, half_rows, after):
    width = parts[0].shape[-1]
    return pl.pallas_call(
        functools.partial(solve_kernel, len(parts), number, half_rows),
        in_specs=[whole_spec()] * len(parts) + [any_spec()] * len(after),
        out_specs=[whole_spec()] * 2,
        out_shape=[
            jax.ShapeDtypeStruct((coded_rows(number, half_rows), width), jnp.int16),
            TOKEN,
        ],
        compiler_params=params(),
        cost_estimate=light(),
        name="filters",
    )(*parts, *after)


def energy_kernel(slots, direct, number, first, merged, *refs):
    pieces = refs[:number]
    energies_out, filters_out, token, energies, filters, energies_sem, filters_sem = refs[-7:]
    token[...] = jnp.zeros_like(token)
    count, blocks, width = merged.shape
    entries = width // 2
    per_slot = count // slots
    half_rows = blocks // 2
    states = entries * lax.axis_size("space")
    puts = []
    for slot in range(slots):
        owner = slot_owner(direct, slot)
        piece = pieces[slot] if direct else pieces[0].at[slot]
        values, codes = read_coded(piece, per_slot, half_rows)
        whole = codes[:, blocks : blocks + 1]
        rest = codes[:, blocks + 1 : blocks + 2]
        total = jnp.exp2(whole * F32(1 / LOG_STEPS)) * (1.0 + rest * F32(1 / FINE))
        gains = F32(states) / total
        codes = jnp.where(lane_low(codes.shape, blocks), codes, swap(codes))
        products = outer(scale_of(codes), per_slot)
        for begin in range(0, per_slot, 4):
            some = range(begin, min(begin + 4, per_slot))
            at = [owner * per_slot + i for i in some]
            z = [merged[f] for f in at]
            scale = [products[i] * F32(0.5 / TOP) for i in some]
            halves = each(unpack, [values[i] for i in some], scale)
            compact = [h[0] for h in halves]
            both = each(
                lambda h: jnp.concatenate([h[0].astype(BF16), h[1].astype(BF16)], 0), halves
            )
            gain = [gains[i : i + 1] for i in some]
            w = each(lambda v: jnp.concatenate([v[:, :entries], v[:, entries:]], 0), z)
            r = each(dot, both, w)
            energy = each(
                lambda v, t: jnp.sum(v * v, axis=0, keepdims=True) * t, r, gain
            )
            for f, c, e in zip(at, compact, energy):
                filters[f, 0] = c[:, :blocks]
                filters[f, 1] = c[:, blocks:]
                energies[pl.ds(f, 1), :] = e
            put = pltpu.make_async_copy(
                filters.at[pl.ds(at[0], len(at))],
                filters_out.at[pl.ds(first + at[0], len(at))],
                filters_sem.at[len(puts)],
            )
            put.start()
            puts.append(put)
    put = pltpu.make_async_copy(
        energies, energies_out.at[pl.ds(first, count)], energies_sem.at[0]
    )
    put.start()
    for p in [*puts, put]:
        p.wait()


def filtered(merged, pieces, slots, direct, carry, owned, first, after):
    count, blocks, width = merged.shape
    entries = width // 2
    fixed = 1 + len(pieces)
    args = [merged, *pieces] + ([] if carry is None else list(carry)) + list(after)
    hbm = pl.BlockSpec(memory_space=pltpu.HBM)
    return pl.pallas_call(
        functools.partial(energy_kernel, slots, direct, len(pieces), first),
        in_specs=[whole_spec()] * fixed
        + ([] if carry is None else [hbm] * 2)
        + [any_spec()] * len(after),
        out_specs=[hbm] * 2 + [whole_spec()],
        out_shape=[
            jax.ShapeDtypeStruct((owned, entries), F32),
            jax.ShapeDtypeStruct((owned, 2, blocks, blocks), F32),
            TOKEN,
        ],
        input_output_aliases={} if carry is None else {fixed: 0, fixed + 1: 1},
        scratch_shapes=[
            pltpu.VMEM((count, entries), F32),
            pltpu.VMEM((count, 2, blocks, blocks), F32),
            pltpu.SemaphoreType.DMA((1,)),
            pltpu.SemaphoreType.DMA((slots * -(-(count // slots) // 4),)),
        ],
        compiler_params=params(),
        cost_estimate=light(),
        name="energy",
    )(*args)


def exchange(arrays, axis):
    size = lax.axis_size(axis)
    got = [arrays[0]]
    for offset in range(1, size):
        pairs = [(i, i ^ offset) for i in range(size)]
        got.append(lax.ppermute(arrays[offset], axis, pairs))
    return got


def plan(owned, slots):
    if slots != 4 or owned != 64:
        return [owned], (("T", 0), ("G", 0), ("F", 0), ("E", 0))
    return SIZES, ORDER


SIZES = [40, 24]
ORDER = (
    ("T", 0), ("T", 1), ("G", 0), ("A", 0), ("G", 1), ("F", 0), ("F", 1), ("E", 0),
    ("E", 1),
)


TIES = {("T", 1): (0,)}


def permute(x, axis, offset):
    pairs = [(i, i ^ offset) for i in range(lax.axis_size(axis))]
    return lax.ppermute(x, axis, pairs)


def on_device(snapshots, entry_weight, freq_index):
    peers = lax.axis_size("tm")
    slots = lax.axis_size("space")
    owned = freq_index.shape[0] // peers
    sizes, order = plan(owned, slots)
    starts = [sum(sizes[:c]) for c in range(len(sizes))]
    paired = slots == 4
    halves = 2 if paired else slots
    weight = entry_weight.reshape(1, -1)
    sent, merged, grams, parts, pieces = {}, {}, {}, {}, {}
    carry = None
    token = []

    def do_transform(c):
        nonlocal token
        joint = [k for k in range(c, len(sizes)) if k == c or c and ("T", k) not in order]
        out, done = transform(
            snapshots, weight, freq_index, peers, [(starts[k], sizes[k]) for k in joint], token
        )
        token = [done]
        for k, own in zip(joint, out):
            sent[k] = [own[0]] + [permute(own[i], "tm", i) for i in range(1, peers)]

    def do_gram(c):
        nonlocal token
        in_steps = paired and ("A", c) in order
        merged[c], grams[c], done = gram(sent[c], halves, paired, in_steps, token)
        token = [done]
        if in_steps:
            grams[c] = [grams[c][0], permute(grams[c][1], "space", 1)]
        elif paired:
            own, other = grams[c]
            parts[c] = [
                own,
                permute(own, "space", 2),
                permute(other, "space", 1),
                permute(other, "space", 3),
            ]
        else:
            parts[c] = [lax.psum_scatter(grams[c][0], "space", scatter_dimension=0, tiled=True)]

    def do_add(c):
        nonlocal token
        half, done = add(*grams[c], token)
        token = [done]
        parts[c] = [half, permute(half, "space", 2)]

    def do_solve(c):
        nonlocal token
        count = sizes[c] // halves
        own, done = solve(parts[c], count, merged[c].shape[1] // 2, token)
        token = [done]
        if paired:
            pieces[c] = [own, permute(own, "space", 1)]
        else:
            pieces[c] = [lax.all_gather(own, "space", axis=0, tiled=False)]

    def do_energy(c):
        nonlocal token, carry
        *carry, done = filtered(
            merged[c], pieces[c], halves, paired, carry, owned, starts[c], token
        )
        token = [done]

    stages = {"T": do_transform, "G": do_gram, "A": do_add, "F": do_solve, "E": do_energy}
    for stage, c in order:
        token = token + [sent[k][1] for k in TIES.get((stage, c), ()) if k in sent]
        stages[stage](c)
    return (carry[0], carry[1])


def solution(mesh):
    in_specs = (P(("grp", "tm"), None, "space"), P(("grp", "space")), P())
    out_specs = (P(("grp", "tm"), "space"), P(("grp", "tm"), None, None, None))
    return jax.shard_map(
        on_device, mesh=mesh, in_specs=in_specs, out_specs=out_specs, check_vma=False
    )
```

```python
import functools
import math

import jax
import jax.numpy as jnp
from jax import lax
from jax.experimental import pallas as pl
from jax.experimental.pallas import tpu as pltpu
from jax.sharding import PartitionSpec as P

F32 = jnp.float32
BF16 = jnp.bfloat16
VMEM_LIMIT = 30 * 1024 * 1024
LANES = 128


def params(**kwargs):
    return pltpu.CompilerParams(vmem_limit_bytes=VMEM_LIMIT, **kwargs)


def whole_spec():
    return pl.BlockSpec(memory_space=pltpu.VMEM)


TOKEN = jax.ShapeDtypeStruct((8, LANES), F32)


def light():
    return pl.CostEstimate(flops=1024, bytes_accessed=1024, transcendentals=0)


def in_hbm(x):
    return pltpu.with_memory_space_constraint(x, pltpu.HBM)


def any_spec():
    return pl.BlockSpec(memory_space=pl.ANY)


def dot(a, b):
    return lax.dot_general(a, b, (((1,), (0,)), ((), ())), preferred_element_type=F32)


def cos_sin(phase, length):
    quarter = length // 4
    eighth = length // 8
    shifted = phase + eighth
    low = (shifted & (quarter - 1)) - eighth
    quadrant = (shifted // quarter) & 3
    x = low.astype(F32) * F32(2.0 * math.pi / length)
    x2 = x * x
    cos = F32(1 / 40320)
    for c in (-1 / 720, 1 / 24, -0.5, 1.0):
        cos = cos * x2 + F32(c)
    sin = F32(1 / 362880)
    for c in (-1 / 5040, 1 / 120, -1 / 6, 1.0):
        sin = sin * x2 + F32(c)
    sin = sin * x
    odd = (quadrant & 1) == 1
    c0 = jnp.where(odd, sin, cos)
    s0 = jnp.where(odd, cos, sin)
    c1 = jnp.where((quadrant == 1) | (quadrant == 2), -c0, c0)
    s1 = jnp.where(quadrant >= 2, -s0, s0)
    return c1, s1


def transform_kernel(peers, parts, group, *refs):
    freq_hbm, weight_hbm, snap_hbm = refs[:3]
    outs, token = refs[-peers * len(parts) - 8 : -8], refs[-8]
    freq, weight, snap, table, wide, small_sem, snap_sem = refs[-7:]
    blocks, length, entries = snap.shape
    steps = blocks // group
    get_freq = pltpu.make_async_copy(freq_hbm, freq, small_sem.at[0])
    get_weight = pltpu.make_async_copy(weight_hbm, weight, small_sem.at[1])
    get_snap = [
        pltpu.make_async_copy(
            snap_hbm.at[pl.ds(i * group, group)], snap.at[pl.ds(i * group, group)], snap_sem.at[i]
        )
        for i in range(steps)
    ]
    token[...] = jnp.zeros_like(token)
    get_freq.start()
    for get in get_snap:
        get.start()
    get_weight.start()

    me = lax.axis_index("tm")
    groups = [
        (peer, first + j)
        for first, count in parts
        for peer in range(peers)
        for j in range(0, count, 8)
    ]
    rows = 8 * len(groups)
    per_peer = freq.shape[0] // peers
    times = lax.broadcasted_iota(jnp.int32, (8, length), 1)
    sub = lax.broadcasted_iota(jnp.int32, (8, length), 0)
    window = 0.5 - 0.5 * cos_sin(times, length)[0]
    scaled = window / F32(math.sqrt(0.375 * length))
    get_freq.wait()

    def eight(index):
        peer, offset = groups[index]
        start = jnp.bitwise_xor(me, peer) * per_peer + offset
        k = jnp.zeros((8, length), jnp.int32)
        for i in range(8):
            k = jnp.where(sub == i, freq[start + i], k)
        cos, sin = cos_sin((k * times) & (length - 1), length)
        return scaled * cos, -(scaled * sin)

    for pair in range(rows // 16):
        re0, im0 = eight(2 * pair)
        re1, im1 = eight(2 * pair + 1)
        table[16 * pair : 16 * pair + 16, :] = jnp.concatenate([re0, re1], 0).astype(BF16)
        table[rows + 16 * pair : rows + 16 * pair + 16, :] = jnp.concatenate(
            [im0, im1], 0
        ).astype(BF16)

    get_weight.wait()
    root = jnp.sqrt(weight[...])
    tiles = entries // LANES
    for step in range(steps):
        get_snap[step].wait()
        for b in range(step * group, (step + 1) * group):
            spec = dot(table[...], snap[b]) * root
            for tile in range(tiles):
                lanes = slice(tile * LANES, (tile + 1) * LANES)
                wide[tile, pl.ds(b, rows, stride=blocks), :] = spec[:rows, lanes]
                wide[tiles + tile, pl.ds(b, rows, stride=blocks), :] = spec[rows:, lanes]
    at = 0
    for out in outs:
        for j in range(out.shape[0]):
            for tile in range(2 * tiles):
                lanes = slice(tile * LANES, (tile + 1) * LANES)
                out[j, :, lanes] = wide[tile, at : at + blocks, :].astype(BF16)
            at += blocks


def transform(snapshots, weight, freq_index, peers, parts, after):
    blocks, length, entries = snapshots.shape
    group = min(blocks, 4)
    total = peers * sum(count for _, count in parts)
    shapes = [
        jax.ShapeDtypeStruct((count, blocks, 2 * entries), BF16)
        for _, count in parts
        for _ in range(peers)
    ]
    hbm = pl.BlockSpec(memory_space=pltpu.HBM)
    out = pl.pallas_call(
        functools.partial(transform_kernel, peers, parts, group),
        in_specs=[hbm] * 3 + [any_spec()] * len(after),
        out_specs=[whole_spec()] * (len(shapes) + 1),
        out_shape=shapes + [TOKEN],
        scratch_shapes=[
            pltpu.SMEM(freq_index.shape, jnp.int32),
            pltpu.VMEM(weight.shape, F32),
            pltpu.VMEM(snapshots.shape, BF16),
            pltpu.VMEM((2 * total, length), BF16),
            pltpu.VMEM((2 * entries // LANES, total * blocks, LANES), F32),
            pltpu.SemaphoreType.DMA((2,)),
            pltpu.SemaphoreType.DMA((blocks // group,)),
        ],
        compiler_params=params(),
        cost_estimate=light(),
        name="transform",
    )(in_hbm(freq_index), in_hbm(weight), in_hbm(snapshots), *after)
    return [out[i * peers : (i + 1) * peers] for i in range(len(parts))], out[-1]


def lane_low(shape, half):
    return lax.broadcasted_iota(jnp.int32, shape, 1) < half


def swap(x):
    return pltpu.roll(x, x.shape[1] // 2, 1)


def each(fn, *lists):
    return [fn(*items) for items in zip(*lists)]


def double(compact):
    return compact + swap(compact)


def pack(both):
    half = both.shape[0]
    low = lane_low((half // 2, 2 * half), half)
    return jnp.where(low, both[: half // 2], both[half // 2 :])


def unpack(packed, scale=None):
    rows, half = packed.shape[0], packed.shape[1] // 2
    low = lane_low(packed.shape, half)
    other = swap(packed)
    both = jnp.concatenate(
        [jnp.where(low, packed, other), jnp.where(low, other, packed)], 0
    )
    turned = jnp.transpose(jnp.concatenate([packed, packed], 0))
    turned = jnp.where(lane_low((half, half), rows), turned[:half], turned[half:])
    turned = jnp.concatenate([turned, turned], 1)
    low = lane_low(both.shape, half)
    total = both + turned
    apart = both - turned
    top = jnp.where(low, total, apart)
    bottom = jnp.where(low, -apart, total)
    scale = F32(0.5) if scale is None else scale
    return scale * top, scale * bottom


def full(compact):
    half = compact.shape[0]
    turned = swap(compact)
    low = lane_low(compact.shape, half)
    return jnp.concatenate([compact, jnp.where(low, -turned, turned)], 0)


TOP = 23169.0
LOG_STEPS = 64.0
FINE = float(2**21)


def place(lines, rows):
    shape = (rows, lines[0].shape[1])
    row = lax.broadcasted_iota(jnp.int32, shape, 0)
    out = jnp.zeros(shape, F32)
    for i, line in enumerate(lines):
        out = jnp.where(row == i, line, out)
    return out


def pad_rows(number):
    return -(-number // 16) * 16


def scale_of(code):
    exponent = jnp.floor(code * F32(1 / 256))
    part = code - exponent * 256
    return (jnp.exp2(exponent) * (1 + part * F32(1 / 128))).astype(BF16)


def outer(scales, number):
    half = scales.shape[1] // 2
    wide = scales.astype(F32)
    row = lax.broadcasted_iota(jnp.int32, scales.shape, 0)
    turned = jnp.transpose(wide)[:half].astype(BF16)
    return [
        dot(turned, jnp.where(row == i, wide, F32(0)).astype(BF16)) for i in range(number)
    ]


def inverse_outer(scales, number):
    half = scales.shape[1] // 2
    rows = scales.shape[0]
    inverse = 1.0 / scales.astype(F32)
    high = inverse.astype(BF16).astype(F32)
    low = inverse - high
    left = jnp.transpose(jnp.concatenate([high, high, low], 0))[:half].astype(BF16)
    right = jnp.concatenate([high, low, high], 0)
    row = lax.broadcasted_iota(jnp.int32, right.shape, 0) & (rows - 1)
    return [
        dot(left, jnp.where(row == i, right, F32(0)).astype(BF16)) for i in range(number)
    ]


def encode(both):
    half, width = both[0].shape
    row = lax.broadcasted_iota(jnp.int32, (half, width), 0)
    lane = lax.broadcasted_iota(jnp.int32, (half, width), 1)
    on = (lane == row) | (lane == row + half)
    diagonal = each(lambda b: jnp.sum(jnp.where(on, b, F32(0)), axis=0, keepdims=True), both)
    root = jnp.sqrt(jnp.maximum(place(diagonal, pad_rows(len(both))), F32(1e-30)))
    exponent = jnp.floor(jnp.log(root) * F32(1 / math.log(2.0)))
    part = jnp.maximum(jnp.ceil((root * jnp.exp2(-exponent) - 1) * 128), F32(0))
    codes = exponent * 256 + part
    scales = scale_of(codes)
    inverse = inverse_outer(scales, len(both))
    value = each(lambda b, p: jnp.round((b * F32(TOP)) * p), both, inverse)
    return each(lambda v: pack(jnp.clip(v, F32(-32767), F32(32767))), value), codes, scales


def spread(values, codes):
    products = outer(scale_of(codes), len(values))
    return each(lambda v, p: v * pack(p * F32(1 / TOP)), values, products)


def to_short(x):
    return x.astype(jnp.int32).astype(jnp.int16)


def from_short(x):
    return x.astype(jnp.int32).astype(F32)


def coded_rows(number, half_rows):
    return number * half_rows + pad_rows(number)


def write_coded(out, values, codes):
    half_rows = values[0].shape[0]
    for i, value in enumerate(values):
        out[i * half_rows : (i + 1) * half_rows, :] = to_short(value)
    out[len(values) * half_rows :, :] = to_short(codes)


def read_coded(ref, number, half_rows):
    codes = from_short(ref[number * half_rows :, :])
    values = [from_short(ref[i * half_rows : (i + 1) * half_rows, :]) for i in range(number)]
    return values, codes


def slot_owner(direct, slot):
    return jnp.bitwise_xor(lax.axis_index("space") & 1, slot) if direct else slot


def gram_kernel(peers, slots, direct, after, *refs):
    pieces, refs = refs[:peers], refs[peers + after :]
    merged, token, grams = refs[0], refs[1], refs[2:]
    token[...] = jnp.zeros_like(token)
    me = lax.axis_index("tm")
    here = pieces[0].shape[1]
    entries = pieces[0].shape[2] // 2
    blocks = here * peers
    per_slot = pieces[0].shape[0] // slots
    stage = None
    if here % 16:
        grams, stage = grams[:-1], grams[-1]
    low = lane_low((blocks, 2 * blocks), blocks)
    for slot in range(slots):
        owner = slot_owner(direct, slot)
        coded = []
        for i in range(per_slot):
            f = owner * per_slot + i
            if stage is None:
                for peer in range(peers):
                    start = pl.multiple_of(jnp.bitwise_xor(me, peer) * here, here)
                    merged[f, pl.ds(start, here), :] = pieces[peer][f]
                z = merged[f]
            else:
                for peer in range(peers):
                    start = pl.multiple_of(jnp.bitwise_xor(me, peer) * here, here)
                    stage[pl.ds(start, here), :] = pieces[peer][f].astype(F32)
                z = stage[...].astype(BF16)
                merged[f] = z
            w = jnp.concatenate([z[:, :entries], z[:, entries:]], 0)
            s = lax.dot_general(w, w, (((1,), (1,)), ((), ())), preferred_element_type=F32)
            s = s * F32(1.0 / blocks)
            top, bottom = s[:blocks], swap(s[blocks:])
            compact = jnp.where(low, top + bottom, top - bottom)
            if direct and slot == 0 and grams[0].dtype == F32:
                grams[0][i] = compact
            elif direct:
                coded.append(double(compact))
            else:
                grams[0][f] = pack(double(compact))
        if coded:
            write_coded(grams[slot], *encode(coded)[:2])


def gram(pieces, slots, direct, in_steps, after):
    peers = len(pieces)
    count, here, width = pieces[0].shape
    blocks = here * peers
    if direct:
        rows = coded_rows(count // slots, blocks // 2)
        shapes = [((rows, 2 * blocks), jnp.int16)] * slots
        if in_steps:
            shapes[0] = ((count // slots, blocks, 2 * blocks), F32)
    else:
        shapes = [((count, blocks // 2, 2 * blocks), F32)]
    out = pl.pallas_call(
        functools.partial(gram_kernel, peers, slots, direct, len(after)),
        in_specs=[whole_spec()] * peers + [any_spec()] * len(after),
        out_specs=[whole_spec()] * (2 + len(shapes)),
        out_shape=[jax.ShapeDtypeStruct((count, blocks, width), BF16), TOKEN]
        + [jax.ShapeDtypeStruct(*s) for s in shapes],
        scratch_shapes=[pltpu.VMEM((blocks, width), F32)] if here % 16 else [],
        compiler_params=params(),
        cost_estimate=light(),
        name="gram",
    )(*pieces, *after)
    return out[0], out[2:], out[1]


def add_kernel(own, other, *refs):
    out, token = refs[-2:]
    token[...] = jnp.zeros_like(token)
    number, blocks, _ = own.shape
    received = spread(*read_coded(other, number, blocks // 2))
    sums = [double(own[i] + unpack(received[i])[0]) for i in range(number)]
    write_coded(out, *encode(sums)[:2])


def add(own, other, after):
    return pl.pallas_call(
        add_kernel,
        in_specs=[whole_spec()] * 2 + [any_spec()] * len(after),
        out_specs=[whole_spec()] * 2,
        out_shape=[jax.ShapeDtypeStruct(other.shape, jnp.int16), TOKEN],
        compiler_params=params(),
        cost_estimate=light(),
        name="add",
    )(own, other, *after)


def split(x):
    high = x.astype(BF16)
    return high, (x - high.astype(F32)).astype(BF16)


def solve_kernel(chunks, half_rows, *refs):
    out, token = refs[-2:]
    token[...] = jnp.zeros_like(token)
    width = out.shape[1]
    half = width // 2
    shape = (half, width)
    row = lax.broadcasted_iota(jnp.int32, shape, 0)
    lane = lax.broadcasted_iota(jnp.int32, shape, 1)
    eye = jnp.where(row == lane, F32(1), F32(0))

    sums, at = [], 0
    for parts, count in chunks:
        ins, at = refs[at : at + parts], at + parts
        if parts == 1:
            sums += [ins[0][i] for i in range(count)]
            continue
        found = [spread(*read_coded(r, count, half_rows)) for r in ins]
        added = each(lambda p, q: p + q, found[0], found[1])
        if parts == 4:
            added = each(lambda p, q, r: p + (q + r), added, found[2], found[3])
        sums += added
    number = len(sums)
    both_halves = each(unpack, sums)
    grams = [h[0] for h in both_halves]
    spots = lax.broadcasted_iota(jnp.int32, sums[0].shape, 1)
    lines = lax.broadcasted_iota(jnp.int32, sums[0].shape, 0)
    on = (spots == lines) | (spots == lines + 3 * half_rows)
    shift = each(
        lambda p: jnp.sum(jnp.where(on, p, F32(0)), keepdims=True) * F32(1.0 / half), sums
    )
    eye_low = jnp.where(row + half == lane, F32(1), F32(0))
    inverse = each(lambda m: 1.0 / m, shift)
    system = each(lambda g, m: g * m + eye, grams, inverse)
    under = each(lambda h, m: h[1] * m + eye_low, both_halves, inverse)
    both = each(
        lambda a, u: jnp.concatenate(split(jnp.concatenate([a, u], 0)), 1), system, under
    )

    def times(v, a):
        wide = dot(v, a)
        return wide[:, :width] + wide[:, width:]


    low_end, high_end = 1.0, float(half + 1)
    mid, radius = (high_end + low_end) / 2, (high_end - low_end) / 2
    ratio = mid / radius
    t = 2 * ratio * ratio - 1
    scale = 2.0 / (radius * radius * t)
    x = each(lambda a: (F32(scale) * (F32(2 * mid) * eye - a)).astype(BF16), system)
    p = each(lambda v, a: eye - times(v, a), x, both)
    x = each(lambda v: v.astype(F32), x)
    for _ in range(3):
        t_next = 2 * t * t - 1
        c = F32(2 * t * t / t_next)
        pf = each(lambda q: full(q).astype(BF16), p)
        xp = each(lambda v, q: jnp.concatenate([v, q], 0).astype(BF16), x, p)
        moved = each(dot, xp, pf)
        x = each(lambda v, m: c * (v + m[:half]), x, moved)
        p = each(lambda m: c * m[half:] - F32(1 / t_next) * eye, moved)
        t = t_next
    for kind in ("scaled", "last"):
        xb = each(lambda v: v.astype(BF16), x)
        xw = each(lambda v: v.astype(F32), xb)
        xf = each(lambda v: full(v).astype(BF16), xw)
        residual = each(lambda v, a: eye - times(v, a), xb, both)
        step = each(lambda r, v: dot(r.astype(BF16), v), residual, xf)
        factor = 1.0 if kind == "last" else 2 * t * t / (2 * t * t - 1)
        x = each(lambda v, m: F32(factor) * (v + m), xw, step)
    values, codes, scales = encode(each(lambda v: double(eye - v), x))
    products = outer(scales, number)
    filters = each(lambda v, p: unpack(v, p * F32(0.5 / TOP)), values, products)
    rounded = each(lambda c: c[0].astype(BF16), filters)
    turned = each(
        lambda c: jnp.concatenate([c[0].astype(BF16), c[1].astype(BF16)], 0), filters
    )
    split_g = each(lambda g: jnp.concatenate(split(g), 0), grams)
    moved = each(dot, split_g, turned)
    moved = each(lambda m: m[:half] + m[half:], moved)
    energy = each(
        lambda c, h: jnp.sum(c.astype(F32) * h, keepdims=True) * F32(half), rounded, moved
    )
    energy = place([jnp.broadcast_to(e, (1, width)) for e in energy], codes.shape[0])
    energy = jnp.maximum(energy, F32(1e-30))
    whole = jnp.floor(jnp.log(energy) * F32(LOG_STEPS / math.log(2.0)))
    rest = jnp.round((energy * jnp.exp2(whole * F32(-1 / LOG_STEPS)) - 1.0) * F32(FINE))
    spot = lax.broadcasted_iota(jnp.int32, codes.shape, 1)
    codes = jnp.where(spot == half, whole, jnp.where(spot == half + 1, rest, codes))
    write_coded(out, values, codes)


def solve(chunks, half_rows, after):
    args = [x for parts, _ in chunks for x in parts]
    width = args[0].shape[-1]
    number = sum(count for _, count in chunks)
    shape = [(len(parts), count) for parts, count in chunks]
    return pl.pallas_call(
        functools.partial(solve_kernel, shape, half_rows),
        in_specs=[whole_spec()] * len(args) + [any_spec()] * len(after),
        out_specs=[whole_spec()] * 2,
        out_shape=[
            jax.ShapeDtypeStruct((coded_rows(number, half_rows), width), jnp.int16),
            TOKEN,
        ],
        compiler_params=params(),
        cost_estimate=light(),
        name="filters",
    )(*args, *after)


def energy_kernel(slots, direct, number, chunks, first, *refs):
    merged, pieces = refs[:chunks], refs[chunks : chunks + number]
    energies_out, filters_out, token, energies, filters, energies_sem, filters_sem = refs[-7:]
    token[...] = jnp.zeros_like(token)
    blocks, width = merged[0].shape[1:]
    entries = width // 2
    counts = [m.shape[0] for m in merged]
    per_slot = sum(counts) // slots
    half_rows = blocks // 2
    states = entries * lax.axis_size("space")
    puts = []
    for slot in range(slots):
        owner = slot_owner(direct, slot)
        piece = pieces[slot] if direct else pieces[0].at[slot]
        values, codes = read_coded(piece, per_slot, half_rows)
        whole = codes[:, blocks : blocks + 1]
        rest = codes[:, blocks + 1 : blocks + 2]
        total = jnp.exp2(whole * F32(1 / LOG_STEPS)) * (1.0 + rest * F32(1 / FINE))
        gains = F32(states) / total
        codes = jnp.where(lane_low(codes.shape, blocks), codes, swap(codes))
        products = outer(scale_of(codes), per_slot)
        base = 0
        for chunk, count in enumerate(counts):
            own = count // slots
            size = 4 if own % 4 == 0 else 1
            for begin in range(0, own, size):
                start = sum(counts[:chunk]) + owner * own + begin
                some = range(base + begin, base + begin + size)
                z = [merged[chunk][owner * own + begin + i] for i in range(size)]
                scale = [products[i] * F32(0.5 / TOP) for i in some]
                halves = each(unpack, [values[i] for i in some], scale)
                both = each(
                    lambda h: jnp.concatenate([h[0].astype(BF16), h[1].astype(BF16)], 0), halves
                )
                w = each(lambda v: jnp.concatenate([v[:, :entries], v[:, entries:]], 0), z)
                r = each(dot, both, w)
                gain = [gains[i : i + 1] for i in some]
                energy = each(
                    lambda v, t: jnp.sum(v * v, axis=0, keepdims=True) * t, r, gain
                )
                for i in range(size):
                    filters[start + i, 0] = halves[i][0][:, :blocks]
                    filters[start + i, 1] = halves[i][0][:, blocks:]
                    energies[pl.ds(start + i, 1), :] = energy[i]
                put = pltpu.make_async_copy(
                    filters.at[pl.ds(start, size)],
                    filters_out.at[pl.ds(first + start, size)],
                    filters_sem.at[len(puts)],
                )
                put.start()
                puts.append(put)
            base += own
    put = pltpu.make_async_copy(
        energies, energies_out.at[pl.ds(first, sum(counts))], energies_sem.at[0]
    )
    put.start()
    for p in [*puts, put]:
        p.wait()


def filtered(merged, pieces, slots, direct, carry, owned, first, after):
    _, blocks, width = merged[0].shape
    count = sum(m.shape[0] for m in merged)
    copies = sum(slots * (m.shape[0] // slots) for m in merged)
    entries = width // 2
    fixed = len(merged) + len(pieces)
    args = [*merged, *pieces] + ([] if carry is None else list(carry)) + list(after)
    hbm = pl.BlockSpec(memory_space=pltpu.HBM)
    return pl.pallas_call(
        functools.partial(energy_kernel, slots, direct, len(pieces), len(merged), first),
        in_specs=[whole_spec()] * fixed
        + ([] if carry is None else [hbm] * 2)
        + [any_spec()] * len(after),
        out_specs=[hbm] * 2 + [whole_spec()],
        out_shape=[
            jax.ShapeDtypeStruct((owned, entries), F32),
            jax.ShapeDtypeStruct((owned, 2, blocks, blocks), F32),
            TOKEN,
        ],
        input_output_aliases={} if carry is None else {fixed: 0, fixed + 1: 1},
        scratch_shapes=[
            pltpu.VMEM((count, entries), F32),
            pltpu.VMEM((count, 2, blocks, blocks), F32),
            pltpu.SemaphoreType.DMA((1,)),
            pltpu.SemaphoreType.DMA((copies,)),
        ],
        compiler_params=params(),
        cost_estimate=light(),
        name="energy",
    )(*args)


def exchange(arrays, axis):
    size = lax.axis_size(axis)
    got = [arrays[0]]
    for offset in range(1, size):
        pairs = [(i, i ^ offset) for i in range(size)]
        got.append(lax.ppermute(arrays[offset], axis, pairs))
    return got


def plan(owned, slots):
    if slots != 4 or owned != 64:
        return [owned], (("T", 0), ("G", 0), ("F", 0), ("E", 0))
    return SIZES, ORDER


SIZES = [24, 24, 16]
ORDER = (
    ("T", 0), ("T", 1), ("G", 0), ("A", 0), ("G", 1), ("F", 0), ("A", 1), ("G", 2),
    ("E", 0), ("F", 1), ("E", 1),
)


TIES = {("T", 1): (0,)}


def permute(x, axis, offset):
    pairs = [(i, i ^ offset) for i in range(lax.axis_size(axis))]
    return lax.ppermute(x, axis, pairs)


def on_device(snapshots, entry_weight, freq_index):
    peers = lax.axis_size("tm")
    slots = lax.axis_size("space")
    owned = freq_index.shape[0] // peers
    sizes, order = plan(owned, slots)
    starts = [sum(sizes[:c]) for c in range(len(sizes))]
    paired = slots == 4
    halves = 2 if paired else slots
    weight = entry_weight.reshape(1, -1)
    sent, merged, grams, parts, pieces = {}, {}, {}, {}, {}
    carry = None
    token = []

    def do_transform(c):
        nonlocal token
        joint = [k for k in range(c, len(sizes)) if k == c or c and ("T", k) not in order]
        out, done = transform(
            snapshots, weight, freq_index, peers, [(starts[k], sizes[k]) for k in joint], token
        )
        token = [done]
        for k, own in zip(joint, out):
            sent[k] = [own[0]] + [permute(own[i], "tm", i) for i in range(1, peers)]

    def do_gram(c):
        nonlocal token
        in_steps = paired and ("A", c) in order
        merged[c], grams[c], done = gram(sent[c], halves, paired, in_steps, token)
        token = [done]
        if in_steps:
            grams[c] = [grams[c][0], permute(grams[c][1], "space", 1)]
        elif paired:
            own, other = grams[c]
            parts[c] = [
                own,
                permute(own, "space", 2),
                permute(other, "space", 1),
                permute(other, "space", 3),
            ]
        else:
            parts[c] = [lax.psum_scatter(grams[c][0], "space", scatter_dimension=0, tiled=True)]

    def do_add(c):
        nonlocal token
        half, done = add(*grams[c], token)
        token = [done]
        parts[c] = [half, permute(half, "space", 2)]

    def joined(stage, c):
        last = c + 1
        while last < len(sizes) and (stage, last) not in order:
            last += 1
        return range(c, last)

    def do_solve(c):
        nonlocal token
        work = [(parts[k], sizes[k] // halves) for k in joined("F", c)]
        own, done = solve(work, merged[c].shape[1] // 2, token)
        token = [done]
        if paired:
            pieces[c] = [own, permute(own, "space", 1)]
        else:
            pieces[c] = [lax.all_gather(own, "space", axis=0, tiled=False)]

    def do_energy(c):
        nonlocal token, carry
        work = [merged[k] for k in joined("E", c)]
        *carry, done = filtered(
            work, pieces[c], halves, paired, carry, owned, starts[c], token
        )
        token = [done]

    stages = {"T": do_transform, "G": do_gram, "A": do_add, "F": do_solve, "E": do_energy}
    for stage, c in order:
        token = token + [sent[k][1] for k in TIES.get((stage, c), ()) if k in sent]
        stages[stage](c)
    return (carry[0], carry[1])


def solution(mesh):
    in_specs = (P(("grp", "tm"), None, "space"), P(("grp", "space")), P())
    out_specs = (P(("grp", "tm"), "space"), P(("grp", "tm"), None, None, None))
    return jax.shard_map(
        on_device, mesh=mesh, in_specs=in_specs, out_specs=out_specs, check_vma=False
    )
```

```python
import functools
import math

import jax
import jax.numpy as jnp
from jax import lax
from jax.experimental import pallas as pl
from jax.experimental.pallas import tpu as pltpu
from jax.sharding import PartitionSpec as P

F32 = jnp.float32
BF16 = jnp.bfloat16
VMEM_LIMIT = 30 * 1024 * 1024
LANES = 128


def params(**kwargs):
    return pltpu.CompilerParams(vmem_limit_bytes=VMEM_LIMIT, **kwargs)


def whole_spec():
    return pl.BlockSpec(memory_space=pltpu.VMEM)


TOKEN = jax.ShapeDtypeStruct((8, LANES), F32)


def light():
    return pl.CostEstimate(flops=1024, bytes_accessed=1024, transcendentals=0)


def in_hbm(x):
    return pltpu.with_memory_space_constraint(x, pltpu.HBM)


def any_spec():
    return pl.BlockSpec(memory_space=pl.ANY)


def dot(a, b):
    return lax.dot_general(a, b, (((1,), (0,)), ((), ())), preferred_element_type=F32)


def cos_sin(phase, length):
    quarter = length // 4
    eighth = length // 8
    shifted = phase + eighth
    low = (shifted & (quarter - 1)) - eighth
    quadrant = (shifted // quarter) & 3
    x = low.astype(F32) * F32(2.0 * math.pi / length)
    x2 = x * x
    cos = F32(1 / 40320)
    for c in (-1 / 720, 1 / 24, -0.5, 1.0):
        cos = cos * x2 + F32(c)
    sin = F32(1 / 362880)
    for c in (-1 / 5040, 1 / 120, -1 / 6, 1.0):
        sin = sin * x2 + F32(c)
    sin = sin * x
    odd = (quadrant & 1) == 1
    c0 = jnp.where(odd, sin, cos)
    s0 = jnp.where(odd, cos, sin)
    c1 = jnp.where((quadrant == 1) | (quadrant == 2), -c0, c0)
    s1 = jnp.where(quadrant >= 2, -s0, s0)
    return c1, s1


def transform_kernel(peers, parts, group, *refs):
    freq_hbm, weight_hbm, snap_hbm = refs[:3]
    outs, token = refs[-peers * len(parts) - 8 : -8], refs[-8]
    freq, weight, snap, table, wide, small_sem, snap_sem = refs[-7:]
    blocks, length, entries = snap.shape
    steps = blocks // group
    get_freq = pltpu.make_async_copy(freq_hbm, freq, small_sem.at[0])
    get_weight = pltpu.make_async_copy(weight_hbm, weight, small_sem.at[1])
    get_snap = [
        pltpu.make_async_copy(
            snap_hbm.at[pl.ds(i * group, group)], snap.at[pl.ds(i * group, group)], snap_sem.at[i]
        )
        for i in range(steps)
    ]
    token[...] = jnp.zeros_like(token)
    get_freq.start()
    for get in get_snap:
        get.start()
    get_weight.start()

    me = lax.axis_index("tm")
    groups = [
        (peer, first + j)
        for first, count in parts
        for peer in range(peers)
        for j in range(0, count, 8)
    ]
    rows = 8 * len(groups)
    per_peer = freq.shape[0] // peers
    times = lax.broadcasted_iota(jnp.int32, (8, length), 1)
    sub = lax.broadcasted_iota(jnp.int32, (8, length), 0)
    window = 0.5 - 0.5 * cos_sin(times, length)[0]
    scaled = window / F32(math.sqrt(0.375 * length))
    get_freq.wait()

    def eight(index):
        peer, offset = groups[index]
        start = jnp.bitwise_xor(me, peer) * per_peer + offset
        k = jnp.zeros((8, length), jnp.int32)
        for i in range(8):
            k = jnp.where(sub == i, freq[start + i], k)
        cos, sin = cos_sin((k * times) & (length - 1), length)
        return scaled * cos, -(scaled * sin)

    for pair in range(rows // 16):
        re0, im0 = eight(2 * pair)
        re1, im1 = eight(2 * pair + 1)
        table[16 * pair : 16 * pair + 16, :] = jnp.concatenate([re0, re1], 0).astype(BF16)
        table[rows + 16 * pair : rows + 16 * pair + 16, :] = jnp.concatenate(
            [im0, im1], 0
        ).astype(BF16)

    get_weight.wait()
    root = jnp.sqrt(weight[...])
    tiles = entries // LANES
    for step in range(steps):
        get_snap[step].wait()
        for b in range(step * group, (step + 1) * group):
            spec = dot(table[...], snap[b]) * root
            for tile in range(tiles):
                lanes = slice(tile * LANES, (tile + 1) * LANES)
                wide[tile, pl.ds(b, rows, stride=blocks), :] = spec[:rows, lanes]
                wide[tiles + tile, pl.ds(b, rows, stride=blocks), :] = spec[rows:, lanes]
    at = 0
    for out in outs:
        for j in range(out.shape[0]):
            for tile in range(2 * tiles):
                lanes = slice(tile * LANES, (tile + 1) * LANES)
                out[j, :, lanes] = wide[tile, at : at + blocks, :].astype(BF16)
            at += blocks


def transform(snapshots, weight, freq_index, peers, parts, after):
    blocks, length, entries = snapshots.shape
    group = min(blocks, 4)
    total = peers * sum(count for _, count in parts)
    shapes = [
        jax.ShapeDtypeStruct((count, blocks, 2 * entries), BF16)
        for _, count in parts
        for _ in range(peers)
    ]
    hbm = pl.BlockSpec(memory_space=pltpu.HBM)
    out = pl.pallas_call(
        functools.partial(transform_kernel, peers, parts, group),
        in_specs=[hbm] * 3 + [any_spec()] * len(after),
        out_specs=[whole_spec()] * (len(shapes) + 1),
        out_shape=shapes + [TOKEN],
        scratch_shapes=[
            pltpu.SMEM(freq_index.shape, jnp.int32),
            pltpu.VMEM(weight.shape, F32),
            pltpu.VMEM(snapshots.shape, BF16),
            pltpu.VMEM((2 * total, length), BF16),
            pltpu.VMEM((2 * entries // LANES, total * blocks, LANES), F32),
            pltpu.SemaphoreType.DMA((2,)),
            pltpu.SemaphoreType.DMA((blocks // group,)),
        ],
        compiler_params=params(),
        cost_estimate=light(),
        name="transform",
    )(in_hbm(freq_index), in_hbm(weight), in_hbm(snapshots), *after)
    return [out[i * peers : (i + 1) * peers] for i in range(len(parts))], out[-1]


def lane_low(shape, half):
    return lax.broadcasted_iota(jnp.int32, shape, 1) < half


def swap(x):
    return pltpu.roll(x, x.shape[1] // 2, 1)


def each(fn, *lists):
    return [fn(*items) for items in zip(*lists)]


def double(compact):
    return compact + swap(compact)


def pack(both):
    half = both.shape[0]
    low = lane_low((half // 2, 2 * half), half)
    return jnp.where(low, both[: half // 2], both[half // 2 :])


def unpack(packed, scale=None):
    rows, half = packed.shape[0], packed.shape[1] // 2
    low = lane_low(packed.shape, half)
    other = swap(packed)
    both = jnp.concatenate(
        [jnp.where(low, packed, other), jnp.where(low, other, packed)], 0
    )
    turned = jnp.transpose(jnp.concatenate([packed, packed], 0))
    turned = jnp.where(lane_low((half, half), rows), turned[:half], turned[half:])
    turned = jnp.concatenate([turned, turned], 1)
    low = lane_low(both.shape, half)
    total = both + turned
    apart = both - turned
    top = jnp.where(low, total, apart)
    bottom = jnp.where(low, -apart, total)
    scale = F32(0.5) if scale is None else scale
    return scale * top, scale * bottom


def full(compact):
    half = compact.shape[0]
    turned = swap(compact)
    low = lane_low(compact.shape, half)
    return jnp.concatenate([compact, jnp.where(low, -turned, turned)], 0)


TOP = 23169.0
LOG_STEPS = 64.0
FINE = float(2**21)


def place(lines, rows):
    shape = (rows, lines[0].shape[1])
    row = lax.broadcasted_iota(jnp.int32, shape, 0)
    out = jnp.zeros(shape, F32)
    for i, line in enumerate(lines):
        out = jnp.where(row == i, line, out)
    return out


def pad_rows(number):
    return -(-number // 16) * 16


def scale_of(code):
    exponent = jnp.floor(code * F32(1 / 256))
    part = code - exponent * 256
    return (jnp.exp2(exponent) * (1 + part * F32(1 / 128))).astype(BF16)


def outer(scales, number):
    half = scales.shape[1] // 2
    wide = scales.astype(F32)
    row = lax.broadcasted_iota(jnp.int32, scales.shape, 0)
    turned = jnp.transpose(wide)[:half].astype(BF16)
    return [
        dot(turned, jnp.where(row == i, wide, F32(0)).astype(BF16)) for i in range(number)
    ]


def inverse_outer(scales, number):
    half = scales.shape[1] // 2
    rows = scales.shape[0]
    inverse = 1.0 / scales.astype(F32)
    high = inverse.astype(BF16).astype(F32)
    low = inverse - high
    left = jnp.transpose(jnp.concatenate([high, high, low], 0))[:half].astype(BF16)
    right = jnp.concatenate([high, low, high], 0)
    row = lax.broadcasted_iota(jnp.int32, right.shape, 0) & (rows - 1)
    return [
        dot(left, jnp.where(row == i, right, F32(0)).astype(BF16)) for i in range(number)
    ]


def encode(both):
    half, width = both[0].shape
    row = lax.broadcasted_iota(jnp.int32, (half, width), 0)
    lane = lax.broadcasted_iota(jnp.int32, (half, width), 1)
    on = (lane == row) | (lane == row + half)
    diagonal = each(lambda b: jnp.sum(jnp.where(on, b, F32(0)), axis=0, keepdims=True), both)
    root = jnp.sqrt(jnp.maximum(place(diagonal, pad_rows(len(both))), F32(1e-30)))
    exponent = jnp.floor(jnp.log(root) * F32(1 / math.log(2.0)))
    part = jnp.maximum(jnp.ceil((root * jnp.exp2(-exponent) - 1) * 128), F32(0))
    codes = exponent * 256 + part
    scales = scale_of(codes)
    inverse = inverse_outer(scales, len(both))
    value = each(lambda b, p: jnp.round((b * F32(TOP)) * p), both, inverse)
    return each(lambda v: pack(jnp.clip(v, F32(-32767), F32(32767))), value), codes, scales


def spread(values, codes):
    products = outer(scale_of(codes), len(values))
    return each(lambda v, p: v * pack(p * F32(1 / TOP)), values, products)


def to_short(x):
    return x.astype(jnp.int32).astype(jnp.int16)


def from_short(x):
    return x.astype(jnp.int32).astype(F32)


def coded_rows(number, half_rows):
    return number * half_rows + pad_rows(number)


def write_coded(out, values, codes):
    half_rows = values[0].shape[0]
    for i, value in enumerate(values):
        out[i * half_rows : (i + 1) * half_rows, :] = to_short(value)
    out[len(values) * half_rows :, :] = to_short(codes)


def read_coded(ref, number, half_rows):
    codes = from_short(ref[number * half_rows :, :])
    values = [from_short(ref[i * half_rows : (i + 1) * half_rows, :]) for i in range(number)]
    return values, codes


def slot_owner(direct, slot):
    return jnp.bitwise_xor(lax.axis_index("space") & 1, slot) if direct else slot


def gram_kernel(peers, slots, direct, after, *refs):
    pieces, refs = refs[:peers], refs[peers + after :]
    merged, token, grams = refs[0], refs[1], refs[2:]
    token[...] = jnp.zeros_like(token)
    me = lax.axis_index("tm")
    here = pieces[0].shape[1]
    entries = pieces[0].shape[2] // 2
    blocks = here * peers
    per_slot = pieces[0].shape[0] // slots
    stage = None
    if here % 16:
        grams, stage = grams[:-1], grams[-1]
    low = lane_low((blocks, 2 * blocks), blocks)
    for slot in range(slots):
        owner = slot_owner(direct, slot)
        coded = []
        for i in range(per_slot):
            f = owner * per_slot + i
            if stage is None:
                for peer in range(peers):
                    start = pl.multiple_of(jnp.bitwise_xor(me, peer) * here, here)
                    merged[f, pl.ds(start, here), :] = pieces[peer][f]
                z = merged[f]
            else:
                for peer in range(peers):
                    start = pl.multiple_of(jnp.bitwise_xor(me, peer) * here, here)
                    stage[pl.ds(start, here), :] = pieces[peer][f].astype(F32)
                z = stage[...].astype(BF16)
                merged[f] = z
            w = jnp.concatenate([z[:, :entries], z[:, entries:]], 0)
            s = lax.dot_general(w, w, (((1,), (1,)), ((), ())), preferred_element_type=F32)
            s = s * F32(1.0 / blocks)
            top, bottom = s[:blocks], swap(s[blocks:])
            compact = jnp.where(low, top + bottom, top - bottom)
            if direct and slot == 0 and grams[0].dtype == F32:
                grams[0][i] = compact
            elif direct:
                coded.append(double(compact))
            else:
                grams[0][f] = pack(double(compact))
        if coded:
            write_coded(grams[slot], *encode(coded)[:2])


def gram(pieces, slots, direct, in_steps, after):
    peers = len(pieces)
    count, here, width = pieces[0].shape
    blocks = here * peers
    if direct:
        rows = coded_rows(count // slots, blocks // 2)
        shapes = [((rows, 2 * blocks), jnp.int16)] * slots
        if in_steps:
            shapes[0] = ((count // slots, blocks, 2 * blocks), F32)
    else:
        shapes = [((count, blocks // 2, 2 * blocks), F32)]
    out = pl.pallas_call(
        functools.partial(gram_kernel, peers, slots, direct, len(after)),
        in_specs=[whole_spec()] * peers + [any_spec()] * len(after),
        out_specs=[whole_spec()] * (2 + len(shapes)),
        out_shape=[jax.ShapeDtypeStruct((count, blocks, width), BF16), TOKEN]
        + [jax.ShapeDtypeStruct(*s) for s in shapes],
        scratch_shapes=[pltpu.VMEM((blocks, width), F32)] if here % 16 else [],
        compiler_params=params(),
        cost_estimate=light(),
        name="gram",
    )(*pieces, *after)
    return out[0], out[2:], out[1]


def add_kernel(own, other, *refs):
    out, token = refs[-2:]
    token[...] = jnp.zeros_like(token)
    number, blocks, _ = own.shape
    received = spread(*read_coded(other, number, blocks // 2))
    sums = [double(own[i] + unpack(received[i])[0]) for i in range(number)]
    write_coded(out, *encode(sums)[:2])


def add(own, other, after):
    return pl.pallas_call(
        add_kernel,
        in_specs=[whole_spec()] * 2 + [any_spec()] * len(after),
        out_specs=[whole_spec()] * 2,
        out_shape=[jax.ShapeDtypeStruct(other.shape, jnp.int16), TOKEN],
        compiler_params=params(),
        cost_estimate=light(),
        name="add",
    )(own, other, *after)


def split(x):
    high = x.astype(BF16)
    return high, (x - high.astype(F32)).astype(BF16)


def solve_kernel(chunks, half_rows, *refs):
    out, token = refs[-2:]
    token[...] = jnp.zeros_like(token)
    width = out.shape[1]
    half = width // 2
    shape = (half, width)
    row = lax.broadcasted_iota(jnp.int32, shape, 0)
    lane = lax.broadcasted_iota(jnp.int32, shape, 1)
    eye = jnp.where(row == lane, F32(1), F32(0))

    sums, at = [], 0
    for parts, count in chunks:
        ins, at = refs[at : at + parts], at + parts
        if parts == 1:
            sums += [ins[0][i] for i in range(count)]
            continue
        found = [spread(*read_coded(r, count, half_rows)) for r in ins]
        added = each(lambda p, q: p + q, found[0], found[1])
        if parts == 4:
            added = each(lambda p, q, r: p + (q + r), added, found[2], found[3])
        sums += added
    number = len(sums)
    both_halves = each(unpack, sums)
    grams = [h[0] for h in both_halves]
    spots = lax.broadcasted_iota(jnp.int32, sums[0].shape, 1)
    lines = lax.broadcasted_iota(jnp.int32, sums[0].shape, 0)
    on = (spots == lines) | (spots == lines + 3 * half_rows)
    shift = each(
        lambda p: jnp.sum(jnp.where(on, p, F32(0)), keepdims=True) * F32(1.0 / half), sums
    )
    eye_low = jnp.where(row + half == lane, F32(1), F32(0))
    inverse = each(lambda m: 1.0 / m, shift)
    system = each(lambda g, m: g * m + eye, grams, inverse)
    under = each(lambda h, m: h[1] * m + eye_low, both_halves, inverse)
    both = each(
        lambda a, u: jnp.concatenate(split(jnp.concatenate([a, u], 0)), 1), system, under
    )

    def times(v, a):
        wide = dot(v, a)
        return wide[:, :width] + wide[:, width:]


    low_end, high_end = 1.0, float(half + 1)
    mid, radius = (high_end + low_end) / 2, (high_end - low_end) / 2
    ratio = mid / radius
    t = 2 * ratio * ratio - 1
    scale = 2.0 / (radius * radius * t)
    x = each(lambda a: (F32(scale) * (F32(2 * mid) * eye - a)).astype(BF16), system)
    p = each(lambda v, a: eye - times(v, a), x, both)
    x = each(lambda v: v.astype(F32), x)
    for _ in range(3):
        t_next = 2 * t * t - 1
        c = F32(2 * t * t / t_next)
        pf = each(lambda q: full(q).astype(BF16), p)
        xp = each(lambda v, q: jnp.concatenate([v, q], 0).astype(BF16), x, p)
        moved = each(dot, xp, pf)
        x = each(lambda v, m: c * (v + m[:half]), x, moved)
        p = each(lambda m: c * m[half:] - F32(1 / t_next) * eye, moved)
        t = t_next
    for kind in ("scaled", "last"):
        xb = each(lambda v: v.astype(BF16), x)
        xw = each(lambda v: v.astype(F32), xb)
        xf = each(lambda v: full(v).astype(BF16), xw)
        residual = each(lambda v, a: eye - times(v, a), xb, both)
        step = each(lambda r, v: dot(r.astype(BF16), v), residual, xf)
        factor = 1.0 if kind == "last" else 2 * t * t / (2 * t * t - 1)
        x = each(lambda v, m: F32(factor) * (v + m), xw, step)
    values, codes, scales = encode(each(lambda v: double(eye - v), x))
    products = outer(scales, number)
    filters = each(lambda v, p: unpack(v, p * F32(0.5 / TOP)), values, products)
    rounded = each(lambda c: c[0].astype(BF16), filters)
    turned = each(
        lambda c: jnp.concatenate([c[0].astype(BF16), c[1].astype(BF16)], 0), filters
    )
    split_g = each(lambda g: jnp.concatenate(split(g), 0), grams)
    moved = each(dot, split_g, turned)
    moved = each(lambda m: m[:half] + m[half:], moved)
    energy = each(
        lambda c, h: jnp.sum(c.astype(F32) * h, keepdims=True) * F32(half), rounded, moved
    )
    energy = place([jnp.broadcast_to(e, (1, width)) for e in energy], codes.shape[0])
    energy = jnp.maximum(energy, F32(1e-30))
    whole = jnp.floor(jnp.log(energy) * F32(LOG_STEPS / math.log(2.0)))
    rest = jnp.round((energy * jnp.exp2(whole * F32(-1 / LOG_STEPS)) - 1.0) * F32(FINE))
    spot = lax.broadcasted_iota(jnp.int32, codes.shape, 1)
    codes = jnp.where(spot == half, whole, jnp.where(spot == half + 1, rest, codes))
    write_coded(out, values, codes)


def solve(chunks, half_rows, after):
    args = [x for parts, _ in chunks for x in parts]
    width = args[0].shape[-1]
    number = sum(count for _, count in chunks)
    shape = [(len(parts), count) for parts, count in chunks]
    return pl.pallas_call(
        functools.partial(solve_kernel, shape, half_rows),
        in_specs=[whole_spec()] * len(args) + [any_spec()] * len(after),
        out_specs=[whole_spec()] * 2,
        out_shape=[
            jax.ShapeDtypeStruct((coded_rows(number, half_rows), width), jnp.int16),
            TOKEN,
        ],
        compiler_params=params(),
        cost_estimate=light(),
        name="filters",
    )(*args, *after)


def energy_kernel(slots, direct, number, chunks, first, *refs):
    merged, pieces = refs[:chunks], refs[chunks : chunks + number]
    energies_out, filters_out, token, energies, filters, energies_sem, filters_sem = refs[-7:]
    token[...] = jnp.zeros_like(token)
    blocks, width = merged[0].shape[1:]
    entries = width // 2
    counts = [m.shape[0] for m in merged]
    per_slot = sum(counts) // slots
    half_rows = blocks // 2
    states = entries * lax.axis_size("space")
    puts = []
    for slot in range(slots):
        owner = slot_owner(direct, slot)
        piece = pieces[slot] if direct else pieces[0].at[slot]
        values, codes = read_coded(piece, per_slot, half_rows)
        whole = codes[:, blocks : blocks + 1]
        rest = codes[:, blocks + 1 : blocks + 2]
        total = jnp.exp2(whole * F32(1 / LOG_STEPS)) * (1.0 + rest * F32(1 / FINE))
        gains = F32(states) / total
        codes = jnp.where(lane_low(codes.shape, blocks), codes, swap(codes))
        products = outer(scale_of(codes), per_slot)
        base = 0
        for chunk, count in enumerate(counts):
            own = count // slots
            size = 4 if own % 4 == 0 else 1
            for begin in range(0, own, size):
                start = sum(counts[:chunk]) + owner * own + begin
                some = range(base + begin, base + begin + size)
                z = [merged[chunk][owner * own + begin + i] for i in range(size)]
                scale = [products[i] * F32(0.5 / TOP) for i in some]
                halves = each(unpack, [values[i] for i in some], scale)
                both = each(
                    lambda h: jnp.concatenate([h[0].astype(BF16), h[1].astype(BF16)], 0), halves
                )
                w = each(lambda v: jnp.concatenate([v[:, :entries], v[:, entries:]], 0), z)
                r = each(dot, both, w)
                gain = [gains[i : i + 1] for i in some]
                energy = each(
                    lambda v, t: jnp.sum(v * v, axis=0, keepdims=True) * t, r, gain
                )
                for i in range(size):
                    filters[start + i, 0] = halves[i][0][:, :blocks]
                    filters[start + i, 1] = -halves[i][1][:, :blocks]
                    energies[pl.ds(start + i, 1), :] = energy[i]
                put = pltpu.make_async_copy(
                    filters.at[pl.ds(start, size)],
                    filters_out.at[pl.ds(first + start, size)],
                    filters_sem.at[len(puts)],
                )
                put.start()
                puts.append(put)
            base += own
    put = pltpu.make_async_copy(
        energies, energies_out.at[pl.ds(first, sum(counts))], energies_sem.at[0]
    )
    put.start()
    for p in [*puts, put]:
        p.wait()


def filtered(merged, pieces, slots, direct, carry, owned, first, after):
    _, blocks, width = merged[0].shape
    count = sum(m.shape[0] for m in merged)
    copies = sum(slots * (m.shape[0] // slots) for m in merged)
    entries = width // 2
    fixed = len(merged) + len(pieces)
    args = [*merged, *pieces] + ([] if carry is None else list(carry)) + list(after)
    hbm = pl.BlockSpec(memory_space=pltpu.HBM)
    return pl.pallas_call(
        functools.partial(energy_kernel, slots, direct, len(pieces), len(merged), first),
        in_specs=[whole_spec()] * fixed
        + ([] if carry is None else [hbm] * 2)
        + [any_spec()] * len(after),
        out_specs=[hbm] * 2 + [whole_spec()],
        out_shape=[
            jax.ShapeDtypeStruct((owned, entries), F32),
            jax.ShapeDtypeStruct((owned, 2, blocks, blocks), F32),
            TOKEN,
        ],
        input_output_aliases={} if carry is None else {fixed: 0, fixed + 1: 1},
        scratch_shapes=[
            pltpu.VMEM((count, entries), F32),
            pltpu.VMEM((count, 2, blocks, blocks), F32),
            pltpu.SemaphoreType.DMA((1,)),
            pltpu.SemaphoreType.DMA((copies,)),
        ],
        compiler_params=params(),
        cost_estimate=light(),
        name="energy",
    )(*args)


def exchange(arrays, axis):
    size = lax.axis_size(axis)
    got = [arrays[0]]
    for offset in range(1, size):
        pairs = [(i, i ^ offset) for i in range(size)]
        got.append(lax.ppermute(arrays[offset], axis, pairs))
    return got


def plan(owned, slots):
    if slots != 4 or owned != 64:
        return [owned], (("T", 0), ("G", 0), ("F", 0), ("E", 0))
    return SIZES, ORDER


SIZES = [24, 24, 16]
ORDER = (
    ("T", 0), ("T", 1), ("G", 0), ("A", 0), ("G", 1), ("F", 0), ("A", 1), ("G", 2),
    ("E", 0), ("F", 1), ("F", 2), ("E", 1), ("E", 2),
)


TIES = {("T", 1): (0,)}


def permute(x, axis, offset):
    pairs = [(i, i ^ offset) for i in range(lax.axis_size(axis))]
    return lax.ppermute(x, axis, pairs)


def on_device(snapshots, entry_weight, freq_index):
    peers = lax.axis_size("tm")
    slots = lax.axis_size("space")
    owned = freq_index.shape[0] // peers
    sizes, order = plan(owned, slots)
    starts = [sum(sizes[:c]) for c in range(len(sizes))]
    paired = slots == 4
    halves = 2 if paired else slots
    weight = entry_weight.reshape(1, -1)
    sent, merged, grams, parts, pieces = {}, {}, {}, {}, {}
    carry = None
    token = []

    def do_transform(c):
        nonlocal token
        joint = [k for k in range(c, len(sizes)) if k == c or c and ("T", k) not in order]
        out, done = transform(
            snapshots, weight, freq_index, peers, [(starts[k], sizes[k]) for k in joint], token
        )
        token = [done]
        for k, own in zip(joint, out):
            sent[k] = [own[0]] + [permute(own[i], "tm", i) for i in range(1, peers)]

    def do_gram(c):
        nonlocal token
        in_steps = paired and ("A", c) in order
        merged[c], grams[c], done = gram(sent[c], halves, paired, in_steps, token)
        token = [done]
        if in_steps:
            grams[c] = [grams[c][0], permute(grams[c][1], "space", 1)]
        elif paired:
            own, other = grams[c]
            parts[c] = [
                own,
                permute(own, "space", 2),
                permute(other, "space", 1),
                permute(other, "space", 3),
            ]
        else:
            parts[c] = [lax.psum_scatter(grams[c][0], "space", scatter_dimension=0, tiled=True)]

    def do_add(c):
        nonlocal token
        half, done = add(*grams[c], token)
        token = [done]
        parts[c] = [half, permute(half, "space", 2)]

    def joined(stage, c):
        last = c + 1
        while last < len(sizes) and (stage, last) not in order:
            last += 1
        return range(c, last)

    def do_solve(c):
        nonlocal token
        work = [(parts[k], sizes[k] // halves) for k in joined("F", c)]
        own, done = solve(work, merged[c].shape[1] // 2, token)
        token = [done]
        if paired:
            pieces[c] = [own, permute(own, "space", 1)]
        else:
            pieces[c] = [lax.all_gather(own, "space", axis=0, tiled=False)]

    def do_energy(c):
        nonlocal token, carry
        work = [merged[k] for k in joined("E", c)]
        *carry, done = filtered(
            work, pieces[c], halves, paired, carry, owned, starts[c], token
        )
        token = [done]

    stages = {"T": do_transform, "G": do_gram, "A": do_add, "F": do_solve, "E": do_energy}
    for stage, c in order:
        token = token + [sent[k][1] for k in TIES.get((stage, c), ()) if k in sent]
        stages[stage](c)
    return (carry[0], carry[1])


def solution(mesh):
    in_specs = (P(("grp", "tm"), None, "space"), P(("grp", "space")), P())
    out_specs = (P(("grp", "tm"), "space"), P(("grp", "tm"), None, None, None))
    return jax.shard_map(
        on_device, mesh=mesh, in_specs=in_specs, out_specs=out_specs, check_vma=False
    )
```

```python
import functools
import math

import jax
import jax.numpy as jnp
from jax import lax
from jax.experimental import pallas as pl
from jax.experimental.pallas import tpu as pltpu
from jax.sharding import PartitionSpec as P

F32 = jnp.float32
BF16 = jnp.bfloat16
VMEM_LIMIT = 30 * 1024 * 1024
LANES = 128


def params(**kwargs):
    return pltpu.CompilerParams(vmem_limit_bytes=VMEM_LIMIT, **kwargs)


def whole_spec():
    return pl.BlockSpec(memory_space=pltpu.VMEM)


TOKEN = jax.ShapeDtypeStruct((8, LANES), F32)


def light():
    return pl.CostEstimate(flops=1024, bytes_accessed=1024, transcendentals=0)


def in_hbm(x):
    return pltpu.with_memory_space_constraint(x, pltpu.HBM)


def any_spec():
    return pl.BlockSpec(memory_space=pl.ANY)


def dot(a, b):
    return lax.dot_general(a, b, (((1,), (0,)), ((), ())), preferred_element_type=F32)


def cos_sin(phase, length):
    quarter = length // 4
    eighth = length // 8
    shifted = phase + eighth
    low = (shifted & (quarter - 1)) - eighth
    quadrant = (shifted // quarter) & 3
    x = low.astype(F32) * F32(2.0 * math.pi / length)
    x2 = x * x
    cos = F32(1 / 40320)
    for c in (-1 / 720, 1 / 24, -0.5, 1.0):
        cos = cos * x2 + F32(c)
    sin = F32(1 / 362880)
    for c in (-1 / 5040, 1 / 120, -1 / 6, 1.0):
        sin = sin * x2 + F32(c)
    sin = sin * x
    odd = (quadrant & 1) == 1
    c0 = jnp.where(odd, sin, cos)
    s0 = jnp.where(odd, cos, sin)
    c1 = jnp.where((quadrant == 1) | (quadrant == 2), -c0, c0)
    s1 = jnp.where(quadrant >= 2, -s0, s0)
    return c1, s1


def transform_kernel(peers, parts, group, *refs):
    freq_hbm, weight_hbm, snap_hbm = refs[:3]
    outs, token = refs[-peers * len(parts) - 8 : -8], refs[-8]
    freq, weight, snap, table, wide, small_sem, snap_sem = refs[-7:]
    blocks, length, entries = snap.shape
    steps = blocks // group
    get_freq = pltpu.make_async_copy(freq_hbm, freq, small_sem.at[0])
    get_weight = pltpu.make_async_copy(weight_hbm, weight, small_sem.at[1])
    get_snap = [
        pltpu.make_async_copy(
            snap_hbm.at[pl.ds(i * group, group)], snap.at[pl.ds(i * group, group)], snap_sem.at[i]
        )
        for i in range(steps)
    ]
    token[...] = jnp.zeros_like(token)
    get_freq.start()
    for get in get_snap:
        get.start()
    get_weight.start()

    me = lax.axis_index("tm")
    groups = [
        (peer, first + j)
        for first, count in parts
        for peer in range(peers)
        for j in range(0, count, 8)
    ]
    rows = 8 * len(groups)
    per_peer = freq.shape[0] // peers
    times = lax.broadcasted_iota(jnp.int32, (8, length), 1)
    sub = lax.broadcasted_iota(jnp.int32, (8, length), 0)
    window = 0.5 - 0.5 * cos_sin(times, length)[0]
    scaled = window / F32(math.sqrt(0.375 * length))
    get_freq.wait()

    def eight(index):
        peer, offset = groups[index]
        start = jnp.bitwise_xor(me, peer) * per_peer + offset
        k = jnp.zeros((8, length), jnp.int32)
        for i in range(8):
            k = jnp.where(sub == i, freq[start + i], k)
        cos, sin = cos_sin((k * times) & (length - 1), length)
        return scaled * cos, -(scaled * sin)

    for pair in range(rows // 16):
        re0, im0 = eight(2 * pair)
        re1, im1 = eight(2 * pair + 1)
        table[16 * pair : 16 * pair + 16, :] = jnp.concatenate([re0, re1], 0).astype(BF16)
        table[rows + 16 * pair : rows + 16 * pair + 16, :] = jnp.concatenate(
            [im0, im1], 0
        ).astype(BF16)

    get_weight.wait()
    root = jnp.sqrt(weight[...])
    tiles = entries // LANES
    for step in range(steps):
        get_snap[step].wait()
        for b in range(step * group, (step + 1) * group):
            spec = dot(table[...], snap[b]) * root
            for tile in range(tiles):
                lanes = slice(tile * LANES, (tile + 1) * LANES)
                wide[tile, pl.ds(b, rows, stride=blocks), :] = spec[:rows, lanes]
                wide[tiles + tile, pl.ds(b, rows, stride=blocks), :] = spec[rows:, lanes]
    at = 0
    for out in outs:
        for j in range(out.shape[0]):
            for tile in range(2 * tiles):
                lanes = slice(tile * LANES, (tile + 1) * LANES)
                out[j, :, lanes] = wide[tile, at : at + blocks, :].astype(BF16)
            at += blocks


def transform(snapshots, weight, freq_index, peers, parts, after):
    blocks, length, entries = snapshots.shape
    group = min(blocks, 4)
    total = peers * sum(count for _, count in parts)
    shapes = [
        jax.ShapeDtypeStruct((count, blocks, 2 * entries), BF16)
        for _, count in parts
        for _ in range(peers)
    ]
    hbm = pl.BlockSpec(memory_space=pltpu.HBM)
    out = pl.pallas_call(
        functools.partial(transform_kernel, peers, parts, group),
        in_specs=[hbm] * 3 + [any_spec()] * len(after),
        out_specs=[whole_spec()] * (len(shapes) + 1),
        out_shape=shapes + [TOKEN],
        scratch_shapes=[
            pltpu.SMEM(freq_index.shape, jnp.int32),
            pltpu.VMEM(weight.shape, F32),
            pltpu.VMEM(snapshots.shape, BF16),
            pltpu.VMEM((2 * total, length), BF16),
            pltpu.VMEM((2 * entries // LANES, total * blocks, LANES), F32),
            pltpu.SemaphoreType.DMA((2,)),
            pltpu.SemaphoreType.DMA((blocks // group,)),
        ],
        compiler_params=params(),
        cost_estimate=light(),
        name="transform",
    )(in_hbm(freq_index), in_hbm(weight), in_hbm(snapshots), *after)
    return [out[i * peers : (i + 1) * peers] for i in range(len(parts))], out[-1]


def lane_low(shape, half):
    return lax.broadcasted_iota(jnp.int32, shape, 1) < half


def swap(x):
    return pltpu.roll(x, x.shape[1] // 2, 1)


def each(fn, *lists):
    return [fn(*items) for items in zip(*lists)]


def double(compact):
    return compact + swap(compact)


def pack(both):
    half = both.shape[0]
    low = lane_low((half // 2, 2 * half), half)
    return jnp.where(low, both[: half // 2], both[half // 2 :])


def unpack(packed, scale=None):
    rows, half = packed.shape[0], packed.shape[1] // 2
    low = lane_low(packed.shape, half)
    other = swap(packed)
    both = jnp.concatenate(
        [jnp.where(low, packed, other), jnp.where(low, other, packed)], 0
    )
    turned = jnp.transpose(jnp.concatenate([packed, packed], 0))
    turned = jnp.where(lane_low((half, half), rows), turned[:half], turned[half:])
    turned = jnp.concatenate([turned, turned], 1)
    low = lane_low(both.shape, half)
    total = both + turned
    apart = both - turned
    top = jnp.where(low, total, apart)
    bottom = jnp.where(low, -apart, total)
    scale = F32(0.5) if scale is None else scale
    return scale * top, scale * bottom


def full(compact):
    half = compact.shape[0]
    turned = swap(compact)
    low = lane_low(compact.shape, half)
    return jnp.concatenate([compact, jnp.where(low, -turned, turned)], 0)


TOP = 23169.0
LOG_STEPS = 64.0
FINE = float(2**21)


def place(lines, rows):
    shape = (rows, lines[0].shape[1])
    row = lax.broadcasted_iota(jnp.int32, shape, 0)
    out = jnp.zeros(shape, F32)
    for i, line in enumerate(lines):
        out = jnp.where(row == i, line, out)
    return out


def pad_rows(number):
    return -(-number // 16) * 16


def scale_of(code):
    exponent = jnp.floor(code * F32(1 / 256))
    part = code - exponent * 256
    return (jnp.exp2(exponent) * (1 + part * F32(1 / 128))).astype(BF16)


def outer(scales, number):
    half = scales.shape[1] // 2
    wide = scales.astype(F32)
    row = lax.broadcasted_iota(jnp.int32, scales.shape, 0)
    turned = jnp.transpose(wide)[:half].astype(BF16)
    return [
        dot(turned, jnp.where(row == i, wide, F32(0)).astype(BF16)) for i in range(number)
    ]


def inverse_outer(scales, number):
    half = scales.shape[1] // 2
    rows = scales.shape[0]
    inverse = 1.0 / scales.astype(F32)
    high = inverse.astype(BF16).astype(F32)
    low = inverse - high
    left = jnp.transpose(jnp.concatenate([high, high, low], 0))[:half].astype(BF16)
    right = jnp.concatenate([high, low, high], 0)
    row = lax.broadcasted_iota(jnp.int32, right.shape, 0) & (rows - 1)
    return [
        dot(left, jnp.where(row == i, right, F32(0)).astype(BF16)) for i in range(number)
    ]


def encode(both):
    half, width = both[0].shape
    row = lax.broadcasted_iota(jnp.int32, (half, width), 0)
    lane = lax.broadcasted_iota(jnp.int32, (half, width), 1)
    on = (lane == row) | (lane == row + half)
    diagonal = each(lambda b: jnp.sum(jnp.where(on, b, F32(0)), axis=0, keepdims=True), both)
    root = jnp.sqrt(jnp.maximum(place(diagonal, pad_rows(len(both))), F32(1e-30)))
    exponent = jnp.floor(jnp.log(root) * F32(1 / math.log(2.0)))
    part = jnp.maximum(jnp.ceil((root * jnp.exp2(-exponent) - 1) * 128), F32(0))
    codes = exponent * 256 + part
    scales = scale_of(codes)
    inverse = inverse_outer(scales, len(both))
    value = each(lambda b, p: jnp.round((b * F32(TOP)) * p), both, inverse)
    return each(lambda v: pack(jnp.clip(v, F32(-32767), F32(32767))), value), codes, scales


def spread(values, codes):
    products = outer(scale_of(codes), len(values))
    return each(lambda v, p: v * pack(p * F32(1 / TOP)), values, products)


def to_short(x):
    return x.astype(jnp.int32).astype(jnp.int16)


def from_short(x):
    return x.astype(jnp.int32).astype(F32)


def coded_rows(number, half_rows):
    return number * half_rows + pad_rows(number)


def write_coded(out, values, codes):
    half_rows = values[0].shape[0]
    for i, value in enumerate(values):
        out[i * half_rows : (i + 1) * half_rows, :] = to_short(value)
    out[len(values) * half_rows :, :] = to_short(codes)


def read_coded(ref, number, half_rows):
    codes = from_short(ref[number * half_rows :, :])
    values = [from_short(ref[i * half_rows : (i + 1) * half_rows, :]) for i in range(number)]
    return values, codes


def slot_owner(direct, slot):
    return jnp.bitwise_xor(lax.axis_index("space") & 1, slot) if direct else slot


def gram_kernel(peers, slots, direct, after, *refs):
    pieces, refs = refs[:peers], refs[peers + after :]
    merged, token, grams = refs[0], refs[1], refs[2:]
    token[...] = jnp.zeros_like(token)
    me = lax.axis_index("tm")
    here = pieces[0].shape[1]
    entries = pieces[0].shape[2] // 2
    blocks = here * peers
    per_slot = pieces[0].shape[0] // slots
    stage = None
    if here % 16:
        grams, stage = grams[:-1], grams[-1]
    low = lane_low((blocks, 2 * blocks), blocks)
    for slot in range(slots):
        owner = slot_owner(direct, slot)
        coded = []
        for i in range(per_slot):
            f = owner * per_slot + i
            if stage is None:
                for peer in range(peers):
                    start = pl.multiple_of(jnp.bitwise_xor(me, peer) * here, here)
                    merged[f, pl.ds(start, here), :] = pieces[peer][f]
                z = merged[f]
            else:
                for peer in range(peers):
                    start = pl.multiple_of(jnp.bitwise_xor(me, peer) * here, here)
                    stage[pl.ds(start, here), :] = pieces[peer][f].astype(F32)
                z = stage[...].astype(BF16)
                merged[f] = z
            w = jnp.concatenate([z[:, :entries], z[:, entries:]], 0)
            s = lax.dot_general(w, w, (((1,), (1,)), ((), ())), preferred_element_type=F32)
            s = s * F32(1.0 / blocks)
            top, bottom = s[:blocks], swap(s[blocks:])
            compact = jnp.where(low, top + bottom, top - bottom)
            if direct and slot == 0 and grams[0].dtype == F32:
                grams[0][i] = compact
            elif direct:
                coded.append(double(compact))
            else:
                grams[0][f] = pack(double(compact))
        if coded:
            write_coded(grams[slot], *encode(coded)[:2])


def gram(pieces, slots, direct, in_steps, after):
    peers = len(pieces)
    count, here, width = pieces[0].shape
    blocks = here * peers
    if direct:
        rows = coded_rows(count // slots, blocks // 2)
        shapes = [((rows, 2 * blocks), jnp.int16)] * slots
        if in_steps:
            shapes[0] = ((count // slots, blocks, 2 * blocks), F32)
    else:
        shapes = [((count, blocks // 2, 2 * blocks), F32)]
    out = pl.pallas_call(
        functools.partial(gram_kernel, peers, slots, direct, len(after)),
        in_specs=[whole_spec()] * peers + [any_spec()] * len(after),
        out_specs=[whole_spec()] * (2 + len(shapes)),
        out_shape=[jax.ShapeDtypeStruct((count, blocks, width), BF16), TOKEN]
        + [jax.ShapeDtypeStruct(*s) for s in shapes],
        scratch_shapes=[pltpu.VMEM((blocks, width), F32)] if here % 16 else [],
        compiler_params=params(),
        cost_estimate=light(),
        name="gram",
    )(*pieces, *after)
    return out[0], out[2:], out[1]


def add_kernel(own, other, *refs):
    out, token = refs[-2:]
    token[...] = jnp.zeros_like(token)
    number, blocks, _ = own.shape
    received = spread(*read_coded(other, number, blocks // 2))
    sums = [double(own[i] + unpack(received[i])[0]) for i in range(number)]
    write_coded(out, *encode(sums)[:2])


def add(own, other, after):
    return pl.pallas_call(
        add_kernel,
        in_specs=[whole_spec()] * 2 + [any_spec()] * len(after),
        out_specs=[whole_spec()] * 2,
        out_shape=[jax.ShapeDtypeStruct(other.shape, jnp.int16), TOKEN],
        compiler_params=params(),
        cost_estimate=light(),
        name="add",
    )(own, other, *after)


def split(x):
    high = x.astype(BF16)
    return high, (x - high.astype(F32)).astype(BF16)


def solve_kernel(chunks, half_rows, *refs):
    out, token = refs[-2:]
    token[...] = jnp.zeros_like(token)
    width = out.shape[1]
    half = width // 2
    shape = (half, width)
    row = lax.broadcasted_iota(jnp.int32, shape, 0)
    lane = lax.broadcasted_iota(jnp.int32, shape, 1)
    eye = jnp.where(row == lane, F32(1), F32(0))

    sums, at = [], 0
    for parts, count in chunks:
        ins, at = refs[at : at + parts], at + parts
        if parts == 1:
            sums += [ins[0][i] for i in range(count)]
            continue
        found = [spread(*read_coded(r, count, half_rows)) for r in ins]
        added = each(lambda p, q: p + q, found[0], found[1])
        if parts == 4:
            added = each(lambda p, q, r: p + (q + r), added, found[2], found[3])
        sums += added
    number = len(sums)
    both_halves = each(unpack, sums)
    grams = [h[0] for h in both_halves]
    spots = lax.broadcasted_iota(jnp.int32, sums[0].shape, 1)
    lines = lax.broadcasted_iota(jnp.int32, sums[0].shape, 0)
    on = (spots == lines) | (spots == lines + 3 * half_rows)
    shift = each(
        lambda p: jnp.sum(jnp.where(on, p, F32(0)), keepdims=True) * F32(1.0 / half), sums
    )
    eye_low = jnp.where(row + half == lane, F32(1), F32(0))
    inverse = each(lambda m: 1.0 / m, shift)
    system = each(lambda g, m: g * m + eye, grams, inverse)
    under = each(lambda h, m: h[1] * m + eye_low, both_halves, inverse)
    both = each(
        lambda a, u: jnp.concatenate(split(jnp.concatenate([a, u], 0)), 1), system, under
    )

    def times(v, a):
        wide = dot(v, a)
        return wide[:, :width] + wide[:, width:]


    low_end, high_end = 1.0, float(half + 1)
    mid, radius = (high_end + low_end) / 2, (high_end - low_end) / 2
    ratio = mid / radius
    t = 2 * ratio * ratio - 1
    scale = 2.0 / (radius * radius * t)
    x = each(lambda a: (F32(scale) * (F32(2 * mid) * eye - a)).astype(BF16), system)
    p = each(lambda v, a: eye - times(v, a), x, both)
    x = each(lambda v: v.astype(F32), x)
    for _ in range(3):
        t_next = 2 * t * t - 1
        c = F32(2 * t * t / t_next)
        pf = each(lambda q: full(q).astype(BF16), p)
        xp = each(lambda v, q: jnp.concatenate([v, q], 0).astype(BF16), x, p)
        moved = each(dot, xp, pf)
        x = each(lambda v, m: c * (v + m[:half]), x, moved)
        p = each(lambda m: c * m[half:] - F32(1 / t_next) * eye, moved)
        t = t_next
    for kind in ("scaled", "last"):
        xb = each(lambda v: v.astype(BF16), x)
        xw = each(lambda v: v.astype(F32), xb)
        xf = each(lambda v: full(v).astype(BF16), xw)
        residual = each(lambda v, a: eye - times(v, a), xb, both)
        step = each(lambda r, v: dot(r.astype(BF16), v), residual, xf)
        factor = 1.0 if kind == "last" else 2 * t * t / (2 * t * t - 1)
        x = each(lambda v, m: F32(factor) * (v + m), xw, step)
    values, codes, scales = encode(each(lambda v: double(eye - v), x))
    products = outer(scales, number)
    filters = each(lambda v, p: unpack(v, p * F32(0.5 / TOP)), values, products)
    rounded = each(lambda c: c[0].astype(BF16), filters)
    turned = each(
        lambda c: jnp.concatenate([c[0].astype(BF16), c[1].astype(BF16)], 0), filters
    )
    split_g = each(lambda g: jnp.concatenate(split(g), 0), grams)
    moved = each(dot, split_g, turned)
    moved = each(lambda m: m[:half] + m[half:], moved)
    energy = each(
        lambda c, h: jnp.sum(c.astype(F32) * h, keepdims=True) * F32(half), rounded, moved
    )
    energy = place([jnp.broadcast_to(e, (1, width)) for e in energy], codes.shape[0])
    energy = jnp.maximum(energy, F32(1e-30))
    whole = jnp.floor(jnp.log(energy) * F32(LOG_STEPS / math.log(2.0)))
    rest = jnp.round((energy * jnp.exp2(whole * F32(-1 / LOG_STEPS)) - 1.0) * F32(FINE))
    spot = lax.broadcasted_iota(jnp.int32, codes.shape, 1)
    codes = jnp.where(spot == half, whole, jnp.where(spot == half + 1, rest, codes))
    write_coded(out, values, codes)


def solve(chunks, half_rows, after):
    args = [x for parts, _ in chunks for x in parts]
    width = args[0].shape[-1]
    number = sum(count for _, count in chunks)
    shape = [(len(parts), count) for parts, count in chunks]
    return pl.pallas_call(
        functools.partial(solve_kernel, shape, half_rows),
        in_specs=[whole_spec()] * len(args) + [any_spec()] * len(after),
        out_specs=[whole_spec()] * 2,
        out_shape=[
            jax.ShapeDtypeStruct((coded_rows(number, half_rows), width), jnp.int16),
            TOKEN,
        ],
        compiler_params=params(),
        cost_estimate=light(),
        name="filters",
    )(*args, *after)


def energy_kernel(slots, direct, number, chunks, first, before, last, *refs):
    merged, pieces = refs[:chunks], refs[chunks : chunks + number]
    earlier = refs[chunks + number : chunks + number + 2]
    puts = []
    if last:
        energies_out, filters_out, token, energies, filters = refs[-8:-3]
    else:
        energies, filters, token = refs[-6:-3]
        if before is not None:
            energies_out, filters_out = refs[-8:-6]
    energies_sem, filters_sem, before_sem = refs[-3:]
    if before is not None:
        for i, (source, target) in enumerate(zip(earlier, (energies_out, filters_out))):
            put = pltpu.make_async_copy(
                source, target.at[pl.ds(before, source.shape[0])], before_sem.at[i]
            )
            put.start()
            puts.append(put)
    own_puts = 0
    token[...] = jnp.zeros_like(token)
    blocks, width = merged[0].shape[1:]
    entries = width // 2
    counts = [m.shape[0] for m in merged]
    per_slot = sum(counts) // slots
    half_rows = blocks // 2
    states = entries * lax.axis_size("space")
    for slot in range(slots):
        owner = slot_owner(direct, slot)
        piece = pieces[slot] if direct else pieces[0].at[slot]
        values, codes = read_coded(piece, per_slot, half_rows)
        whole = codes[:, blocks : blocks + 1]
        rest = codes[:, blocks + 1 : blocks + 2]
        total = jnp.exp2(whole * F32(1 / LOG_STEPS)) * (1.0 + rest * F32(1 / FINE))
        gains = F32(states) / total
        codes = jnp.where(lane_low(codes.shape, blocks), codes, swap(codes))
        products = outer(scale_of(codes), per_slot)
        base = 0
        for chunk, count in enumerate(counts):
            own = count // slots
            size = 4 if own % 4 == 0 else 1
            for begin in range(0, own, size):
                start = sum(counts[:chunk]) + owner * own + begin
                some = range(base + begin, base + begin + size)
                z = [merged[chunk][owner * own + begin + i] for i in range(size)]
                scale = [products[i] * F32(0.5 / TOP) for i in some]
                halves = each(unpack, [values[i] for i in some], scale)
                both = each(
                    lambda h: jnp.concatenate([h[0].astype(BF16), h[1].astype(BF16)], 0), halves
                )
                w = each(lambda v: jnp.concatenate([v[:, :entries], v[:, entries:]], 0), z)
                r = each(dot, both, w)
                gain = [gains[i : i + 1] for i in some]
                energy = each(
                    lambda v, t: jnp.sum(v * v, axis=0, keepdims=True) * t, r, gain
                )
                for i in range(size):
                    filters[start + i, 0] = halves[i][0][:, :blocks]
                    filters[start + i, 1] = -halves[i][1][:, :blocks]
                    energies[pl.ds(start + i, 1), :] = energy[i]
                if last:
                    put = pltpu.make_async_copy(
                        filters.at[pl.ds(start, size)],
                        filters_out.at[pl.ds(first + start, size)],
                        filters_sem.at[own_puts],
                    )
                    put.start()
                    puts.append(put)
                    own_puts += 1
            base += own
    if last:
        put = pltpu.make_async_copy(
            energies, energies_out.at[pl.ds(first, sum(counts))], energies_sem.at[0]
        )
        put.start()
        puts.append(put)
    for put in puts:
        put.wait()


def filtered(merged, pieces, slots, direct, earlier, carry, owned, first, last, after):
    _, blocks, width = merged[0].shape
    count = sum(m.shape[0] for m in merged)
    copies = sum(slots * (m.shape[0] // slots) for m in merged)
    entries = width // 2
    fixed = len(merged) + len(pieces) + (2 if earlier else 0)
    args = [*merged, *pieces, *(earlier[:2] if earlier else ()), *(carry or ()), *after]
    hbm = pl.BlockSpec(memory_space=pltpu.HBM)
    writes = bool(earlier) or last
    own = [
        jax.ShapeDtypeStruct((count, entries), F32),
        jax.ShapeDtypeStruct((count, 2, blocks, blocks), F32),
    ]
    whole = [
        jax.ShapeDtypeStruct((owned, entries), F32),
        jax.ShapeDtypeStruct((owned, 2, blocks, blocks), F32),
    ]
    scratch = [pltpu.VMEM(o.shape, F32) for o in own] if last else []
    out = pl.pallas_call(
        functools.partial(
            energy_kernel, slots, direct, len(pieces), len(merged), first,
            earlier[2] if earlier else None, last,
        ),
        in_specs=[whole_spec()] * fixed
        + ([hbm] * 2 if carry else [])
        + [any_spec()] * len(after),
        out_specs=([hbm] * 2 if writes else [])
        + ([] if last else [whole_spec()] * 2)
        + [whole_spec()],
        out_shape=(whole if writes else []) + ([] if last else own) + [TOKEN],
        input_output_aliases={fixed: 0, fixed + 1: 1} if carry else {},
        scratch_shapes=scratch
        + [
            pltpu.SemaphoreType.DMA((1,)),
            pltpu.SemaphoreType.DMA((copies,)),
            pltpu.SemaphoreType.DMA((2,)),
        ],
        compiler_params=params(),
        cost_estimate=light(),
        name="energy",
    )(*args)
    carry = list(out[:2]) if writes else None
    earlier = None if last else (*out[-3:-1], first)
    return carry, earlier, out[-1]


def plan(owned, slots):
    if slots != 4 or owned != 64:
        return [owned], (("T", 0), ("G", 0), ("F", 0), ("E", 0))
    return SIZES, ORDER


SIZES = [24, 24, 16]
ORDER = (
    ("T", 0), ("T", 1), ("G", 0), ("A", 0), ("G", 1), ("F", 0), ("A", 1), ("G", 2),
    ("E", 0), ("F", 1), ("F", 2), ("E", 1), ("E", 2),
)


TIES = {("T", 1): (0,)}


def permute(x, axis, offset):
    pairs = [(i, i ^ offset) for i in range(lax.axis_size(axis))]
    return lax.ppermute(x, axis, pairs)


def on_device(snapshots, entry_weight, freq_index):
    peers = lax.axis_size("tm")
    slots = lax.axis_size("space")
    owned = freq_index.shape[0] // peers
    sizes, order = plan(owned, slots)
    starts = [sum(sizes[:c]) for c in range(len(sizes))]
    paired = slots == 4
    halves = 2 if paired else slots
    weight = entry_weight.reshape(1, -1)
    sent, merged, grams, parts, pieces = {}, {}, {}, {}, {}
    carry = None
    earlier = None
    token = []

    def do_transform(c):
        nonlocal token
        joint = [k for k in range(c, len(sizes)) if k == c or c and ("T", k) not in order]
        out, done = transform(
            snapshots, weight, freq_index, peers, [(starts[k], sizes[k]) for k in joint], token
        )
        token = [done]
        for k, own in zip(joint, out):
            sent[k] = [own[0]] + [permute(own[i], "tm", i) for i in range(1, peers)]

    def do_gram(c):
        nonlocal token
        in_steps = paired and ("A", c) in order
        merged[c], grams[c], done = gram(sent[c], halves, paired, in_steps, token)
        token = [done]
        if in_steps:
            grams[c] = [grams[c][0], permute(grams[c][1], "space", 1)]
        elif paired:
            own, other = grams[c]
            parts[c] = [
                own,
                permute(own, "space", 2),
                permute(other, "space", 1),
                permute(other, "space", 3),
            ]
        else:
            parts[c] = [lax.psum_scatter(grams[c][0], "space", scatter_dimension=0, tiled=True)]

    def do_add(c):
        nonlocal token
        half, done = add(*grams[c], token)
        token = [done]
        parts[c] = [half, permute(half, "space", 2)]

    def joined(stage, c):
        last = c + 1
        while last < len(sizes) and (stage, last) not in order:
            last += 1
        return range(c, last)

    def do_solve(c):
        nonlocal token
        work = [(parts[k], sizes[k] // halves) for k in joined("F", c)]
        own, done = solve(work, merged[c].shape[1] // 2, token)
        token = [done]
        if paired:
            pieces[c] = [own, permute(own, "space", 1)]
        else:
            pieces[c] = [lax.all_gather(own, "space", axis=0, tiled=False)]

    def do_energy(c):
        nonlocal token, carry, earlier
        chunks = joined("E", c)
        carry, earlier, done = filtered(
            [merged[k] for k in chunks], pieces[c], halves, paired, earlier, carry, owned,
            starts[c], chunks[-1] == len(sizes) - 1, token,
        )
        token = [done]

    stages = {"T": do_transform, "G": do_gram, "A": do_add, "F": do_solve, "E": do_energy}
    for stage, c in order:
        token = token + [sent[k][1] for k in TIES.get((stage, c), ()) if k in sent]
        stages[stage](c)
    return (carry[0], carry[1])


def solution(mesh):
    in_specs = (P(("grp", "tm"), None, "space"), P(("grp", "space")), P())
    out_specs = (P(("grp", "tm"), "space"), P(("grp", "tm"), None, None, None))
    return jax.shard_map(
        on_device, mesh=mesh, in_specs=in_specs, out_specs=out_specs, check_vma=False
    )
```

```python
import functools
import math

import jax
import jax.numpy as jnp
from jax import lax
from jax.experimental import pallas as pl
from jax.experimental.pallas import tpu as pltpu
from jax.sharding import PartitionSpec as P

F32 = jnp.float32
BF16 = jnp.bfloat16
VMEM_LIMIT = 30 * 1024 * 1024
LANES = 128


def params(**kwargs):
    return pltpu.CompilerParams(vmem_limit_bytes=VMEM_LIMIT, **kwargs)


def whole_spec():
    return pl.BlockSpec(memory_space=pltpu.VMEM)


TOKEN = jax.ShapeDtypeStruct((8, LANES), F32)


def light():
    return pl.CostEstimate(flops=1024, bytes_accessed=1024, transcendentals=0)


def in_hbm(x):
    return pltpu.with_memory_space_constraint(x, pltpu.HBM)


def any_spec():
    return pl.BlockSpec(memory_space=pl.ANY)


def dot(a, b):
    return lax.dot_general(a, b, (((1,), (0,)), ((), ())), preferred_element_type=F32)


def cos_sin(phase, length):
    quarter = length // 4
    eighth = length // 8
    shifted = phase + eighth
    low = (shifted & (quarter - 1)) - eighth
    quadrant = (shifted // quarter) & 3
    x = low.astype(F32) * F32(2.0 * math.pi / length)
    x2 = x * x
    cos = F32(1 / 40320)
    for c in (-1 / 720, 1 / 24, -0.5, 1.0):
        cos = cos * x2 + F32(c)
    sin = F32(1 / 362880)
    for c in (-1 / 5040, 1 / 120, -1 / 6, 1.0):
        sin = sin * x2 + F32(c)
    sin = sin * x
    odd = (quadrant & 1) == 1
    c0 = jnp.where(odd, sin, cos)
    s0 = jnp.where(odd, cos, sin)
    c1 = jnp.where((quadrant == 1) | (quadrant == 2), -c0, c0)
    s1 = jnp.where(quadrant >= 2, -s0, s0)
    return c1, s1


def transform_kernel(peers, parts, group, *refs):
    freq_hbm, weight_hbm, snap_hbm = refs[:3]
    outs, token = refs[-peers * len(parts) - 8 : -8], refs[-8]
    freq, weight, snap, table, wide, small_sem, snap_sem = refs[-7:]
    blocks, length, entries = snap.shape
    steps = blocks // group
    get_freq = pltpu.make_async_copy(freq_hbm, freq, small_sem.at[0])
    get_weight = pltpu.make_async_copy(weight_hbm, weight, small_sem.at[1])
    get_snap = [
        pltpu.make_async_copy(
            snap_hbm.at[pl.ds(i * group, group)], snap.at[pl.ds(i * group, group)], snap_sem.at[i]
        )
        for i in range(steps)
    ]
    token[...] = jnp.zeros_like(token)
    get_freq.start()
    for get in get_snap:
        get.start()
    get_weight.start()

    me = lax.axis_index("tm")
    groups = [
        (peer, first + j)
        for first, count in parts
        for peer in range(peers)
        for j in range(0, count, 8)
    ]
    rows = 8 * len(groups)
    per_peer = freq.shape[0] // peers
    times = lax.broadcasted_iota(jnp.int32, (8, length), 1)
    sub = lax.broadcasted_iota(jnp.int32, (8, length), 0)
    window = 0.5 - 0.5 * cos_sin(times, length)[0]
    scaled = window / F32(math.sqrt(0.375 * length))
    get_freq.wait()

    def eight(index):
        peer, offset = groups[index]
        start = jnp.bitwise_xor(me, peer) * per_peer + offset
        k = jnp.zeros((8, length), jnp.int32)
        for i in range(8):
            k = jnp.where(sub == i, freq[start + i], k)
        cos, sin = cos_sin((k * times) & (length - 1), length)
        return scaled * cos, -(scaled * sin)

    for pair in range(rows // 16):
        re0, im0 = eight(2 * pair)
        re1, im1 = eight(2 * pair + 1)
        table[16 * pair : 16 * pair + 16, :] = jnp.concatenate([re0, re1], 0).astype(BF16)
        table[rows + 16 * pair : rows + 16 * pair + 16, :] = jnp.concatenate(
            [im0, im1], 0
        ).astype(BF16)

    get_weight.wait()
    root = jnp.sqrt(weight[...])
    tiles = entries // LANES
    for step in range(steps):
        get_snap[step].wait()
        for b in range(step * group, (step + 1) * group):
            spec = dot(table[...], snap[b]) * root
            for tile in range(tiles):
                lanes = slice(tile * LANES, (tile + 1) * LANES)
                wide[tile, pl.ds(b, rows, stride=blocks), :] = spec[:rows, lanes]
                wide[tiles + tile, pl.ds(b, rows, stride=blocks), :] = spec[rows:, lanes]
    at = 0
    for out in outs:
        for j in range(out.shape[0]):
            for tile in range(2 * tiles):
                lanes = slice(tile * LANES, (tile + 1) * LANES)
                out[j, :, lanes] = wide[tile, at : at + blocks, :].astype(BF16)
            at += blocks


def transform(snapshots, weight, freq_index, peers, parts, after):
    blocks, length, entries = snapshots.shape
    group = min(blocks, 4)
    total = peers * sum(count for _, count in parts)
    shapes = [
        jax.ShapeDtypeStruct((count, blocks, 2 * entries), BF16)
        for _, count in parts
        for _ in range(peers)
    ]
    hbm = pl.BlockSpec(memory_space=pltpu.HBM)
    out = pl.pallas_call(
        functools.partial(transform_kernel, peers, parts, group),
        in_specs=[hbm] * 3 + [any_spec()] * len(after),
        out_specs=[whole_spec()] * (len(shapes) + 1),
        out_shape=shapes + [TOKEN],
        scratch_shapes=[
            pltpu.SMEM(freq_index.shape, jnp.int32),
            pltpu.VMEM(weight.shape, F32),
            pltpu.VMEM(snapshots.shape, BF16),
            pltpu.VMEM((2 * total, length), BF16),
            pltpu.VMEM((2 * entries // LANES, total * blocks, LANES), F32),
            pltpu.SemaphoreType.DMA((2,)),
            pltpu.SemaphoreType.DMA((blocks // group,)),
        ],
        compiler_params=params(),
        cost_estimate=light(),
        name="transform",
    )(in_hbm(freq_index), in_hbm(weight), in_hbm(snapshots), *after)
    return [out[i * peers : (i + 1) * peers] for i in range(len(parts))], out[-1]


def lane_low(shape, half):
    return lax.broadcasted_iota(jnp.int32, shape, 1) < half


def swap(x):
    return pltpu.roll(x, x.shape[1] // 2, 1)


def each(fn, *lists):
    return [fn(*items) for items in zip(*lists)]


def double(compact):
    return compact + swap(compact)


def pack(both):
    half = both.shape[0]
    low = lane_low((half // 2, 2 * half), half)
    return jnp.where(low, both[: half // 2], both[half // 2 :])


def unpack(packed, scale=None):
    rows, half = packed.shape[0], packed.shape[1] // 2
    low = lane_low(packed.shape, half)
    other = swap(packed)
    both = jnp.concatenate(
        [jnp.where(low, packed, other), jnp.where(low, other, packed)], 0
    )
    turned = jnp.transpose(jnp.concatenate([packed, packed], 0))
    turned = jnp.where(lane_low((half, half), rows), turned[:half], turned[half:])
    turned = jnp.concatenate([turned, turned], 1)
    low = lane_low(both.shape, half)
    total = both + turned
    apart = both - turned
    top = jnp.where(low, total, apart)
    bottom = jnp.where(low, -apart, total)
    scale = F32(0.5) if scale is None else scale
    return scale * top, scale * bottom


def full(compact):
    half = compact.shape[0]
    turned = swap(compact)
    low = lane_low(compact.shape, half)
    return jnp.concatenate([compact, jnp.where(low, -turned, turned)], 0)


TOP = 23169.0
LOG_STEPS = 64.0
FINE = float(2**21)


def place(lines, rows):
    shape = (rows, lines[0].shape[1])
    row = lax.broadcasted_iota(jnp.int32, shape, 0)
    out = jnp.zeros(shape, F32)
    for i, line in enumerate(lines):
        out = jnp.where(row == i, line, out)
    return out


def pad_rows(number):
    return -(-number // 16) * 16


def scale_of(code):
    exponent = jnp.floor(code * F32(1 / 256))
    part = code - exponent * 256
    return (jnp.exp2(exponent) * (1 + part * F32(1 / 128))).astype(BF16)


def outer(scales, number):
    half = scales.shape[1] // 2
    wide = scales.astype(F32)
    row = lax.broadcasted_iota(jnp.int32, scales.shape, 0)
    turned = jnp.transpose(wide)[:half].astype(BF16)
    return [
        dot(turned, jnp.where(row == i, wide, F32(0)).astype(BF16)) for i in range(number)
    ]


def inverse_outer(scales, number):
    half = scales.shape[1] // 2
    rows = scales.shape[0]
    inverse = 1.0 / scales.astype(F32)
    high = inverse.astype(BF16).astype(F32)
    low = inverse - high
    left = jnp.transpose(jnp.concatenate([high, high, low], 0))[:half].astype(BF16)
    right = jnp.concatenate([high, low, high], 0)
    row = lax.broadcasted_iota(jnp.int32, right.shape, 0) & (rows - 1)
    return [
        dot(left, jnp.where(row == i, right, F32(0)).astype(BF16)) for i in range(number)
    ]


def encode(both):
    half, width = both[0].shape
    row = lax.broadcasted_iota(jnp.int32, (half, width), 0)
    lane = lax.broadcasted_iota(jnp.int32, (half, width), 1)
    on = (lane == row) | (lane == row + half)
    diagonal = each(lambda b: jnp.sum(jnp.where(on, b, F32(0)), axis=0, keepdims=True), both)
    root = jnp.sqrt(jnp.maximum(place(diagonal, pad_rows(len(both))), F32(1e-30)))
    exponent = jnp.floor(jnp.log(root) * F32(1 / math.log(2.0)))
    part = jnp.maximum(jnp.ceil((root * jnp.exp2(-exponent) - 1) * 128), F32(0))
    codes = exponent * 256 + part
    scales = scale_of(codes)
    inverse = inverse_outer(scales, len(both))
    value = each(lambda b, p: jnp.round((b * F32(TOP)) * p), both, inverse)
    return each(lambda v: pack(jnp.clip(v, F32(-32767), F32(32767))), value), codes, scales


def spread(values, codes):
    products = outer(scale_of(codes), len(values))
    return each(lambda v, p: v * pack(p * F32(1 / TOP)), values, products)


def to_short(x):
    return x.astype(jnp.int32).astype(jnp.int16)


def from_short(x):
    return x.astype(jnp.int32).astype(F32)


def coded_rows(number, half_rows):
    return number * half_rows + pad_rows(number)


def write_coded(out, values, codes):
    half_rows = values[0].shape[0]
    for i, value in enumerate(values):
        out[i * half_rows : (i + 1) * half_rows, :] = to_short(value)
    out[len(values) * half_rows :, :] = to_short(codes)


def read_coded(ref, number, half_rows):
    codes = from_short(ref[number * half_rows :, :])
    values = [from_short(ref[i * half_rows : (i + 1) * half_rows, :]) for i in range(number)]
    return values, codes


def slot_owner(direct, slot):
    return jnp.bitwise_xor(lax.axis_index("space") & 1, slot) if direct else slot


def gram_kernel(peers, slots, direct, after, *refs):
    pieces, refs = refs[:peers], refs[peers + after :]
    merged, token, grams = refs[0], refs[1], refs[2:]
    token[...] = jnp.zeros_like(token)
    me = lax.axis_index("tm")
    here = pieces[0].shape[1]
    entries = pieces[0].shape[2] // 2
    blocks = here * peers
    per_slot = pieces[0].shape[0] // slots
    stage = None
    if here % 16:
        grams, stage = grams[:-1], grams[-1]
    low = lane_low((blocks, 2 * blocks), blocks)
    for slot in range(slots):
        owner = slot_owner(direct, slot)
        coded = []
        for i in range(per_slot):
            f = owner * per_slot + i
            if stage is None:
                for peer in range(peers):
                    start = pl.multiple_of(jnp.bitwise_xor(me, peer) * here, here)
                    merged[f, pl.ds(start, here), :] = pieces[peer][f]
                z = merged[f]
            else:
                for peer in range(peers):
                    start = pl.multiple_of(jnp.bitwise_xor(me, peer) * here, here)
                    stage[pl.ds(start, here), :] = pieces[peer][f].astype(F32)
                z = stage[...].astype(BF16)
                merged[f] = z
            w = jnp.concatenate([z[:, :entries], z[:, entries:]], 0)
            s = lax.dot_general(w, w, (((1,), (1,)), ((), ())), preferred_element_type=F32)
            s = s * F32(1.0 / blocks)
            top, bottom = s[:blocks], swap(s[blocks:])
            compact = jnp.where(low, top + bottom, top - bottom)
            if direct and slot == 0 and grams[0].dtype == F32:
                grams[0][i] = compact
            elif direct:
                coded.append(double(compact))
            else:
                grams[0][f] = pack(double(compact))
        if coded:
            write_coded(grams[slot], *encode(coded)[:2])


def gram(pieces, slots, direct, in_steps, after):
    peers = len(pieces)
    count, here, width = pieces[0].shape
    blocks = here * peers
    if direct:
        rows = coded_rows(count // slots, blocks // 2)
        shapes = [((rows, 2 * blocks), jnp.int16)] * slots
        if in_steps:
            shapes[0] = ((count // slots, blocks, 2 * blocks), F32)
    else:
        shapes = [((count, blocks // 2, 2 * blocks), F32)]
    out = pl.pallas_call(
        functools.partial(gram_kernel, peers, slots, direct, len(after)),
        in_specs=[whole_spec()] * peers + [any_spec()] * len(after),
        out_specs=[whole_spec()] * (2 + len(shapes)),
        out_shape=[jax.ShapeDtypeStruct((count, blocks, width), BF16), TOKEN]
        + [jax.ShapeDtypeStruct(*s) for s in shapes],
        scratch_shapes=[pltpu.VMEM((blocks, width), F32)] if here % 16 else [],
        compiler_params=params(),
        cost_estimate=light(),
        name="gram",
    )(*pieces, *after)
    return out[0], out[2:], out[1]


def add_kernel(own, other, *refs):
    out, token = refs[-2:]
    token[...] = jnp.zeros_like(token)
    number, blocks, _ = own.shape
    received = spread(*read_coded(other, number, blocks // 2))
    sums = [double(own[i] + unpack(received[i])[0]) for i in range(number)]
    write_coded(out, *encode(sums)[:2])


def add(own, other, after):
    return pl.pallas_call(
        add_kernel,
        in_specs=[whole_spec()] * 2 + [any_spec()] * len(after),
        out_specs=[whole_spec()] * 2,
        out_shape=[jax.ShapeDtypeStruct(other.shape, jnp.int16), TOKEN],
        compiler_params=params(),
        cost_estimate=light(),
        name="add",
    )(own, other, *after)


def split(x):
    high = x.astype(BF16)
    return high, (x - high.astype(F32)).astype(BF16)


def solve_kernel(chunks, half_rows, *refs):
    out, token = refs[-2:]
    token[...] = jnp.zeros_like(token)
    width = out.shape[1]
    half = width // 2
    shape = (half, width)
    row = lax.broadcasted_iota(jnp.int32, shape, 0)
    lane = lax.broadcasted_iota(jnp.int32, shape, 1)
    eye = jnp.where(row == lane, F32(1), F32(0))

    sums, at = [], 0
    for parts, count in chunks:
        ins, at = refs[at : at + parts], at + parts
        if parts == 1:
            sums += [ins[0][i] for i in range(count)]
            continue
        found = [spread(*read_coded(r, count, half_rows)) for r in ins]
        added = each(lambda p, q: p + q, found[0], found[1])
        if parts == 4:
            added = each(lambda p, q, r: p + (q + r), added, found[2], found[3])
        sums += added
    number = len(sums)
    both_halves = each(unpack, sums)
    grams = [h[0] for h in both_halves]
    spots = lax.broadcasted_iota(jnp.int32, sums[0].shape, 1)
    lines = lax.broadcasted_iota(jnp.int32, sums[0].shape, 0)
    on = (spots == lines) | (spots == lines + 3 * half_rows)
    shift = each(
        lambda p: jnp.sum(jnp.where(on, p, F32(0)), keepdims=True) * F32(1.0 / half), sums
    )
    eye_low = jnp.where(row + half == lane, F32(1), F32(0))
    inverse = each(lambda m: 1.0 / m, shift)
    system = each(lambda g, m: g * m + eye, grams, inverse)
    under = each(lambda h, m: h[1] * m + eye_low, both_halves, inverse)
    both = each(
        lambda a, u: jnp.concatenate(split(jnp.concatenate([a, u], 0)), 1), system, under
    )

    def times(v, a):
        wide = dot(v, a)
        return wide[:, :width] + wide[:, width:]


    low_end, high_end = 1.0, float(half + 1)
    mid, radius = (high_end + low_end) / 2, (high_end - low_end) / 2
    ratio = mid / radius
    t = 2 * ratio * ratio - 1
    scale = 2.0 / (radius * radius * t)
    x = each(lambda a: (F32(scale) * (F32(2 * mid) * eye - a)).astype(BF16), system)
    p = each(lambda v, a: eye - times(v, a), x, both)
    x = each(lambda v: v.astype(F32), x)
    for _ in range(3):
        t_next = 2 * t * t - 1
        c = F32(2 * t * t / t_next)
        pf = each(lambda q: full(q).astype(BF16), p)
        xp = each(lambda v, q: jnp.concatenate([v, q], 0).astype(BF16), x, p)
        moved = each(dot, xp, pf)
        x = each(lambda v, m: c * (v + m[:half]), x, moved)
        p = each(lambda m: c * m[half:] - F32(1 / t_next) * eye, moved)
        t = t_next
    for kind in ("scaled", "last"):
        xb = each(lambda v: v.astype(BF16), x)
        xw = each(lambda v: v.astype(F32), xb)
        xf = each(lambda v: full(v).astype(BF16), xw)
        residual = each(lambda v, a: eye - times(v, a), xb, both)
        step = each(lambda r, v: dot(r.astype(BF16), v), residual, xf)
        factor = 1.0 if kind == "last" else 2 * t * t / (2 * t * t - 1)
        x = each(lambda v, m: F32(factor) * (v + m), xw, step)
    values, codes, scales = encode(each(lambda v: double(eye - v), x))
    products = outer(scales, number)
    filters = each(lambda v, p: unpack(v, p * F32(0.5 / TOP)), values, products)
    rounded = each(lambda c: c[0].astype(BF16), filters)
    turned = each(
        lambda c: jnp.concatenate([c[0].astype(BF16), c[1].astype(BF16)], 0), filters
    )
    split_g = each(lambda g: jnp.concatenate(split(g), 0), grams)
    moved = each(dot, split_g, turned)
    moved = each(lambda m: m[:half] + m[half:], moved)
    energy = each(
        lambda c, h: jnp.sum(c.astype(F32) * h, keepdims=True) * F32(half), rounded, moved
    )
    energy = place([jnp.broadcast_to(e, (1, width)) for e in energy], codes.shape[0])
    energy = jnp.maximum(energy, F32(1e-30))
    whole = jnp.floor(jnp.log(energy) * F32(LOG_STEPS / math.log(2.0)))
    rest = jnp.round((energy * jnp.exp2(whole * F32(-1 / LOG_STEPS)) - 1.0) * F32(FINE))
    spot = lax.broadcasted_iota(jnp.int32, codes.shape, 1)
    codes = jnp.where(spot == half, whole, jnp.where(spot == half + 1, rest, codes))
    write_coded(out, values, codes)


def solve(chunks, half_rows, after):
    args = [x for parts, _ in chunks for x in parts]
    width = args[0].shape[-1]
    number = sum(count for _, count in chunks)
    shape = [(len(parts), count) for parts, count in chunks]
    return pl.pallas_call(
        functools.partial(solve_kernel, shape, half_rows),
        in_specs=[whole_spec()] * len(args) + [any_spec()] * len(after),
        out_specs=[whole_spec()] * 2,
        out_shape=[
            jax.ShapeDtypeStruct((coded_rows(number, half_rows), width), jnp.int16),
            TOKEN,
        ],
        compiler_params=params(),
        cost_estimate=light(),
        name="filters",
    )(*args, *after)


def energy_kernel(slots, direct, number, chunks, first, before, last, *refs):
    merged, pieces = refs[:chunks], refs[chunks : chunks + number]
    earlier = refs[chunks + number : chunks + number + 2]
    puts = []
    if last:
        energies_out, filters_out, token, energies, filters = refs[-8:-3]
    else:
        energies, filters, token = refs[-6:-3]
        if before is not None:
            energies_out, filters_out = refs[-8:-6]
    energies_sem, filters_sem, before_sem = refs[-3:]
    if before is not None:
        number_before = earlier[0].shape[0]
        put = pltpu.make_async_copy(
            earlier[0], energies_out.at[pl.ds(before, number_before)], before_sem.at[0]
        )
        put.start()
        puts.append(put)
        for i in range(number_before // 2):
            put = pltpu.make_async_copy(
                earlier[1].at[pl.ds(2 * i, 2)],
                filters_out.at[pl.ds(before + 2 * i, 2)],
                before_sem.at[1 + i],
            )
            put.start()
            puts.append(put)
    own_puts = 0
    token[...] = jnp.zeros_like(token)
    blocks, width = merged[0].shape[1:]
    entries = width // 2
    counts = [m.shape[0] for m in merged]
    per_slot = sum(counts) // slots
    half_rows = blocks // 2
    states = entries * lax.axis_size("space")
    for slot in range(slots):
        owner = slot_owner(direct, slot)
        piece = pieces[slot] if direct else pieces[0].at[slot]
        values, codes = read_coded(piece, per_slot, half_rows)
        whole = codes[:, blocks : blocks + 1]
        rest = codes[:, blocks + 1 : blocks + 2]
        total = jnp.exp2(whole * F32(1 / LOG_STEPS)) * (1.0 + rest * F32(1 / FINE))
        gains = F32(states) / total
        codes = jnp.where(lane_low(codes.shape, blocks), codes, swap(codes))
        products = outer(scale_of(codes), per_slot)
        base = 0
        for chunk, count in enumerate(counts):
            own = count // slots
            size = 4 if own % 4 == 0 else 1
            for begin in range(0, own, size):
                start = sum(counts[:chunk]) + owner * own + begin
                some = range(base + begin, base + begin + size)
                z = [merged[chunk][owner * own + begin + i] for i in range(size)]
                scale = [products[i] * F32(0.5 / TOP) for i in some]
                halves = each(unpack, [values[i] for i in some], scale)
                both = each(
                    lambda h: jnp.concatenate([h[0].astype(BF16), h[1].astype(BF16)], 0), halves
                )
                w = each(lambda v: jnp.concatenate([v[:, :entries], v[:, entries:]], 0), z)
                r = each(dot, both, w)
                gain = [gains[i : i + 1] for i in some]
                energy = each(
                    lambda v, t: jnp.sum(v * v, axis=0, keepdims=True) * t, r, gain
                )
                for i in range(size):
                    filters[start + i, 0] = halves[i][0][:, :blocks]
                    filters[start + i, 1] = -halves[i][1][:, :blocks]
                    energies[pl.ds(start + i, 1), :] = energy[i]
                if last:
                    put = pltpu.make_async_copy(
                        filters.at[pl.ds(start, size)],
                        filters_out.at[pl.ds(first + start, size)],
                        filters_sem.at[own_puts],
                    )
                    put.start()
                    puts.append(put)
                    own_puts += 1
            base += own
    if last:
        put = pltpu.make_async_copy(
            energies, energies_out.at[pl.ds(first, sum(counts))], energies_sem.at[0]
        )
        put.start()
        puts.append(put)
    for put in puts:
        put.wait()


def filtered(merged, pieces, slots, direct, earlier, carry, owned, first, last, after):
    _, blocks, width = merged[0].shape
    count = sum(m.shape[0] for m in merged)
    copies = sum(slots * (m.shape[0] // slots) for m in merged)
    entries = width // 2
    fixed = len(merged) + len(pieces) + (2 if earlier else 0)
    args = [*merged, *pieces, *(earlier[:2] if earlier else ()), *(carry or ()), *after]
    hbm = pl.BlockSpec(memory_space=pltpu.HBM)
    writes = bool(earlier) or last
    own = [
        jax.ShapeDtypeStruct((count, entries), F32),
        jax.ShapeDtypeStruct((count, 2, blocks, blocks), F32),
    ]
    whole = [
        jax.ShapeDtypeStruct((owned, entries), F32),
        jax.ShapeDtypeStruct((owned, 2, blocks, blocks), F32),
    ]
    scratch = [pltpu.VMEM(o.shape, F32) for o in own] if last else []
    out = pl.pallas_call(
        functools.partial(
            energy_kernel, slots, direct, len(pieces), len(merged), first,
            earlier[2] if earlier else None, last,
        ),
        in_specs=[whole_spec()] * fixed
        + ([hbm] * 2 if carry else [])
        + [any_spec()] * len(after),
        out_specs=([hbm] * 2 if writes else [])
        + ([] if last else [whole_spec()] * 2)
        + [whole_spec()],
        out_shape=(whole if writes else []) + ([] if last else own) + [TOKEN],
        input_output_aliases={fixed: 0, fixed + 1: 1} if carry else {},
        scratch_shapes=scratch
        + [
            pltpu.SemaphoreType.DMA((1,)),
            pltpu.SemaphoreType.DMA((copies,)),
            pltpu.SemaphoreType.DMA((1 + owned // 2,)),
        ],
        compiler_params=params(),
        cost_estimate=light(),
        name="energy",
    )(*args)
    carry = list(out[:2]) if writes else None
    earlier = None if last else (*out[-3:-1], first)
    return carry, earlier, out[-1]


def plan(owned, slots):
    if slots != 4 or owned != 64:
        return [owned], (("T", 0), ("G", 0), ("F", 0), ("E", 0))
    return SIZES, ORDER


SIZES = [24, 24, 16]
ORDER = (
    ("T", 0), ("T", 1), ("G", 0), ("A", 0), ("G", 1), ("F", 0), ("A", 1), ("G", 2),
    ("E", 0), ("F", 1), ("F", 2), ("E", 1), ("E", 2),
)


TIES = {("T", 1): (0,)}


def permute(x, axis, offset):
    pairs = [(i, i ^ offset) for i in range(lax.axis_size(axis))]
    return lax.ppermute(x, axis, pairs)


def on_device(snapshots, entry_weight, freq_index):
    peers = lax.axis_size("tm")
    slots = lax.axis_size("space")
    owned = freq_index.shape[0] // peers
    sizes, order = plan(owned, slots)
    starts = [sum(sizes[:c]) for c in range(len(sizes))]
    paired = slots == 4
    halves = 2 if paired else slots
    weight = entry_weight.reshape(1, -1)
    sent, merged, grams, parts, pieces = {}, {}, {}, {}, {}
    carry = None
    earlier = None
    token = []

    def do_transform(c):
        nonlocal token
        joint = [k for k in range(c, len(sizes)) if k == c or c and ("T", k) not in order]
        out, done = transform(
            snapshots, weight, freq_index, peers, [(starts[k], sizes[k]) for k in joint], token
        )
        token = [done]
        for k, own in zip(joint, out):
            sent[k] = [own[0]] + [permute(own[i], "tm", i) for i in range(1, peers)]

    def do_gram(c):
        nonlocal token
        in_steps = paired and ("A", c) in order
        merged[c], grams[c], done = gram(sent[c], halves, paired, in_steps, token)
        token = [done]
        if in_steps:
            grams[c] = [grams[c][0], permute(grams[c][1], "space", 1)]
        elif paired:
            own, other = grams[c]
            parts[c] = [
                own,
                permute(own, "space", 2),
                permute(other, "space", 1),
                permute(other, "space", 3),
            ]
        else:
            parts[c] = [lax.psum_scatter(grams[c][0], "space", scatter_dimension=0, tiled=True)]

    def do_add(c):
        nonlocal token
        half, done = add(*grams[c], token)
        token = [done]
        parts[c] = [half, permute(half, "space", 2)]

    def joined(stage, c):
        last = c + 1
        while last < len(sizes) and (stage, last) not in order:
            last += 1
        return range(c, last)

    def do_solve(c):
        nonlocal token
        work = [(parts[k], sizes[k] // halves) for k in joined("F", c)]
        own, done = solve(work, merged[c].shape[1] // 2, token)
        token = [done]
        if paired:
            pieces[c] = [own, permute(own, "space", 1)]
        else:
            pieces[c] = [lax.all_gather(own, "space", axis=0, tiled=False)]

    def do_energy(c):
        nonlocal token, carry, earlier
        chunks = joined("E", c)
        carry, earlier, done = filtered(
            [merged[k] for k in chunks], pieces[c], halves, paired, earlier, carry, owned,
            starts[c], chunks[-1] == len(sizes) - 1, token,
        )
        token = [done]

    stages = {"T": do_transform, "G": do_gram, "A": do_add, "F": do_solve, "E": do_energy}
    for stage, c in order:
        token = token + [sent[k][1] for k in TIES.get((stage, c), ()) if k in sent]
        stages[stage](c)
    return (carry[0], carry[1])


def solution(mesh):
    in_specs = (P(("grp", "tm"), None, "space"), P(("grp", "space")), P())
    out_specs = (P(("grp", "tm"), "space"), P(("grp", "tm"), None, None, None))
    return jax.shard_map(
        on_device, mesh=mesh, in_specs=in_specs, out_specs=out_specs, check_vma=False
    )
```

```python
import functools
import math

import jax
import jax.numpy as jnp
from jax import lax
from jax.experimental import pallas as pl
from jax.experimental.pallas import tpu as pltpu
from jax.sharding import PartitionSpec as P

F32 = jnp.float32
BF16 = jnp.bfloat16
VMEM_LIMIT = 30 * 1024 * 1024
LANES = 128


def params(**kwargs):
    return pltpu.CompilerParams(vmem_limit_bytes=VMEM_LIMIT, **kwargs)


def whole_spec():
    return pl.BlockSpec(memory_space=pltpu.VMEM)


TOKEN = jax.ShapeDtypeStruct((8, LANES), F32)


def light():
    return pl.CostEstimate(flops=1024, bytes_accessed=1024, transcendentals=0)


def in_hbm(x):
    return pltpu.with_memory_space_constraint(x, pltpu.HBM)


def any_spec():
    return pl.BlockSpec(memory_space=pl.ANY)


def dot(a, b):
    return lax.dot_general(a, b, (((1,), (0,)), ((), ())), preferred_element_type=F32)


def cos_sin(phase, length):
    quarter = length // 4
    eighth = length // 8
    shifted = phase + eighth
    low = (shifted & (quarter - 1)) - eighth
    quadrant = (shifted // quarter) & 3
    x = low.astype(F32) * F32(2.0 * math.pi / length)
    x2 = x * x
    cos = F32(1 / 40320)
    for c in (-1 / 720, 1 / 24, -0.5, 1.0):
        cos = cos * x2 + F32(c)
    sin = F32(1 / 362880)
    for c in (-1 / 5040, 1 / 120, -1 / 6, 1.0):
        sin = sin * x2 + F32(c)
    sin = sin * x
    odd = (quadrant & 1) == 1
    c0 = jnp.where(odd, sin, cos)
    s0 = jnp.where(odd, cos, sin)
    c1 = jnp.where((quadrant == 1) | (quadrant == 2), -c0, c0)
    s1 = jnp.where(quadrant >= 2, -s0, s0)
    return c1, s1


def transform_kernel(peers, parts, group, *refs):
    freq_hbm, weight_hbm, snap_hbm = refs[:3]
    outs, token = refs[-peers * len(parts) - 8 : -8], refs[-8]
    freq, weight, snap, table, wide, small_sem, snap_sem = refs[-7:]
    blocks, length, entries = snap.shape
    steps = blocks // group
    get_freq = pltpu.make_async_copy(freq_hbm, freq, small_sem.at[0])
    get_weight = pltpu.make_async_copy(weight_hbm, weight, small_sem.at[1])
    get_snap = [
        pltpu.make_async_copy(
            snap_hbm.at[pl.ds(i * group, group)], snap.at[pl.ds(i * group, group)], snap_sem.at[i]
        )
        for i in range(steps)
    ]
    token[...] = jnp.zeros_like(token)
    get_freq.start()
    for get in get_snap:
        get.start()
    get_weight.start()

    me = lax.axis_index("tm")
    groups = [
        (peer, first + j)
        for first, count in parts
        for peer in range(peers)
        for j in range(0, count, 8)
    ]
    rows = 8 * len(groups)
    per_peer = freq.shape[0] // peers
    times = lax.broadcasted_iota(jnp.int32, (8, length), 1)
    sub = lax.broadcasted_iota(jnp.int32, (8, length), 0)
    window = 0.5 - 0.5 * cos_sin(times, length)[0]
    scaled = window / F32(math.sqrt(0.375 * length))
    get_freq.wait()

    def eight(index):
        peer, offset = groups[index]
        start = jnp.bitwise_xor(me, peer) * per_peer + offset
        k = jnp.zeros((8, length), jnp.int32)
        for i in range(8):
            k = jnp.where(sub == i, freq[start + i], k)
        cos, sin = cos_sin((k * times) & (length - 1), length)
        return scaled * cos, -(scaled * sin)

    for pair in range(rows // 16):
        re0, im0 = eight(2 * pair)
        re1, im1 = eight(2 * pair + 1)
        table[16 * pair : 16 * pair + 16, :] = jnp.concatenate([re0, re1], 0).astype(BF16)
        table[rows + 16 * pair : rows + 16 * pair + 16, :] = jnp.concatenate(
            [im0, im1], 0
        ).astype(BF16)

    get_weight.wait()
    root = jnp.sqrt(weight[...])
    tiles = entries // LANES
    for step in range(steps):
        get_snap[step].wait()
        for b in range(step * group, (step + 1) * group):
            spec = dot(table[...], snap[b]) * root
            for tile in range(tiles):
                lanes = slice(tile * LANES, (tile + 1) * LANES)
                wide[tile, pl.ds(b, rows, stride=blocks), :] = spec[:rows, lanes]
                wide[tiles + tile, pl.ds(b, rows, stride=blocks), :] = spec[rows:, lanes]
    at = 0
    for out in outs:
        for j in range(out.shape[0]):
            for tile in range(2 * tiles):
                lanes = slice(tile * LANES, (tile + 1) * LANES)
                out[j, :, lanes] = wide[tile, at : at + blocks, :].astype(BF16)
            at += blocks


def transform(snapshots, weight, freq_index, peers, parts, after):
    blocks, length, entries = snapshots.shape
    group = min(blocks, 4)
    total = peers * sum(count for _, count in parts)
    shapes = [
        jax.ShapeDtypeStruct((count, blocks, 2 * entries), BF16)
        for _, count in parts
        for _ in range(peers)
    ]
    hbm = pl.BlockSpec(memory_space=pltpu.HBM)
    out = pl.pallas_call(
        functools.partial(transform_kernel, peers, parts, group),
        in_specs=[hbm] * 3 + [any_spec()] * len(after),
        out_specs=[whole_spec()] * (len(shapes) + 1),
        out_shape=shapes + [TOKEN],
        scratch_shapes=[
            pltpu.SMEM(freq_index.shape, jnp.int32),
            pltpu.VMEM(weight.shape, F32),
            pltpu.VMEM(snapshots.shape, BF16),
            pltpu.VMEM((2 * total, length), BF16),
            pltpu.VMEM((2 * entries // LANES, total * blocks, LANES), F32),
            pltpu.SemaphoreType.DMA((2,)),
            pltpu.SemaphoreType.DMA((blocks // group,)),
        ],
        compiler_params=params(),
        cost_estimate=light(),
        name="transform",
    )(in_hbm(freq_index), in_hbm(weight), in_hbm(snapshots), *after)
    return [out[i * peers : (i + 1) * peers] for i in range(len(parts))], out[-1]


def lane_low(shape, half):
    return lax.broadcasted_iota(jnp.int32, shape, 1) < half


def swap(x):
    return pltpu.roll(x, x.shape[1] // 2, 1)


def each(fn, *lists):
    return [fn(*items) for items in zip(*lists)]


def double(compact):
    return compact + swap(compact)


def pack(both):
    half = both.shape[0]
    low = lane_low((half // 2, 2 * half), half)
    return jnp.where(low, both[: half // 2], both[half // 2 :])


def unpack(packed, scale=None):
    rows, half = packed.shape[0], packed.shape[1] // 2
    low = lane_low(packed.shape, half)
    other = swap(packed)
    both = jnp.concatenate(
        [jnp.where(low, packed, other), jnp.where(low, other, packed)], 0
    )
    turned = jnp.transpose(jnp.concatenate([packed, packed], 0))
    turned = jnp.where(lane_low((half, half), rows), turned[:half], turned[half:])
    turned = jnp.concatenate([turned, turned], 1)
    low = lane_low(both.shape, half)
    total = both + turned
    apart = both - turned
    top = jnp.where(low, total, apart)
    bottom = jnp.where(low, -apart, total)
    scale = F32(0.5) if scale is None else scale
    return scale * top, scale * bottom


def full(compact):
    half = compact.shape[0]
    turned = swap(compact)
    low = lane_low(compact.shape, half)
    return jnp.concatenate([compact, jnp.where(low, -turned, turned)], 0)


TOP = 23169.0
LOG_STEPS = 64.0
FINE = float(2**21)


def place(lines, rows):
    shape = (rows, lines[0].shape[1])
    row = lax.broadcasted_iota(jnp.int32, shape, 0)
    out = jnp.zeros(shape, F32)
    for i, line in enumerate(lines):
        out = jnp.where(row == i, line, out)
    return out


def pad_rows(number):
    return -(-number // 16) * 16


def scale_of(code):
    exponent = jnp.floor(code * F32(1 / 256))
    part = code - exponent * 256
    return (jnp.exp2(exponent) * (1 + part * F32(1 / 128))).astype(BF16)


def outer(scales, number):
    half = scales.shape[1] // 2
    wide = scales.astype(F32)
    row = lax.broadcasted_iota(jnp.int32, scales.shape, 0)
    turned = jnp.transpose(wide)[:half].astype(BF16)
    return [
        dot(turned, jnp.where(row == i, wide, F32(0)).astype(BF16)) for i in range(number)
    ]


def inverse_outer(scales, number):
    half = scales.shape[1] // 2
    rows = scales.shape[0]
    inverse = 1.0 / scales.astype(F32)
    high = inverse.astype(BF16).astype(F32)
    low = inverse - high
    left = jnp.transpose(jnp.concatenate([high, high, low], 0))[:half].astype(BF16)
    right = jnp.concatenate([high, low, high], 0)
    row = lax.broadcasted_iota(jnp.int32, right.shape, 0) & (rows - 1)
    return [
        dot(left, jnp.where(row == i, right, F32(0)).astype(BF16)) for i in range(number)
    ]


def encode(both):
    half, width = both[0].shape
    row = lax.broadcasted_iota(jnp.int32, (half, width), 0)
    lane = lax.broadcasted_iota(jnp.int32, (half, width), 1)
    on = (lane == row) | (lane == row + half)
    diagonal = each(lambda b: jnp.sum(jnp.where(on, b, F32(0)), axis=0, keepdims=True), both)
    root = jnp.sqrt(jnp.maximum(place(diagonal, pad_rows(len(both))), F32(1e-30)))
    exponent = jnp.floor(jnp.log(root) * F32(1 / math.log(2.0)))
    part = jnp.maximum(jnp.ceil((root * jnp.exp2(-exponent) - 1) * 128), F32(0))
    codes = exponent * 256 + part
    scales = scale_of(codes)
    inverse = inverse_outer(scales, len(both))
    value = each(lambda b, p: jnp.round((b * F32(TOP)) * p), both, inverse)
    return each(lambda v: pack(jnp.clip(v, F32(-32767), F32(32767))), value), codes, scales


def spread(values, codes):
    products = outer(scale_of(codes), len(values))
    return each(lambda v, p: v * pack(p * F32(1 / TOP)), values, products)


def to_short(x):
    return x.astype(jnp.int32).astype(jnp.int16)


def from_short(x):
    return x.astype(jnp.int32).astype(F32)


def coded_rows(number, half_rows):
    return number * half_rows + pad_rows(number)


def write_coded(out, values, codes):
    half_rows = values[0].shape[0]
    for i, value in enumerate(values):
        out[i * half_rows : (i + 1) * half_rows, :] = to_short(value)
    out[len(values) * half_rows :, :] = to_short(codes)


def read_coded(ref, number, half_rows):
    codes = from_short(ref[number * half_rows :, :])
    values = [from_short(ref[i * half_rows : (i + 1) * half_rows, :]) for i in range(number)]
    return values, codes


def slot_owner(direct, slot):
    return jnp.bitwise_xor(lax.axis_index("space") & 1, slot) if direct else slot


def gram_kernel(peers, slots, direct, after, *refs):
    pieces, refs = refs[:peers], refs[peers + after :]
    merged, token, grams = refs[0], refs[1], refs[2:]
    token[...] = jnp.zeros_like(token)
    me = lax.axis_index("tm")
    here = pieces[0].shape[1]
    entries = pieces[0].shape[2] // 2
    blocks = here * peers
    per_slot = pieces[0].shape[0] // slots
    stage = None
    if here % 16:
        grams, stage = grams[:-1], grams[-1]
    low = lane_low((blocks, 2 * blocks), blocks)
    for slot in range(slots):
        owner = slot_owner(direct, slot)
        coded = []
        for i in range(per_slot):
            f = owner * per_slot + i
            if stage is None:
                for peer in range(peers):
                    start = pl.multiple_of(jnp.bitwise_xor(me, peer) * here, here)
                    merged[f, pl.ds(start, here), :] = pieces[peer][f]
                z = merged[f]
            else:
                for peer in range(peers):
                    start = pl.multiple_of(jnp.bitwise_xor(me, peer) * here, here)
                    stage[pl.ds(start, here), :] = pieces[peer][f].astype(F32)
                z = stage[...].astype(BF16)
                merged[f] = z
            w = jnp.concatenate([z[:, :entries], z[:, entries:]], 0)
            s = lax.dot_general(w, w, (((1,), (1,)), ((), ())), preferred_element_type=F32)
            s = s * F32(1.0 / blocks)
            top, bottom = s[:blocks], swap(s[blocks:])
            compact = jnp.where(low, top + bottom, top - bottom)
            if direct and slot == 0 and grams[0].dtype == F32:
                grams[0][i] = compact
            elif direct:
                coded.append(double(compact))
            else:
                grams[0][f] = pack(double(compact))
        if coded:
            write_coded(grams[slot], *encode(coded)[:2])


def gram(pieces, slots, direct, in_steps, after):
    peers = len(pieces)
    count, here, width = pieces[0].shape
    blocks = here * peers
    if direct:
        rows = coded_rows(count // slots, blocks // 2)
        shapes = [((rows, 2 * blocks), jnp.int16)] * slots
        if in_steps:
            shapes[0] = ((count // slots, blocks, 2 * blocks), F32)
    else:
        shapes = [((count, blocks // 2, 2 * blocks), F32)]
    out = pl.pallas_call(
        functools.partial(gram_kernel, peers, slots, direct, len(after)),
        in_specs=[whole_spec()] * peers + [any_spec()] * len(after),
        out_specs=[whole_spec()] * (2 + len(shapes)),
        out_shape=[jax.ShapeDtypeStruct((count, blocks, width), BF16), TOKEN]
        + [jax.ShapeDtypeStruct(*s) for s in shapes],
        scratch_shapes=[pltpu.VMEM((blocks, width), F32)] if here % 16 else [],
        compiler_params=params(),
        cost_estimate=light(),
        name="gram",
    )(*pieces, *after)
    return out[0], out[2:], out[1]


def add_kernel(own, other, *refs):
    out, token = refs[-2:]
    token[...] = jnp.zeros_like(token)
    number, blocks, _ = own.shape
    received = spread(*read_coded(other, number, blocks // 2))
    sums = [double(own[i] + unpack(received[i])[0]) for i in range(number)]
    write_coded(out, *encode(sums)[:2])


def add(own, other, after):
    return pl.pallas_call(
        add_kernel,
        in_specs=[whole_spec()] * 2 + [any_spec()] * len(after),
        out_specs=[whole_spec()] * 2,
        out_shape=[jax.ShapeDtypeStruct(other.shape, jnp.int16), TOKEN],
        compiler_params=params(),
        cost_estimate=light(),
        name="add",
    )(own, other, *after)


def split(x):
    high = x.astype(BF16)
    return high, (x - high.astype(F32)).astype(BF16)


def solve_kernel(chunks, half_rows, *refs):
    out, token = refs[-2:]
    token[...] = jnp.zeros_like(token)
    width = out.shape[1]
    half = width // 2
    shape = (half, width)
    row = lax.broadcasted_iota(jnp.int32, shape, 0)
    lane = lax.broadcasted_iota(jnp.int32, shape, 1)
    eye = jnp.where(row == lane, F32(1), F32(0))

    sums, at = [], 0
    for parts, count in chunks:
        ins, at = refs[at : at + parts], at + parts
        if parts == 1:
            sums += [ins[0][i] for i in range(count)]
            continue
        found = [spread(*read_coded(r, count, half_rows)) for r in ins]
        added = each(lambda p, q: p + q, found[0], found[1])
        if parts == 4:
            added = each(lambda p, q, r: p + (q + r), added, found[2], found[3])
        sums += added
    number = len(sums)
    both_halves = each(unpack, sums)
    grams = [h[0] for h in both_halves]
    spots = lax.broadcasted_iota(jnp.int32, sums[0].shape, 1)
    lines = lax.broadcasted_iota(jnp.int32, sums[0].shape, 0)
    on = (spots == lines) | (spots == lines + 3 * half_rows)
    shift = each(
        lambda p: jnp.sum(jnp.where(on, p, F32(0)), keepdims=True) * F32(1.0 / half), sums
    )
    eye_low = jnp.where(row + half == lane, F32(1), F32(0))
    inverse = each(lambda m: 1.0 / m, shift)
    system = each(lambda g, m: g * m + eye, grams, inverse)
    under = each(lambda h, m: h[1] * m + eye_low, both_halves, inverse)
    both = each(
        lambda a, u: jnp.concatenate(split(jnp.concatenate([a, u], 0)), 1), system, under
    )

    def times(v, a):
        wide = dot(v, a)
        return wide[:, :width] + wide[:, width:]


    low_end, high_end = 1.0, float(half + 1)
    mid, radius = (high_end + low_end) / 2, (high_end - low_end) / 2
    ratio = mid / radius
    t = 2 * ratio * ratio - 1
    scale = 2.0 / (radius * radius * t)
    x = each(lambda a: (F32(scale) * (F32(2 * mid) * eye - a)).astype(BF16), system)
    p = each(lambda v, a: eye - times(v, a), x, both)
    x = each(lambda v: v.astype(F32), x)
    for _ in range(3):
        t_next = 2 * t * t - 1
        c = F32(2 * t * t / t_next)
        pf = each(lambda q: full(q).astype(BF16), p)
        xp = each(lambda v, q: jnp.concatenate([v, q], 0).astype(BF16), x, p)
        moved = each(dot, xp, pf)
        x = each(lambda v, m: c * (v + m[:half]), x, moved)
        p = each(lambda m: c * m[half:] - F32(1 / t_next) * eye, moved)
        t = t_next
    for kind in ("scaled", "last"):
        xb = each(lambda v: v.astype(BF16), x)
        xw = each(lambda v: v.astype(F32), xb)
        xf = each(lambda v: full(v).astype(BF16), xw)
        residual = each(lambda v, a: eye - times(v, a), xb, both)
        step = each(lambda r, v: dot(r.astype(BF16), v), residual, xf)
        factor = 1.0 if kind == "last" else 2 * t * t / (2 * t * t - 1)
        x = each(lambda v, m: F32(factor) * (v + m), xw, step)
    values, codes, scales = encode(each(lambda v: double(eye - v), x))
    products = outer(scales, number)
    filters = each(lambda v, p: unpack(v, p * F32(0.5 / TOP)), values, products)
    rounded = each(lambda c: c[0].astype(BF16), filters)
    turned = each(
        lambda c: jnp.concatenate([c[0].astype(BF16), c[1].astype(BF16)], 0), filters
    )
    split_g = each(lambda g: jnp.concatenate(split(g), 0), grams)
    moved = each(dot, split_g, turned)
    moved = each(lambda m: m[:half] + m[half:], moved)
    energy = each(
        lambda c, h: jnp.sum(c.astype(F32) * h, keepdims=True) * F32(half), rounded, moved
    )
    energy = place([jnp.broadcast_to(e, (1, width)) for e in energy], codes.shape[0])
    energy = jnp.maximum(energy, F32(1e-30))
    whole = jnp.floor(jnp.log(energy) * F32(LOG_STEPS / math.log(2.0)))
    rest = jnp.round((energy * jnp.exp2(whole * F32(-1 / LOG_STEPS)) - 1.0) * F32(FINE))
    spot = lax.broadcasted_iota(jnp.int32, codes.shape, 1)
    codes = jnp.where(spot == half, whole, jnp.where(spot == half + 1, rest, codes))
    write_coded(out, values, codes)


def solve(chunks, half_rows, after):
    args = [x for parts, _ in chunks for x in parts]
    width = args[0].shape[-1]
    number = sum(count for _, count in chunks)
    shape = [(len(parts), count) for parts, count in chunks]
    return pl.pallas_call(
        functools.partial(solve_kernel, shape, half_rows),
        in_specs=[whole_spec()] * len(args) + [any_spec()] * len(after),
        out_specs=[whole_spec()] * 2,
        out_shape=[
            jax.ShapeDtypeStruct((coded_rows(number, half_rows), width), jnp.int16),
            TOKEN,
        ],
        compiler_params=params(),
        cost_estimate=light(),
        name="filters",
    )(*args, *after)


def energy_kernel(slots, direct, number, chunks, first, *refs):
    merged, pieces = refs[:chunks], refs[chunks : chunks + number]
    energies_out, filters_out, token, energies, filters, energies_sem, filters_sem = refs[-7:]
    token[...] = jnp.zeros_like(token)
    blocks, width = merged[0].shape[1:]
    entries = width // 2
    counts = [m.shape[0] for m in merged]
    per_slot = sum(counts) // slots
    half_rows = blocks // 2
    states = entries * lax.axis_size("space")
    puts = []
    for slot in range(slots):
        owner = slot_owner(direct, slot)
        piece = pieces[slot] if direct else pieces[0].at[slot]
        values, codes = read_coded(piece, per_slot, half_rows)
        whole = codes[:, blocks : blocks + 1]
        rest = codes[:, blocks + 1 : blocks + 2]
        total = jnp.exp2(whole * F32(1 / LOG_STEPS)) * (1.0 + rest * F32(1 / FINE))
        gains = F32(states) / total
        codes = jnp.where(lane_low(codes.shape, blocks), codes, swap(codes))
        products = outer(scale_of(codes), per_slot)
        base = 0
        for chunk, count in enumerate(counts):
            own = count // slots
            size = 4 if own % 4 == 0 else 1
            for begin in range(0, own, size):
                start = sum(counts[:chunk]) + owner * own + begin
                some = range(base + begin, base + begin + size)
                z = [merged[chunk][owner * own + begin + i] for i in range(size)]
                scale = [products[i] * F32(0.5 / TOP) for i in some]
                halves = each(unpack, [values[i] for i in some], scale)
                both = each(
                    lambda h: jnp.concatenate([h[0].astype(BF16), h[1].astype(BF16)], 0), halves
                )
                w = each(lambda v: jnp.concatenate([v[:, :entries], v[:, entries:]], 0), z)
                r = each(dot, both, w)
                gain = [gains[i : i + 1] for i in some]
                energy = each(
                    lambda v, t: jnp.sum(v * v, axis=0, keepdims=True) * t, r, gain
                )
                for i in range(size):
                    filters[start + i, 0] = halves[i][0][:, :blocks]
                    filters[start + i, 1] = -halves[i][1][:, :blocks]
                    energies[pl.ds(start + i, 1), :] = energy[i]
                put = pltpu.make_async_copy(
                    filters.at[pl.ds(start, size)],
                    filters_out.at[pl.ds(first + start, size)],
                    filters_sem.at[len(puts)],
                )
                put.start()
                puts.append(put)
            base += own
    put = pltpu.make_async_copy(
        energies, energies_out.at[pl.ds(first, sum(counts))], energies_sem.at[0]
    )
    put.start()
    for p in [*puts, put]:
        p.wait()


def filtered(merged, pieces, slots, direct, carry, owned, first, after):
    _, blocks, width = merged[0].shape
    count = sum(m.shape[0] for m in merged)
    copies = sum(slots * (m.shape[0] // slots) for m in merged)
    entries = width // 2
    fixed = len(merged) + len(pieces)
    args = [*merged, *pieces] + ([] if carry is None else list(carry)) + list(after)
    hbm = pl.BlockSpec(memory_space=pltpu.HBM)
    return pl.pallas_call(
        functools.partial(energy_kernel, slots, direct, len(pieces), len(merged), first),
        in_specs=[whole_spec()] * fixed
        + ([] if carry is None else [hbm] * 2)
        + [any_spec()] * len(after),
        out_specs=[hbm] * 2 + [whole_spec()],
        out_shape=[
            jax.ShapeDtypeStruct((owned, entries), F32),
            jax.ShapeDtypeStruct((owned, 2, blocks, blocks), F32),
            TOKEN,
        ],
        input_output_aliases={} if carry is None else {fixed: 0, fixed + 1: 1},
        scratch_shapes=[
            pltpu.VMEM((count, entries), F32),
            pltpu.VMEM((count, 2, blocks, blocks), F32),
            pltpu.SemaphoreType.DMA((1,)),
            pltpu.SemaphoreType.DMA((copies,)),
        ],
        compiler_params=params(),
        cost_estimate=light(),
        name="energy",
    )(*args)


def exchange(arrays, axis):
    size = lax.axis_size(axis)
    got = [arrays[0]]
    for offset in range(1, size):
        pairs = [(i, i ^ offset) for i in range(size)]
        got.append(lax.ppermute(arrays[offset], axis, pairs))
    return got


def plan(owned, slots):
    if slots != 4 or owned != 64:
        return [owned], (("T", 0), ("G", 0), ("F", 0), ("E", 0))
    return SIZES, ORDER


SIZES = [24, 24, 16]
ORDER = (
    ("T", 0), ("T", 1), ("G", 0), ("F", 0), ("G", 1), ("E", 0), ("A", 1), ("G", 2),
    ("F", 1), ("F", 2), ("E", 1), ("E", 2),
)


TIES = {("T", 1): (0,)}


def permute(x, axis, offset):
    pairs = [(i, i ^ offset) for i in range(lax.axis_size(axis))]
    return lax.ppermute(x, axis, pairs)


def on_device(snapshots, entry_weight, freq_index):
    peers = lax.axis_size("tm")
    slots = lax.axis_size("space")
    owned = freq_index.shape[0] // peers
    sizes, order = plan(owned, slots)
    starts = [sum(sizes[:c]) for c in range(len(sizes))]
    paired = slots == 4
    halves = 2 if paired else slots
    weight = entry_weight.reshape(1, -1)
    sent, merged, grams, parts, pieces = {}, {}, {}, {}, {}
    carry = None
    token = []

    def do_transform(c):
        nonlocal token
        joint = [k for k in range(c, len(sizes)) if k == c or c and ("T", k) not in order]
        out, done = transform(
            snapshots, weight, freq_index, peers, [(starts[k], sizes[k]) for k in joint], token
        )
        token = [done]
        for k, own in zip(joint, out):
            sent[k] = [own[0]] + [permute(own[i], "tm", i) for i in range(1, peers)]

    def do_gram(c):
        nonlocal token
        in_steps = paired and ("A", c) in order
        merged[c], grams[c], done = gram(sent[c], halves, paired, in_steps, token)
        token = [done]
        if in_steps:
            grams[c] = [grams[c][0], permute(grams[c][1], "space", 1)]
        elif paired:
            own, other = grams[c]
            parts[c] = [
                own,
                permute(own, "space", 2),
                permute(other, "space", 1),
                permute(other, "space", 3),
            ]
        else:
            parts[c] = [lax.psum_scatter(grams[c][0], "space", scatter_dimension=0, tiled=True)]

    def do_add(c):
        nonlocal token
        half, done = add(*grams[c], token)
        token = [done]
        parts[c] = [half, permute(half, "space", 2)]

    def joined(stage, c):
        last = c + 1
        while last < len(sizes) and (stage, last) not in order:
            last += 1
        return range(c, last)

    def do_solve(c):
        nonlocal token
        work = [(parts[k], sizes[k] // halves) for k in joined("F", c)]
        own, done = solve(work, merged[c].shape[1] // 2, token)
        token = [done]
        if paired:
            pieces[c] = [own, permute(own, "space", 1)]
        else:
            pieces[c] = [lax.all_gather(own, "space", axis=0, tiled=False)]

    def do_energy(c):
        nonlocal token, carry
        work = [merged[k] for k in joined("E", c)]
        *carry, done = filtered(
            work, pieces[c], halves, paired, carry, owned, starts[c], token
        )
        token = [done]

    stages = {"T": do_transform, "G": do_gram, "A": do_add, "F": do_solve, "E": do_energy}
    for stage, c in order:
        token = token + [sent[k][1] for k in TIES.get((stage, c), ()) if k in sent]
        stages[stage](c)
    return (carry[0], carry[1])


def solution(mesh):
    in_specs = (P(("grp", "tm"), None, "space"), P(("grp", "space")), P())
    out_specs = (P(("grp", "tm"), "space"), P(("grp", "tm"), None, None, None))
    return jax.shard_map(
        on_device, mesh=mesh, in_specs=in_specs, out_specs=out_specs, check_vma=False
    )
```

```python
import functools
import math

import jax
import jax.numpy as jnp
from jax import lax
from jax.experimental import pallas as pl
from jax.experimental.pallas import tpu as pltpu
from jax.sharding import PartitionSpec as P

F32 = jnp.float32
BF16 = jnp.bfloat16
VMEM_LIMIT = 30 * 1024 * 1024
LANES = 128


def params(**kwargs):
    return pltpu.CompilerParams(vmem_limit_bytes=VMEM_LIMIT, **kwargs)


def whole_spec():
    return pl.BlockSpec(memory_space=pltpu.VMEM)


TOKEN = jax.ShapeDtypeStruct((8, LANES), F32)


def light():
    return pl.CostEstimate(flops=1024, bytes_accessed=1024, transcendentals=0)


def in_hbm(x):
    return pltpu.with_memory_space_constraint(x, pltpu.HBM)


def any_spec():
    return pl.BlockSpec(memory_space=pl.ANY)


def dot(a, b):
    return lax.dot_general(a, b, (((1,), (0,)), ((), ())), preferred_element_type=F32)


def cos_sin(phase, length):
    quarter = length // 4
    eighth = length // 8
    shifted = phase + eighth
    low = (shifted & (quarter - 1)) - eighth
    quadrant = (shifted // quarter) & 3
    x = low.astype(F32) * F32(2.0 * math.pi / length)
    x2 = x * x
    cos = F32(1 / 40320)
    for c in (-1 / 720, 1 / 24, -0.5, 1.0):
        cos = cos * x2 + F32(c)
    sin = F32(1 / 362880)
    for c in (-1 / 5040, 1 / 120, -1 / 6, 1.0):
        sin = sin * x2 + F32(c)
    sin = sin * x
    odd = (quadrant & 1) == 1
    c0 = jnp.where(odd, sin, cos)
    s0 = jnp.where(odd, cos, sin)
    c1 = jnp.where((quadrant == 1) | (quadrant == 2), -c0, c0)
    s1 = jnp.where(quadrant >= 2, -s0, s0)
    return c1, s1


def transform_kernel(peers, parts, group, *refs):
    freq_hbm, weight_hbm, snap_hbm = refs[:3]
    outs, token = refs[-peers * len(parts) - 8 : -8], refs[-8]
    freq, weight, snap, table, wide, small_sem, snap_sem = refs[-7:]
    blocks, length, entries = snap.shape
    steps = blocks // group
    get_freq = pltpu.make_async_copy(freq_hbm, freq, small_sem.at[0])
    get_weight = pltpu.make_async_copy(weight_hbm, weight, small_sem.at[1])
    get_snap = [
        pltpu.make_async_copy(
            snap_hbm.at[pl.ds(i * group, group)], snap.at[pl.ds(i * group, group)], snap_sem.at[i]
        )
        for i in range(steps)
    ]
    token[...] = jnp.zeros_like(token)
    get_freq.start()
    for get in get_snap:
        get.start()
    get_weight.start()

    me = lax.axis_index("tm")
    groups = [
        (peer, first + j)
        for first, count in parts
        for peer in range(peers)
        for j in range(0, count, 8)
    ]
    rows = 8 * len(groups)
    per_peer = freq.shape[0] // peers
    times = lax.broadcasted_iota(jnp.int32, (8, length), 1)
    sub = lax.broadcasted_iota(jnp.int32, (8, length), 0)
    window = 0.5 - 0.5 * cos_sin(times, length)[0]
    scaled = window / F32(math.sqrt(0.375 * length))
    get_freq.wait()

    def eight(index):
        peer, offset = groups[index]
        start = jnp.bitwise_xor(me, peer) * per_peer + offset
        k = jnp.zeros((8, length), jnp.int32)
        for i in range(8):
            k = jnp.where(sub == i, freq[start + i], k)
        cos, sin = cos_sin((k * times) & (length - 1), length)
        return scaled * cos, -(scaled * sin)

    for pair in range(rows // 16):
        re0, im0 = eight(2 * pair)
        re1, im1 = eight(2 * pair + 1)
        table[16 * pair : 16 * pair + 16, :] = jnp.concatenate([re0, re1], 0).astype(BF16)
        table[rows + 16 * pair : rows + 16 * pair + 16, :] = jnp.concatenate(
            [im0, im1], 0
        ).astype(BF16)

    get_weight.wait()
    root = jnp.sqrt(weight[...])
    tiles = entries // LANES
    for step in range(steps):
        get_snap[step].wait()
        for b in range(step * group, (step + 1) * group):
            spec = dot(table[...], snap[b]) * root
            for tile in range(tiles):
                lanes = slice(tile * LANES, (tile + 1) * LANES)
                wide[tile, pl.ds(b, rows, stride=blocks), :] = spec[:rows, lanes]
                wide[tiles + tile, pl.ds(b, rows, stride=blocks), :] = spec[rows:, lanes]
    at = 0
    for out in outs:
        for j in range(out.shape[0]):
            for tile in range(2 * tiles):
                lanes = slice(tile * LANES, (tile + 1) * LANES)
                out[j, :, lanes] = wide[tile, at : at + blocks, :].astype(BF16)
            at += blocks


def transform(snapshots, weight, freq_index, peers, parts, after):
    blocks, length, entries = snapshots.shape
    group = min(blocks, 4)
    total = peers * sum(count for _, count in parts)
    shapes = [
        jax.ShapeDtypeStruct((count, blocks, 2 * entries), BF16)
        for _, count in parts
        for _ in range(peers)
    ]
    hbm = pl.BlockSpec(memory_space=pltpu.HBM)
    out = pl.pallas_call(
        functools.partial(transform_kernel, peers, parts, group),
        in_specs=[hbm] * 3 + [any_spec()] * len(after),
        out_specs=[whole_spec()] * (len(shapes) + 1),
        out_shape=shapes + [TOKEN],
        scratch_shapes=[
            pltpu.SMEM(freq_index.shape, jnp.int32),
            pltpu.VMEM(weight.shape, F32),
            pltpu.VMEM(snapshots.shape, BF16),
            pltpu.VMEM((2 * total, length), BF16),
            pltpu.VMEM((2 * entries // LANES, total * blocks, LANES), F32),
            pltpu.SemaphoreType.DMA((2,)),
            pltpu.SemaphoreType.DMA((blocks // group,)),
        ],
        compiler_params=params(),
        cost_estimate=light(),
        name="transform",
    )(in_hbm(freq_index), in_hbm(weight), in_hbm(snapshots), *after)
    return [out[i * peers : (i + 1) * peers] for i in range(len(parts))], out[-1]


def lane_low(shape, half):
    return lax.broadcasted_iota(jnp.int32, shape, 1) < half


def swap(x):
    return pltpu.roll(x, x.shape[1] // 2, 1)


def each(fn, *lists):
    return [fn(*items) for items in zip(*lists)]


def double(compact):
    return compact + swap(compact)


def pack(both):
    half = both.shape[0]
    low = lane_low((half // 2, 2 * half), half)
    return jnp.where(low, both[: half // 2], both[half // 2 :])


def unpack(packed, scale=None):
    rows, half = packed.shape[0], packed.shape[1] // 2
    low = lane_low(packed.shape, half)
    other = swap(packed)
    both = jnp.concatenate(
        [jnp.where(low, packed, other), jnp.where(low, other, packed)], 0
    )
    turned = jnp.transpose(jnp.concatenate([packed, packed], 0))
    turned = jnp.where(lane_low((half, half), rows), turned[:half], turned[half:])
    turned = jnp.concatenate([turned, turned], 1)
    low = lane_low(both.shape, half)
    total = both + turned
    apart = both - turned
    top = jnp.where(low, total, apart)
    bottom = jnp.where(low, -apart, total)
    scale = F32(0.5) if scale is None else scale
    return scale * top, scale * bottom


def full(compact):
    half = compact.shape[0]
    turned = swap(compact)
    low = lane_low(compact.shape, half)
    return jnp.concatenate([compact, jnp.where(low, -turned, turned)], 0)


TOP = 23169.0
LOG_STEPS = 64.0
FINE = float(2**21)


def place(lines, rows):
    shape = (rows, lines[0].shape[1])
    row = lax.broadcasted_iota(jnp.int32, shape, 0)
    out = jnp.zeros(shape, F32)
    for i, line in enumerate(lines):
        out = jnp.where(row == i, line, out)
    return out


def pad_rows(number):
    return -(-number // 16) * 16


def scale_of(code):
    exponent = jnp.floor(code * F32(1 / 256))
    part = code - exponent * 256
    return (jnp.exp2(exponent) * (1 + part * F32(1 / 128))).astype(BF16)


def outer(scales, number):
    half = scales.shape[1] // 2
    wide = scales.astype(F32)
    row = lax.broadcasted_iota(jnp.int32, scales.shape, 0)
    turned = jnp.transpose(wide)[:half].astype(BF16)
    return [
        dot(turned, jnp.where(row == i, wide, F32(0)).astype(BF16)) for i in range(number)
    ]


def inverse_outer(scales, number):
    half = scales.shape[1] // 2
    rows = scales.shape[0]
    inverse = 1.0 / scales.astype(F32)
    high = inverse.astype(BF16).astype(F32)
    low = inverse - high
    left = jnp.transpose(jnp.concatenate([high, high, low], 0))[:half].astype(BF16)
    right = jnp.concatenate([high, low, high], 0)
    row = lax.broadcasted_iota(jnp.int32, right.shape, 0) & (rows - 1)
    return [
        dot(left, jnp.where(row == i, right, F32(0)).astype(BF16)) for i in range(number)
    ]


def encode(both):
    half, width = both[0].shape
    row = lax.broadcasted_iota(jnp.int32, (half, width), 0)
    lane = lax.broadcasted_iota(jnp.int32, (half, width), 1)
    on = (lane == row) | (lane == row + half)
    diagonal = each(lambda b: jnp.sum(jnp.where(on, b, F32(0)), axis=0, keepdims=True), both)
    root = jnp.sqrt(jnp.maximum(place(diagonal, pad_rows(len(both))), F32(1e-36)))
    exponent = jnp.floor(jnp.log(root) * F32(1 / math.log(2.0)))
    part = jnp.maximum(jnp.ceil((root * jnp.exp2(-exponent) - 1) * 128), F32(0))
    codes = exponent * 256 + part
    scales = scale_of(codes)
    inverse = inverse_outer(scales, len(both))
    value = each(lambda b, p: jnp.round((b * F32(TOP)) * p), both, inverse)
    return each(lambda v: pack(jnp.clip(v, F32(-32767), F32(32767))), value), codes, scales


def spread(values, codes):
    products = outer(scale_of(codes), len(values))
    return each(lambda v, p: (v * F32(1 / TOP)) * pack(p), values, products)


def to_short(x):
    return x.astype(jnp.int32).astype(jnp.int16)


def from_short(x):
    return x.astype(jnp.int32).astype(F32)


def coded_rows(number, half_rows):
    return number * half_rows + pad_rows(number)


def write_coded(out, values, codes):
    half_rows = values[0].shape[0]
    for i, value in enumerate(values):
        out[i * half_rows : (i + 1) * half_rows, :] = to_short(value)
    out[len(values) * half_rows :, :] = to_short(codes)


def read_coded(ref, number, half_rows):
    codes = from_short(ref[number * half_rows :, :])
    values = [from_short(ref[i * half_rows : (i + 1) * half_rows, :]) for i in range(number)]
    return values, codes


def slot_owner(direct, slot):
    return jnp.bitwise_xor(lax.axis_index("space") & 1, slot) if direct else slot


def gram_kernel(peers, slots, direct, after, *refs):
    pieces, refs = refs[:peers], refs[peers + after :]
    merged, token, grams = refs[0], refs[1], refs[2:]
    token[...] = jnp.zeros_like(token)
    me = lax.axis_index("tm")
    here = pieces[0].shape[1]
    entries = pieces[0].shape[2] // 2
    blocks = here * peers
    per_slot = pieces[0].shape[0] // slots
    stage = None
    if here % 16:
        grams, stage = grams[:-1], grams[-1]
    low = lane_low((blocks, 2 * blocks), blocks)
    for slot in range(slots):
        owner = slot_owner(direct, slot)
        coded = []
        for i in range(per_slot):
            f = owner * per_slot + i
            if stage is None:
                for peer in range(peers):
                    start = pl.multiple_of(jnp.bitwise_xor(me, peer) * here, here)
                    merged[f, pl.ds(start, here), :] = pieces[peer][f]
                z = merged[f]
            else:
                for peer in range(peers):
                    start = pl.multiple_of(jnp.bitwise_xor(me, peer) * here, here)
                    stage[pl.ds(start, here), :] = pieces[peer][f].astype(F32)
                z = stage[...].astype(BF16)
                merged[f] = z
            w = jnp.concatenate([z[:, :entries], z[:, entries:]], 0)
            s = lax.dot_general(w, w, (((1,), (1,)), ((), ())), preferred_element_type=F32)
            s = s * F32(1.0 / blocks)
            top, bottom = s[:blocks], swap(s[blocks:])
            compact = jnp.where(low, top + bottom, top - bottom)
            if direct and slot == 0 and grams[0].dtype == F32:
                grams[0][i] = compact
            elif direct:
                coded.append(double(compact))
            else:
                grams[0][f] = pack(double(compact))
        if coded:
            write_coded(grams[slot], *encode(coded)[:2])


def gram(pieces, slots, direct, in_steps, after):
    peers = len(pieces)
    count, here, width = pieces[0].shape
    blocks = here * peers
    if direct:
        rows = coded_rows(count // slots, blocks // 2)
        shapes = [((rows, 2 * blocks), jnp.int16)] * slots
        if in_steps:
            shapes[0] = ((count // slots, blocks, 2 * blocks), F32)
    else:
        shapes = [((count, blocks // 2, 2 * blocks), F32)]
    out = pl.pallas_call(
        functools.partial(gram_kernel, peers, slots, direct, len(after)),
        in_specs=[whole_spec()] * peers + [any_spec()] * len(after),
        out_specs=[whole_spec()] * (2 + len(shapes)),
        out_shape=[jax.ShapeDtypeStruct((count, blocks, width), BF16), TOKEN]
        + [jax.ShapeDtypeStruct(*s) for s in shapes],
        scratch_shapes=[pltpu.VMEM((blocks, width), F32)] if here % 16 else [],
        compiler_params=params(),
        cost_estimate=light(),
        name="gram",
    )(*pieces, *after)
    return out[0], out[2:], out[1]


def add_kernel(own, other, *refs):
    out, token = refs[-2:]
    token[...] = jnp.zeros_like(token)
    number, blocks, _ = own.shape
    received = spread(*read_coded(other, number, blocks // 2))
    sums = [double(own[i] + unpack(received[i])[0]) for i in range(number)]
    write_coded(out, *encode(sums)[:2])


def add(own, other, after):
    return pl.pallas_call(
        add_kernel,
        in_specs=[whole_spec()] * 2 + [any_spec()] * len(after),
        out_specs=[whole_spec()] * 2,
        out_shape=[jax.ShapeDtypeStruct(other.shape, jnp.int16), TOKEN],
        compiler_params=params(),
        cost_estimate=light(),
        name="add",
    )(own, other, *after)


def split(x):
    high = x.astype(BF16)
    return high, (x - high.astype(F32)).astype(BF16)


def solve_kernel(chunks, half_rows, *refs):
    out, token = refs[-2:]
    token[...] = jnp.zeros_like(token)
    width = out.shape[1]
    half = width // 2
    shape = (half, width)
    row = lax.broadcasted_iota(jnp.int32, shape, 0)
    lane = lax.broadcasted_iota(jnp.int32, shape, 1)
    eye = jnp.where(row == lane, F32(1), F32(0))

    sums, at = [], 0
    for parts, count in chunks:
        ins, at = refs[at : at + parts], at + parts
        if parts == 1:
            sums += [ins[0][i] for i in range(count)]
            continue
        found = [spread(*read_coded(r, count, half_rows)) for r in ins]
        added = each(lambda p, q: p + q, found[0], found[1])
        if parts == 4:
            added = each(lambda p, q, r: p + (q + r), added, found[2], found[3])
        sums += added
    number = len(sums)
    both_halves = each(unpack, sums)
    grams = [h[0] for h in both_halves]
    spots = lax.broadcasted_iota(jnp.int32, sums[0].shape, 1)
    lines = lax.broadcasted_iota(jnp.int32, sums[0].shape, 0)
    on = (spots == lines) | (spots == lines + 3 * half_rows)
    shift = each(
        lambda p: jnp.sum(jnp.where(on, p, F32(0)), keepdims=True) * F32(1.0 / half), sums
    )
    eye_low = jnp.where(row + half == lane, F32(1), F32(0))
    inverse = each(lambda m: 1.0 / m, shift)
    system = each(lambda g, m: g * m + eye, grams, inverse)
    under = each(lambda h, m: h[1] * m + eye_low, both_halves, inverse)
    both = each(
        lambda a, u: jnp.concatenate(split(jnp.concatenate([a, u], 0)), 1), system, under
    )

    def times(v, a):
        wide = dot(v, a)
        return wide[:, :width] + wide[:, width:]


    low_end, high_end = 1.0, float(half + 1)
    mid, radius = (high_end + low_end) / 2, (high_end - low_end) / 2
    ratio = mid / radius
    t = 2 * ratio * ratio - 1
    scale = 2.0 / (radius * radius * t)
    x = each(lambda a: (F32(scale) * (F32(2 * mid) * eye - a)).astype(BF16), system)
    p = each(lambda v, a: eye - times(v, a), x, both)
    x = each(lambda v: v.astype(F32), x)
    for _ in range(3):
        t_next = 2 * t * t - 1
        c = F32(2 * t * t / t_next)
        pf = each(lambda q: full(q).astype(BF16), p)
        xp = each(lambda v, q: jnp.concatenate([v, q], 0).astype(BF16), x, p)
        moved = each(dot, xp, pf)
        x = each(lambda v, m: c * (v + m[:half]), x, moved)
        p = each(lambda m: c * m[half:] - F32(1 / t_next) * eye, moved)
        t = t_next
    for kind in ("scaled", "last"):
        xb = each(lambda v: v.astype(BF16), x)
        xw = each(lambda v: v.astype(F32), xb)
        xf = each(lambda v: full(v).astype(BF16), xw)
        residual = each(lambda v, a: eye - times(v, a), xb, both)
        step = each(lambda r, v: dot(r.astype(BF16), v), residual, xf)
        factor = 1.0 if kind == "last" else 2 * t * t / (2 * t * t - 1)
        x = each(lambda v, m: F32(factor) * (v + m), xw, step)
    values, codes, scales = encode(each(lambda v: double(eye - v), x))
    products = outer(scales, number)
    filters = each(lambda v, p: unpack(v * F32(0.5 / TOP), p), values, products)
    rounded = each(lambda c: c[0].astype(BF16), filters)
    turned = each(
        lambda c: jnp.concatenate([c[0].astype(BF16), c[1].astype(BF16)], 0), filters
    )
    split_g = each(lambda g: jnp.concatenate(split(g), 0), grams)
    moved = each(dot, split_g, turned)
    moved = each(lambda m: m[:half] + m[half:], moved)
    energy = each(
        lambda c, h: jnp.sum(c.astype(F32) * h, keepdims=True) * F32(half), rounded, moved
    )
    energy = place([jnp.broadcast_to(e, (1, width)) for e in energy], codes.shape[0])
    energy = jnp.maximum(energy, F32(1e-36))
    whole = jnp.floor(jnp.log(energy) * F32(LOG_STEPS / math.log(2.0)))
    rest = jnp.round((energy * jnp.exp2(whole * F32(-1 / LOG_STEPS)) - 1.0) * F32(FINE))
    spot = lax.broadcasted_iota(jnp.int32, codes.shape, 1)
    codes = jnp.where(spot == half, whole, jnp.where(spot == half + 1, rest, codes))
    write_coded(out, values, codes)


def solve(chunks, half_rows, after):
    args = [x for parts, _ in chunks for x in parts]
    width = args[0].shape[-1]
    number = sum(count for _, count in chunks)
    shape = [(len(parts), count) for parts, count in chunks]
    return pl.pallas_call(
        functools.partial(solve_kernel, shape, half_rows),
        in_specs=[whole_spec()] * len(args) + [any_spec()] * len(after),
        out_specs=[whole_spec()] * 2,
        out_shape=[
            jax.ShapeDtypeStruct((coded_rows(number, half_rows), width), jnp.int16),
            TOKEN,
        ],
        compiler_params=params(),
        cost_estimate=light(),
        name="filters",
    )(*args, *after)


def energy_kernel(slots, direct, number, chunks, first, *refs):
    merged, pieces = refs[:chunks], refs[chunks : chunks + number]
    energies_out, filters_out, token, energies, filters, energies_sem, filters_sem = refs[-7:]
    token[...] = jnp.zeros_like(token)
    blocks, width = merged[0].shape[1:]
    entries = width // 2
    counts = [m.shape[0] for m in merged]
    per_slot = sum(counts) // slots
    half_rows = blocks // 2
    states = entries * lax.axis_size("space")
    puts = []
    for slot in range(slots):
        owner = slot_owner(direct, slot)
        piece = pieces[slot] if direct else pieces[0].at[slot]
        values, codes = read_coded(piece, per_slot, half_rows)
        whole = codes[:, blocks : blocks + 1]
        rest = codes[:, blocks + 1 : blocks + 2]
        total = jnp.exp2(whole * F32(1 / LOG_STEPS)) * (1.0 + rest * F32(1 / FINE))
        gains = F32(states) / total
        codes = jnp.where(lane_low(codes.shape, blocks), codes, swap(codes))
        products = outer(scale_of(codes), per_slot)
        base = 0
        for chunk, count in enumerate(counts):
            own = count // slots
            size = 4 if own % 4 == 0 else 1
            for begin in range(0, own, size):
                start = sum(counts[:chunk]) + owner * own + begin
                some = range(base + begin, base + begin + size)
                z = [merged[chunk][owner * own + begin + i] for i in range(size)]
                scale = [products[i] for i in some]
                halves = each(unpack, [values[i] * F32(0.5 / TOP) for i in some], scale)
                both = each(
                    lambda h: jnp.concatenate([h[0].astype(BF16), h[1].astype(BF16)], 0), halves
                )
                w = each(lambda v: jnp.concatenate([v[:, :entries], v[:, entries:]], 0), z)
                r = each(dot, both, w)
                gain = [gains[i : i + 1] for i in some]
                energy = each(
                    lambda v, t: jnp.sum(v * v, axis=0, keepdims=True) * t, r, gain
                )
                for i in range(size):
                    filters[start + i, 0] = halves[i][0][:, :blocks]
                    filters[start + i, 1] = -halves[i][1][:, :blocks]
                    energies[pl.ds(start + i, 1), :] = energy[i]
                put = pltpu.make_async_copy(
                    filters.at[pl.ds(start, size)],
                    filters_out.at[pl.ds(first + start, size)],
                    filters_sem.at[len(puts)],
                )
                put.start()
                puts.append(put)
            base += own
    put = pltpu.make_async_copy(
        energies, energies_out.at[pl.ds(first, sum(counts))], energies_sem.at[0]
    )
    put.start()
    for p in [*puts, put]:
        p.wait()


def filtered(merged, pieces, slots, direct, carry, owned, first, after):
    _, blocks, width = merged[0].shape
    count = sum(m.shape[0] for m in merged)
    copies = sum(slots * (m.shape[0] // slots) for m in merged)
    entries = width // 2
    fixed = len(merged) + len(pieces)
    args = [*merged, *pieces] + ([] if carry is None else list(carry)) + list(after)
    hbm = pl.BlockSpec(memory_space=pltpu.HBM)
    return pl.pallas_call(
        functools.partial(energy_kernel, slots, direct, len(pieces), len(merged), first),
        in_specs=[whole_spec()] * fixed
        + ([] if carry is None else [hbm] * 2)
        + [any_spec()] * len(after),
        out_specs=[hbm] * 2 + [whole_spec()],
        out_shape=[
            jax.ShapeDtypeStruct((owned, entries), F32),
            jax.ShapeDtypeStruct((owned, 2, blocks, blocks), F32),
            TOKEN,
        ],
        input_output_aliases={} if carry is None else {fixed: 0, fixed + 1: 1},
        scratch_shapes=[
            pltpu.VMEM((count, entries), F32),
            pltpu.VMEM((count, 2, blocks, blocks), F32),
            pltpu.SemaphoreType.DMA((1,)),
            pltpu.SemaphoreType.DMA((copies,)),
        ],
        compiler_params=params(),
        cost_estimate=light(),
        name="energy",
    )(*args)


def plan(owned, slots):
    if slots != 4 or owned != 64:
        return [owned], (("T", 0), ("G", 0), ("F", 0), ("E", 0))
    return SIZES, ORDER


SIZES = [24, 24, 16]
ORDER = (
    ("T", 0), ("T", 1), ("G", 0), ("A", 0), ("G", 1), ("F", 0), ("A", 1), ("G", 2),
    ("E", 0), ("F", 1), ("F", 2), ("E", 1), ("E", 2),
)


TIES = {("T", 1): (0,)}


def permute(x, axis, offset):
    pairs = [(i, i ^ offset) for i in range(lax.axis_size(axis))]
    return lax.ppermute(x, axis, pairs)


def on_device(snapshots, entry_weight, freq_index):
    peers = lax.axis_size("tm")
    slots = lax.axis_size("space")
    owned = freq_index.shape[0] // peers
    sizes, order = plan(owned, slots)
    starts = [sum(sizes[:c]) for c in range(len(sizes))]
    paired = slots == 4
    halves = 2 if paired else slots
    weight = entry_weight.reshape(1, -1)
    sent, merged, grams, parts, pieces = {}, {}, {}, {}, {}
    carry = None
    token = []

    def do_transform(c):
        nonlocal token
        joint = [k for k in range(c, len(sizes)) if k == c or c and ("T", k) not in order]
        out, done = transform(
            snapshots, weight, freq_index, peers, [(starts[k], sizes[k]) for k in joint], token
        )
        token = [done]
        for k, own in zip(joint, out):
            sent[k] = [own[0]] + [permute(own[i], "tm", i) for i in range(1, peers)]

    def do_gram(c):
        nonlocal token
        in_steps = paired and ("A", c) in order
        merged[c], grams[c], done = gram(sent[c], halves, paired, in_steps, token)
        token = [done]
        if in_steps:
            grams[c] = [grams[c][0], permute(grams[c][1], "space", 1)]
        elif paired:
            own, other = grams[c]
            parts[c] = [
                own,
                permute(own, "space", 2),
                permute(other, "space", 1),
                permute(other, "space", 3),
            ]
        else:
            parts[c] = [lax.psum_scatter(grams[c][0], "space", scatter_dimension=0, tiled=True)]

    def do_add(c):
        nonlocal token
        half, done = add(*grams[c], token)
        token = [done]
        parts[c] = [half, permute(half, "space", 2)]

    def joined(stage, c):
        last = c + 1
        while last < len(sizes) and (stage, last) not in order:
            last += 1
        return range(c, last)

    def do_solve(c):
        nonlocal token
        work = [(parts[k], sizes[k] // halves) for k in joined("F", c)]
        own, done = solve(work, merged[c].shape[1] // 2, token)
        token = [done]
        if paired:
            pieces[c] = [own, permute(own, "space", 1)]
        else:
            pieces[c] = [lax.all_gather(own, "space", axis=0, tiled=False)]

    def do_energy(c):
        nonlocal token, carry
        work = [merged[k] for k in joined("E", c)]
        *carry, done = filtered(
            work, pieces[c], halves, paired, carry, owned, starts[c], token
        )
        token = [done]

    stages = {"T": do_transform, "G": do_gram, "A": do_add, "F": do_solve, "E": do_energy}
    for stage, c in order:
        token = token + [sent[k][1] for k in TIES.get((stage, c), ()) if k in sent]
        stages[stage](c)
    return (carry[0], carry[1])


def solution(mesh):
    in_specs = (P(("grp", "tm"), None, "space"), P(("grp", "space")), P())
    out_specs = (P(("grp", "tm"), "space"), P(("grp", "tm"), None, None, None))
    return jax.shard_map(
        on_device, mesh=mesh, in_specs=in_specs, out_specs=out_specs, check_vma=False
    )
```

```python
import functools
import math

import jax
import jax.numpy as jnp
from jax import lax
from jax.experimental import pallas as pl
from jax.experimental.pallas import tpu as pltpu
from jax.sharding import PartitionSpec as P

F32 = jnp.float32
BF16 = jnp.bfloat16
VMEM_LIMIT = 30 * 1024 * 1024
LANES = 128


def params(**kwargs):
    return pltpu.CompilerParams(vmem_limit_bytes=VMEM_LIMIT, **kwargs)


def whole_spec():
    return pl.BlockSpec(memory_space=pltpu.VMEM)


TOKEN = jax.ShapeDtypeStruct((8, LANES), F32)


def light():
    return pl.CostEstimate(flops=1024, bytes_accessed=1024, transcendentals=0)


def in_hbm(x):
    return pltpu.with_memory_space_constraint(x, pltpu.HBM)


def any_spec():
    return pl.BlockSpec(memory_space=pl.ANY)


def dot(a, b):
    return lax.dot_general(a, b, (((1,), (0,)), ((), ())), preferred_element_type=F32)


def cos_sin(phase, length):
    quarter = length // 4
    eighth = length // 8
    shifted = phase + eighth
    low = (shifted & (quarter - 1)) - eighth
    quadrant = (shifted // quarter) & 3
    x = low.astype(F32) * F32(2.0 * math.pi / length)
    x2 = x * x
    cos = F32(1 / 40320)
    for c in (-1 / 720, 1 / 24, -0.5, 1.0):
        cos = cos * x2 + F32(c)
    sin = F32(1 / 362880)
    for c in (-1 / 5040, 1 / 120, -1 / 6, 1.0):
        sin = sin * x2 + F32(c)
    sin = sin * x
    odd = (quadrant & 1) == 1
    c0 = jnp.where(odd, sin, cos)
    s0 = jnp.where(odd, cos, sin)
    c1 = jnp.where((quadrant == 1) | (quadrant == 2), -c0, c0)
    s1 = jnp.where(quadrant >= 2, -s0, s0)
    return c1, s1


def transform_kernel(peers, parts, group, *refs):
    freq_hbm, weight_hbm, snap_hbm = refs[:3]
    outs, token = refs[-peers * len(parts) - 8 : -8], refs[-8]
    freq, weight, snap, table, wide, small_sem, snap_sem = refs[-7:]
    blocks, length, entries = snap.shape
    steps = blocks // group
    get_freq = pltpu.make_async_copy(freq_hbm, freq, small_sem.at[0])
    get_weight = pltpu.make_async_copy(weight_hbm, weight, small_sem.at[1])
    get_snap = [
        pltpu.make_async_copy(
            snap_hbm.at[pl.ds(i * group, group)], snap.at[pl.ds(i * group, group)], snap_sem.at[i]
        )
        for i in range(steps)
    ]
    token[...] = jnp.zeros_like(token)
    get_freq.start()
    for get in get_snap:
        get.start()
    get_weight.start()

    me = lax.axis_index("tm")
    groups = [
        (peer, first + j)
        for first, count in parts
        for peer in range(peers)
        for j in range(0, count, 8)
    ]
    rows = 8 * len(groups)
    per_peer = freq.shape[0] // peers
    times = lax.broadcasted_iota(jnp.int32, (8, length), 1)
    sub = lax.broadcasted_iota(jnp.int32, (8, length), 0)
    window = 0.5 - 0.5 * cos_sin(times, length)[0]
    scaled = window / F32(math.sqrt(0.375 * length))
    get_freq.wait()

    def eight(index):
        peer, offset = groups[index]
        start = jnp.bitwise_xor(me, peer) * per_peer + offset
        k = jnp.zeros((8, length), jnp.int32)
        for i in range(8):
            k = jnp.where(sub == i, freq[start + i], k)
        cos, sin = cos_sin((k * times) & (length - 1), length)
        return scaled * cos, -(scaled * sin)

    for pair in range(rows // 16):
        re0, im0 = eight(2 * pair)
        re1, im1 = eight(2 * pair + 1)
        table[16 * pair : 16 * pair + 16, :] = jnp.concatenate([re0, re1], 0).astype(BF16)
        table[rows + 16 * pair : rows + 16 * pair + 16, :] = jnp.concatenate(
            [im0, im1], 0
        ).astype(BF16)

    get_weight.wait()
    root = jnp.sqrt(weight[...])
    tiles = entries // LANES
    for step in range(steps):
        get_snap[step].wait()
        for b in range(step * group, (step + 1) * group):
            spec = dot(table[...], snap[b]) * root
            for tile in range(tiles):
                lanes = slice(tile * LANES, (tile + 1) * LANES)
                wide[tile, pl.ds(b, rows, stride=blocks), :] = spec[:rows, lanes]
                wide[tiles + tile, pl.ds(b, rows, stride=blocks), :] = spec[rows:, lanes]
    at = 0
    for out in outs:
        for j in range(out.shape[0]):
            for tile in range(2 * tiles):
                lanes = slice(tile * LANES, (tile + 1) * LANES)
                out[j, :, lanes] = wide[tile, at : at + blocks, :].astype(BF16)
            at += blocks


def transform(snapshots, weight, freq_index, peers, parts, after):
    blocks, length, entries = snapshots.shape
    group = min(blocks, 4)
    total = peers * sum(count for _, count in parts)
    shapes = [
        jax.ShapeDtypeStruct((count, blocks, 2 * entries), BF16)
        for _, count in parts
        for _ in range(peers)
    ]
    hbm = pl.BlockSpec(memory_space=pltpu.HBM)
    out = pl.pallas_call(
        functools.partial(transform_kernel, peers, parts, group),
        in_specs=[hbm] * 3 + [any_spec()] * len(after),
        out_specs=[whole_spec()] * (len(shapes) + 1),
        out_shape=shapes + [TOKEN],
        scratch_shapes=[
            pltpu.SMEM(freq_index.shape, jnp.int32),
            pltpu.VMEM(weight.shape, F32),
            pltpu.VMEM(snapshots.shape, BF16),
            pltpu.VMEM((2 * total, length), BF16),
            pltpu.VMEM((2 * entries // LANES, total * blocks, LANES), F32),
            pltpu.SemaphoreType.DMA((2,)),
            pltpu.SemaphoreType.DMA((blocks // group,)),
        ],
        compiler_params=params(),
        cost_estimate=light(),
        name="transform",
    )(in_hbm(freq_index), in_hbm(weight), in_hbm(snapshots), *after)
    return [out[i * peers : (i + 1) * peers] for i in range(len(parts))], out[-1]


def lane_low(shape, half):
    return lax.broadcasted_iota(jnp.int32, shape, 1) < half


def swap(x):
    return pltpu.roll(x, x.shape[1] // 2, 1)


def each(fn, *lists):
    return [fn(*items) for items in zip(*lists)]


def double(compact):
    return compact + swap(compact)


def pack(both):
    half = both.shape[0]
    low = lane_low((half // 2, 2 * half), half)
    return jnp.where(low, both[: half // 2], both[half // 2 :])


def unpack(packed, scale=None):
    rows, half = packed.shape[0], packed.shape[1] // 2
    low = lane_low(packed.shape, half)
    other = swap(packed)
    both = jnp.concatenate(
        [jnp.where(low, packed, other), jnp.where(low, other, packed)], 0
    )
    turned = jnp.transpose(jnp.concatenate([packed, packed], 0))
    turned = jnp.where(lane_low((half, half), rows), turned[:half], turned[half:])
    turned = jnp.concatenate([turned, turned], 1)
    low = lane_low(both.shape, half)
    total = both + turned
    apart = both - turned
    top = jnp.where(low, total, apart)
    bottom = jnp.where(low, -apart, total)
    scale = F32(0.5) if scale is None else scale
    return scale * top, scale * bottom


def full(compact):
    half = compact.shape[0]
    turned = swap(compact)
    low = lane_low(compact.shape, half)
    return jnp.concatenate([compact, jnp.where(low, -turned, turned)], 0)


TOP = 23169.0
LOG_STEPS = 64.0
FINE = float(2**21)


def place(lines, rows):
    shape = (rows, lines[0].shape[1])
    row = lax.broadcasted_iota(jnp.int32, shape, 0)
    out = jnp.zeros(shape, F32)
    for i, line in enumerate(lines):
        out = jnp.where(row == i, line, out)
    return out


def pad_rows(number):
    return -(-number // 16) * 16


def scale_of(code):
    exponent = jnp.floor(code * F32(1 / 256))
    part = code - exponent * 256
    return (jnp.exp2(exponent) * (1 + part * F32(1 / 128))).astype(BF16)


def outer(scales, number):
    half = scales.shape[1] // 2
    wide = scales.astype(F32)
    row = lax.broadcasted_iota(jnp.int32, scales.shape, 0)
    turned = jnp.transpose(wide)[:half].astype(BF16)
    return [
        dot(turned, jnp.where(row == i, wide, F32(0)).astype(BF16)) for i in range(number)
    ]


def inverse_outer(scales, number):
    half = scales.shape[1] // 2
    rows = scales.shape[0]
    inverse = 1.0 / scales.astype(F32)
    high = inverse.astype(BF16).astype(F32)
    low = inverse - high
    left = jnp.transpose(jnp.concatenate([high, high, low], 0))[:half].astype(BF16)
    right = jnp.concatenate([high, low, high], 0)
    row = lax.broadcasted_iota(jnp.int32, right.shape, 0) & (rows - 1)
    return [
        dot(left, jnp.where(row == i, right, F32(0)).astype(BF16)) for i in range(number)
    ]


def encode(both):
    half, width = both[0].shape
    row = lax.broadcasted_iota(jnp.int32, (half, width), 0)
    lane = lax.broadcasted_iota(jnp.int32, (half, width), 1)
    on = (lane == row) | (lane == row + half)
    diagonal = each(lambda b: jnp.sum(jnp.where(on, b, F32(0)), axis=0, keepdims=True), both)
    root = jnp.sqrt(jnp.maximum(place(diagonal, pad_rows(len(both))), F32(1e-36)))
    exponent = jnp.floor(jnp.log(root) * F32(1 / math.log(2.0)))
    part = jnp.maximum(jnp.ceil((root * jnp.exp2(-exponent) - 1) * 128), F32(0))
    codes = exponent * 256 + part
    scales = scale_of(codes)
    inverse = inverse_outer(scales, len(both))
    value = each(lambda b, p: jnp.round((b * F32(TOP)) * p), both, inverse)
    return each(lambda v: pack(jnp.clip(v, F32(-32767), F32(32767))), value), codes, scales


def spread(values, codes):
    products = outer(scale_of(codes), len(values))
    return each(lambda v, p: (v * F32(1 / TOP)) * pack(p), values, products)


def to_short(x):
    return x.astype(jnp.int32).astype(jnp.int16)


def from_short(x):
    return x.astype(jnp.int32).astype(F32)


def coded_rows(number, half_rows):
    return number * half_rows + pad_rows(number)


def write_coded(out, values, codes):
    half_rows = values[0].shape[0]
    for i, value in enumerate(values):
        out[i * half_rows : (i + 1) * half_rows, :] = to_short(value)
    out[len(values) * half_rows :, :] = to_short(codes)


def read_coded(ref, number, half_rows):
    codes = from_short(ref[number * half_rows :, :])
    values = [from_short(ref[i * half_rows : (i + 1) * half_rows, :]) for i in range(number)]
    return values, codes


def slot_owner(direct, slot):
    return jnp.bitwise_xor(lax.axis_index("space") & 1, slot) if direct else slot


def gram_kernel(peers, slots, direct, after, *refs):
    pieces, refs = refs[:peers], refs[peers + after :]
    merged, token, grams = refs[0], refs[1], refs[2:]
    token[...] = jnp.zeros_like(token)
    me = lax.axis_index("tm")
    here = pieces[0].shape[1]
    entries = pieces[0].shape[2] // 2
    blocks = here * peers
    per_slot = pieces[0].shape[0] // slots
    stage = None
    if here % 16:
        grams, stage = grams[:-1], grams[-1]
    low = lane_low((blocks, 2 * blocks), blocks)
    for slot in range(slots):
        owner = slot_owner(direct, slot)
        coded = []
        for i in range(per_slot):
            f = owner * per_slot + i
            if stage is None:
                for peer in range(peers):
                    start = pl.multiple_of(jnp.bitwise_xor(me, peer) * here, here)
                    merged[f, pl.ds(start, here), :] = pieces[peer][f]
                z = merged[f]
            else:
                for peer in range(peers):
                    start = pl.multiple_of(jnp.bitwise_xor(me, peer) * here, here)
                    stage[pl.ds(start, here), :] = pieces[peer][f].astype(F32)
                z = stage[...].astype(BF16)
                merged[f] = z
            w = jnp.concatenate([z[:, :entries], z[:, entries:]], 0)
            s = lax.dot_general(w, w, (((1,), (1,)), ((), ())), preferred_element_type=F32)
            s = s * F32(1.0 / blocks)
            top, bottom = s[:blocks], swap(s[blocks:])
            compact = jnp.where(low, top + bottom, top - bottom)
            if direct and slot == 0 and grams[0].dtype == F32:
                grams[0][i] = compact
            elif direct:
                coded.append(double(compact))
            else:
                grams[0][f] = pack(double(compact))
        if coded:
            write_coded(grams[slot], *encode(coded)[:2])


def gram(pieces, slots, direct, in_steps, after):
    peers = len(pieces)
    count, here, width = pieces[0].shape
    blocks = here * peers
    if direct:
        rows = coded_rows(count // slots, blocks // 2)
        shapes = [((rows, 2 * blocks), jnp.int16)] * slots
        if in_steps:
            shapes[0] = ((count // slots, blocks, 2 * blocks), F32)
    else:
        shapes = [((count, blocks // 2, 2 * blocks), F32)]
    out = pl.pallas_call(
        functools.partial(gram_kernel, peers, slots, direct, len(after)),
        in_specs=[whole_spec()] * peers + [any_spec()] * len(after),
        out_specs=[whole_spec()] * (2 + len(shapes)),
        out_shape=[jax.ShapeDtypeStruct((count, blocks, width), BF16), TOKEN]
        + [jax.ShapeDtypeStruct(*s) for s in shapes],
        scratch_shapes=[pltpu.VMEM((blocks, width), F32)] if here % 16 else [],
        compiler_params=params(),
        cost_estimate=light(),
        name="gram",
    )(*pieces, *after)
    return out[0], out[2:], out[1]


def add_kernel(own, other, *refs):
    out, token = refs[-2:]
    token[...] = jnp.zeros_like(token)
    number, blocks, _ = own.shape
    received = spread(*read_coded(other, number, blocks // 2))
    sums = [double(own[i] + unpack(received[i])[0]) for i in range(number)]
    write_coded(out, *encode(sums)[:2])


def add(own, other, after):
    return pl.pallas_call(
        add_kernel,
        in_specs=[whole_spec()] * 2 + [any_spec()] * len(after),
        out_specs=[whole_spec()] * 2,
        out_shape=[jax.ShapeDtypeStruct(other.shape, jnp.int16), TOKEN],
        compiler_params=params(),
        cost_estimate=light(),
        name="add",
    )(own, other, *after)


def split(x):
    high = x.astype(BF16)
    return high, (x - high.astype(F32)).astype(BF16)


def solve_kernel(chunks, half_rows, before, *refs):
    out, token = refs[-2:]
    puts = []
    if before is not None:
        energies_out, filters_out, out, token, sem = refs[-5:]
        inputs = sum(parts for parts, _ in chunks)
        for i, target in enumerate((energies_out, filters_out)):
            source = refs[inputs + i]
            put = pltpu.make_async_copy(
                source, target.at[pl.ds(before, source.shape[0])], sem.at[i]
            )
            put.start()
            puts.append(put)
    token[...] = jnp.zeros_like(token)
    width = out.shape[1]
    half = width // 2
    shape = (half, width)
    row = lax.broadcasted_iota(jnp.int32, shape, 0)
    lane = lax.broadcasted_iota(jnp.int32, shape, 1)
    eye = jnp.where(row == lane, F32(1), F32(0))

    sums, at = [], 0
    for parts, count in chunks:
        ins, at = refs[at : at + parts], at + parts
        if parts == 1:
            sums += [ins[0][i] for i in range(count)]
            continue
        found = [spread(*read_coded(r, count, half_rows)) for r in ins]
        added = each(lambda p, q: p + q, found[0], found[1])
        if parts == 4:
            added = each(lambda p, q, r: p + (q + r), added, found[2], found[3])
        sums += added
    number = len(sums)
    both_halves = each(unpack, sums)
    grams = [h[0] for h in both_halves]
    spots = lax.broadcasted_iota(jnp.int32, sums[0].shape, 1)
    lines = lax.broadcasted_iota(jnp.int32, sums[0].shape, 0)
    on = (spots == lines) | (spots == lines + 3 * half_rows)
    shift = each(
        lambda p: jnp.sum(jnp.where(on, p, F32(0)), keepdims=True) * F32(1.0 / half), sums
    )
    eye_low = jnp.where(row + half == lane, F32(1), F32(0))
    inverse = each(lambda m: 1.0 / m, shift)
    system = each(lambda g, m: g * m + eye, grams, inverse)
    under = each(lambda h, m: h[1] * m + eye_low, both_halves, inverse)
    both = each(
        lambda a, u: jnp.concatenate(split(jnp.concatenate([a, u], 0)), 1), system, under
    )

    def times(v, a):
        wide = dot(v, a)
        return wide[:, :width] + wide[:, width:]


    low_end, high_end = 1.0, float(half + 1)
    mid, radius = (high_end + low_end) / 2, (high_end - low_end) / 2
    ratio = mid / radius
    t = 2 * ratio * ratio - 1
    scale = 2.0 / (radius * radius * t)
    x = each(lambda a: (F32(scale) * (F32(2 * mid) * eye - a)).astype(BF16), system)
    p = each(lambda v, a: eye - times(v, a), x, both)
    x = each(lambda v: v.astype(F32), x)
    for _ in range(3):
        t_next = 2 * t * t - 1
        c = F32(2 * t * t / t_next)
        pf = each(lambda q: full(q).astype(BF16), p)
        xp = each(lambda v, q: jnp.concatenate([v, q], 0).astype(BF16), x, p)
        moved = each(dot, xp, pf)
        x = each(lambda v, m: c * (v + m[:half]), x, moved)
        p = each(lambda m: c * m[half:] - F32(1 / t_next) * eye, moved)
        t = t_next
    for kind in ("scaled", "last"):
        xb = each(lambda v: v.astype(BF16), x)
        xw = each(lambda v: v.astype(F32), xb)
        xf = each(lambda v: full(v).astype(BF16), xw)
        residual = each(lambda v, a: eye - times(v, a), xb, both)
        step = each(lambda r, v: dot(r.astype(BF16), v), residual, xf)
        factor = 1.0 if kind == "last" else 2 * t * t / (2 * t * t - 1)
        x = each(lambda v, m: F32(factor) * (v + m), xw, step)
    values, codes, scales = encode(each(lambda v: double(eye - v), x))
    products = outer(scales, number)
    filters = each(lambda v, p: unpack(v * F32(0.5 / TOP), p), values, products)
    rounded = each(lambda c: c[0].astype(BF16), filters)
    turned = each(
        lambda c: jnp.concatenate([c[0].astype(BF16), c[1].astype(BF16)], 0), filters
    )
    split_g = each(lambda g: jnp.concatenate(split(g), 0), grams)
    moved = each(dot, split_g, turned)
    moved = each(lambda m: m[:half] + m[half:], moved)
    energy = each(
        lambda c, h: jnp.sum(c.astype(F32) * h, keepdims=True) * F32(half), rounded, moved
    )
    energy = place([jnp.broadcast_to(e, (1, width)) for e in energy], codes.shape[0])
    energy = jnp.maximum(energy, F32(1e-36))
    whole = jnp.floor(jnp.log(energy) * F32(LOG_STEPS / math.log(2.0)))
    rest = jnp.round((energy * jnp.exp2(whole * F32(-1 / LOG_STEPS)) - 1.0) * F32(FINE))
    spot = lax.broadcasted_iota(jnp.int32, codes.shape, 1)
    codes = jnp.where(spot == half, whole, jnp.where(spot == half + 1, rest, codes))
    write_coded(out, values, codes)
    for put in puts:
        put.wait()


def solve(chunks, half_rows, earlier, owned, after):
    args = [x for parts, _ in chunks for x in parts]
    width = args[0].shape[-1]
    number = sum(count for _, count in chunks)
    shape = [(len(parts), count) for parts, count in chunks]
    results = list(earlier[:2]) if earlier else []
    hbm = pl.BlockSpec(memory_space=pltpu.HBM)
    out = pl.pallas_call(
        functools.partial(solve_kernel, shape, half_rows, earlier[2] if earlier else None),
        in_specs=[whole_spec()] * (len(args) + len(results)) + [any_spec()] * len(after),
        out_specs=[hbm] * len(results) + [whole_spec()] * 2,
        out_shape=[jax.ShapeDtypeStruct((owned, *r.shape[1:]), F32) for r in results]
        + [
            jax.ShapeDtypeStruct((coded_rows(number, half_rows), width), jnp.int16),
            TOKEN,
        ],
        scratch_shapes=[pltpu.SemaphoreType.DMA((2,))] if results else [],
        compiler_params=params(),
        cost_estimate=light(),
        name="filters",
    )(*args, *results, *after)
    return out[-2], out[-1], list(out[:2]) if results else None


def energy_kernel(slots, direct, number, chunks, first, before, last, *refs):
    merged, pieces = refs[:chunks], refs[chunks : chunks + number]
    earlier = refs[chunks + number : chunks + number + 2]
    puts = []
    if last:
        energies_out, filters_out, token, energies, filters = refs[-8:-3]
    else:
        energies, filters, token = refs[-6:-3]
        if before is not None:
            energies_out, filters_out = refs[-8:-6]
    energies_sem, filters_sem, before_sem = refs[-3:]
    if before is not None:
        for i, (source, target) in enumerate(zip(earlier, (energies_out, filters_out))):
            put = pltpu.make_async_copy(
                source, target.at[pl.ds(before, source.shape[0])], before_sem.at[i]
            )
            put.start()
            puts.append(put)
    own_puts = 0
    token[...] = jnp.zeros_like(token)
    blocks, width = merged[0].shape[1:]
    entries = width // 2
    counts = [m.shape[0] for m in merged]
    per_slot = sum(counts) // slots
    half_rows = blocks // 2
    states = entries * lax.axis_size("space")
    for slot in range(slots):
        owner = slot_owner(direct, slot)
        piece = pieces[slot] if direct else pieces[0].at[slot]
        values, codes = read_coded(piece, per_slot, half_rows)
        whole = codes[:, blocks : blocks + 1]
        rest = codes[:, blocks + 1 : blocks + 2]
        total = jnp.exp2(whole * F32(1 / LOG_STEPS)) * (1.0 + rest * F32(1 / FINE))
        gains = F32(states) / total
        codes = jnp.where(lane_low(codes.shape, blocks), codes, swap(codes))
        products = outer(scale_of(codes), per_slot)
        base = 0
        for chunk, count in enumerate(counts):
            own = count // slots
            size = 4 if own % 4 == 0 else 1
            for begin in range(0, own, size):
                start = sum(counts[:chunk]) + owner * own + begin
                some = range(base + begin, base + begin + size)
                z = [merged[chunk][owner * own + begin + i] for i in range(size)]
                scale = [products[i] for i in some]
                halves = each(unpack, [values[i] * F32(0.5 / TOP) for i in some], scale)
                both = each(
                    lambda h: jnp.concatenate([h[0].astype(BF16), h[1].astype(BF16)], 0), halves
                )
                w = each(lambda v: jnp.concatenate([v[:, :entries], v[:, entries:]], 0), z)
                r = each(dot, both, w)
                gain = [gains[i : i + 1] for i in some]
                energy = each(
                    lambda v, t: jnp.sum(v * v, axis=0, keepdims=True) * t, r, gain
                )
                for i in range(size):
                    filters[start + i, 0] = halves[i][0][:, :blocks]
                    filters[start + i, 1] = -halves[i][1][:, :blocks]
                    energies[pl.ds(start + i, 1), :] = energy[i]
                if last:
                    put = pltpu.make_async_copy(
                        filters.at[pl.ds(start, size)],
                        filters_out.at[pl.ds(first + start, size)],
                        filters_sem.at[own_puts],
                    )
                    put.start()
                    puts.append(put)
                    own_puts += 1
            base += own
    if last:
        put = pltpu.make_async_copy(
            energies, energies_out.at[pl.ds(first, sum(counts))], energies_sem.at[0]
        )
        put.start()
        puts.append(put)
    for put in puts:
        put.wait()


def filtered(merged, pieces, slots, direct, earlier, carry, owned, first, last, after):
    _, blocks, width = merged[0].shape
    count = sum(m.shape[0] for m in merged)
    copies = sum(slots * (m.shape[0] // slots) for m in merged)
    entries = width // 2
    fixed = len(merged) + len(pieces) + (2 if earlier else 0)
    args = [*merged, *pieces, *(earlier[:2] if earlier else ()), *(carry or ()), *after]
    hbm = pl.BlockSpec(memory_space=pltpu.HBM)
    writes = bool(earlier) or last
    own = [
        jax.ShapeDtypeStruct((count, entries), F32),
        jax.ShapeDtypeStruct((count, 2, blocks, blocks), F32),
    ]
    whole = [
        jax.ShapeDtypeStruct((owned, entries), F32),
        jax.ShapeDtypeStruct((owned, 2, blocks, blocks), F32),
    ]
    scratch = [pltpu.VMEM(o.shape, F32) for o in own] if last else []
    out = pl.pallas_call(
        functools.partial(
            energy_kernel, slots, direct, len(pieces), len(merged), first,
            earlier[2] if earlier else None, last,
        ),
        in_specs=[whole_spec()] * fixed
        + ([hbm] * 2 if carry else [])
        + [any_spec()] * len(after),
        out_specs=([hbm] * 2 if writes else [])
        + ([] if last else [whole_spec()] * 2)
        + [whole_spec()],
        out_shape=(whole if writes else []) + ([] if last else own) + [TOKEN],
        input_output_aliases={fixed: 0, fixed + 1: 1} if carry else {},
        scratch_shapes=scratch
        + [
            pltpu.SemaphoreType.DMA((1,)),
            pltpu.SemaphoreType.DMA((copies,)),
            pltpu.SemaphoreType.DMA((2,)),
        ],
        compiler_params=params(),
        cost_estimate=light(),
        name="energy",
    )(*args)
    carry = list(out[:2]) if writes else None
    earlier = None if last else (*out[-3:-1], first)
    return carry, earlier, out[-1]


def plan(owned, slots):
    if slots != 4 or owned != 64:
        return [owned], (("T", 0), ("G", 0), ("F", 0), ("E", 0))
    return SIZES, ORDER


SIZES = [24, 24, 16]
ORDER = (
    ("T", 0), ("T", 1), ("G", 0), ("A", 0), ("G", 1), ("F", 0), ("A", 1), ("G", 2),
    ("E", 0), ("F", 1), ("F", 2), ("E", 1), ("E", 2),
)


TIES = {("T", 1): (0,)}


def permute(x, axis, offset):
    pairs = [(i, i ^ offset) for i in range(lax.axis_size(axis))]
    return lax.ppermute(x, axis, pairs)


def on_device(snapshots, entry_weight, freq_index):
    peers = lax.axis_size("tm")
    slots = lax.axis_size("space")
    owned = freq_index.shape[0] // peers
    sizes, order = plan(owned, slots)
    starts = [sum(sizes[:c]) for c in range(len(sizes))]
    paired = slots == 4
    halves = 2 if paired else slots
    weight = entry_weight.reshape(1, -1)
    sent, merged, grams, parts, pieces = {}, {}, {}, {}, {}
    carry = None
    earlier = None
    token = []

    def do_transform(c):
        nonlocal token
        joint = [k for k in range(c, len(sizes)) if k == c or c and ("T", k) not in order]
        out, done = transform(
            snapshots, weight, freq_index, peers, [(starts[k], sizes[k]) for k in joint], token
        )
        token = [done]
        for k, own in zip(joint, out):
            sent[k] = [own[0]] + [permute(own[i], "tm", i) for i in range(1, peers)]

    def do_gram(c):
        nonlocal token
        in_steps = paired and ("A", c) in order
        merged[c], grams[c], done = gram(sent[c], halves, paired, in_steps, token)
        token = [done]
        if in_steps:
            grams[c] = [grams[c][0], permute(grams[c][1], "space", 1)]
        elif paired:
            own, other = grams[c]
            parts[c] = [
                own,
                permute(own, "space", 2),
                permute(other, "space", 1),
                permute(other, "space", 3),
            ]
        else:
            parts[c] = [lax.psum_scatter(grams[c][0], "space", scatter_dimension=0, tiled=True)]

    def do_add(c):
        nonlocal token
        half, done = add(*grams[c], token)
        token = [done]
        parts[c] = [half, permute(half, "space", 2)]

    def joined(stage, c):
        last = c + 1
        while last < len(sizes) and (stage, last) not in order:
            last += 1
        return range(c, last)

    def do_solve(c):
        nonlocal token, carry, earlier
        work = [(parts[k], sizes[k] // halves) for k in joined("F", c)]
        own, done, written = solve(work, merged[c].shape[1] // 2, earlier, owned, token)
        if written:
            carry, earlier = written, None
        token = [done]
        if paired:
            pieces[c] = [own, permute(own, "space", 1)]
        else:
            pieces[c] = [lax.all_gather(own, "space", axis=0, tiled=False)]

    def do_energy(c):
        nonlocal token, carry, earlier
        chunks = joined("E", c)
        copies = c > 0 or len(sizes) == 1
        carry, earlier, done = filtered(
            [merged[k] for k in chunks], pieces[c], halves, paired, earlier, carry, owned,
            starts[c], copies, token,
        )
        token = [done]

    stages = {"T": do_transform, "G": do_gram, "A": do_add, "F": do_solve, "E": do_energy}
    for stage, c in order:
        token = token + [sent[k][1] for k in TIES.get((stage, c), ()) if k in sent]
        stages[stage](c)
    return (carry[0], carry[1])


def solution(mesh):
    in_specs = (P(("grp", "tm"), None, "space"), P(("grp", "space")), P())
    out_specs = (P(("grp", "tm"), "space"), P(("grp", "tm"), None, None, None))
    return jax.shard_map(
        on_device, mesh=mesh, in_specs=in_specs, out_specs=out_specs, check_vma=False
    )
```

```python
import functools
import math

import jax
import jax.numpy as jnp
from jax import lax
from jax.experimental import pallas as pl
from jax.experimental.pallas import tpu as pltpu
from jax.sharding import PartitionSpec as P

F32 = jnp.float32
BF16 = jnp.bfloat16
VMEM_LIMIT = 30 * 1024 * 1024
LANES = 128


def params(**kwargs):
    return pltpu.CompilerParams(vmem_limit_bytes=VMEM_LIMIT, **kwargs)


def whole_spec():
    return pl.BlockSpec(memory_space=pltpu.VMEM)


TOKEN = jax.ShapeDtypeStruct((8, LANES), F32)


def light():
    return pl.CostEstimate(flops=1024, bytes_accessed=1024, transcendentals=0)


def in_hbm(x):
    return pltpu.with_memory_space_constraint(x, pltpu.HBM)


def any_spec():
    return pl.BlockSpec(memory_space=pl.ANY)


def dot(a, b):
    return lax.dot_general(a, b, (((1,), (0,)), ((), ())), preferred_element_type=F32)


def cos_sin(phase, length):
    quarter = length // 4
    eighth = length // 8
    shifted = phase + eighth
    low = (shifted & (quarter - 1)) - eighth
    quadrant = (shifted // quarter) & 3
    x = low.astype(F32) * F32(2.0 * math.pi / length)
    x2 = x * x
    cos = F32(1 / 40320)
    for c in (-1 / 720, 1 / 24, -0.5, 1.0):
        cos = cos * x2 + F32(c)
    sin = F32(1 / 362880)
    for c in (-1 / 5040, 1 / 120, -1 / 6, 1.0):
        sin = sin * x2 + F32(c)
    sin = sin * x
    odd = (quadrant & 1) == 1
    c0 = jnp.where(odd, sin, cos)
    s0 = jnp.where(odd, cos, sin)
    c1 = jnp.where((quadrant == 1) | (quadrant == 2), -c0, c0)
    s1 = jnp.where(quadrant >= 2, -s0, s0)
    return c1, s1


def transform_kernel(peers, parts, group, *refs):
    freq_hbm, weight_hbm, snap_hbm = refs[:3]
    outs, token = refs[-peers * len(parts) - 8 : -8], refs[-8]
    freq, weight, snap, table, wide, small_sem, snap_sem = refs[-7:]
    blocks, length, entries = snap.shape
    steps = blocks // group
    get_freq = pltpu.make_async_copy(freq_hbm, freq, small_sem.at[0])
    get_weight = pltpu.make_async_copy(weight_hbm, weight, small_sem.at[1])
    get_snap = [
        pltpu.make_async_copy(
            snap_hbm.at[pl.ds(i * group, group)], snap.at[pl.ds(i * group, group)], snap_sem.at[i]
        )
        for i in range(steps)
    ]
    token[...] = jnp.zeros_like(token)
    get_freq.start()
    for get in get_snap:
        get.start()
    get_weight.start()

    me = lax.axis_index("tm")
    groups = [
        (peer, first + j)
        for first, count in parts
        for peer in range(peers)
        for j in range(0, count, 8)
    ]
    rows = 8 * len(groups)
    per_peer = freq.shape[0] // peers
    times = lax.broadcasted_iota(jnp.int32, (8, length), 1)
    sub = lax.broadcasted_iota(jnp.int32, (8, length), 0)
    window = 0.5 - 0.5 * cos_sin(times, length)[0]
    scaled = window / F32(math.sqrt(0.375 * length))
    get_freq.wait()

    def eight(index):
        peer, offset = groups[index]
        start = jnp.bitwise_xor(me, peer) * per_peer + offset
        k = jnp.zeros((8, length), jnp.int32)
        for i in range(8):
            k = jnp.where(sub == i, freq[start + i], k)
        cos, sin = cos_sin((k * times) & (length - 1), length)
        return scaled * cos, -(scaled * sin)

    for pair in range(rows // 16):
        re0, im0 = eight(2 * pair)
        re1, im1 = eight(2 * pair + 1)
        table[16 * pair : 16 * pair + 16, :] = jnp.concatenate([re0, re1], 0).astype(BF16)
        table[rows + 16 * pair : rows + 16 * pair + 16, :] = jnp.concatenate(
            [im0, im1], 0
        ).astype(BF16)

    get_weight.wait()
    root = jnp.sqrt(weight[...])
    tiles = entries // LANES
    for step in range(steps):
        get_snap[step].wait()
        for b in range(step * group, (step + 1) * group):
            spec = dot(table[...], snap[b]) * root
            for tile in range(tiles):
                lanes = slice(tile * LANES, (tile + 1) * LANES)
                wide[tile, pl.ds(b, rows, stride=blocks), :] = spec[:rows, lanes]
                wide[tiles + tile, pl.ds(b, rows, stride=blocks), :] = spec[rows:, lanes]
    at = 0
    for out in outs:
        for j in range(out.shape[0]):
            for tile in range(2 * tiles):
                lanes = slice(tile * LANES, (tile + 1) * LANES)
                out[j, :, lanes] = wide[tile, at : at + blocks, :].astype(BF16)
            at += blocks


def transform(snapshots, weight, freq_index, peers, parts, after):
    blocks, length, entries = snapshots.shape
    group = min(blocks, 4)
    total = peers * sum(count for _, count in parts)
    shapes = [
        jax.ShapeDtypeStruct((count, blocks, 2 * entries), BF16)
        for _, count in parts
        for _ in range(peers)
    ]
    hbm = pl.BlockSpec(memory_space=pltpu.HBM)
    out = pl.pallas_call(
        functools.partial(transform_kernel, peers, parts, group),
        in_specs=[hbm] * 3 + [any_spec()] * len(after),
        out_specs=[whole_spec()] * (len(shapes) + 1),
        out_shape=shapes + [TOKEN],
        scratch_shapes=[
            pltpu.SMEM(freq_index.shape, jnp.int32),
            pltpu.VMEM(weight.shape, F32),
            pltpu.VMEM(snapshots.shape, BF16),
            pltpu.VMEM((2 * total, length), BF16),
            pltpu.VMEM((2 * entries // LANES, total * blocks, LANES), F32),
            pltpu.SemaphoreType.DMA((2,)),
            pltpu.SemaphoreType.DMA((blocks // group,)),
        ],
        compiler_params=params(),
        cost_estimate=light(),
        name="transform",
    )(in_hbm(freq_index), in_hbm(weight), in_hbm(snapshots), *after)
    return [out[i * peers : (i + 1) * peers] for i in range(len(parts))], out[-1]


def lane_low(shape, half):
    return lax.broadcasted_iota(jnp.int32, shape, 1) < half


def swap(x):
    return pltpu.roll(x, x.shape[1] // 2, 1)


def each(fn, *lists):
    return [fn(*items) for items in zip(*lists)]


def double(compact):
    return compact + swap(compact)


def pack(both):
    half = both.shape[0]
    low = lane_low((half // 2, 2 * half), half)
    return jnp.where(low, both[: half // 2], both[half // 2 :])


def unpack(packed, scale=None):
    rows, half = packed.shape[0], packed.shape[1] // 2
    low = lane_low(packed.shape, half)
    other = swap(packed)
    both = jnp.concatenate(
        [jnp.where(low, packed, other), jnp.where(low, other, packed)], 0
    )
    turned = jnp.transpose(jnp.concatenate([packed, packed], 0))
    turned = jnp.where(lane_low((half, half), rows), turned[:half], turned[half:])
    turned = jnp.concatenate([turned, turned], 1)
    low = lane_low(both.shape, half)
    total = both + turned
    apart = both - turned
    top = jnp.where(low, total, apart)
    bottom = jnp.where(low, -apart, total)
    scale = F32(0.5) if scale is None else scale
    return scale * top, scale * bottom


def full(compact):
    half = compact.shape[0]
    turned = swap(compact)
    low = lane_low(compact.shape, half)
    return jnp.concatenate([compact, jnp.where(low, -turned, turned)], 0)


TOP = 23169.0
LOG_STEPS = 64.0
FINE = float(2**21)


def place(lines, rows):
    shape = (rows, lines[0].shape[1])
    row = lax.broadcasted_iota(jnp.int32, shape, 0)
    out = jnp.zeros(shape, F32)
    for i, line in enumerate(lines):
        out = jnp.where(row == i, line, out)
    return out


def pad_rows(number):
    return -(-number // 16) * 16


def scale_of(code):
    exponent = jnp.floor(code * F32(1 / 256))
    part = code - exponent * 256
    return (jnp.exp2(exponent) * (1 + part * F32(1 / 128))).astype(BF16)


def outer(scales, number):
    half = scales.shape[1] // 2
    wide = scales.astype(F32)
    row = lax.broadcasted_iota(jnp.int32, scales.shape, 0)
    turned = jnp.transpose(wide)[:half].astype(BF16)
    return [
        dot(turned, jnp.where(row == i, wide, F32(0)).astype(BF16)) for i in range(number)
    ]


def inverse_outer(scales, number):
    half = scales.shape[1] // 2
    rows = scales.shape[0]
    inverse = 1.0 / scales.astype(F32)
    high = inverse.astype(BF16).astype(F32)
    low = inverse - high
    left = jnp.transpose(jnp.concatenate([high, high, low], 0))[:half].astype(BF16)
    right = jnp.concatenate([high, low, high], 0)
    row = lax.broadcasted_iota(jnp.int32, right.shape, 0) & (rows - 1)
    return [
        dot(left, jnp.where(row == i, right, F32(0)).astype(BF16)) for i in range(number)
    ]


def encode(both):
    half, width = both[0].shape
    row = lax.broadcasted_iota(jnp.int32, (half, width), 0)
    lane = lax.broadcasted_iota(jnp.int32, (half, width), 1)
    on = (lane == row) | (lane == row + half)
    diagonal = each(lambda b: jnp.sum(jnp.where(on, b, F32(0)), axis=0, keepdims=True), both)
    root = jnp.sqrt(jnp.maximum(place(diagonal, pad_rows(len(both))), F32(1e-36)))
    exponent = jnp.floor(jnp.log(root) * F32(1 / math.log(2.0)))
    part = jnp.maximum(jnp.ceil((root * jnp.exp2(-exponent) - 1) * 128), F32(0))
    codes = exponent * 256 + part
    scales = scale_of(codes)
    inverse = inverse_outer(scales, len(both))
    value = each(lambda b, p: jnp.round((b * F32(TOP)) * p), both, inverse)
    return each(lambda v: pack(jnp.clip(v, F32(-32767), F32(32767))), value), codes, scales


def spread(values, codes):
    products = outer(scale_of(codes), len(values))
    return each(lambda v, p: (v * F32(1 / TOP)) * pack(p), values, products)


def to_short(x):
    return x.astype(jnp.int32).astype(jnp.int16)


def from_short(x):
    return x.astype(jnp.int32).astype(F32)


def coded_rows(number, half_rows):
    return number * half_rows + pad_rows(number)


def write_coded(out, values, codes):
    half_rows = values[0].shape[0]
    for i, value in enumerate(values):
        out[i * half_rows : (i + 1) * half_rows, :] = to_short(value)
    out[len(values) * half_rows :, :] = to_short(codes)


def read_coded(ref, number, half_rows):
    codes = from_short(ref[number * half_rows :, :])
    values = [from_short(ref[i * half_rows : (i + 1) * half_rows, :]) for i in range(number)]
    return values, codes


def slot_owner(direct, slot):
    return jnp.bitwise_xor(lax.axis_index("space") & 1, slot) if direct else slot


def gram_kernel(peers, slots, direct, after, *refs):
    pieces, refs = refs[:peers], refs[peers + after :]
    merged, token, grams = refs[0], refs[1], refs[2:]
    token[...] = jnp.zeros_like(token)
    me = lax.axis_index("tm")
    here = pieces[0].shape[1]
    entries = pieces[0].shape[2] // 2
    blocks = here * peers
    per_slot = pieces[0].shape[0] // slots
    stage = None
    if here % 16:
        grams, stage = grams[:-1], grams[-1]
    low = lane_low((blocks, 2 * blocks), blocks)
    for slot in range(slots):
        owner = slot_owner(direct, slot)
        coded = []
        for i in range(per_slot):
            f = owner * per_slot + i
            if stage is None:
                for peer in range(peers):
                    start = pl.multiple_of(jnp.bitwise_xor(me, peer) * here, here)
                    merged[f, pl.ds(start, here), :] = pieces[peer][f]
                z = merged[f]
            else:
                for peer in range(peers):
                    start = pl.multiple_of(jnp.bitwise_xor(me, peer) * here, here)
                    stage[pl.ds(start, here), :] = pieces[peer][f].astype(F32)
                z = stage[...].astype(BF16)
                merged[f] = z
            w = jnp.concatenate([z[:, :entries], z[:, entries:]], 0)
            s = lax.dot_general(w, w, (((1,), (1,)), ((), ())), preferred_element_type=F32)
            s = s * F32(1.0 / blocks)
            top, bottom = s[:blocks], swap(s[blocks:])
            compact = jnp.where(low, top + bottom, top - bottom)
            if direct and slot == 0 and grams[0].dtype == F32:
                grams[0][i] = compact
            elif direct:
                coded.append(double(compact))
            else:
                grams[0][f] = pack(double(compact))
        if coded:
            write_coded(grams[slot], *encode(coded)[:2])


def gram(pieces, slots, direct, in_steps, after):
    peers = len(pieces)
    count, here, width = pieces[0].shape
    blocks = here * peers
    if direct:
        rows = coded_rows(count // slots, blocks // 2)
        shapes = [((rows, 2 * blocks), jnp.int16)] * slots
        if in_steps:
            shapes[0] = ((count // slots, blocks, 2 * blocks), F32)
    else:
        shapes = [((count, blocks // 2, 2 * blocks), F32)]
    out = pl.pallas_call(
        functools.partial(gram_kernel, peers, slots, direct, len(after)),
        in_specs=[whole_spec()] * peers + [any_spec()] * len(after),
        out_specs=[whole_spec()] * (2 + len(shapes)),
        out_shape=[jax.ShapeDtypeStruct((count, blocks, width), BF16), TOKEN]
        + [jax.ShapeDtypeStruct(*s) for s in shapes],
        scratch_shapes=[pltpu.VMEM((blocks, width), F32)] if here % 16 else [],
        compiler_params=params(),
        cost_estimate=light(),
        name="gram",
    )(*pieces, *after)
    return out[0], out[2:], out[1]


def add_kernel(own, other, *refs):
    out, token = refs[-2:]
    token[...] = jnp.zeros_like(token)
    number, blocks, _ = own.shape
    received = spread(*read_coded(other, number, blocks // 2))
    sums = [double(own[i] + unpack(received[i])[0]) for i in range(number)]
    write_coded(out, *encode(sums)[:2])


def add(own, other, after):
    return pl.pallas_call(
        add_kernel,
        in_specs=[whole_spec()] * 2 + [any_spec()] * len(after),
        out_specs=[whole_spec()] * 2,
        out_shape=[jax.ShapeDtypeStruct(other.shape, jnp.int16), TOKEN],
        compiler_params=params(),
        cost_estimate=light(),
        name="add",
    )(own, other, *after)


def split(x):
    high = x.astype(BF16)
    return high, (x - high.astype(F32)).astype(BF16)


def solve_kernel(chunks, half_rows, before, *refs):
    out, token = refs[-2:]
    puts = []
    if before is not None:
        energies_out, filters_out, out, token, sem = refs[-5:]
        inputs = sum(parts for parts, _ in chunks)
        for i, target in enumerate((energies_out, filters_out)):
            source = refs[inputs + i]
            put = pltpu.make_async_copy(
                source, target.at[pl.ds(before, source.shape[0])], sem.at[i]
            )
            put.start()
            puts.append(put)
    token[...] = jnp.zeros_like(token)
    width = out.shape[1]
    half = width // 2
    shape = (half, width)
    row = lax.broadcasted_iota(jnp.int32, shape, 0)
    lane = lax.broadcasted_iota(jnp.int32, shape, 1)
    eye = jnp.where(row == lane, F32(1), F32(0))

    sums, at = [], 0
    for parts, count in chunks:
        ins, at = refs[at : at + parts], at + parts
        if parts == 1:
            sums += [ins[0][i] for i in range(count)]
            continue
        found = [spread(*read_coded(r, count, half_rows)) for r in ins]
        added = each(lambda p, q: p + q, found[0], found[1])
        if parts == 4:
            added = each(lambda p, q, r: p + (q + r), added, found[2], found[3])
        sums += added
    number = len(sums)
    both_halves = each(unpack, sums)
    grams = [h[0] for h in both_halves]
    spots = lax.broadcasted_iota(jnp.int32, sums[0].shape, 1)
    lines = lax.broadcasted_iota(jnp.int32, sums[0].shape, 0)
    on = (spots == lines) | (spots == lines + 3 * half_rows)
    shift = each(
        lambda p: jnp.sum(jnp.where(on, p, F32(0)), keepdims=True) * F32(1.0 / half), sums
    )
    eye_low = jnp.where(row + half == lane, F32(1), F32(0))
    inverse = each(lambda m: 1.0 / m, shift)
    system = each(lambda g, m: g * m + eye, grams, inverse)
    under = each(lambda h, m: h[1] * m + eye_low, both_halves, inverse)
    both = each(
        lambda a, u: jnp.concatenate(split(jnp.concatenate([a, u], 0)), 1), system, under
    )

    def times(v, a):
        wide = dot(v, a)
        return wide[:, :width] + wide[:, width:]


    low_end, high_end = 1.0, float(half + 1)
    mid, radius = (high_end + low_end) / 2, (high_end - low_end) / 2
    ratio = mid / radius
    t = 2 * ratio * ratio - 1
    scale = 2.0 / (radius * radius * t)
    x = each(lambda a: (F32(scale) * (F32(2 * mid) * eye - a)).astype(BF16), system)
    p = each(lambda v, a: eye - times(v, a), x, both)
    x = each(lambda v: v.astype(F32), x)
    for _ in range(3):
        t_next = 2 * t * t - 1
        c = F32(2 * t * t / t_next)
        pf = each(lambda q: full(q).astype(BF16), p)
        xp = each(lambda v, q: jnp.concatenate([v, q], 0).astype(BF16), x, p)
        moved = each(dot, xp, pf)
        x = each(lambda v, m: c * (v + m[:half]), x, moved)
        p = each(lambda m: c * m[half:] - F32(1 / t_next) * eye, moved)
        t = t_next
    for kind in ("scaled", "last"):
        xb = each(lambda v: v.astype(BF16), x)
        xw = each(lambda v: v.astype(F32), xb)
        xf = each(lambda v: full(v).astype(BF16), xw)
        residual = each(lambda v, a: eye - times(v, a), xb, both)
        step = each(lambda r, v: dot(r.astype(BF16), v), residual, xf)
        factor = 1.0 if kind == "last" else 2 * t * t / (2 * t * t - 1)
        x = each(lambda v, m: F32(factor) * (v + m), xw, step)
    values, codes, scales = encode(each(lambda v: double(eye - v), x))
    products = outer(scales, number)
    filters = each(lambda v, p: unpack(v * F32(0.5 / TOP), p), values, products)
    rounded = each(lambda c: c[0].astype(BF16), filters)
    turned = each(
        lambda c: jnp.concatenate([c[0].astype(BF16), c[1].astype(BF16)], 0), filters
    )
    split_g = each(lambda g: jnp.concatenate(split(g), 0), grams)
    moved = each(dot, split_g, turned)
    moved = each(lambda m: m[:half] + m[half:], moved)
    energy = each(
        lambda c, h: jnp.sum(c.astype(F32) * h, keepdims=True) * F32(half), rounded, moved
    )
    energy = place([jnp.broadcast_to(e, (1, width)) for e in energy], codes.shape[0])
    energy = jnp.maximum(energy, F32(1e-36))
    whole = jnp.floor(jnp.log(energy) * F32(LOG_STEPS / math.log(2.0)))
    rest = jnp.round((energy * jnp.exp2(whole * F32(-1 / LOG_STEPS)) - 1.0) * F32(FINE))
    spot = lax.broadcasted_iota(jnp.int32, codes.shape, 1)
    codes = jnp.where(spot == half, whole, jnp.where(spot == half + 1, rest, codes))
    write_coded(out, values, codes)
    for put in puts:
        put.wait()


def solve(chunks, half_rows, earlier, owned, after):
    args = [x for parts, _ in chunks for x in parts]
    width = args[0].shape[-1]
    number = sum(count for _, count in chunks)
    shape = [(len(parts), count) for parts, count in chunks]
    results = list(earlier[:2]) if earlier else []
    hbm = pl.BlockSpec(memory_space=pltpu.HBM)
    out = pl.pallas_call(
        functools.partial(solve_kernel, shape, half_rows, earlier[2] if earlier else None),
        in_specs=[whole_spec()] * (len(args) + len(results)) + [any_spec()] * len(after),
        out_specs=[hbm] * len(results) + [whole_spec()] * 2,
        out_shape=[jax.ShapeDtypeStruct((owned, *r.shape[1:]), F32) for r in results]
        + [
            jax.ShapeDtypeStruct((coded_rows(number, half_rows), width), jnp.int16),
            TOKEN,
        ],
        scratch_shapes=[pltpu.SemaphoreType.DMA((2,))] if results else [],
        compiler_params=params(),
        cost_estimate=light(),
        name="filters",
    )(*args, *results, *after)
    return out[-2], out[-1], list(out[:2]) if results else None


def energy_kernel(slots, direct, number, chunks, first, before, last, *refs):
    merged, pieces = refs[:chunks], refs[chunks : chunks + number]
    earlier = refs[chunks + number : chunks + number + 2]
    puts = []
    if last:
        energies_out, filters_out, token, energies, filters = refs[-8:-3]
    else:
        energies, filters, token = refs[-6:-3]
        if before is not None:
            energies_out, filters_out = refs[-8:-6]
    energies_sem, filters_sem, before_sem = refs[-3:]
    if before is not None:
        for i, (source, target) in enumerate(zip(earlier, (energies_out, filters_out))):
            put = pltpu.make_async_copy(
                source, target.at[pl.ds(before, source.shape[0])], before_sem.at[i]
            )
            put.start()
            puts.append(put)
    own_puts = 0
    token[...] = jnp.zeros_like(token)
    blocks, width = merged[0].shape[1:]
    entries = width // 2
    counts = [m.shape[0] for m in merged]
    per_slot = sum(counts) // slots
    half_rows = blocks // 2
    states = entries * lax.axis_size("space")
    for slot in range(slots):
        owner = slot_owner(direct, slot)
        piece = pieces[slot] if direct else pieces[0].at[slot]
        values, codes = read_coded(piece, per_slot, half_rows)
        whole = codes[:, blocks : blocks + 1]
        rest = codes[:, blocks + 1 : blocks + 2]
        total = jnp.exp2(whole * F32(1 / LOG_STEPS)) * (1.0 + rest * F32(1 / FINE))
        gains = F32(states) / total
        codes = jnp.where(lane_low(codes.shape, blocks), codes, swap(codes))
        products = outer(scale_of(codes), per_slot)
        base = 0
        for chunk, count in enumerate(counts):
            own = count // slots
            size = 4 if own % 4 == 0 else 1
            for begin in range(0, own, size):
                start = sum(counts[:chunk]) + owner * own + begin
                some = range(base + begin, base + begin + size)
                z = [merged[chunk][owner * own + begin + i] for i in range(size)]
                scale = [products[i] for i in some]
                halves = each(unpack, [values[i] * F32(0.5 / TOP) for i in some], scale)
                both = each(
                    lambda h: jnp.concatenate([h[0].astype(BF16), h[1].astype(BF16)], 0), halves
                )
                w = each(lambda v: jnp.concatenate([v[:, :entries], v[:, entries:]], 0), z)
                r = each(dot, both, w)
                gain = [gains[i : i + 1] for i in some]
                energy = each(
                    lambda v, t: jnp.sum(v * v, axis=0, keepdims=True) * t, r, gain
                )
                for i in range(size):
                    filters[start + i, 0] = halves[i][0][:, :blocks]
                    filters[start + i, 1] = -halves[i][1][:, :blocks]
                    energies[pl.ds(start + i, 1), :] = energy[i]
                if last:
                    put = pltpu.make_async_copy(
                        filters.at[pl.ds(start, size)],
                        filters_out.at[pl.ds(first + start, size)],
                        filters_sem.at[own_puts],
                    )
                    put.start()
                    puts.append(put)
                    own_puts += 1
            base += own
    if last:
        put = pltpu.make_async_copy(
            energies, energies_out.at[pl.ds(first, sum(counts))], energies_sem.at[0]
        )
        put.start()
        puts.append(put)
    for put in puts:
        put.wait()


def filtered(merged, pieces, slots, direct, earlier, carry, owned, first, last, after):
    _, blocks, width = merged[0].shape
    count = sum(m.shape[0] for m in merged)
    copies = sum(slots * (m.shape[0] // slots) for m in merged)
    entries = width // 2
    fixed = len(merged) + len(pieces) + (2 if earlier else 0)
    args = [*merged, *pieces, *(earlier[:2] if earlier else ()), *(carry or ()), *after]
    hbm = pl.BlockSpec(memory_space=pltpu.HBM)
    writes = bool(earlier) or last
    own = [
        jax.ShapeDtypeStruct((count, entries), F32),
        jax.ShapeDtypeStruct((count, 2, blocks, blocks), F32),
    ]
    whole = [
        jax.ShapeDtypeStruct((owned, entries), F32),
        jax.ShapeDtypeStruct((owned, 2, blocks, blocks), F32),
    ]
    scratch = [pltpu.VMEM(o.shape, F32) for o in own] if last else []
    out = pl.pallas_call(
        functools.partial(
            energy_kernel, slots, direct, len(pieces), len(merged), first,
            earlier[2] if earlier else None, last,
        ),
        in_specs=[whole_spec()] * fixed
        + ([hbm] * 2 if carry else [])
        + [any_spec()] * len(after),
        out_specs=([hbm] * 2 if writes else [])
        + ([] if last else [whole_spec()] * 2)
        + [whole_spec()],
        out_shape=(whole if writes else []) + ([] if last else own) + [TOKEN],
        input_output_aliases={fixed: 0, fixed + 1: 1} if carry else {},
        scratch_shapes=scratch
        + [
            pltpu.SemaphoreType.DMA((1,)),
            pltpu.SemaphoreType.DMA((copies,)),
            pltpu.SemaphoreType.DMA((2,)),
        ],
        compiler_params=params(),
        cost_estimate=light(),
        name="energy",
    )(*args)
    carry = list(out[:2]) if writes else None
    earlier = None if last else (*out[-3:-1], first)
    return carry, earlier, out[-1]


def plan(owned, slots):
    if slots != 4 or owned != 64:
        return [owned], (("T", 0), ("G", 0), ("F", 0), ("E", 0))
    return SIZES, ORDER


SIZES = [24, 24, 16]
ORDER = (
    ("T", 0), ("T", 1), ("G", 0), ("A", 0), ("G", 1), ("F", 0), ("A", 1), ("G", 2),
    ("E", 0), ("F", 1), ("F", 2), ("E", 1), ("E", 2),
)


TIES = {("T", 1): (0,)}


def permute(x, axis, offset):
    pairs = [(i, i ^ offset) for i in range(lax.axis_size(axis))]
    return lax.ppermute(x, axis, pairs)


def on_device(snapshots, entry_weight, freq_index):
    peers = lax.axis_size("tm")
    slots = lax.axis_size("space")
    owned = freq_index.shape[0] // peers
    sizes, order = plan(owned, slots)
    starts = [sum(sizes[:c]) for c in range(len(sizes))]
    paired = slots == 4
    halves = 2 if paired else slots
    weight = entry_weight.reshape(1, -1)
    sent, merged, grams, parts, pieces = {}, {}, {}, {}, {}
    carry = None
    earlier = None
    token = []

    def do_transform(c):
        nonlocal token
        joint = [k for k in range(c, len(sizes)) if k == c or c and ("T", k) not in order]
        out, done = transform(
            snapshots, weight, freq_index, peers, [(starts[k], sizes[k]) for k in joint], token
        )
        token = [done]
        for k, own in zip(joint, out):
            sent[k] = [own[0]] + [permute(own[i], "tm", i) for i in range(1, peers)]

    def do_gram(c):
        nonlocal token
        in_steps = paired and ("A", c) in order
        merged[c], grams[c], done = gram(sent[c], halves, paired, in_steps, token)
        token = [done]
        if in_steps:
            grams[c] = [grams[c][0], permute(grams[c][1], "space", 1)]
        elif paired:
            own, other = grams[c]
            parts[c] = [
                own,
                permute(own, "space", 2),
                permute(other, "space", 1),
                permute(other, "space", 3),
            ]
        else:
            parts[c] = [lax.psum_scatter(grams[c][0], "space", scatter_dimension=0, tiled=True)]

    def do_add(c):
        nonlocal token
        half, done = add(*grams[c], token)
        token = [done]
        parts[c] = [half, permute(half, "space", 2)]

    def joined(stage, c):
        last = c + 1
        while last < len(sizes) and (stage, last) not in order:
            last += 1
        return range(c, last)

    def do_solve(c):
        nonlocal token, carry, earlier
        work = [(parts[k], sizes[k] // halves) for k in joined("F", c)]
        own, done, written = solve(work, merged[c].shape[1] // 2, earlier, owned, token)
        if written:
            carry, earlier = written, None
        token = [done]
        if paired:
            pieces[c] = [own, permute(own, "space", 1)]
        else:
            pieces[c] = [lax.all_gather(own, "space", axis=0, tiled=False)]

    def do_energy(c):
        nonlocal token, carry, earlier
        chunks = joined("E", c)
        copies = chunks[-1] == len(sizes) - 1
        written, earlier, done = filtered(
            [merged[k] for k in chunks], pieces[c], halves, paired, earlier,
            carry if copies or earlier else None, owned, starts[c], copies, token,
        )
        carry = written or carry
        token = [done]

    stages = {"T": do_transform, "G": do_gram, "A": do_add, "F": do_solve, "E": do_energy}
    for stage, c in order:
        token = token + [sent[k][1] for k in TIES.get((stage, c), ()) if k in sent]
        stages[stage](c)
    return (carry[0], carry[1])


def solution(mesh):
    in_specs = (P(("grp", "tm"), None, "space"), P(("grp", "space")), P())
    out_specs = (P(("grp", "tm"), "space"), P(("grp", "tm"), None, None, None))
    return jax.shard_map(
        on_device, mesh=mesh, in_specs=in_specs, out_specs=out_specs, check_vma=False
    )
```
